32 devices in a mesh: seq: 16 (over z, y, x), chan: 2 (over core).
Axes of the slice: x: 2, y: 2, z: 4, core: 2. Of those that a mesh axis runs over, the one named last changes fastest.
Arguments:
- values: bfloat16 [4096, 4096], P('seq', 'chan'), may hold values from -6 to 6
- gates: bfloat16 [4096, 4096], P('seq', 'chan'), may hold values from -144 to 144
- filter_taps: bfloat16 [4096, 4096], P('seq', 'chan'), may hold values from -0.0625 to 0.0625, as said below
- skip_gain: float32 [4096], P('chan'), may hold values from -0.125 to 0.125
- out_weight: bfloat16 [4096, 2048], P('chan'), may hold values from -0.09375 to 0.09375
Outputs:
- projected: bfloat16 [2048, 4096], P('chan', 'seq')
The draws below stay inside these ranges and needn't reach their ends.
Inputs may be any that keep to these rules, and one draw needn't show every extreme that they name: `filter_taps`: a causal filter for each channel.
All inputs are finite; a program needn't handle non-finite values.
Results may differ from the reference program's by a relative error of at most 0.0049.
Values may be sent and summed in bfloat16 or wider, within the bound.
No kernel may reach another device: no remote copies, remote signals or barrier semaphores. Data moves between devices by JAX's collectives and lax.ppermute only.
A program may use at most 128 MiB of HBM per device.

```python
import math
import jax
import jax.numpy as jnp
from jax import lax

D = 4096
DOUT = 2048
TOK_DEV = 256
TOKENS = 4096


tap_level = 0.03125


def draw_filter_taps(key, part):
    keys = jax.random.split(jax.random.fold_in(key, 17), 6)
    lag_blocks = TOKENS // TOK_DEV
    steps = jnp.arange(TOKENS, dtype=jnp.float32)[:, None]
    fast_tau = jnp.exp(jax.random.uniform(keys[0], (1, D), jnp.float32, math.log(30.0), math.log(TOKENS / 8.0)))
    fast_noise = jax.random.truncated_normal(keys[3], -4.0, 4.0, (TOKENS, D), jnp.float32)
    base_noise = jax.random.truncated_normal(keys[4], -4.0, 4.0, (TOKENS, D), jnp.float32)
    share = jnp.exp(jax.random.uniform(keys[1], (1, D), jnp.float32, math.log(0.1), math.log(0.5)))
    slow_tau = jnp.exp(jax.random.uniform(keys[2], (1, D), jnp.float32, math.log(0.5 * TOKENS), math.log(4.0 * TOKENS)))
    slow_noise = base_noise
    fast = jnp.exp(-steps / fast_tau) * jnp.sqrt(2.0 / fast_tau) * fast_noise
    slow = jnp.exp(-steps / slow_tau) * jnp.sqrt(2.0 / slow_tau) * slow_noise
    mixed = jnp.sqrt(1.0 - share) * fast + jnp.sqrt(share) * slow
    levels = jnp.exp(jax.random.uniform(keys[5], (lag_blocks, 1, D), jnp.float32, -0.5, 0.5))
    taps = (mixed.reshape(lag_blocks, TOK_DEV, D) * levels).reshape(TOKENS, D) * tap_level
    return taps.astype(jnp.bfloat16)


def shard_levels(stream_key, extent, cuts, least, top_value):
    gain, own = 1.0, jax.random.fold_in(stream_key, 6)
    for dim, blocks in cuts:
        draws = jnp.exp(jax.random.uniform(jax.random.fold_in(own, dim), (blocks,), jnp.float32, least / len(cuts), top_value / len(cuts)))
        gain = gain * jnp.repeat(draws, extent[dim] // blocks).reshape([-1 if axis == dim else 1 for axis in range(len(extent))])
    return gain


def bell_draw(key, extent, scale, reach, cuts=(), held_as=jnp.bfloat16):
    values = scale * jax.random.normal(key, extent, jnp.float32)
    if cuts:
        values = values * shard_levels(key, extent, cuts, -0.22, 0.18)
    return jnp.clip(values, -reach, reach).astype(held_as)


def setup_inputs(seed: int = 0) -> dict:
    splits = jax.random.split(jax.random.key(seed), 6)
    values = bell_draw(splits[0], (TOKENS, D), 1.0, 6.0, ((0, 16), (1, 2)))
    gates = bell_draw(splits[1], (TOKENS, D), 24.0, 144.0, ((0, 16), (1, 2)))
    filter_taps = draw_filter_taps(jax.random.fold_in(splits[5], 71), 0)
    skip_gain = bell_draw(splits[3], (D,), 0.03125, 0.125, ((0, 2),), jnp.float32)
    out_weight = bell_draw(splits[4], (D, DOUT), D ** -0.5, 0.09375, ((0, 2),))
    return {"values": values, "gates": gates, "filter_taps": filter_taps, "skip_gain": skip_gain, "out_weight": out_weight}


def reference(values, gates, filter_taps, skip_gain, out_weight):
    length = values.shape[0]
    width = values.shape[1]
    blocks = width // 128
    value_blocks = jnp.moveaxis(values.astype(jnp.float32).reshape(length, blocks, 128), 1, 0)
    filter_blocks = jnp.moveaxis(filter_taps.astype(jnp.float32).reshape(length, blocks, 128), 1, 0)

    def convolve(pair):
        signal, taps = pair
        signal_freq = jnp.fft.rfft(signal, n=2 * length, axis=0)
        taps_freq = jnp.fft.rfft(taps, n=2 * length, axis=0)
        return jnp.fft.irfft(signal_freq * taps_freq, n=2 * length, axis=0)[:length]

    conv_blocks = lax.map(convolve, (value_blocks, filter_blocks))
    conv = jnp.moveaxis(conv_blocks, 0, 1).reshape(length, width).astype(jnp.float32)
    gated = (gates.astype(jnp.float32) * (conv + skip_gain[None, :] * values.astype(jnp.float32))).astype(jnp.bfloat16)
    projected = lax.dot_general(out_weight, gated, (((0,), (1,)), ((), ())), preferred_element_type=jnp.float32)
    return projected.astype(jnp.bfloat16)
```

```python
import functools
import math

import jax
import jax.numpy as jnp
import ml_dtypes
import numpy as np
from jax import lax
from jax.experimental import pallas as pl
from jax.experimental.pallas import tpu as pltpu
from jax.sharding import PartitionSpec as P

TWO_PI = 2.0 * math.pi
HIGH = lax.Precision.HIGHEST
RADIX = 16
LANES = 128
VMEM_BYTES = 56 * 1024 * 1024


def angle_table(first, second, period):
    product = first[:, None] * second[None, :] % period
    angles = product.astype(jnp.float32) * (TWO_PI / period)
    return (jnp.cos(angles), jnp.sin(angles))


def mix(equation, left, right):
    return jnp.einsum(equation, left, right, precision=HIGH)


def outer_forward(data, outer_cos, outer_sin, twist_cos, twist_sin, equation):
    source = data.astype(jnp.float32)
    real = mix(equation, outer_cos, source)
    imag = -mix(equation, outer_sin, source)
    cos_part = twist_cos[:, :, None]
    sin_part = twist_sin[:, :, None]
    return (real * cos_part + imag * sin_part, imag * cos_part - real * sin_part)


def inner_filter(spectra, inner_cos, inner_sin):
    value_re, value_im, taps_re, taps_im = spectra

    def forward(real, imag):
        out_re = mix("kr,jrc->jkc", inner_cos, real) + mix("kr,jrc->jkc", inner_sin, imag)
        out_im = mix("kr,jrc->jkc", inner_cos, imag) - mix("kr,jrc->jkc", inner_sin, real)
        return (out_re, out_im)

    value_fre, value_fim = forward(value_re, value_im)
    taps_fre, taps_fim = forward(taps_re, taps_im)
    prod_re = value_fre * taps_fre - value_fim * taps_fim
    prod_im = value_fre * taps_fim + value_fim * taps_fre
    back_re = mix("rk,jkc->jrc", inner_cos, prod_re) - mix("rk,jkc->jrc", inner_sin, prod_im)
    back_im = mix("rk,jkc->jrc", inner_cos, prod_im) + mix("rk,jkc->jrc", inner_sin, prod_re)
    return (back_re, back_im)


def untwist(real, imag, twist_cos, twist_sin):
    cos_part = twist_cos[:, :, None]
    sin_part = twist_sin[:, :, None]
    return (real * cos_part - imag * sin_part, imag * cos_part + real * sin_part)


def channels_plan(values, filter_taps):
    rows, width = values.shape
    blocks = lax.axis_size("seq")
    length = 2 * blocks * rows
    narrow = width // blocks
    whole_values, whole_taps = (
        lax.all_to_all(values, "seq", split_axis=1, concat_axis=0, tiled=True),
        lax.all_to_all(filter_taps, "seq", split_axis=1, concat_axis=0, tiled=True),
    )
    freq_ids = jnp.arange(2 * blocks, dtype=jnp.int32)
    block_ids = jnp.arange(blocks, dtype=jnp.int32)
    all_rows = jnp.arange(rows, dtype=jnp.int32)
    outer_cos, outer_sin = angle_table(freq_ids, block_ids, 2 * blocks)
    twist_cos, twist_sin = angle_table(freq_ids, all_rows, length)
    tables = (outer_cos, outer_sin, twist_cos, twist_sin, "ka,arc->krc")
    value_re, value_im = outer_forward(whole_values.reshape(blocks, rows, narrow), *tables)
    taps_re, taps_im = outer_forward(whole_taps.reshape(blocks, rows, narrow), *tables)
    inner_cos, inner_sin = angle_table(all_rows, all_rows, rows)
    back_re, back_im = inner_filter((value_re, value_im, taps_re, taps_im), inner_cos, inner_sin)
    turned_re, turned_im = untwist(back_re, back_im, twist_cos, twist_sin)
    final_cos, final_sin = angle_table(block_ids, freq_ids, 2 * blocks)
    signal = (
        mix("ak,krc->arc", final_cos, turned_re) - mix("ak,krc->arc", final_sin, turned_im)
    ) / length
    returned = lax.all_to_all(signal, "seq", split_axis=0, concat_axis=2, tiled=True)
    return returned[0]


def general_local(values, gates, filter_taps, skip_gain, out_weight):
    conv = channels_plan(values, filter_taps)
    gated = (
        gates.astype(jnp.float32) * (conv + skip_gain[None, :] * values.astype(jnp.float32))
    ).astype(jnp.bfloat16)
    projected = lax.psum_scatter(
        lax.dot_general(
            out_weight, gated, (((0,), (1,)), ((), ())), preferred_element_type=jnp.float32
        ),
        "chan",
        scatter_dimension=0,
        tiled=True,
    )
    return projected.astype(jnp.bfloat16)


def split_table(table):
    high = table.astype(ml_dtypes.bfloat16)
    low = (table - high.astype(np.float64)).astype(ml_dtypes.bfloat16)
    return high, low


@functools.lru_cache(maxsize=None)
def transform_tables(length):
    inner = length // RADIX
    q = np.arange(RADIX)[:, None, None]
    k = np.arange(inner)[None, :, None]
    m = np.arange(inner)[None, None, :]
    phase = ((RADIX * m + q) * (4 * k + 1)) % (4 * length)
    angles = phase * (TWO_PI / (4 * length))
    table = np.concatenate([np.cos(angles), -np.sin(angles)], axis=1)
    forward = np.stack(split_table(table), axis=1)
    backward = np.stack(split_table(table.transpose(0, 2, 1) / length), axis=1)
    return forward, backward


@functools.lru_cache(maxsize=None)
def row_order(rows):
    chunk = rows // RADIX
    order = np.zeros((rows, rows), np.float32)
    for q in range(RADIX):
        for j in range(chunk):
            order[q * chunk + j, RADIX * j + q] = 1.0
    return order.astype(ml_dtypes.bfloat16)


def turn(point, index, sign):
    re, im = point
    index %= 16
    if index == 0:
        return point
    if index == 4:
        return (-im, re) if sign > 0 else (im, -re)
    if index == 8:
        return (-re, -im)
    half = math.sqrt(0.5)
    if index == 2:
        return ((re - im) * half, (re + im) * half) if sign > 0 else ((re + im) * half, (im - re) * half)
    if index == 6:
        return ((-re - im) * half, (re - im) * half) if sign > 0 else ((im - re) * half, (-re - im) * half)
    cos = math.cos(TWO_PI * index / 16)
    sin = sign * math.sin(TWO_PI * index / 16)
    return (re * cos - im * sin, re * sin + im * cos)


def four_points(points, sign):
    a, b, c, d = points
    ac = (a[0] + c[0], a[1] + c[1])
    am = (a[0] - c[0], a[1] - c[1])
    bd = (b[0] + d[0], b[1] + d[1])
    bm = (b[0] - d[0], b[1] - d[1])
    if sign < 0:
        side = (bm[1], -bm[0])
    else:
        side = (-bm[1], bm[0])
    return (
        (ac[0] + bd[0], ac[1] + bd[1]),
        (am[0] + side[0], am[1] + side[1]),
        (ac[0] - bd[0], ac[1] - bd[1]),
        (am[0] - side[0], am[1] - side[1]),
    )


def sixteen_points(points, sign):
    out = [None] * 16
    columns = []
    for low in range(4):
        column = four_points([points[low + 4 * high] for high in range(4)], sign)
        columns.append([turn(column[k], low * k, sign) for k in range(4)])
    for k in range(4):
        row = four_points([columns[low][k] for low in range(4)], sign)
        for high in range(4):
            out[k + 4 * high] = row[high]
    return out


def arrange_kernel(group, order_ref, values_ref, taps_ref, out_ref):
    order = order_ref[...]
    for index, source in enumerate((values_ref, taps_ref)):
        moved = jnp.dot(order, source[...], preferred_element_type=jnp.float32).astype(jnp.bfloat16)
        for part in range(group):
            out_ref[part, index] = moved[:, part * LANES : (part + 1) * LANES]


def arrange(values, taps, blocks):
    rows, width = values.shape
    group = 4
    return pl.pallas_call(
        functools.partial(arrange_kernel, group),
        grid=(blocks // group,),
        out_shape=jax.ShapeDtypeStruct((blocks, 2, rows, LANES), jnp.bfloat16),
        in_specs=[
            pl.BlockSpec((rows, rows), lambda i: (0, 0)),
            pl.BlockSpec((rows, group * LANES), lambda i: (0, i)),
            pl.BlockSpec((rows, group * LANES), lambda i: (0, i)),
        ],
        out_specs=pl.BlockSpec((group, 2, rows, LANES), lambda i: (i, 0, 0, 0)),
        compiler_params=pltpu.CompilerParams(vmem_limit_bytes=VMEM_BYTES),
        name="arrange_rows",
    )(jnp.asarray(row_order(rows)), values, taps)


def convolve_kernel(step_q, steps, streams_ref, forward_ref, backward_ref, out_ref, spectra):
    phase, step = pl.program_id(0), pl.program_id(1)
    blocks, _, _, chunk, lanes = streams_ref.shape
    inner = blocks * chunk
    half = inner

    @pl.when(phase == 0)
    def _():
        for part in range(step_q):
            q = step * step_q + part
            value = streams_ref[:, 0, pl.ds(q, 1), :, :].reshape(inner, lanes)
            taps = streams_ref[:, 1, pl.ds(q, 1), :, :].reshape(inner, lanes)
            pair = jnp.concatenate([value, taps], axis=1)
            spectra[q] = jnp.dot(
                forward_ref[part, 0], pair, preferred_element_type=jnp.float32
            ) + jnp.dot(forward_ref[part, 1], pair, preferred_element_type=jnp.float32)

    @pl.when((phase == 0) & (step == steps - 1))
    def _():
        def rows_step(index, carry):
            upper = pl.ds(pl.multiple_of(index * 8, 8), 8)
            lower = pl.ds(pl.multiple_of(half + index * 8, 8), 8)
            left, right = pl.ds(0, lanes), pl.ds(lanes, lanes)
            value = sixteen_points(
                [(spectra[q, upper, left], spectra[q, lower, left]) for q in range(RADIX)], -1
            )
            taps = sixteen_points(
                [(spectra[q, upper, right], spectra[q, lower, right]) for q in range(RADIX)], -1
            )
            product = [
                (a[0] * b[0] - a[1] * b[1], a[0] * b[1] + a[1] * b[0]) for a, b in zip(value, taps)
            ]
            back = sixteen_points(product, 1)
            for q in range(RADIX):
                spectra[q, upper, left] = back[q][0]
                spectra[q, lower, left] = back[q][1]
            return carry

        lax.fori_loop(0, half // 8, rows_step, 0)

    @pl.when(phase == 1)
    def _():
        for part in range(step_q):
            q = step * step_q + part
            points = spectra[q, :, pl.ds(0, lanes)]
            high = points.astype(jnp.bfloat16)
            low = (points - high.astype(jnp.float32)).astype(jnp.bfloat16)
            both = jnp.dot(
                backward_ref[part, 0],
                jnp.concatenate([high, low], axis=1),
                preferred_element_type=jnp.float32,
            )
            signal = (
                both[:, :lanes]
                + both[:, lanes:]
                + jnp.dot(backward_ref[part, 1], high, preferred_element_type=jnp.float32)
            )
            out_ref[:, part] = signal.astype(jnp.bfloat16).reshape(blocks, chunk, lanes)


def convolve(streams, blocks, rows):
    length = blocks * rows
    chunk = rows // RADIX
    inner = length // RADIX
    forward, backward = transform_tables(length)
    step_q = 2
    steps = RADIX // step_q
    return pl.pallas_call(
        functools.partial(convolve_kernel, step_q, steps),
        grid=(2, steps),
        out_shape=jax.ShapeDtypeStruct((blocks, RADIX, chunk, LANES), jnp.bfloat16),
        in_specs=[
            pl.BlockSpec((blocks, 2, RADIX, chunk, LANES), lambda p, i: (0, 0, 0, 0, 0)),
            pl.BlockSpec(
                (step_q, 2, 2 * inner, inner),
                lambda p, i: (i * (1 - p) + (steps - 1) * p, 0, 0, 0),
            ),
            pl.BlockSpec((step_q, 2, inner, 2 * inner), lambda p, i: (i * p, 0, 0, 0)),
        ],
        out_specs=pl.BlockSpec((blocks, step_q, chunk, LANES), lambda p, i: (0, i * p, 0, 0)),
        scratch_shapes=[pltpu.VMEM((RADIX, 2 * inner, 2 * LANES), jnp.float32)],
        compiler_params=pltpu.CompilerParams(vmem_limit_bytes=VMEM_BYTES),
        name="long_convolution",
    )(
        streams.reshape(blocks, 2, RADIX, chunk, LANES),
        jnp.asarray(forward),
        jnp.asarray(backward),
    )


def gate_kernel(group, half_ref, order_ref, conv_ref, gates_ref, values_ref, skip_ref, weight_ref, gated_ref, out_ref):
    del half_ref
    step = pl.program_id(0)
    conv = jnp.concatenate([conv_ref[part] for part in range(group)], axis=1)
    conv = jnp.dot(order_ref[...], conv, preferred_element_type=jnp.float32)
    direct = skip_ref[...] * values_ref[...].astype(jnp.float32)
    gated = (gates_ref[...].astype(jnp.float32) * (conv + direct)).astype(jnp.bfloat16)
    gated_ref[...] = gated
    term = jnp.dot(gated, weight_ref[...], preferred_element_type=jnp.float32)

    @pl.when(step == 0)
    def _():
        out_ref[...] = term

    @pl.when(step > 0)
    def _():
        out_ref[...] += term


def gate_and_project(half, conv, gates, values, skip_gain, out_weight):
    blocks, rows, lanes = conv.shape
    width, features = out_weight.shape
    group = 4
    wide = group * lanes
    return pl.pallas_call(
        functools.partial(gate_kernel, group),
        grid_spec=pltpu.PrefetchScalarGridSpec(
            num_scalar_prefetch=1,
            grid=(blocks // group,),
            in_specs=[
                pl.BlockSpec((rows, rows), lambda i, h: (0, 0)),
                pl.BlockSpec((group, rows, lanes), lambda i, h: (i, 0, 0)),
                pl.BlockSpec((rows, wide), lambda i, h: (0, i)),
                pl.BlockSpec((rows, wide), lambda i, h: (0, i)),
                pl.BlockSpec((1, wide), lambda i, h: (0, i)),
                pl.BlockSpec((wide, features // 2), lambda i, h: (i, 1 - h[0])),
            ],
            out_specs=[
                pl.BlockSpec((rows, wide), lambda i, h: (0, i)),
                pl.BlockSpec((rows, features // 2), lambda i, h: (0, 0)),
            ],
        ),
        out_shape=[
            jax.ShapeDtypeStruct((rows, width), jnp.bfloat16),
            jax.ShapeDtypeStruct((rows, features // 2), jnp.float32),
        ],
        compiler_params=pltpu.CompilerParams(vmem_limit_bytes=VMEM_BYTES),
        cost_estimate=pl.CostEstimate(
            flops=rows * width * features, bytes_accessed=width * features + 8 * rows * width, transcendentals=0
        ),
        name="gate_project_sent",
    )(half, jnp.asarray(row_order(rows).T), conv, gates, values, skip_gain[None, :], out_weight)


def kept_kernel(half_ref, gated_ref, weight_ref, out_ref):
    del half_ref
    step = pl.program_id(0)
    term = jnp.dot(gated_ref[...], weight_ref[...], preferred_element_type=jnp.float32)

    @pl.when(step == 0)
    def _():
        out_ref[...] = term

    @pl.when(step > 0)
    def _():
        out_ref[...] += term


def project_kept(half, gated, out_weight):
    rows, width = gated.shape
    features = out_weight.shape[1]
    deep = width // 4
    return pl.pallas_call(
        kept_kernel,
        grid_spec=pltpu.PrefetchScalarGridSpec(
            num_scalar_prefetch=1,
            grid=(4,),
            in_specs=[
                pl.BlockSpec((rows, deep), lambda i, h: (0, i)),
                pl.BlockSpec((deep, features // 2), lambda i, h: (i, h[0])),
            ],
            out_specs=pl.BlockSpec((rows, features // 2), lambda i, h: (0, 0)),
        ),
        out_shape=jax.ShapeDtypeStruct((rows, features // 2), jnp.float32),
        compiler_params=pltpu.CompilerParams(vmem_limit_bytes=VMEM_BYTES),
        cost_estimate=pl.CostEstimate(
            flops=rows * width * features, bytes_accessed=width * features + 4 * rows * width, transcendentals=0
        ),
        name="project_kept",
    )(half, gated, out_weight)


def join_kernel(kept_ref, came_ref, out_ref):
    out_ref[...] = (kept_ref[...] + came_ref[...]).T.astype(jnp.bfloat16)


def join(kept, came):
    rows, features = kept.shape
    wide = features // 4
    return pl.pallas_call(
        join_kernel,
        grid=(4,),
        in_specs=[pl.BlockSpec((rows, wide), lambda i: (0, i))] * 2,
        out_specs=pl.BlockSpec((wide, rows), lambda i: (i, 0)),
        out_shape=jax.ShapeDtypeStruct((features, rows), jnp.bfloat16),
        compiler_params=pltpu.CompilerParams(vmem_limit_bytes=VMEM_BYTES),
        name="join_halves",
    )(kept, came)


def kernel_local(values, gates, filter_taps, skip_gain, out_weight):
    rows, _ = values.shape
    blocks = lax.axis_size("seq")
    streams = arrange(values, filter_taps, blocks)
    streams = lax.all_to_all(streams, "seq", split_axis=0, concat_axis=0, tiled=True)
    conv = convolve(streams, blocks, rows).reshape(blocks, rows, LANES)
    conv = lax.all_to_all(conv, "seq", split_axis=0, concat_axis=0, tiled=True)
    half = lax.axis_index("chan").astype(jnp.int32)[None]
    gated, sent = gate_and_project(half, conv, gates, values, skip_gain, out_weight)
    came = lax.ppermute(sent, "chan", [(0, 1), (1, 0)])
    kept = project_kept(half, gated, out_weight)
    return join(kept, came)


def takes_kernels(mesh, values, out_weight):
    blocks, halves = mesh.shape["seq"], mesh.shape["chan"]
    rows = values.shape[0] // blocks
    return (
        halves == 2
        and blocks % 4 == 0
        and rows == 256
        and blocks * rows == 4096
        and values.shape[1] == halves * blocks * LANES
        and out_weight.shape[1] % (8 * LANES) == 0
    )


def solution(mesh):
    placed = (P("seq", "chan"), P("seq", "chan"), P("seq", "chan"), P("chan"), P("chan", None))

    def whole(values, gates, filter_taps, skip_gain, out_weight):
        local = kernel_local if takes_kernels(mesh, values, out_weight) else general_local
        return jax.shard_map(
            local, mesh=mesh, in_specs=placed, out_specs=P("chan", "seq"), check_vma=False
        )(values, gates, filter_taps, skip_gain, out_weight)

    return whole
```

```python
import functools
import math

import jax
import jax.numpy as jnp
import ml_dtypes
import numpy as np
from jax import lax
from jax.experimental import pallas as pl
from jax.experimental.pallas import tpu as pltpu
from jax.sharding import PartitionSpec as P

TWO_PI = 2.0 * math.pi
HIGH = lax.Precision.HIGHEST
RADIX = 16
LANES = 128
HALF = 64
VMEM_BYTES = 40 * 1024 * 1024
SMALL_BYTES = 24 * 1024 * 1024


def angle_table(first, second, period):
    product = first[:, None] * second[None, :] % period
    angles = product.astype(jnp.float32) * (TWO_PI / period)
    return (jnp.cos(angles), jnp.sin(angles))


def mix(equation, left, right):
    return jnp.einsum(equation, left, right, precision=HIGH)


def outer_forward(data, outer_cos, outer_sin, twist_cos, twist_sin, equation):
    source = data.astype(jnp.float32)
    real = mix(equation, outer_cos, source)
    imag = -mix(equation, outer_sin, source)
    cos_part = twist_cos[:, :, None]
    sin_part = twist_sin[:, :, None]
    return (real * cos_part + imag * sin_part, imag * cos_part - real * sin_part)


def inner_filter(spectra, inner_cos, inner_sin):
    value_re, value_im, taps_re, taps_im = spectra

    def forward(real, imag):
        out_re = mix("kr,jrc->jkc", inner_cos, real) + mix("kr,jrc->jkc", inner_sin, imag)
        out_im = mix("kr,jrc->jkc", inner_cos, imag) - mix("kr,jrc->jkc", inner_sin, real)
        return (out_re, out_im)

    value_fre, value_fim = forward(value_re, value_im)
    taps_fre, taps_fim = forward(taps_re, taps_im)
    prod_re = value_fre * taps_fre - value_fim * taps_fim
    prod_im = value_fre * taps_fim + value_fim * taps_fre
    back_re = mix("rk,jkc->jrc", inner_cos, prod_re) - mix("rk,jkc->jrc", inner_sin, prod_im)
    back_im = mix("rk,jkc->jrc", inner_cos, prod_im) + mix("rk,jkc->jrc", inner_sin, prod_re)
    return (back_re, back_im)


def untwist(real, imag, twist_cos, twist_sin):
    cos_part = twist_cos[:, :, None]
    sin_part = twist_sin[:, :, None]
    return (real * cos_part - imag * sin_part, imag * cos_part + real * sin_part)


def channels_plan(values, filter_taps):
    rows, width = values.shape
    blocks = lax.axis_size("seq")
    length = 2 * blocks * rows
    narrow = width // blocks
    whole_values, whole_taps = (
        lax.all_to_all(values, "seq", split_axis=1, concat_axis=0, tiled=True),
        lax.all_to_all(filter_taps, "seq", split_axis=1, concat_axis=0, tiled=True),
    )
    freq_ids = jnp.arange(2 * blocks, dtype=jnp.int32)
    block_ids = jnp.arange(blocks, dtype=jnp.int32)
    all_rows = jnp.arange(rows, dtype=jnp.int32)
    outer_cos, outer_sin = angle_table(freq_ids, block_ids, 2 * blocks)
    twist_cos, twist_sin = angle_table(freq_ids, all_rows, length)
    tables = (outer_cos, outer_sin, twist_cos, twist_sin, "ka,arc->krc")
    value_re, value_im = outer_forward(whole_values.reshape(blocks, rows, narrow), *tables)
    taps_re, taps_im = outer_forward(whole_taps.reshape(blocks, rows, narrow), *tables)
    inner_cos, inner_sin = angle_table(all_rows, all_rows, rows)
    back_re, back_im = inner_filter((value_re, value_im, taps_re, taps_im), inner_cos, inner_sin)
    turned_re, turned_im = untwist(back_re, back_im, twist_cos, twist_sin)
    final_cos, final_sin = angle_table(block_ids, freq_ids, 2 * blocks)
    signal = (
        mix("ak,krc->arc", final_cos, turned_re) - mix("ak,krc->arc", final_sin, turned_im)
    ) / length
    returned = lax.all_to_all(signal, "seq", split_axis=0, concat_axis=2, tiled=True)
    return returned[0]


def general_local(values, gates, filter_taps, skip_gain, out_weight):
    conv = channels_plan(values, filter_taps)
    gated = (
        gates.astype(jnp.float32) * (conv + skip_gain[None, :] * values.astype(jnp.float32))
    ).astype(jnp.bfloat16)
    projected = lax.psum_scatter(
        lax.dot_general(
            out_weight, gated, (((0,), (1,)), ((), ())), preferred_element_type=jnp.float32
        ),
        "chan",
        scatter_dimension=0,
        tiled=True,
    )
    return projected.astype(jnp.bfloat16)


def split_table(table):
    high = table.astype(ml_dtypes.bfloat16)
    low = (table - high.astype(np.float64)).astype(ml_dtypes.bfloat16)
    return high, low


@functools.lru_cache(maxsize=None)
def transform_tables(length):
    inner = length // RADIX
    q = np.arange(RADIX)[:, None, None]
    k = np.arange(inner)[None, :, None]
    m = np.arange(inner)[None, None, :]
    phase = ((RADIX * m + q) * (4 * k + 1)) % (4 * length)
    angles = phase * (TWO_PI / (4 * length))
    table = np.concatenate([np.cos(angles), -np.sin(angles)], axis=1)
    forward = np.concatenate(split_table(table), axis=2)
    backward = np.concatenate(split_table(table.transpose(0, 2, 1) / length), axis=1)
    return tuple(
        np.ascontiguousarray(part.reshape(2, RADIX // 2, *part.shape[1:]).swapaxes(0, 1))
        for part in (forward, backward)
    )


@functools.lru_cache(maxsize=None)
def row_order(rows):
    chunk = rows // RADIX
    order = np.zeros((rows, rows), np.float32)
    for q in range(RADIX):
        for j in range(chunk):
            order[q * chunk + j, RADIX * j + q] = 1.0
    return order.astype(ml_dtypes.bfloat16)


def turn(point, index, sign):
    re, im = point
    index %= 16
    if index == 0:
        return point
    if index == 4:
        return (-im, re) if sign > 0 else (im, -re)
    if index == 8:
        return (-re, -im)
    half = math.sqrt(0.5)
    if index == 2:
        return ((re - im) * half, (re + im) * half) if sign > 0 else ((re + im) * half, (im - re) * half)
    if index == 6:
        return ((-re - im) * half, (re - im) * half) if sign > 0 else ((im - re) * half, (-re - im) * half)
    cos = math.cos(TWO_PI * index / 16)
    sin = sign * math.sin(TWO_PI * index / 16)
    return (re * cos - im * sin, re * sin + im * cos)


def four_points(points, sign):
    a, b, c, d = points
    ac = (a[0] + c[0], a[1] + c[1])
    am = (a[0] - c[0], a[1] - c[1])
    bd = (b[0] + d[0], b[1] + d[1])
    bm = (b[0] - d[0], b[1] - d[1])
    if sign < 0:
        side = (bm[1], -bm[0])
    else:
        side = (-bm[1], bm[0])
    return (
        (ac[0] + bd[0], ac[1] + bd[1]),
        (am[0] + side[0], am[1] + side[1]),
        (ac[0] - bd[0], ac[1] - bd[1]),
        (am[0] - side[0], am[1] - side[1]),
    )


def sixteen_points(points, sign):
    out = [None] * 16
    columns = []
    for low in range(4):
        column = four_points([points[low + 4 * high] for high in range(4)], sign)
        columns.append([turn(column[k], low * k, sign) for k in range(4)])
    for k in range(4):
        row = four_points([columns[low][k] for low in range(4)], sign)
        for high in range(4):
            out[k + 4 * high] = row[high]
    return out


def left_lanes(rows):
    return lax.broadcasted_iota(jnp.int32, (rows, LANES), 1) < HALF


def swap_halves(block):
    return pltpu.roll(block, HALF, 1)


def arrange_kernel(blocks, me_ref, order_ref, values_ref, taps_ref, *rest):
    outs, packed = rest[:blocks], rest[blocks]
    me = me_ref[0]
    order = order_ref[...]
    left = left_lanes(order.shape[0])
    for pair in range(blocks // 2):
        lanes = pl.ds(pair * LANES, LANES)
        both = jnp.concatenate([values_ref[:, lanes], taps_ref[:, lanes]], axis=1)
        moved = jnp.dot(order, both, preferred_element_type=jnp.float32)
        value, taps = moved[:, :LANES], moved[:, LANES:]
        packed[2 * pair] = jnp.where(left, value, swap_halves(taps)).astype(jnp.bfloat16)
        packed[2 * pair + 1] = jnp.where(left, swap_halves(value), taps).astype(jnp.bfloat16)
    for slot in range(blocks):
        outs[slot][...] = packed[me ^ slot]


def arrange(me, values, taps, blocks, chunk):
    rows = values.shape[0]
    wide = blocks * HALF
    return pl.pallas_call(
        functools.partial(arrange_kernel, blocks),
        grid_spec=pltpu.PrefetchScalarGridSpec(
            num_scalar_prefetch=1,
            grid=(1,),
            in_specs=[
                pl.BlockSpec((rows, rows), lambda i, me: (0, 0)),
                pl.BlockSpec((rows, wide), lambda i, me: (0, chunk)),
                pl.BlockSpec((rows, wide), lambda i, me: (0, chunk)),
            ],
            out_specs=[pl.BlockSpec((rows, LANES), lambda i, me: (0, 0))] * blocks,
            scratch_shapes=[pltpu.VMEM((blocks, rows, LANES), jnp.bfloat16)],
        ),
        out_shape=[jax.ShapeDtypeStruct((rows, LANES), jnp.bfloat16)] * blocks,
        compiler_params=pltpu.CompilerParams(vmem_limit_bytes=VMEM_BYTES),
        name=f"arrange_{chunk}",
    )(me, jnp.asarray(row_order(rows)), values, taps)


def convolve_kernel(blocks, pairs, me_ref, *rest):
    slots = rest[:blocks]
    forward_ref, backward_ref = rest[blocks : blocks + 2]
    outs = rest[blocks + 2 : 2 * blocks + 2]
    streams, spectra, signals = rest[2 * blocks + 2 :]
    me = me_ref[0]
    phase, step = pl.program_id(0), pl.program_id(1)
    chunk = streams.shape[2]
    inner = blocks * chunk
    part_rows = inner // 2

    @pl.when((phase == 0) & (step == 0))
    def _():
        for slot in range(blocks):
            streams[me ^ slot] = slots[slot][...].reshape(RADIX, chunk, LANES)

    @pl.when(phase == 0)
    def _():
        for part in range(2):
            q = step + part * pairs
            stream = streams[:, pl.ds(q, 1)].reshape(inner, LANES)
            spectra[q] = jnp.dot(
                forward_ref[0, part],
                jnp.concatenate([stream, stream], axis=0),
                preferred_element_type=jnp.float32,
            )

    @pl.when((phase == 0) & (step == pairs - 1))
    def _():
        left = left_lanes(8)

        def rows_step(index, carry):
            starts = [pl.multiple_of(base + index * 8, 8) for base in range(0, 2 * inner, part_rows)]
            first_re, second_re, first_im, second_im = [pl.ds(start, 8) for start in starts]
            first = sixteen_points([(spectra[q, first_re], spectra[q, first_im]) for q in range(RADIX)], -1)
            second = sixteen_points([(spectra[q, second_re], spectra[q, second_im]) for q in range(RADIX)], -1)
            product = []
            for one, two in zip(first, second):
                a = [jnp.where(left, x, y) for x, y in zip(one, two)]
                b = [swap_halves(jnp.where(left, y, x)) for x, y in zip(one, two)]
                product.append((a[0] * b[0] - a[1] * b[1], a[0] * b[1] + a[1] * b[0]))
            back = sixteen_points(product, 1)
            for q in range(RADIX):
                spectra[q, first_re] = back[q][0]
                spectra[q, first_im] = back[q][1]
            return carry

        lax.fori_loop(0, part_rows // 8, rows_step, 0)

    @pl.when(phase == 1)
    def _():
        left = left_lanes(part_rows)
        sides = []
        for part in range(2):
            q = step + part * pairs
            pieces = []
            for base in (0, inner):
                points = spectra[q, pl.ds(base, part_rows)]
                high = points.astype(jnp.bfloat16).astype(jnp.float32)
                low = points - high
                pieces.append(jnp.where(left, high, swap_halves(low)).astype(jnp.bfloat16))
                pieces.append(jnp.where(left, swap_halves(high), low).astype(jnp.bfloat16))
            terms = jnp.dot(
                backward_ref[0, part],
                jnp.concatenate(pieces, axis=0),
                preferred_element_type=jnp.float32,
            )
            total = terms[:inner] + terms[inner:]
            sides.append(total + swap_halves(total))
        signal = jnp.where(left_lanes(inner), sides[0], sides[1]).astype(jnp.bfloat16)
        signals[:, pl.ds(step, 1)] = signal.reshape(blocks, 1, chunk, LANES)

    @pl.when((phase == 1) & (step == pairs - 1))
    def _():
        for slot in range(blocks):
            outs[slot][...] = signals[me ^ slot].reshape(pairs * chunk, LANES)


def convolve(me, slots, blocks, chunk_id):
    rows = slots[0].shape[0]
    length = blocks * rows
    chunk = rows // RADIX
    inner = length // RADIX
    pairs = RADIX // 2
    forward, backward = transform_tables(length)
    whole = lambda p, i, me: (0, 0)
    table = (1, 2, 2 * inner, 2 * inner)
    return pl.pallas_call(
        functools.partial(convolve_kernel, blocks, pairs),
        grid_spec=pltpu.PrefetchScalarGridSpec(
            num_scalar_prefetch=1,
            grid=(2, pairs),
            in_specs=[pl.BlockSpec((rows, LANES), whole)] * blocks
            + [
                pl.BlockSpec(table, lambda p, i, me: (i * (1 - p) + (pairs - 1) * p, 0, 0, 0)),
                pl.BlockSpec(table, lambda p, i, me: (i * p, 0, 0, 0)),
            ],
            out_specs=[pl.BlockSpec((pairs * chunk, LANES), whole)] * blocks,
            scratch_shapes=[
                pltpu.VMEM((blocks, RADIX, chunk, LANES), jnp.bfloat16),
                pltpu.VMEM((RADIX, 2 * inner, LANES), jnp.float32),
                pltpu.VMEM((blocks, pairs, chunk, LANES), jnp.bfloat16),
            ],
        ),
        out_shape=[jax.ShapeDtypeStruct((pairs * chunk, LANES), jnp.bfloat16)] * blocks,
        compiler_params=pltpu.CompilerParams(vmem_limit_bytes=VMEM_BYTES),
        cost_estimate=pl.CostEstimate(
            flops=2 * RADIX * 2 * (2 * inner) * (2 * inner) * LANES * 2,
            bytes_accessed=RADIX * 2 * (2 * inner) ** 2 * 2,
            transcendentals=0,
        ),
        name=f"long_convolution_{chunk_id}",
    )(me, *slots, jnp.asarray(forward), jnp.asarray(backward))


def gate_kernel(blocks, joined, me_ref, *rest):
    slots = rest[:blocks]
    if joined:
        order_ref, gates_ref, values_ref, skip_ref, weight_ref, base_ref, out_ref, gated_ref, parts = rest[blocks:]
    else:
        order_ref, gates_ref, values_ref, skip_ref, weight_ref, out_ref, parts = rest[blocks:]
    me = me_ref[0]
    step = pl.program_id(0)

    @pl.when(step == 0)
    def _():
        for slot in range(blocks):
            parts[me ^ slot] = slots[slot][...]

    wide = gates_ref.shape[1]
    pairs = wide // LANES
    left = left_lanes(parts.shape[1])
    columns = []
    for pair in range(pairs):
        even = parts[2 * (step * pairs + pair)].astype(jnp.float32)
        odd = parts[2 * (step * pairs + pair) + 1].astype(jnp.float32)
        low = jnp.where(left, even, swap_halves(odd))
        high = jnp.where(left, swap_halves(even), odd)
        columns.append(jnp.concatenate([low, high], axis=0).astype(jnp.bfloat16))
    conv = jnp.dot(
        order_ref[...], jnp.concatenate(columns, axis=1), preferred_element_type=jnp.float32
    )
    direct = skip_ref[...] * values_ref[...].astype(jnp.float32)
    gated = (gates_ref[...].astype(jnp.float32) * (conv + direct)).astype(jnp.bfloat16)
    if joined:
        gated_ref[...] = gated
    term = jnp.dot(gated, weight_ref[...], preferred_element_type=jnp.float32)

    @pl.when(step == 0)
    def _():
        out_ref[...] = base_ref[...] + term if joined else term

    @pl.when(step > 0)
    def _():
        out_ref[...] += term


def gate_and_project(me, slots, gates, values, skip_gain, out_weight, chunk, base=None):
    blocks = len(slots)
    rows = gates.shape[0]
    features = out_weight.shape[1]
    steps = 4
    wide = blocks * HALF // steps
    joined = base is not None
    taken = features // 2 if joined else features
    in_specs = [pl.BlockSpec(slots[0].shape, lambda i, me: (0, 0))] * blocks + [
        pl.BlockSpec((rows, rows), lambda i, me: (0, 0)),
        pl.BlockSpec((rows, wide), lambda i, me: (0, chunk * steps + i)),
        pl.BlockSpec((rows, wide), lambda i, me: (0, chunk * steps + i)),
        pl.BlockSpec((1, wide), lambda i, me: (0, chunk * steps + i)),
    ]
    operands = [me, *slots, jnp.asarray(row_order(rows).T), gates, values, skip_gain[None, :], out_weight]
    out_specs = [pl.BlockSpec((rows, taken), lambda i, me: (0, 0))]
    out_shape = [jax.ShapeDtypeStruct((rows, taken), jnp.float32)]
    if joined:
        in_specs.append(pl.BlockSpec((wide, taken), lambda i, me: (chunk * steps + i, 1 - me[1])))
        in_specs.append(pl.BlockSpec((rows, taken), lambda i, me: (0, 1 - me[1])))
        operands.append(base)
        out_specs.append(pl.BlockSpec((rows, wide), lambda i, me: (0, i)))
        out_shape.append(jax.ShapeDtypeStruct((rows, steps * wide), jnp.bfloat16))
    else:
        in_specs.append(pl.BlockSpec((wide, taken), lambda i, me: (chunk * steps + i, 0)))
    return pl.pallas_call(
        functools.partial(gate_kernel, blocks, joined),
        grid_spec=pltpu.PrefetchScalarGridSpec(
            num_scalar_prefetch=1,
            grid=(steps,),
            in_specs=in_specs,
            out_specs=out_specs,
            scratch_shapes=[pltpu.VMEM((blocks, *slots[0].shape), jnp.bfloat16)],
        ),
        out_shape=out_shape,
        compiler_params=pltpu.CompilerParams(vmem_limit_bytes=SMALL_BYTES),
        cost_estimate=pl.CostEstimate(
            flops=2 * rows * steps * wide * taken,
            bytes_accessed=2 * steps * wide * taken + 12 * rows * steps * wide,
            transcendentals=0,
        ),
        name=f"gate_project_{chunk}",
    )(*operands)


def kept_kernel(me_ref, gated_ref, weight_ref, base_ref, out_ref):
    del me_ref
    step = pl.program_id(0)
    term = jnp.dot(gated_ref[...], weight_ref[...], preferred_element_type=jnp.float32)

    @pl.when(step == 0)
    def _():
        out_ref[...] = base_ref[...] + term

    @pl.when(step > 0)
    def _():
        out_ref[...] += term


def project_kept(me, gated, out_weight, base):
    rows, width = gated.shape
    features = out_weight.shape[1]
    steps = 2
    deep = width // steps
    return pl.pallas_call(
        kept_kernel,
        grid_spec=pltpu.PrefetchScalarGridSpec(
            num_scalar_prefetch=1,
            grid=(steps,),
            in_specs=[
                pl.BlockSpec((rows, deep), lambda i, me: (0, i)),
                pl.BlockSpec((deep, features // 2), lambda i, me: (steps + i, me[1])),
                pl.BlockSpec((rows, features // 2), lambda i, me: (0, me[1])),
            ],
            out_specs=pl.BlockSpec((rows, features // 2), lambda i, me: (0, 0)),
        ),
        out_shape=jax.ShapeDtypeStruct((rows, features // 2), jnp.float32),
        compiler_params=pltpu.CompilerParams(vmem_limit_bytes=SMALL_BYTES),
        cost_estimate=pl.CostEstimate(
            flops=rows * width * features, bytes_accessed=width * features + 8 * rows * width, transcendentals=0
        ),
        name="project_kept",
    )(me, gated, out_weight, base)


def join_kernel(kept_ref, came_ref, out_ref):
    out_ref[...] = (kept_ref[...] + came_ref[...]).astype(jnp.bfloat16).T


def join(kept, came):
    rows, features = kept.shape
    wide = features // 4
    return pl.pallas_call(
        join_kernel,
        grid=(4,),
        in_specs=[pl.BlockSpec((rows, wide), lambda i: (0, i))] * 2,
        out_specs=pl.BlockSpec((wide, rows), lambda i: (i, 0)),
        out_shape=jax.ShapeDtypeStruct((features, rows), jnp.bfloat16),
        compiler_params=pltpu.CompilerParams(vmem_limit_bytes=SMALL_BYTES),
        name="join_halves",
    )(kept, came)


def exchange(slots):
    blocks = len(slots)
    return [slots[0]] + [
        lax.ppermute(slots[slot], "seq", [(j, j ^ slot) for j in range(blocks)]) for slot in range(1, blocks)
    ]


def kernel_local(values, gates, filter_taps, skip_gain, out_weight):
    blocks = lax.axis_size("seq")
    me = jnp.stack([lax.axis_index("seq"), lax.axis_index("chan")]).astype(jnp.int32)
    came = [exchange(arrange(me, values, filter_taps, blocks, chunk)) for chunk in range(2)]
    back = [exchange(convolve(me, came[chunk], blocks, chunk)) for chunk in range(2)]
    (base,) = gate_and_project(me, back[0], gates, values, skip_gain, out_weight, 0)
    sent, gated = gate_and_project(me, back[1], gates, values, skip_gain, out_weight, 1, base)
    other = lax.ppermute(sent, "chan", [(0, 1), (1, 0)])
    kept = project_kept(me, gated, out_weight, base)
    return join(kept, other)


def takes_kernels(mesh, values, out_weight):
    blocks, halves = mesh.shape["seq"], mesh.shape["chan"]
    rows = values.shape[0] // blocks
    return (
        halves == 2
        and blocks == 16
        and rows == 256
        and values.shape[1] == halves * blocks * LANES
        and out_weight.shape[1] % (8 * LANES) == 0
    )


def solution(mesh):
    placed = (P("seq", "chan"), P("seq", "chan"), P("seq", "chan"), P("chan"), P("chan", None))

    def whole(values, gates, filter_taps, skip_gain, out_weight):
        local = kernel_local if takes_kernels(mesh, values, out_weight) else general_local
        return jax.shard_map(
            local, mesh=mesh, in_specs=placed, out_specs=P("chan", "seq"), check_vma=False
        )(values, gates, filter_taps, skip_gain, out_weight)

    return whole
```

```python
import functools
import math

import jax
import jax.numpy as jnp
import ml_dtypes
import numpy as np
from jax import lax
from jax.experimental import pallas as pl
from jax.experimental.pallas import tpu as pltpu
from jax.sharding import PartitionSpec as P

TWO_PI = 2.0 * math.pi
HIGH = lax.Precision.HIGHEST
RADIX = 16
LANES = 128
HALF = 64
VMEM_BYTES = 40 * 1024 * 1024
SMALL_BYTES = 24 * 1024 * 1024


def angle_table(first, second, period):
    product = first[:, None] * second[None, :] % period
    angles = product.astype(jnp.float32) * (TWO_PI / period)
    return (jnp.cos(angles), jnp.sin(angles))


def mix(equation, left, right):
    return jnp.einsum(equation, left, right, precision=HIGH)


def outer_forward(data, outer_cos, outer_sin, twist_cos, twist_sin, equation):
    source = data.astype(jnp.float32)
    real = mix(equation, outer_cos, source)
    imag = -mix(equation, outer_sin, source)
    cos_part = twist_cos[:, :, None]
    sin_part = twist_sin[:, :, None]
    return (real * cos_part + imag * sin_part, imag * cos_part - real * sin_part)


def inner_filter(spectra, inner_cos, inner_sin):
    value_re, value_im, taps_re, taps_im = spectra

    def forward(real, imag):
        out_re = mix("kr,jrc->jkc", inner_cos, real) + mix("kr,jrc->jkc", inner_sin, imag)
        out_im = mix("kr,jrc->jkc", inner_cos, imag) - mix("kr,jrc->jkc", inner_sin, real)
        return (out_re, out_im)

    value_fre, value_fim = forward(value_re, value_im)
    taps_fre, taps_fim = forward(taps_re, taps_im)
    prod_re = value_fre * taps_fre - value_fim * taps_fim
    prod_im = value_fre * taps_fim + value_fim * taps_fre
    back_re = mix("rk,jkc->jrc", inner_cos, prod_re) - mix("rk,jkc->jrc", inner_sin, prod_im)
    back_im = mix("rk,jkc->jrc", inner_cos, prod_im) + mix("rk,jkc->jrc", inner_sin, prod_re)
    return (back_re, back_im)


def untwist(real, imag, twist_cos, twist_sin):
    cos_part = twist_cos[:, :, None]
    sin_part = twist_sin[:, :, None]
    return (real * cos_part - imag * sin_part, imag * cos_part + real * sin_part)


def channels_plan(values, filter_taps):
    rows, width = values.shape
    blocks = lax.axis_size("seq")
    length = 2 * blocks * rows
    narrow = width // blocks
    whole_values, whole_taps = (
        lax.all_to_all(values, "seq", split_axis=1, concat_axis=0, tiled=True),
        lax.all_to_all(filter_taps, "seq", split_axis=1, concat_axis=0, tiled=True),
    )
    freq_ids = jnp.arange(2 * blocks, dtype=jnp.int32)
    block_ids = jnp.arange(blocks, dtype=jnp.int32)
    all_rows = jnp.arange(rows, dtype=jnp.int32)
    outer_cos, outer_sin = angle_table(freq_ids, block_ids, 2 * blocks)
    twist_cos, twist_sin = angle_table(freq_ids, all_rows, length)
    tables = (outer_cos, outer_sin, twist_cos, twist_sin, "ka,arc->krc")
    value_re, value_im = outer_forward(whole_values.reshape(blocks, rows, narrow), *tables)
    taps_re, taps_im = outer_forward(whole_taps.reshape(blocks, rows, narrow), *tables)
    inner_cos, inner_sin = angle_table(all_rows, all_rows, rows)
    back_re, back_im = inner_filter((value_re, value_im, taps_re, taps_im), inner_cos, inner_sin)
    turned_re, turned_im = untwist(back_re, back_im, twist_cos, twist_sin)
    final_cos, final_sin = angle_table(block_ids, freq_ids, 2 * blocks)
    signal = (
        mix("ak,krc->arc", final_cos, turned_re) - mix("ak,krc->arc", final_sin, turned_im)
    ) / length
    returned = lax.all_to_all(signal, "seq", split_axis=0, concat_axis=2, tiled=True)
    return returned[0]


def general_local(values, gates, filter_taps, skip_gain, out_weight):
    conv = channels_plan(values, filter_taps)
    gated = (
        gates.astype(jnp.float32) * (conv + skip_gain[None, :] * values.astype(jnp.float32))
    ).astype(jnp.bfloat16)
    projected = lax.psum_scatter(
        lax.dot_general(
            out_weight, gated, (((0,), (1,)), ((), ())), preferred_element_type=jnp.float32
        ),
        "chan",
        scatter_dimension=0,
        tiled=True,
    )
    return projected.astype(jnp.bfloat16)


def split_table(table):
    high = table.astype(ml_dtypes.bfloat16)
    low = (table - high.astype(np.float64)).astype(ml_dtypes.bfloat16)
    return high, low


@functools.lru_cache(maxsize=None)
def transform_tables(length):
    inner = length // RADIX
    k = np.arange(inner)[:, None]
    m = np.arange(inner)[None, :]
    angles = (RADIX * m * (4 * k + 1)) % (4 * length) * (TWO_PI / (4 * length))
    table = np.concatenate([np.cos(angles), -np.sin(angles)], axis=0)
    forward = np.concatenate(split_table(table), axis=1)
    backward = np.concatenate(split_table(table.T / length), axis=0)
    turns = (np.arange(RADIX)[None, :] * (4 * k + 1)) % (4 * length) * (TWO_PI / (4 * length))
    turns = np.concatenate([np.cos(turns), np.sin(turns)], axis=1)
    turns = np.pad(turns, ((0, 0), (0, LANES - 2 * RADIX))).astype(np.float32)
    return forward, backward, turns


@functools.lru_cache(maxsize=None)
def row_order(rows):
    chunk = rows // RADIX
    order = np.zeros((rows, rows), np.float32)
    for q in range(RADIX):
        for j in range(chunk):
            order[q * chunk + j, RADIX * j + q] = 1.0
    return order.astype(ml_dtypes.bfloat16)


def turn(point, index, sign):
    re, im = point
    index %= 16
    if index == 0:
        return point
    if index == 4:
        return (-im, re) if sign > 0 else (im, -re)
    if index == 8:
        return (-re, -im)
    half = math.sqrt(0.5)
    if index == 2:
        return ((re - im) * half, (re + im) * half) if sign > 0 else ((re + im) * half, (im - re) * half)
    if index == 6:
        return ((-re - im) * half, (re - im) * half) if sign > 0 else ((im - re) * half, (-re - im) * half)
    cos = math.cos(TWO_PI * index / 16)
    sin = sign * math.sin(TWO_PI * index / 16)
    return (re * cos - im * sin, re * sin + im * cos)


def four_points(points, sign):
    a, b, c, d = points
    ac = (a[0] + c[0], a[1] + c[1])
    am = (a[0] - c[0], a[1] - c[1])
    bd = (b[0] + d[0], b[1] + d[1])
    bm = (b[0] - d[0], b[1] - d[1])
    if sign < 0:
        side = (bm[1], -bm[0])
    else:
        side = (-bm[1], bm[0])
    return (
        (ac[0] + bd[0], ac[1] + bd[1]),
        (am[0] + side[0], am[1] + side[1]),
        (ac[0] - bd[0], ac[1] - bd[1]),
        (am[0] - side[0], am[1] - side[1]),
    )


def sixteen_points(points, sign):
    out = [None] * 16
    columns = []
    for low in range(4):
        column = four_points([points[low + 4 * high] for high in range(4)], sign)
        columns.append([turn(column[k], low * k, sign) for k in range(4)])
    for k in range(4):
        row = four_points([columns[low][k] for low in range(4)], sign)
        for high in range(4):
            out[k + 4 * high] = row[high]
    return out


def left_lanes(rows):
    return lax.broadcasted_iota(jnp.int32, (rows, LANES), 1) < HALF


def swap_halves(block):
    return pltpu.roll(block, HALF, 1)


def arrange_kernel(blocks, pieces, slotted, chunk, me_ref, order_hbm, values_hbm, taps_hbm, *rest):
    outs = rest[: blocks if slotted else 1]
    order_ref, values_ref, taps_ref, packed, sems = rest[len(outs) :]
    wide = values_ref.shape[1]
    piece = wide // pieces
    loads = [pltpu.make_async_copy(order_hbm, order_ref, sems.at[2 * pieces])]
    for part in range(pieces):
        lanes = pl.ds(chunk * wide + part * piece, piece)
        to = pl.ds(part * piece, piece)
        loads.append(pltpu.make_async_copy(values_hbm.at[:, lanes], values_ref.at[:, to], sems.at[2 * part]))
        loads.append(pltpu.make_async_copy(taps_hbm.at[:, lanes], taps_ref.at[:, to], sems.at[2 * part + 1]))
    for load in loads:
        load.start()
    loads[0].wait()
    left = left_lanes(order_ref.shape[0])
    target = packed if slotted else outs[0]
    for part in range(pieces):
        loads[2 * part + 1].wait()
        loads[2 * part + 2].wait()
        for pair in range(part * piece // LANES, (part + 1) * piece // LANES):
            lanes = pl.ds(pair * LANES, LANES)
            both = jnp.concatenate([values_ref[:, lanes], taps_ref[:, lanes]], axis=1)
            moved = jnp.dot(order_ref[...], both, preferred_element_type=jnp.float32)
            value, taps = moved[:, :LANES], moved[:, LANES:]
            target[2 * pair] = jnp.where(left, value, swap_halves(taps)).astype(jnp.bfloat16)
            target[2 * pair + 1] = jnp.where(left, swap_halves(value), taps).astype(jnp.bfloat16)
    if slotted:
        me = me_ref[0]
        for slot in range(blocks):
            outs[slot][...] = packed[me ^ slot]


def arrange(me, values, taps, blocks, chunk, slotted):
    rows = values.shape[0]
    wide = blocks * HALF
    pieces = 4
    if slotted:
        out_shape = [jax.ShapeDtypeStruct((rows, LANES), jnp.bfloat16)] * blocks
    else:
        out_shape = [jax.ShapeDtypeStruct((blocks, rows, LANES), jnp.bfloat16)]
    return pl.pallas_call(
        functools.partial(arrange_kernel, blocks, pieces, slotted, chunk),
        in_specs=[pl.BlockSpec(memory_space=pltpu.SMEM)] + [pl.BlockSpec(memory_space=pltpu.HBM)] * 3,
        out_specs=[pl.BlockSpec(memory_space=pltpu.VMEM)] * len(out_shape),
        out_shape=out_shape,
        scratch_shapes=[
            pltpu.VMEM((rows, rows), jnp.bfloat16),
            pltpu.VMEM((rows, wide), jnp.bfloat16),
            pltpu.VMEM((rows, wide), jnp.bfloat16),
            pltpu.VMEM((blocks, rows, LANES) if slotted else (16, LANES), jnp.bfloat16),
            pltpu.SemaphoreType.DMA((2 * pieces + 1,)),
        ],
        compiler_params=pltpu.CompilerParams(vmem_limit_bytes=VMEM_BYTES),
        name=f"arrange_{chunk}",
    )(me, jnp.asarray(row_order(rows)), values, taps)


def turned(point, turns, q, sign):
    if q == 0:
        return point
    re, im = point
    cos, sin = turns[0][q], turns[1][q]
    if sign < 0:
        return (re * cos + im * sin, im * cos - re * sin)
    return (re * cos - im * sin, im * cos + re * sin)


def spread(turns_ref, rows):
    block = turns_ref[rows]
    columns = [jnp.broadcast_to(block[:, i : i + 1], block.shape) for i in range(2 * RADIX)]
    return columns[:RADIX], columns[RADIX:]


def convolve_kernel(blocks, slots_in, slots_out, me_ref, *rest):
    count_in = blocks if slots_in else 1
    count_out = blocks if slots_out else 1
    slots = rest[:count_in]
    forward_ref, backward_ref, turns_ref = rest[count_in : count_in + 3]
    outs = rest[count_in + 3 : count_in + 3 + count_out]
    streams, spectra, signals = rest[count_in + 3 + count_out :]
    me = me_ref[0]
    chunk = streams.shape[2]
    inner = blocks * chunk
    part_rows = inner // 2
    pairs = RADIX // 2
    if slots_in:
        for slot in range(blocks):
            streams[me ^ slot] = slots[slot][...].reshape(RADIX, chunk, LANES)

    def stream_of(q):
        if slots_in:
            return streams[:, pl.ds(q, 1)].reshape(inner, LANES)
        return slots[0][:, pl.ds(pl.multiple_of(q * chunk, chunk), chunk)].reshape(inner, LANES)

    def forward_step(pair, carry):
        both = jnp.concatenate([stream_of(2 * pair), stream_of(2 * pair + 1)], axis=1)
        result = jnp.dot(
            forward_ref[...], jnp.concatenate([both, both], axis=0), preferred_element_type=jnp.float32
        )
        spectra[2 * pair] = result[:, :LANES]
        spectra[2 * pair + 1] = result[:, LANES:]
        return carry

    lax.fori_loop(0, pairs, forward_step, 0)
    left = left_lanes(8)

    def rows_step(index, carry):
        starts = [pl.multiple_of(base + index * 8, 8) for base in range(0, 2 * inner, part_rows)]
        first_re, second_re, first_im, second_im = [pl.ds(start, 8) for start in starts]
        first_turns = spread(turns_ref, first_re)
        second_turns = spread(turns_ref, second_re)
        first = sixteen_points(
            [turned((spectra[q, first_re], spectra[q, first_im]), first_turns, q, -1) for q in range(RADIX)], -1
        )
        second = sixteen_points(
            [turned((spectra[q, second_re], spectra[q, second_im]), second_turns, q, -1) for q in range(RADIX)], -1
        )
        product = []
        for one, two in zip(first, second):
            a = [jnp.where(left, x, y) for x, y in zip(one, two)]
            b = [swap_halves(jnp.where(left, y, x)) for x, y in zip(one, two)]
            product.append((a[0] * b[0] - a[1] * b[1], a[0] * b[1] + a[1] * b[0]))
        back = sixteen_points(product, 1)
        mixed = [
            [jnp.where(left, x, y) for x, y in zip(one, two)] for one, two in zip(first_turns, second_turns)
        ]
        for q in range(RADIX):
            spectra[q, first_re], spectra[q, first_im] = turned(back[q], mixed, q, 1)
        return carry

    lax.fori_loop(0, part_rows // 8, rows_step, 0)
    left_part = left_lanes(part_rows)
    left_inner = left_lanes(inner)

    def backward_step(pair, carry):
        columns = []
        for q in (pair, pair + pairs):
            pieces = []
            for base in (0, inner):
                points = spectra[q, pl.ds(base, part_rows)]
                high = points.astype(jnp.bfloat16).astype(jnp.float32)
                low = points - high
                pieces.append(jnp.where(left_part, high, swap_halves(low)).astype(jnp.bfloat16))
                pieces.append(jnp.where(left_part, swap_halves(high), low).astype(jnp.bfloat16))
            columns.append(jnp.concatenate(pieces, axis=0))
        terms = jnp.dot(
            backward_ref[...], jnp.concatenate(columns, axis=1), preferred_element_type=jnp.float32
        )
        total = terms[:inner] + terms[inner:]
        sides = [part + swap_halves(part) for part in (total[:, :LANES], total[:, LANES:])]
        signal = jnp.where(left_inner, *sides).astype(jnp.bfloat16).reshape(blocks, chunk, LANES)
        if slots_out:
            signals[:, pl.ds(pair, 1)] = signal[:, None]
        else:
            outs[0][:, pl.ds(pl.multiple_of(pair * chunk, chunk), chunk)] = signal
        return carry

    lax.fori_loop(0, pairs, backward_step, 0)
    if slots_out:
        for slot in range(blocks):
            outs[slot][...] = signals[me ^ slot].reshape(pairs * chunk, LANES)


def convolve(me, slots, blocks, chunk_id, slots_out):
    slots_in = len(slots) > 1
    rows = slots[0].shape[-2]
    length = blocks * rows
    chunk = rows // RADIX
    inner = length // RADIX
    pairs = RADIX // 2
    if slots_out:
        out_shape = [jax.ShapeDtypeStruct((pairs * chunk, LANES), jnp.bfloat16)] * blocks
    else:
        out_shape = [jax.ShapeDtypeStruct((blocks, pairs * chunk, LANES), jnp.bfloat16)]
    return pl.pallas_call(
        functools.partial(convolve_kernel, blocks, slots_in, slots_out),
        in_specs=[pl.BlockSpec(memory_space=pltpu.SMEM)]
        + [pl.BlockSpec(memory_space=pltpu.VMEM)] * (len(slots) + 3),
        out_specs=[pl.BlockSpec(memory_space=pltpu.VMEM)] * len(out_shape),
        out_shape=out_shape,
        scratch_shapes=[
            pltpu.VMEM((blocks, RADIX, chunk, LANES) if slots_in else (1, 1, chunk, LANES), jnp.bfloat16),
            pltpu.VMEM((RADIX, 2 * inner, LANES), jnp.float32),
            pltpu.VMEM((blocks, pairs, chunk, LANES) if slots_out else (1, 1, chunk, LANES), jnp.bfloat16),
        ],
        compiler_params=pltpu.CompilerParams(vmem_limit_bytes=SMALL_BYTES),
        cost_estimate=pl.CostEstimate(
            flops=3 * 10**9, bytes_accessed=24 * 10**6, transcendentals=0
        ),
        name=f"long_convolution_{chunk_id}",
    )(me, *slots, *(jnp.asarray(table) for table in transform_tables(length)))


def gate_kernel(count, joined, me_ref, *rest):
    slots, rest = rest[:count], rest[count:]
    if joined:
        order_ref, gates_ref, values_ref, skip_ref, weight_ref, base_ref, out_ref, gated_ref, parts = rest
    else:
        order_ref, gates_ref, values_ref, skip_ref, weight_ref, out_ref, parts = rest
    me = me_ref[0]
    step = pl.program_id(0)

    if count > 1:

        @pl.when(step == 0)
        def _():
            for slot in range(count):
                parts[me ^ slot] = slots[slot][...]

    else:
        parts = slots[0]

    wide = gates_ref.shape[1]
    pairs = wide // LANES
    left = left_lanes(parts.shape[1])
    columns = []
    for pair in range(pairs):
        even = parts[2 * (step * pairs + pair)].astype(jnp.float32)
        odd = parts[2 * (step * pairs + pair) + 1].astype(jnp.float32)
        low = jnp.where(left, even, swap_halves(odd))
        high = jnp.where(left, swap_halves(even), odd)
        columns.append(jnp.concatenate([low, high], axis=0).astype(jnp.bfloat16))
    conv = jnp.dot(
        order_ref[...], jnp.concatenate(columns, axis=1), preferred_element_type=jnp.float32
    )
    direct = skip_ref[...] * values_ref[...].astype(jnp.float32)
    gated = (gates_ref[...].astype(jnp.float32) * (conv + direct)).astype(jnp.bfloat16)
    if joined:
        gated_ref[...] = gated
    term = jnp.dot(gated, weight_ref[...], preferred_element_type=jnp.float32)

    @pl.when(step == 0)
    def _():
        out_ref[...] = base_ref[...] + term if joined else term

    @pl.when(step > 0)
    def _():
        out_ref[...] += term


def gate_and_project(me, slots, gates, values, skip_gain, out_weight, chunk, base=None):
    count = len(slots)
    blocks = lax.axis_size("seq")
    block_shape = slots[0].shape[-2:]
    rows = gates.shape[0]
    features = out_weight.shape[1]
    steps = 4
    wide = blocks * HALF // steps
    joined = base is not None
    taken = features // 2 if joined else features
    in_specs = [pl.BlockSpec(slot.shape, lambda i, me, rank=slot.ndim: (0,) * rank) for slot in slots] + [
        pl.BlockSpec((rows, rows), lambda i, me: (0, 0)),
        pl.BlockSpec((rows, wide), lambda i, me: (0, chunk * steps + i)),
        pl.BlockSpec((rows, wide), lambda i, me: (0, chunk * steps + i)),
        pl.BlockSpec((1, wide), lambda i, me: (0, chunk * steps + i)),
    ]
    operands = [me, *slots, jnp.asarray(row_order(rows).T), gates, values, skip_gain[None, :], out_weight]
    out_specs = [pl.BlockSpec((rows, taken), lambda i, me: (0, 0))]
    out_shape = [jax.ShapeDtypeStruct((rows, taken), jnp.float32)]
    if joined:
        in_specs.append(pl.BlockSpec((wide, taken), lambda i, me: (chunk * steps + i, 1 - me[1])))
        in_specs.append(pl.BlockSpec((rows, taken), lambda i, me: (0, 1 - me[1])))
        operands.append(base)
        out_specs.append(pl.BlockSpec((rows, wide), lambda i, me: (0, i)))
        out_shape.append(jax.ShapeDtypeStruct((rows, steps * wide), jnp.bfloat16))
    else:
        in_specs.append(pl.BlockSpec((wide, taken), lambda i, me: (chunk * steps + i, 0)))
    return pl.pallas_call(
        functools.partial(gate_kernel, count, joined),
        grid_spec=pltpu.PrefetchScalarGridSpec(
            num_scalar_prefetch=1,
            grid=(steps,),
            in_specs=in_specs,
            out_specs=out_specs,
            scratch_shapes=[pltpu.VMEM((blocks if count > 1 else 1, *block_shape), jnp.bfloat16)],
        ),
        out_shape=out_shape,
        compiler_params=pltpu.CompilerParams(vmem_limit_bytes=SMALL_BYTES),
        cost_estimate=pl.CostEstimate(
            flops=2 * rows * steps * wide * taken,
            bytes_accessed=2 * steps * wide * taken + 12 * rows * steps * wide,
            transcendentals=0,
        ),
        name=f"gate_project_{chunk}",
    )(*operands)


def kept_kernel(me_ref, gated_ref, weight_ref, base_ref, out_ref):
    del me_ref
    step = pl.program_id(0)
    term = jnp.dot(gated_ref[...], weight_ref[...], preferred_element_type=jnp.float32)

    @pl.when(step == 0)
    def _():
        out_ref[...] = base_ref[...] + term

    @pl.when(step > 0)
    def _():
        out_ref[...] += term


def project_kept(me, gated, out_weight, base):
    rows, width = gated.shape
    features = out_weight.shape[1]
    steps = 2
    deep = width // steps
    return pl.pallas_call(
        kept_kernel,
        grid_spec=pltpu.PrefetchScalarGridSpec(
            num_scalar_prefetch=1,
            grid=(steps,),
            in_specs=[
                pl.BlockSpec((rows, deep), lambda i, me: (0, i)),
                pl.BlockSpec((deep, features // 2), lambda i, me: (steps + i, me[1])),
                pl.BlockSpec((rows, features // 2), lambda i, me: (0, me[1])),
            ],
            out_specs=pl.BlockSpec((rows, features // 2), lambda i, me: (0, 0)),
        ),
        out_shape=jax.ShapeDtypeStruct((rows, features // 2), jnp.float32),
        compiler_params=pltpu.CompilerParams(vmem_limit_bytes=SMALL_BYTES),
        cost_estimate=pl.CostEstimate(
            flops=rows * width * features, bytes_accessed=width * features + 8 * rows * width, transcendentals=0
        ),
        name="project_kept",
    )(me, gated, out_weight, base)


def join_kernel(kept_ref, came_ref, out_ref):
    out_ref[...] = (kept_ref[...] + came_ref[...]).astype(jnp.bfloat16).T


def join(kept, came):
    rows, features = kept.shape
    wide = features // 4
    return pl.pallas_call(
        join_kernel,
        grid=(4,),
        in_specs=[pl.BlockSpec((rows, wide), lambda i: (0, i))] * 2,
        out_specs=pl.BlockSpec((wide, rows), lambda i: (i, 0)),
        out_shape=jax.ShapeDtypeStruct((features, rows), jnp.bfloat16),
        compiler_params=pltpu.CompilerParams(vmem_limit_bytes=SMALL_BYTES),
        name="join_halves",
    )(kept, came)


def exchange(slots):
    blocks = len(slots)
    upper, lower = list(range(blocks // 2, blocks)), list(range(1, blocks // 2))
    order = [slot for pair in zip(upper, lower + [0]) for slot in pair if slot]
    came = {0: slots[0]}
    for slot in order:
        came[slot] = lax.ppermute(slots[slot], "seq", [(j, j ^ slot) for j in range(blocks)])
    return [came[slot] for slot in range(blocks)]


def swap_blocks(array):
    return [lax.all_to_all(array, "seq", split_axis=0, concat_axis=0, tiled=True)]


def kernel_local(values, gates, filter_taps, skip_gain, out_weight):
    blocks = lax.axis_size("seq")
    me = jnp.stack([lax.axis_index("seq"), lax.axis_index("chan")]).astype(jnp.int32)
    first = exchange(arrange(me, values, filter_taps, blocks, 0, True))
    second = swap_blocks(*arrange(me, values, filter_taps, blocks, 1, False))
    first = swap_blocks(*convolve(me, first, blocks, 0, False))
    second = exchange(convolve(me, second, blocks, 1, True))
    (base,) = gate_and_project(me, first, gates, values, skip_gain, out_weight, 0)
    sent, gated = gate_and_project(me, second, gates, values, skip_gain, out_weight, 1, base)
    other = lax.ppermute(sent, "chan", [(0, 1), (1, 0)])
    kept = project_kept(me, gated, out_weight, base)
    return join(kept, other)


def takes_kernels(mesh, values, out_weight):
    blocks, halves = mesh.shape["seq"], mesh.shape["chan"]
    rows = values.shape[0] // blocks
    return (
        halves == 2
        and blocks == 16
        and rows == 256
        and values.shape[1] == halves * blocks * LANES
        and out_weight.shape[1] % (8 * LANES) == 0
    )


def solution(mesh):
    placed = (P("seq", "chan"), P("seq", "chan"), P("seq", "chan"), P("chan"), P("chan", None))

    def whole(values, gates, filter_taps, skip_gain, out_weight):
        local = kernel_local if takes_kernels(mesh, values, out_weight) else general_local
        return jax.shard_map(
            local, mesh=mesh, in_specs=placed, out_specs=P("chan", "seq"), check_vma=False
        )(values, gates, filter_taps, skip_gain, out_weight)

    return whole
```

```python
import functools
import math

import jax
import jax.numpy as jnp
import ml_dtypes
import numpy as np
from jax import lax
from jax.experimental import pallas as pl
from jax.experimental.pallas import tpu as pltpu
from jax.sharding import PartitionSpec as P

TWO_PI = 2.0 * math.pi
HIGH = lax.Precision.HIGHEST
RADIX = 16
LANES = 128
HALF = 64
VMEM_BYTES = 60 * 1024 * 1024


def angle_table(first, second, period):
    product = first[:, None] * second[None, :] % period
    angles = product.astype(jnp.float32) * (TWO_PI / period)
    return (jnp.cos(angles), jnp.sin(angles))


def mix(equation, left, right):
    return jnp.einsum(equation, left, right, precision=HIGH)


def outer_forward(data, outer_cos, outer_sin, twist_cos, twist_sin, equation):
    source = data.astype(jnp.float32)
    real = mix(equation, outer_cos, source)
    imag = -mix(equation, outer_sin, source)
    cos_part = twist_cos[:, :, None]
    sin_part = twist_sin[:, :, None]
    return (real * cos_part + imag * sin_part, imag * cos_part - real * sin_part)


def inner_filter(spectra, inner_cos, inner_sin):
    value_re, value_im, taps_re, taps_im = spectra

    def forward(real, imag):
        out_re = mix("kr,jrc->jkc", inner_cos, real) + mix("kr,jrc->jkc", inner_sin, imag)
        out_im = mix("kr,jrc->jkc", inner_cos, imag) - mix("kr,jrc->jkc", inner_sin, real)
        return (out_re, out_im)

    value_fre, value_fim = forward(value_re, value_im)
    taps_fre, taps_fim = forward(taps_re, taps_im)
    prod_re = value_fre * taps_fre - value_fim * taps_fim
    prod_im = value_fre * taps_fim + value_fim * taps_fre
    back_re = mix("rk,jkc->jrc", inner_cos, prod_re) - mix("rk,jkc->jrc", inner_sin, prod_im)
    back_im = mix("rk,jkc->jrc", inner_cos, prod_im) + mix("rk,jkc->jrc", inner_sin, prod_re)
    return (back_re, back_im)


def untwist(real, imag, twist_cos, twist_sin):
    cos_part = twist_cos[:, :, None]
    sin_part = twist_sin[:, :, None]
    return (real * cos_part - imag * sin_part, imag * cos_part + real * sin_part)


def channels_plan(values, filter_taps):
    rows, width = values.shape
    blocks = lax.axis_size("seq")
    length = 2 * blocks * rows
    narrow = width // blocks
    whole_values, whole_taps = (
        lax.all_to_all(values, "seq", split_axis=1, concat_axis=0, tiled=True),
        lax.all_to_all(filter_taps, "seq", split_axis=1, concat_axis=0, tiled=True),
    )
    freq_ids = jnp.arange(2 * blocks, dtype=jnp.int32)
    block_ids = jnp.arange(blocks, dtype=jnp.int32)
    all_rows = jnp.arange(rows, dtype=jnp.int32)
    outer_cos, outer_sin = angle_table(freq_ids, block_ids, 2 * blocks)
    twist_cos, twist_sin = angle_table(freq_ids, all_rows, length)
    tables = (outer_cos, outer_sin, twist_cos, twist_sin, "ka,arc->krc")
    value_re, value_im = outer_forward(whole_values.reshape(blocks, rows, narrow), *tables)
    taps_re, taps_im = outer_forward(whole_taps.reshape(blocks, rows, narrow), *tables)
    inner_cos, inner_sin = angle_table(all_rows, all_rows, rows)
    back_re, back_im = inner_filter((value_re, value_im, taps_re, taps_im), inner_cos, inner_sin)
    turned_re, turned_im = untwist(back_re, back_im, twist_cos, twist_sin)
    final_cos, final_sin = angle_table(block_ids, freq_ids, 2 * blocks)
    signal = (
        mix("ak,krc->arc", final_cos, turned_re) - mix("ak,krc->arc", final_sin, turned_im)
    ) / length
    returned = lax.all_to_all(signal, "seq", split_axis=0, concat_axis=2, tiled=True)
    return returned[0]


def general_local(values, gates, filter_taps, skip_gain, out_weight):
    conv = channels_plan(values, filter_taps)
    gated = (
        gates.astype(jnp.float32) * (conv + skip_gain[None, :] * values.astype(jnp.float32))
    ).astype(jnp.bfloat16)
    projected = lax.psum_scatter(
        lax.dot_general(
            out_weight, gated, (((0,), (1,)), ((), ())), preferred_element_type=jnp.float32
        ),
        "chan",
        scatter_dimension=0,
        tiled=True,
    )
    return projected.astype(jnp.bfloat16)


def split_table(table):
    high = table.astype(ml_dtypes.bfloat16)
    low = (table - high.astype(np.float64)).astype(ml_dtypes.bfloat16)
    return high, low


@functools.lru_cache(maxsize=None)
def transform_tables(length):
    inner = length // RADIX
    k = np.arange(inner)[:, None]
    m = np.arange(inner)[None, :]
    angles = (RADIX * m * (4 * k + 1)) % (4 * length) * (TWO_PI / (4 * length))
    table = np.concatenate([np.cos(angles), -np.sin(angles)], axis=0)
    forward = np.concatenate(split_table(table), axis=1)
    backward = np.concatenate(split_table(table.T / length), axis=0)
    turns = (np.arange(RADIX)[None, :] * (4 * k + 1)) % (4 * length) * (TWO_PI / (4 * length))
    turns = np.concatenate([np.cos(turns), np.sin(turns)], axis=1)
    turns = np.pad(turns, ((0, 0), (0, LANES - 2 * RADIX))).astype(np.float32)
    return forward, backward, turns


def tables_in_order(length):
    forward, backward, turns = transform_tables(length)
    return forward, turns, backward


@functools.lru_cache(maxsize=None)
def row_order(rows):
    chunk = rows // RADIX
    order = np.zeros((rows, rows), np.float32)
    for q in range(RADIX):
        for j in range(chunk):
            order[q * chunk + j, RADIX * j + q] = 1.0
    return order.astype(ml_dtypes.bfloat16)


def turn(point, index, sign):
    re, im = point
    index %= 16
    if index == 0:
        return point
    if index == 4:
        return (-im, re) if sign > 0 else (im, -re)
    if index == 8:
        return (-re, -im)
    half = math.sqrt(0.5)
    if index == 2:
        return ((re - im) * half, (re + im) * half) if sign > 0 else ((re + im) * half, (im - re) * half)
    if index == 6:
        return ((-re - im) * half, (re - im) * half) if sign > 0 else ((im - re) * half, (-re - im) * half)
    cos = math.cos(TWO_PI * index / 16)
    sin = sign * math.sin(TWO_PI * index / 16)
    return (re * cos - im * sin, re * sin + im * cos)


def four_points(points, sign):
    a, b, c, d = points
    ac = (a[0] + c[0], a[1] + c[1])
    am = (a[0] - c[0], a[1] - c[1])
    bd = (b[0] + d[0], b[1] + d[1])
    bm = (b[0] - d[0], b[1] - d[1])
    if sign < 0:
        side = (bm[1], -bm[0])
    else:
        side = (-bm[1], bm[0])
    return (
        (ac[0] + bd[0], ac[1] + bd[1]),
        (am[0] + side[0], am[1] + side[1]),
        (ac[0] - bd[0], ac[1] - bd[1]),
        (am[0] - side[0], am[1] - side[1]),
    )


def sixteen_points(points, sign):
    out = [None] * 16
    columns = []
    for low in range(4):
        column = four_points([points[low + 4 * high] for high in range(4)], sign)
        columns.append([turn(column[k], low * k, sign) for k in range(4)])
    for k in range(4):
        row = four_points([columns[low][k] for low in range(4)], sign)
        for high in range(4):
            out[k + 4 * high] = row[high]
    return out


def left_lanes(rows):
    return lax.broadcasted_iota(jnp.int32, (rows, LANES), 1) < HALF


def swap_halves(block):
    return pltpu.roll(block, HALF, 1)


def arrange_kernel(pieces, chunk, order_hbm, values_hbm, taps_hbm, out_hbm, order_ref, values_ref, taps_ref, packed, sems):
    wide = values_ref.shape[1]
    piece = wide // pieces
    loads = [pltpu.make_async_copy(order_hbm, order_ref, sems.at[3 * pieces])]
    stores = []
    for part in range(pieces):
        lanes = pl.ds(chunk * wide + part * piece, piece)
        to = pl.ds(part * piece, piece)
        loads.append(pltpu.make_async_copy(values_hbm.at[:, lanes], values_ref.at[:, to], sems.at[3 * part]))
        loads.append(pltpu.make_async_copy(taps_hbm.at[:, lanes], taps_ref.at[:, to], sems.at[3 * part + 1]))
        taken = pl.ds(part * piece // HALF, piece // HALF)
        stores.append(pltpu.make_async_copy(packed.at[taken], out_hbm.at[taken], sems.at[3 * part + 2]))
    for load in loads:
        load.start()
    loads[0].wait()
    left = left_lanes(order_ref.shape[0])
    for part in range(pieces):
        loads[2 * part + 1].wait()
        loads[2 * part + 2].wait()
        for pair in range(part * piece // LANES, (part + 1) * piece // LANES):
            lanes = pl.ds(pair * LANES, LANES)
            both = jnp.concatenate([values_ref[:, lanes], taps_ref[:, lanes]], axis=1)
            moved = jnp.dot(order_ref[...], both, preferred_element_type=jnp.float32)
            value, taps = moved[:, :LANES], moved[:, LANES:]
            packed[2 * pair] = jnp.where(left, value, swap_halves(taps)).astype(jnp.bfloat16)
            packed[2 * pair + 1] = jnp.where(left, swap_halves(value), taps).astype(jnp.bfloat16)
        stores[part].start()
    for store in stores:
        store.wait()


def arrange(values, taps, blocks, chunk):
    rows = values.shape[0]
    wide = blocks * HALF
    pieces = 4
    return pl.pallas_call(
        functools.partial(arrange_kernel, pieces, chunk),
        in_specs=[pl.BlockSpec(memory_space=pl.ANY)] * 3,
        out_specs=pl.BlockSpec(memory_space=pl.ANY),
        out_shape=jax.ShapeDtypeStruct((blocks, rows, LANES), jnp.bfloat16),
        scratch_shapes=[
            pltpu.VMEM((rows, rows), jnp.bfloat16),
            pltpu.VMEM((rows, wide), jnp.bfloat16),
            pltpu.VMEM((rows, wide), jnp.bfloat16),
            pltpu.VMEM((blocks, rows, LANES), jnp.bfloat16),
            pltpu.SemaphoreType.DMA((3 * pieces + 1,)),
        ],
        compiler_params=pltpu.CompilerParams(vmem_limit_bytes=VMEM_BYTES),
        cost_estimate=pl.CostEstimate(
            flops=4 * rows * rows * wide, bytes_accessed=8 * rows * wide, transcendentals=0
        ),
        name=f"arrange_{chunk}",
    )(jnp.asarray(row_order(rows)), values, taps)


def turned(point, turns, q, sign):
    if q == 0:
        return point
    re, im = point
    cos, sin = turns[0][q], turns[1][q]
    if sign < 0:
        return (re * cos + im * sin, im * cos - re * sin)
    return (re * cos - im * sin, im * cos + re * sin)


def spread(turns_ref, rows):
    block = turns_ref[rows]
    columns = [jnp.broadcast_to(block[:, i : i + 1], block.shape) for i in range(2 * RADIX)]
    return columns[:RADIX], columns[RADIX:]


def convolve_kernel(
    streams_hbm, forward_hbm, turns_hbm, backward_hbm, out_hbm,
    streams, forward_ref, turns_ref, backward_ref, spectra, signals, sems,
):
    blocks, rows, _ = streams.shape
    chunk = rows // RADIX
    inner = blocks * chunk
    part_rows = inner // 2
    pairs = RADIX // 2
    pieces = 4
    piece = rows // pieces
    loads = [pltpu.make_async_copy(forward_hbm, forward_ref, sems.at[0])]
    for part in range(pieces):
        taken = pl.ds(part * piece, piece)
        loads.append(pltpu.make_async_copy(streams_hbm.at[:, taken], streams.at[:, taken], sems.at[1 + part]))
    loads.append(pltpu.make_async_copy(turns_hbm, turns_ref, sems.at[1 + pieces]))
    loads.append(pltpu.make_async_copy(backward_hbm, backward_ref, sems.at[2 + pieces]))
    for load in loads:
        load.start()
    loads[0].wait()

    def stream_of(q):
        return streams[:, pl.ds(pl.multiple_of(q * chunk, chunk), chunk)].reshape(inner, LANES)

    def forward_step(pair, carry):
        both = jnp.concatenate([stream_of(2 * pair), stream_of(2 * pair + 1)], axis=1)
        result = jnp.dot(
            forward_ref[...], jnp.concatenate([both, both], axis=0), preferred_element_type=jnp.float32
        )
        spectra[2 * pair] = result[:, :LANES]
        spectra[2 * pair + 1] = result[:, LANES:]
        return carry

    for part in range(pieces):
        loads[1 + part].wait()
        lax.fori_loop(part * pairs // pieces, (part + 1) * pairs // pieces, forward_step, 0)
    loads[1 + pieces].wait()
    left = left_lanes(8)

    def rows_step(index, carry):
        starts = [pl.multiple_of(base + index * 8, 8) for base in range(0, 2 * inner, part_rows)]
        first_re, second_re, first_im, second_im = [pl.ds(start, 8) for start in starts]
        first_turns = spread(turns_ref, first_re)
        second_turns = spread(turns_ref, second_re)
        first = sixteen_points(
            [turned((spectra[q, first_re], spectra[q, first_im]), first_turns, q, -1) for q in range(RADIX)], -1
        )
        second = sixteen_points(
            [turned((spectra[q, second_re], spectra[q, second_im]), second_turns, q, -1) for q in range(RADIX)], -1
        )
        product = []
        for one, two in zip(first, second):
            a = [jnp.where(left, x, y) for x, y in zip(one, two)]
            b = [swap_halves(jnp.where(left, y, x)) for x, y in zip(one, two)]
            product.append((a[0] * b[0] - a[1] * b[1], a[0] * b[1] + a[1] * b[0]))
        back = sixteen_points(product, 1)
        mixed = [
            [jnp.where(left, x, y) for x, y in zip(one, two)] for one, two in zip(first_turns, second_turns)
        ]
        for q in range(RADIX):
            spectra[q, first_re], spectra[q, first_im] = turned(back[q], mixed, q, 1)
        return carry

    lax.fori_loop(0, part_rows // 8, rows_step, 0)
    loads[2 + pieces].wait()
    left_part = left_lanes(part_rows)
    left_inner = left_lanes(inner)

    def backward_step(pair, carry):
        columns = []
        for q in (pair, pair + pairs):
            pieces = []
            for base in (0, inner):
                points = spectra[q, pl.ds(base, part_rows)]
                high = points.astype(jnp.bfloat16).astype(jnp.float32)
                low = points - high
                pieces.append(jnp.where(left_part, high, swap_halves(low)).astype(jnp.bfloat16))
                pieces.append(jnp.where(left_part, swap_halves(high), low).astype(jnp.bfloat16))
            columns.append(jnp.concatenate(pieces, axis=0))
        terms = jnp.dot(
            backward_ref[...], jnp.concatenate(columns, axis=1), preferred_element_type=jnp.float32
        )
        total = terms[:inner] + terms[inner:]
        sides = [part + swap_halves(part) for part in (total[:, :LANES], total[:, LANES:])]
        signal = jnp.where(left_inner, *sides).astype(jnp.bfloat16).reshape(blocks, chunk, LANES)
        signals[:, pl.ds(pl.multiple_of(pair * chunk, chunk), chunk)] = signal
        return carry

    stores = []
    half = pairs * chunk // 2
    for part in range(2):
        lax.fori_loop(part * pairs // 2, (part + 1) * pairs // 2, backward_step, 0)
        taken = pl.ds(part * half, half)
        stores.append(pltpu.make_async_copy(signals.at[:, taken], out_hbm.at[:, taken], sems.at[3 + pieces + part]))
        stores[part].start()
    for store in stores:
        store.wait()


def convolve(streams, chunk_id):
    blocks, rows, _ = streams.shape
    length = blocks * rows
    inner = length // RADIX
    return pl.pallas_call(
        convolve_kernel,
        in_specs=[pl.BlockSpec(memory_space=pl.ANY)] * 4,
        out_specs=pl.BlockSpec(memory_space=pl.ANY),
        out_shape=jax.ShapeDtypeStruct((blocks, rows // 2, LANES), jnp.bfloat16),
        scratch_shapes=[
            pltpu.VMEM((blocks, rows, LANES), jnp.bfloat16),
            pltpu.VMEM((2 * inner, 2 * inner), jnp.bfloat16),
            pltpu.VMEM((inner, LANES), jnp.float32),
            pltpu.VMEM((2 * inner, 2 * inner), jnp.bfloat16),
            pltpu.VMEM((RADIX, 2 * inner, LANES), jnp.float32),
            pltpu.VMEM((blocks, rows // 2, LANES), jnp.bfloat16),
            pltpu.SemaphoreType.DMA((9,)),
        ],
        compiler_params=pltpu.CompilerParams(vmem_limit_bytes=VMEM_BYTES),
        cost_estimate=pl.CostEstimate(flops=6 * 10**9, bytes_accessed=24 * 10**6, transcendentals=0),
        name=f"long_convolution_{chunk_id}",
    )(streams, *(jnp.asarray(table) for table in tables_in_order(length)))


def gate_kernel(joined, me_ref, parts, *rest):
    if joined:
        order_ref, gates_ref, values_ref, skip_ref, weight_ref, base_ref, out_ref, gated_ref = rest
    else:
        order_ref, gates_ref, values_ref, skip_ref, weight_ref, out_ref = rest
    del me_ref
    step = pl.program_id(0)
    wide = gates_ref.shape[1]
    pairs = wide // LANES
    left = left_lanes(parts.shape[1])
    columns = []
    for pair in range(pairs):
        even = parts[2 * (step * pairs + pair)].astype(jnp.float32)
        odd = parts[2 * (step * pairs + pair) + 1].astype(jnp.float32)
        low = jnp.where(left, even, swap_halves(odd))
        high = jnp.where(left, swap_halves(even), odd)
        columns.append(jnp.concatenate([low, high], axis=0).astype(jnp.bfloat16))
    conv = jnp.dot(
        order_ref[...], jnp.concatenate(columns, axis=1), preferred_element_type=jnp.float32
    )
    direct = skip_ref[...] * values_ref[...].astype(jnp.float32)
    gated = (gates_ref[...].astype(jnp.float32) * (conv + direct)).astype(jnp.bfloat16)
    if joined:
        gated_ref[...] = gated
    term = jnp.dot(gated, weight_ref[...], preferred_element_type=jnp.float32)

    @pl.when(step == 0)
    def _():
        out_ref[...] = base_ref[...] + term if joined else term

    @pl.when(step > 0)
    def _():
        out_ref[...] += term


def gate_and_project(me, parts, gates, values, skip_gain, out_weight, chunk, base=None):
    blocks = parts.shape[0]
    rows = gates.shape[0]
    features = out_weight.shape[1]
    steps = 4
    wide = blocks * HALF // steps
    joined = base is not None
    taken = features // 2 if joined else features
    in_specs = [
        pl.BlockSpec(parts.shape, lambda i, me: (0, 0, 0)),
        pl.BlockSpec((rows, rows), lambda i, me: (0, 0)),
        pl.BlockSpec((rows, wide), lambda i, me: (0, chunk * steps + i)),
        pl.BlockSpec((rows, wide), lambda i, me: (0, chunk * steps + i)),
        pl.BlockSpec((1, wide), lambda i, me: (0, chunk * steps + i)),
    ]
    operands = [me, parts, jnp.asarray(row_order(rows).T), gates, values, skip_gain[None, :], out_weight]
    out_specs = [pl.BlockSpec((rows, taken), lambda i, me: (0, 0))]
    out_shape = [jax.ShapeDtypeStruct((rows, taken), jnp.float32)]
    if joined:
        in_specs.append(pl.BlockSpec((wide, taken), lambda i, me: (chunk * steps + i, 1 - me[1])))
        in_specs.append(pl.BlockSpec((rows, taken), lambda i, me: (0, 1 - me[1])))
        operands.append(base)
        out_specs.append(pl.BlockSpec((rows, wide), lambda i, me: (0, i)))
        out_shape.append(jax.ShapeDtypeStruct((rows, steps * wide), jnp.bfloat16))
    else:
        in_specs.append(pl.BlockSpec((wide, taken), lambda i, me: (chunk * steps + i, 0)))
    return pl.pallas_call(
        functools.partial(gate_kernel, joined),
        grid_spec=pltpu.PrefetchScalarGridSpec(
            num_scalar_prefetch=1,
            grid=(steps,),
            in_specs=in_specs,
            out_specs=out_specs,
        ),
        out_shape=out_shape,
        compiler_params=pltpu.CompilerParams(vmem_limit_bytes=VMEM_BYTES),
        cost_estimate=pl.CostEstimate(
            flops=2 * rows * steps * wide * taken,
            bytes_accessed=2 * steps * wide * taken + 12 * rows * steps * wide,
            transcendentals=0,
        ),
        name=f"gate_project_{chunk}",
    )(*operands)


def kept_kernel(me_ref, gated_ref, weight_ref, base_ref, out_ref):
    del me_ref
    step = pl.program_id(0)
    term = jnp.dot(gated_ref[...], weight_ref[...], preferred_element_type=jnp.float32)

    @pl.when(step == 0)
    def _():
        out_ref[...] = base_ref[...] + term

    @pl.when(step > 0)
    def _():
        out_ref[...] += term


def project_kept(me, gated, out_weight, base):
    rows, width = gated.shape
    features = out_weight.shape[1]
    steps = 2
    deep = width // steps
    return pl.pallas_call(
        kept_kernel,
        grid_spec=pltpu.PrefetchScalarGridSpec(
            num_scalar_prefetch=1,
            grid=(steps,),
            in_specs=[
                pl.BlockSpec((rows, deep), lambda i, me: (0, i)),
                pl.BlockSpec((deep, features // 2), lambda i, me: (steps + i, me[1])),
                pl.BlockSpec((rows, features // 2), lambda i, me: (0, me[1])),
            ],
            out_specs=pl.BlockSpec((rows, features // 2), lambda i, me: (0, 0)),
        ),
        out_shape=jax.ShapeDtypeStruct((rows, features // 2), jnp.float32),
        compiler_params=pltpu.CompilerParams(vmem_limit_bytes=VMEM_BYTES),
        cost_estimate=pl.CostEstimate(
            flops=rows * width * features, bytes_accessed=width * features + 8 * rows * width, transcendentals=0
        ),
        name="project_kept",
    )(me, gated, out_weight, base)


def join_kernel(kept_ref, came_ref, out_ref):
    out_ref[...] = (kept_ref[...] + came_ref[...]).astype(jnp.bfloat16).T


def join(kept, came):
    rows, features = kept.shape
    wide = features // 4
    return pl.pallas_call(
        join_kernel,
        grid=(4,),
        in_specs=[pl.BlockSpec((rows, wide), lambda i: (0, i))] * 2,
        out_specs=pl.BlockSpec((wide, rows), lambda i: (i, 0)),
        out_shape=jax.ShapeDtypeStruct((features, rows), jnp.bfloat16),
        compiler_params=pltpu.CompilerParams(vmem_limit_bytes=VMEM_BYTES),
        name="join_halves",
    )(kept, came)


def swap_blocks(array):
    return lax.all_to_all(array, "seq", split_axis=0, concat_axis=0, tiled=True)


def kernel_local(values, gates, filter_taps, skip_gain, out_weight):
    blocks = lax.axis_size("seq")
    me = jnp.stack([lax.axis_index("seq"), lax.axis_index("chan")]).astype(jnp.int32)
    streams = [swap_blocks(arrange(values, filter_taps, blocks, chunk)) for chunk in range(2)]
    conv = [swap_blocks(convolve(streams[chunk], chunk)) for chunk in range(2)]
    (base,) = gate_and_project(me, conv[0], gates, values, skip_gain, out_weight, 0)
    sent, gated = gate_and_project(me, conv[1], gates, values, skip_gain, out_weight, 1, base)
    other = lax.ppermute(sent, "chan", [(0, 1), (1, 0)])
    kept = project_kept(me, gated, out_weight, base)
    return join(kept, other)


def takes_kernels(mesh, values, out_weight):
    blocks, halves = mesh.shape["seq"], mesh.shape["chan"]
    rows = values.shape[0] // blocks
    return (
        halves == 2
        and blocks == 16
        and rows == 256
        and values.shape[1] == halves * blocks * LANES
        and out_weight.shape[1] % (8 * LANES) == 0
    )


def solution(mesh):
    placed = (P("seq", "chan"), P("seq", "chan"), P("seq", "chan"), P("chan"), P("chan", None))

    def whole(values, gates, filter_taps, skip_gain, out_weight):
        local = kernel_local if takes_kernels(mesh, values, out_weight) else general_local
        return jax.shard_map(
            local, mesh=mesh, in_specs=placed, out_specs=P("chan", "seq"), check_vma=False
        )(values, gates, filter_taps, skip_gain, out_weight)

    return whole
```

```python
import functools
import math

import jax
import jax.numpy as jnp
import ml_dtypes
import numpy as np
from jax import lax
from jax.experimental import pallas as pl
from jax.experimental.pallas import tpu as pltpu
from jax.sharding import PartitionSpec as P

TWO_PI = 2.0 * math.pi
HIGH = lax.Precision.HIGHEST
RADIX = 16
LANES = 128
Q_ORDER = [low + 4 * high for low in range(4) for high in range(4)]
VMEM_BYTES = 60 * 1024 * 1024


def angle_table(first, second, period):
    product = first[:, None] * second[None, :] % period
    angles = product.astype(jnp.float32) * (TWO_PI / period)
    return (jnp.cos(angles), jnp.sin(angles))


def mix(equation, left, right):
    return jnp.einsum(equation, left, right, precision=HIGH)


def outer_forward(data, outer_cos, outer_sin, twist_cos, twist_sin, equation):
    source = data.astype(jnp.float32)
    real = mix(equation, outer_cos, source)
    imag = -mix(equation, outer_sin, source)
    cos_part = twist_cos[:, :, None]
    sin_part = twist_sin[:, :, None]
    return (real * cos_part + imag * sin_part, imag * cos_part - real * sin_part)


def inner_filter(spectra, inner_cos, inner_sin):
    value_re, value_im, taps_re, taps_im = spectra

    def forward(real, imag):
        out_re = mix("kr,jrc->jkc", inner_cos, real) + mix("kr,jrc->jkc", inner_sin, imag)
        out_im = mix("kr,jrc->jkc", inner_cos, imag) - mix("kr,jrc->jkc", inner_sin, real)
        return (out_re, out_im)

    value_fre, value_fim = forward(value_re, value_im)
    taps_fre, taps_fim = forward(taps_re, taps_im)
    prod_re = value_fre * taps_fre - value_fim * taps_fim
    prod_im = value_fre * taps_fim + value_fim * taps_fre
    back_re = mix("rk,jkc->jrc", inner_cos, prod_re) - mix("rk,jkc->jrc", inner_sin, prod_im)
    back_im = mix("rk,jkc->jrc", inner_cos, prod_im) + mix("rk,jkc->jrc", inner_sin, prod_re)
    return (back_re, back_im)


def untwist(real, imag, twist_cos, twist_sin):
    cos_part = twist_cos[:, :, None]
    sin_part = twist_sin[:, :, None]
    return (real * cos_part - imag * sin_part, imag * cos_part + real * sin_part)


def channels_plan(values, filter_taps):
    rows, width = values.shape
    blocks = lax.axis_size("seq")
    length = 2 * blocks * rows
    narrow = width // blocks
    whole_values, whole_taps = (
        lax.all_to_all(values, "seq", split_axis=1, concat_axis=0, tiled=True),
        lax.all_to_all(filter_taps, "seq", split_axis=1, concat_axis=0, tiled=True),
    )
    freq_ids = jnp.arange(2 * blocks, dtype=jnp.int32)
    block_ids = jnp.arange(blocks, dtype=jnp.int32)
    all_rows = jnp.arange(rows, dtype=jnp.int32)
    outer_cos, outer_sin = angle_table(freq_ids, block_ids, 2 * blocks)
    twist_cos, twist_sin = angle_table(freq_ids, all_rows, length)
    tables = (outer_cos, outer_sin, twist_cos, twist_sin, "ka,arc->krc")
    value_re, value_im = outer_forward(whole_values.reshape(blocks, rows, narrow), *tables)
    taps_re, taps_im = outer_forward(whole_taps.reshape(blocks, rows, narrow), *tables)
    inner_cos, inner_sin = angle_table(all_rows, all_rows, rows)
    back_re, back_im = inner_filter((value_re, value_im, taps_re, taps_im), inner_cos, inner_sin)
    turned_re, turned_im = untwist(back_re, back_im, twist_cos, twist_sin)
    final_cos, final_sin = angle_table(block_ids, freq_ids, 2 * blocks)
    signal = (
        mix("ak,krc->arc", final_cos, turned_re) - mix("ak,krc->arc", final_sin, turned_im)
    ) / length
    returned = lax.all_to_all(signal, "seq", split_axis=0, concat_axis=2, tiled=True)
    return returned[0]


def general_local(values, gates, filter_taps, skip_gain, out_weight):
    conv = channels_plan(values, filter_taps)
    gated = (
        gates.astype(jnp.float32) * (conv + skip_gain[None, :] * values.astype(jnp.float32))
    ).astype(jnp.bfloat16)
    projected = lax.psum_scatter(
        lax.dot_general(
            out_weight, gated, (((0,), (1,)), ((), ())), preferred_element_type=jnp.float32
        ),
        "chan",
        scatter_dimension=0,
        tiled=True,
    )
    return projected.astype(jnp.bfloat16)


def split_table(table):
    high = table.astype(ml_dtypes.bfloat16)
    low = (table - high.astype(np.float64)).astype(ml_dtypes.bfloat16)
    return high, low


@functools.lru_cache(maxsize=None)
def transform_tables(length):
    inner = length // RADIX
    k = np.arange(inner)[:, None]
    m = np.arange(inner)[None, :]
    angles = (RADIX * m * (4 * k + 1)) % (4 * length) * (TWO_PI / (4 * length))
    table = np.concatenate([np.cos(angles), -np.sin(angles)], axis=0)
    forward = np.concatenate(split_table(table), axis=1)
    backward = np.concatenate(split_table(table.T / length), axis=0)
    turns = (np.array(Q_ORDER)[:, None] * (4 * k.T + 1)) % (4 * length) * (TWO_PI / (4 * length))
    turns = np.stack([np.cos(turns), np.sin(turns)], axis=1).astype(np.float32)
    turns = np.ascontiguousarray(np.broadcast_to(turns[..., None], (*turns.shape, LANES)))
    return forward, turns, backward


@functools.lru_cache(maxsize=None)
def row_order(rows):
    chunk = rows // RADIX
    order = np.zeros((rows, rows), np.float32)
    for i, q in enumerate(Q_ORDER):
        for j in range(chunk):
            order[i * chunk + j, RADIX * j + q] = 1.0
    return order.astype(ml_dtypes.bfloat16)


def turn(point, index, sign):
    re, im = point
    index %= 16
    if index == 0:
        return point
    if index == 4:
        return (-im, re) if sign > 0 else (im, -re)
    if index == 8:
        return (-re, -im)
    half = math.sqrt(0.5)
    if index == 2:
        return ((re - im) * half, (re + im) * half) if sign > 0 else ((re + im) * half, (im - re) * half)
    if index == 6:
        return ((-re - im) * half, (re - im) * half) if sign > 0 else ((im - re) * half, (-re - im) * half)
    cos = math.cos(TWO_PI * index / 16)
    sin = sign * math.sin(TWO_PI * index / 16)
    return (re * cos - im * sin, re * sin + im * cos)


def four_points(points, sign):
    a, b, c, d = points
    ac = (a[0] + c[0], a[1] + c[1])
    am = (a[0] - c[0], a[1] - c[1])
    bd = (b[0] + d[0], b[1] + d[1])
    bm = (b[0] - d[0], b[1] - d[1])
    if sign < 0:
        side = (bm[1], -bm[0])
    else:
        side = (-bm[1], bm[0])
    return (
        (ac[0] + bd[0], ac[1] + bd[1]),
        (am[0] + side[0], am[1] + side[1]),
        (ac[0] - bd[0], ac[1] - bd[1]),
        (am[0] - side[0], am[1] - side[1]),
    )


def turned(point, cos, sin, sign):
    re, im = point
    if sign < 0:
        return (re * cos + im * sin, im * cos - re * sin)
    return (re * cos - im * sin, im * cos + re * sin)


def arrange_kernel(pieces, order_hbm, values_hbm, taps_hbm, out_hbm, order_ref, values_ref, taps_ref, packed, sems):
    piece = values_ref.shape[1] // pieces
    loads = [pltpu.make_async_copy(order_hbm, order_ref, sems.at[3 * pieces])]
    stores = []
    for part in range(pieces):
        lanes = pl.ds(part * piece, piece)
        loads.append(pltpu.make_async_copy(values_hbm.at[:, lanes], values_ref.at[:, lanes], sems.at[3 * part]))
        loads.append(pltpu.make_async_copy(taps_hbm.at[:, lanes], taps_ref.at[:, lanes], sems.at[3 * part + 1]))
        taken = pl.ds(part * piece // LANES, piece // LANES)
        stores.append(pltpu.make_async_copy(packed.at[taken], out_hbm.at[taken], sems.at[3 * part + 2]))
    for load in loads:
        load.start()
    loads[0].wait()
    for part in range(pieces):
        for side, source in enumerate((values_ref, taps_ref)):
            loads[2 * part + 1 + side].wait()
            lanes = pl.ds(part * piece, piece)
            moved = jnp.dot(order_ref[...], source[:, lanes], preferred_element_type=jnp.float32).astype(jnp.bfloat16)
            for block in range(piece // LANES):
                packed[part * piece // LANES + block, :, pl.ds(side * LANES, LANES)] = moved[
                    :, block * LANES : (block + 1) * LANES
                ]
        stores[part].start()
    for store in stores:
        store.wait()


def arrange(values, taps, blocks):
    rows, wide = values.shape
    pieces = 8
    return pl.pallas_call(
        functools.partial(arrange_kernel, pieces),
        in_specs=[pl.BlockSpec(memory_space=pl.ANY)] * 3,
        out_specs=pl.BlockSpec(memory_space=pl.ANY),
        out_shape=jax.ShapeDtypeStruct((blocks, rows, 2 * LANES), jnp.bfloat16),
        scratch_shapes=[
            pltpu.VMEM((rows, rows), jnp.bfloat16),
            pltpu.VMEM((rows, wide), jnp.bfloat16),
            pltpu.VMEM((rows, wide), jnp.bfloat16),
            pltpu.VMEM((blocks, rows, 2 * LANES), jnp.bfloat16),
            pltpu.SemaphoreType.DMA((3 * pieces + 1,)),
        ],
        compiler_params=pltpu.CompilerParams(vmem_limit_bytes=VMEM_BYTES),
        cost_estimate=pl.CostEstimate(
            flops=4 * rows * rows * wide, bytes_accessed=8 * rows * wide, transcendentals=0
        ),
        name="arrange_rows",
    )(jnp.asarray(row_order(rows)), values, taps)


def convolve_kernel(
    streams_hbm, forward_hbm, turns_hbm, backward_hbm, out_hbm,
    streams, forward_ref, turns_ref, backward_ref,
    raw_even, raw_odd, columns, mixed, halves_even, halves_odd, signals, sems,
):
    blocks, rows, _ = streams.shape
    chunk = rows // RADIX
    inner = blocks * chunk
    group = rows // 4
    raws = (raw_even, raw_odd)
    halves = (halves_even, halves_odd)
    load_forward = pltpu.make_async_copy(forward_hbm, forward_ref, sems.at[0])
    load_backward = pltpu.make_async_copy(backward_hbm, backward_ref, sems.at[1])
    load_streams, load_turns, stores = [], [], []
    for low in range(4):
        taken = pl.ds(low * group, group)
        load_streams.append(pltpu.make_async_copy(streams_hbm.at[:, taken], streams.at[:, taken], sems.at[2 + low]))
        four = pl.ds(4 * low, 4)
        load_turns.append(pltpu.make_async_copy(turns_hbm.at[four], turns_ref.at[four], sems.at[6 + low]))
        stores.append(pltpu.make_async_copy(signals.at[:, taken], out_hbm.at[:, taken], sems.at[10 + low]))
    load_forward.start()
    load_streams[0].start()
    load_streams[1].start()
    load_turns[0].start()
    load_streams[2].start()
    load_turns[1].start()
    load_streams[3].start()
    load_turns[2].start()
    load_turns[3].start()
    load_backward.start()

    def transform(low, high):
        taken = pl.ds(pl.multiple_of(low * group + high * chunk, chunk), chunk)
        stream = streams[:, taken].reshape(inner, 2 * LANES)
        raws[low % 2][high] = jnp.dot(
            forward_ref[...], jnp.concatenate([stream, stream], axis=0), preferred_element_type=jnp.float32
        )

    def first_pass(low, start):
        raw = raws[low % 2]
        upper, lower = pl.ds(start, 8), pl.ds(inner + start, 8)
        for side in range(2):
            lanes = pl.ds(side * LANES, LANES)
            points = []
            for high in range(4):
                point = (raw[high, upper, lanes], raw[high, lower, lanes])
                if low + high:
                    turns = [turns_ref[4 * low + high, part, upper] for part in range(2)]
                    point = turned(point, *turns, -1)
                points.append(point)
            for k, point in enumerate(four_points(points, -1)):
                point = turn(point, low * k, -1)
                columns[4 * low + k, upper, lanes] = point[0]
                columns[4 * low + k, lower, lanes] = point[1]

    def first_rows(low, start, count):
        for part in range(count):
            first_pass(low, pl.multiple_of(start + 8 * part, 8))

    steps = inner // 4

    load_forward.wait()
    load_streams[0].wait()

    def alone(high, carry):
        transform(0, high)
        return carry

    lax.fori_loop(0, 4, alone, 0)
    for low in range(1, 4):
        load_streams[low].wait()
        load_turns[low - 1].wait()

        def beside(high, carry, low=low):
            transform(low, high)
            first_rows(low - 1, high * steps, steps // 8)
            return carry

        lax.fori_loop(0, 4, beside, 0)
    load_turns[3].wait()

    def middle(index, carry):
        start = pl.multiple_of(index * 8, 8)
        first_pass(3, start)
        upper, lower = pl.ds(start, 8), pl.ds(inner + start, 8)
        for k in range(4):
            sides = []
            for side in range(2):
                lanes = pl.ds(side * LANES, LANES)
                points = [(columns[4 * low + k, upper, lanes], columns[4 * low + k, lower, lanes]) for low in range(4)]
                sides.append(four_points(points, -1))
            product = [
                (a[0] * b[0] - a[1] * b[1], a[0] * b[1] + a[1] * b[0]) for a, b in zip(*sides)
            ]
            for part, point in enumerate(four_points(product, 1)):
                point = turn(point, k * part, 1)
                mixed[4 * part + k, upper] = point[0]
                mixed[4 * part + k, lower] = point[1]
        return carry

    lax.fori_loop(0, inner // 8, middle, 0)

    def last_pass(low, start):
        target = halves[low % 2]
        upper, lower = pl.ds(start, 16), pl.ds(inner + start, 16)
        points = [(mixed[4 * low + k, upper], mixed[4 * low + k, lower]) for k in range(4)]
        for high, point in enumerate(four_points(points, 1)):
            if low + high:
                turns = [turns_ref[4 * low + high, part, upper] for part in range(2)]
                point = turned(point, *turns, 1)
            for part, taken in zip(point, (upper, lower)):
                rounded = part.astype(jnp.bfloat16)
                target[high, taken, pl.ds(0, LANES)] = rounded
                target[high, taken, pl.ds(LANES, LANES)] = (part - rounded.astype(jnp.float32)).astype(jnp.bfloat16)

    def last_rows(low, start, count):
        for part in range(count):
            last_pass(low, pl.multiple_of(start + 16 * part, 16))

    def restore(low, high):
        terms = jnp.dot(backward_ref[...], halves[low % 2][high], preferred_element_type=jnp.float32)
        signal = terms[:inner, :LANES] + terms[:inner, LANES:] + terms[inner:, :LANES]
        taken = pl.ds(pl.multiple_of(low * group + high * chunk, chunk), chunk)
        signals[:, taken] = signal.astype(jnp.bfloat16).reshape(blocks, chunk, LANES)

    def prepare(index, carry):
        last_rows(0, index * steps, steps // 16)
        return carry

    lax.fori_loop(0, 4, prepare, 0)
    load_backward.wait()
    for low in range(4):

        def back(high, carry, low=low):
            restore(low, high)
            if low < 3:
                last_rows(low + 1, high * steps, steps // 16)
            return carry

        lax.fori_loop(0, 4, back, 0)
        stores[low].start()
    for store in stores:
        store.wait()


def convolve(streams):
    blocks, rows, lanes = streams.shape
    length = blocks * rows
    inner = length // RADIX
    return pl.pallas_call(
        convolve_kernel,
        in_specs=[pl.BlockSpec(memory_space=pl.ANY)] * 4,
        out_specs=pl.BlockSpec(memory_space=pl.ANY),
        out_shape=jax.ShapeDtypeStruct((blocks, rows, LANES), jnp.bfloat16),
        scratch_shapes=[
            pltpu.VMEM(streams.shape, jnp.bfloat16),
            pltpu.VMEM((2 * inner, 2 * inner), jnp.bfloat16),
            pltpu.VMEM((RADIX, 2, inner, LANES), jnp.float32),
            pltpu.VMEM((2 * inner, 2 * inner), jnp.bfloat16),
            pltpu.VMEM((4, 2 * inner, lanes), jnp.float32),
            pltpu.VMEM((4, 2 * inner, lanes), jnp.float32),
            pltpu.VMEM((RADIX, 2 * inner, lanes), jnp.float32),
            pltpu.VMEM((RADIX, 2 * inner, LANES), jnp.float32),
            pltpu.VMEM((4, 2 * inner, lanes), jnp.bfloat16),
            pltpu.VMEM((4, 2 * inner, lanes), jnp.bfloat16),
            pltpu.VMEM((blocks, rows, LANES), jnp.bfloat16),
            pltpu.SemaphoreType.DMA((14,)),
        ],
        compiler_params=pltpu.CompilerParams(vmem_limit_bytes=VMEM_BYTES),
        cost_estimate=pl.CostEstimate(flops=9 * 10**9, bytes_accessed=9 * 10**6, transcendentals=0),
        name="long_convolution",
    )(streams, *(jnp.asarray(table) for table in transform_tables(length)))


def gate_kernel(group, half_ref, order_ref, conv_ref, gates_ref, values_ref, skip_ref, weight_ref, gated_ref, out_ref):
    del half_ref
    step = pl.program_id(0)
    conv = jnp.concatenate([conv_ref[part] for part in range(group)], axis=1)
    conv = jnp.dot(order_ref[...], conv, preferred_element_type=jnp.float32)
    direct = skip_ref[...] * values_ref[...].astype(jnp.float32)
    gated = (gates_ref[...].astype(jnp.float32) * (conv + direct)).astype(jnp.bfloat16)
    gated_ref[...] = gated
    term = jnp.dot(gated, weight_ref[...], preferred_element_type=jnp.float32)

    @pl.when(step == 0)
    def _():
        out_ref[...] = term

    @pl.when(step > 0)
    def _():
        out_ref[...] += term


def gate_and_project(half, conv, gates, values, skip_gain, out_weight):
    blocks, rows, lanes = conv.shape
    width, features = out_weight.shape
    group = 4
    wide = group * lanes
    return pl.pallas_call(
        functools.partial(gate_kernel, group),
        grid_spec=pltpu.PrefetchScalarGridSpec(
            num_scalar_prefetch=1,
            grid=(blocks // group,),
            in_specs=[
                pl.BlockSpec((rows, rows), lambda i, h: (0, 0)),
                pl.BlockSpec((group, rows, lanes), lambda i, h: (i, 0, 0)),
                pl.BlockSpec((rows, wide), lambda i, h: (0, i)),
                pl.BlockSpec((rows, wide), lambda i, h: (0, i)),
                pl.BlockSpec((1, wide), lambda i, h: (0, i)),
                pl.BlockSpec((wide, features // 2), lambda i, h: (i, 1 - h[0])),
            ],
            out_specs=[
                pl.BlockSpec((rows, wide), lambda i, h: (0, i)),
                pl.BlockSpec((rows, features // 2), lambda i, h: (0, 0)),
            ],
        ),
        out_shape=[
            jax.ShapeDtypeStruct((rows, width), jnp.bfloat16),
            jax.ShapeDtypeStruct((rows, features // 2), jnp.float32),
        ],
        compiler_params=pltpu.CompilerParams(vmem_limit_bytes=VMEM_BYTES),
        cost_estimate=pl.CostEstimate(
            flops=rows * width * features, bytes_accessed=width * features + 8 * rows * width, transcendentals=0
        ),
        name="gate_project_sent",
    )(half, jnp.asarray(row_order(rows).T), conv, gates, values, skip_gain[None, :], out_weight)


def kept_kernel(half_ref, gated_ref, weight_ref, out_ref):
    del half_ref
    step = pl.program_id(0)
    term = jnp.dot(gated_ref[...], weight_ref[...], preferred_element_type=jnp.float32)

    @pl.when(step == 0)
    def _():
        out_ref[...] = term

    @pl.when(step > 0)
    def _():
        out_ref[...] += term


def project_kept(half, gated, out_weight):
    rows, width = gated.shape
    features = out_weight.shape[1]
    deep = width // 4
    return pl.pallas_call(
        kept_kernel,
        grid_spec=pltpu.PrefetchScalarGridSpec(
            num_scalar_prefetch=1,
            grid=(4,),
            in_specs=[
                pl.BlockSpec((rows, deep), lambda i, h: (0, i)),
                pl.BlockSpec((deep, features // 2), lambda i, h: (i, h[0])),
            ],
            out_specs=pl.BlockSpec((rows, features // 2), lambda i, h: (0, 0)),
        ),
        out_shape=jax.ShapeDtypeStruct((rows, features // 2), jnp.float32),
        compiler_params=pltpu.CompilerParams(vmem_limit_bytes=VMEM_BYTES),
        cost_estimate=pl.CostEstimate(
            flops=rows * width * features, bytes_accessed=width * features + 4 * rows * width, transcendentals=0
        ),
        name="project_kept",
    )(half, gated, out_weight)


def join_kernel(kept_ref, came_ref, out_ref):
    out_ref[...] = (kept_ref[...] + came_ref[...]).astype(jnp.bfloat16).T


def join(kept, came):
    rows, features = kept.shape
    wide = features // 4
    return pl.pallas_call(
        join_kernel,
        grid=(4,),
        in_specs=[pl.BlockSpec((rows, wide), lambda i: (0, i))] * 2,
        out_specs=pl.BlockSpec((wide, rows), lambda i: (i, 0)),
        out_shape=jax.ShapeDtypeStruct((features, rows), jnp.bfloat16),
        compiler_params=pltpu.CompilerParams(vmem_limit_bytes=VMEM_BYTES),
        name="join_halves",
    )(kept, came)


def swap_blocks(array):
    return lax.all_to_all(array, "seq", split_axis=0, concat_axis=0, tiled=True)


def kernel_local(values, gates, filter_taps, skip_gain, out_weight):
    blocks = lax.axis_size("seq")
    conv = swap_blocks(convolve(swap_blocks(arrange(values, filter_taps, blocks))))
    half = lax.axis_index("chan").astype(jnp.int32)[None]
    gated, sent = gate_and_project(half, conv, gates, values, skip_gain, out_weight)
    other = lax.ppermute(sent, "chan", [(0, 1), (1, 0)])
    kept = project_kept(half, gated, out_weight)
    return join(kept, other)


def takes_kernels(mesh, values, out_weight):
    blocks, halves = mesh.shape["seq"], mesh.shape["chan"]
    rows = values.shape[0] // blocks
    return (
        halves == 2
        and blocks == 16
        and rows == 256
        and values.shape[1] == halves * blocks * LANES
        and out_weight.shape[1] % (8 * LANES) == 0
    )


def solution(mesh):
    placed = (P("seq", "chan"), P("seq", "chan"), P("seq", "chan"), P("chan"), P("chan", None))

    def whole(values, gates, filter_taps, skip_gain, out_weight):
        local = kernel_local if takes_kernels(mesh, values, out_weight) else general_local
        return jax.shard_map(
            local, mesh=mesh, in_specs=placed, out_specs=P("chan", "seq"), check_vma=False
        )(values, gates, filter_taps, skip_gain, out_weight)

    return whole
```

```python
import functools
import math

import jax
import jax.numpy as jnp
import ml_dtypes
import numpy as np
from jax import lax
from jax.experimental import pallas as pl
from jax.experimental.pallas import tpu as pltpu
from jax.sharding import PartitionSpec as P

TWO_PI = 2.0 * math.pi
HIGH = lax.Precision.HIGHEST
RADIX = 16
LANES = 128
Q_ORDER = [low + 4 * high for low in range(4) for high in range(4)]
VMEM_BYTES = 60 * 1024 * 1024
STAGE_BYTES = 52 * 1024 * 1024
TAIL_BYTES = 16 * 1024 * 1024


def angle_table(first, second, period):
    product = first[:, None] * second[None, :] % period
    angles = product.astype(jnp.float32) * (TWO_PI / period)
    return (jnp.cos(angles), jnp.sin(angles))


def mix(equation, left, right):
    return jnp.einsum(equation, left, right, precision=HIGH)


def outer_forward(data, outer_cos, outer_sin, twist_cos, twist_sin, equation):
    source = data.astype(jnp.float32)
    real = mix(equation, outer_cos, source)
    imag = -mix(equation, outer_sin, source)
    cos_part = twist_cos[:, :, None]
    sin_part = twist_sin[:, :, None]
    return (real * cos_part + imag * sin_part, imag * cos_part - real * sin_part)


def inner_filter(spectra, inner_cos, inner_sin):
    value_re, value_im, taps_re, taps_im = spectra

    def forward(real, imag):
        out_re = mix("kr,jrc->jkc", inner_cos, real) + mix("kr,jrc->jkc", inner_sin, imag)
        out_im = mix("kr,jrc->jkc", inner_cos, imag) - mix("kr,jrc->jkc", inner_sin, real)
        return (out_re, out_im)

    value_fre, value_fim = forward(value_re, value_im)
    taps_fre, taps_fim = forward(taps_re, taps_im)
    prod_re = value_fre * taps_fre - value_fim * taps_fim
    prod_im = value_fre * taps_fim + value_fim * taps_fre
    back_re = mix("rk,jkc->jrc", inner_cos, prod_re) - mix("rk,jkc->jrc", inner_sin, prod_im)
    back_im = mix("rk,jkc->jrc", inner_cos, prod_im) + mix("rk,jkc->jrc", inner_sin, prod_re)
    return (back_re, back_im)


def untwist(real, imag, twist_cos, twist_sin):
    cos_part = twist_cos[:, :, None]
    sin_part = twist_sin[:, :, None]
    return (real * cos_part - imag * sin_part, imag * cos_part + real * sin_part)


def channels_plan(values, filter_taps):
    rows, width = values.shape
    blocks = lax.axis_size("seq")
    length = 2 * blocks * rows
    narrow = width // blocks
    whole_values, whole_taps = (
        lax.all_to_all(values, "seq", split_axis=1, concat_axis=0, tiled=True),
        lax.all_to_all(filter_taps, "seq", split_axis=1, concat_axis=0, tiled=True),
    )
    freq_ids = jnp.arange(2 * blocks, dtype=jnp.int32)
    block_ids = jnp.arange(blocks, dtype=jnp.int32)
    all_rows = jnp.arange(rows, dtype=jnp.int32)
    outer_cos, outer_sin = angle_table(freq_ids, block_ids, 2 * blocks)
    twist_cos, twist_sin = angle_table(freq_ids, all_rows, length)
    tables = (outer_cos, outer_sin, twist_cos, twist_sin, "ka,arc->krc")
    value_re, value_im = outer_forward(whole_values.reshape(blocks, rows, narrow), *tables)
    taps_re, taps_im = outer_forward(whole_taps.reshape(blocks, rows, narrow), *tables)
    inner_cos, inner_sin = angle_table(all_rows, all_rows, rows)
    back_re, back_im = inner_filter((value_re, value_im, taps_re, taps_im), inner_cos, inner_sin)
    turned_re, turned_im = untwist(back_re, back_im, twist_cos, twist_sin)
    final_cos, final_sin = angle_table(block_ids, freq_ids, 2 * blocks)
    signal = (
        mix("ak,krc->arc", final_cos, turned_re) - mix("ak,krc->arc", final_sin, turned_im)
    ) / length
    returned = lax.all_to_all(signal, "seq", split_axis=0, concat_axis=2, tiled=True)
    return returned[0]


def general_local(values, gates, filter_taps, skip_gain, out_weight):
    conv = channels_plan(values, filter_taps)
    gated = (
        gates.astype(jnp.float32) * (conv + skip_gain[None, :] * values.astype(jnp.float32))
    ).astype(jnp.bfloat16)
    projected = lax.psum_scatter(
        lax.dot_general(
            out_weight, gated, (((0,), (1,)), ((), ())), preferred_element_type=jnp.float32
        ),
        "chan",
        scatter_dimension=0,
        tiled=True,
    )
    return projected.astype(jnp.bfloat16)


def split_table(table):
    high = table.astype(ml_dtypes.bfloat16)
    low = (table - high.astype(np.float64)).astype(ml_dtypes.bfloat16)
    return high, low


@functools.lru_cache(maxsize=None)
def transform_tables(length):
    inner = length // RADIX
    k = np.arange(inner)[:, None]
    m = np.arange(inner)[None, :]
    angles = (RADIX * m * (4 * k + 1)) % (4 * length) * (TWO_PI / (4 * length))
    table = np.concatenate([np.cos(angles), -np.sin(angles)], axis=0)
    forward = np.concatenate(split_table(table), axis=1)
    backward = np.concatenate(split_table(table.T / length), axis=0)
    turns = (np.array(Q_ORDER)[:, None] * (4 * k.T + 1)) % (4 * length) * (TWO_PI / (4 * length))
    turns = np.stack([np.cos(turns), np.sin(turns)], axis=1).astype(np.float32)
    turns = np.ascontiguousarray(np.broadcast_to(turns[..., None], (*turns.shape, LANES)))
    return forward, turns, backward


@functools.lru_cache(maxsize=None)
def row_order(rows):
    chunk = rows // RADIX
    order = np.zeros((rows, rows), np.float32)
    for i, q in enumerate(Q_ORDER):
        for j in range(chunk):
            order[i * chunk + j, RADIX * j + q] = 1.0
    return order.astype(ml_dtypes.bfloat16)


def turn(point, index, sign):
    re, im = point
    index %= 16
    if index == 0:
        return point
    if index == 4:
        return (-im, re) if sign > 0 else (im, -re)
    if index == 8:
        return (-re, -im)
    half = math.sqrt(0.5)
    if index == 2:
        return ((re - im) * half, (re + im) * half) if sign > 0 else ((re + im) * half, (im - re) * half)
    if index == 6:
        return ((-re - im) * half, (re - im) * half) if sign > 0 else ((im - re) * half, (-re - im) * half)
    cos = math.cos(TWO_PI * index / 16)
    sin = sign * math.sin(TWO_PI * index / 16)
    return (re * cos - im * sin, re * sin + im * cos)


def four_points(points, sign):
    a, b, c, d = points
    ac = (a[0] + c[0], a[1] + c[1])
    am = (a[0] - c[0], a[1] - c[1])
    bd = (b[0] + d[0], b[1] + d[1])
    bm = (b[0] - d[0], b[1] - d[1])
    if sign < 0:
        side = (bm[1], -bm[0])
    else:
        side = (-bm[1], bm[0])
    return (
        (ac[0] + bd[0], ac[1] + bd[1]),
        (am[0] + side[0], am[1] + side[1]),
        (ac[0] - bd[0], ac[1] - bd[1]),
        (am[0] - side[0], am[1] - side[1]),
    )


def turned(point, cos, sin, sign):
    re, im = point
    if sign < 0:
        return (re * cos + im * sin, im * cos - re * sin)
    return (re * cos - im * sin, im * cos + re * sin)


def arrange_kernel(pieces, order_hbm, values_hbm, taps_hbm, out_hbm, order_ref, values_ref, taps_ref, packed, sems):
    piece = values_ref.shape[1] // pieces
    loads = [pltpu.make_async_copy(order_hbm, order_ref, sems.at[3 * pieces])]
    stores = []
    for part in range(pieces):
        lanes = pl.ds(part * piece, piece)
        loads.append(pltpu.make_async_copy(values_hbm.at[:, lanes], values_ref.at[:, lanes], sems.at[3 * part]))
        loads.append(pltpu.make_async_copy(taps_hbm.at[:, lanes], taps_ref.at[:, lanes], sems.at[3 * part + 1]))
        taken = pl.ds(part * piece // LANES, piece // LANES)
        stores.append(pltpu.make_async_copy(packed.at[taken], out_hbm.at[taken], sems.at[3 * part + 2]))
    for load in loads:
        load.start()
    loads[0].wait()
    for part in range(pieces):
        loads[2 * part + 1].wait()
        loads[2 * part + 2].wait()
        lanes = pl.ds(part * piece, piece)
        both = jnp.concatenate([values_ref[:, lanes], taps_ref[:, lanes]], axis=1)
        moved = jnp.dot(order_ref[...], both, preferred_element_type=jnp.float32).astype(jnp.bfloat16)
        for block in range(piece // LANES):
            for side in range(2):
                start = side * piece + block * LANES
                packed[part * piece // LANES + block, :, pl.ds(side * LANES, LANES)] = moved[:, start : start + LANES]
        stores[part].start()
    for store in stores:
        store.wait()


def arrange(values, taps, blocks):
    rows, wide = values.shape
    pieces = 4
    return pl.pallas_call(
        functools.partial(arrange_kernel, pieces),
        in_specs=[pl.BlockSpec(memory_space=pl.ANY)] * 3,
        out_specs=pl.BlockSpec(memory_space=pl.ANY),
        out_shape=jax.ShapeDtypeStruct((blocks, rows, 2 * LANES), jnp.bfloat16),
        scratch_shapes=[
            pltpu.VMEM((rows, rows), jnp.bfloat16),
            pltpu.VMEM((rows, wide), jnp.bfloat16),
            pltpu.VMEM((rows, wide), jnp.bfloat16),
            pltpu.VMEM((blocks, rows, 2 * LANES), jnp.bfloat16),
            pltpu.SemaphoreType.DMA((3 * pieces + 1,)),
        ],
        compiler_params=pltpu.CompilerParams(vmem_limit_bytes=VMEM_BYTES),
        cost_estimate=pl.CostEstimate(
            flops=4 * rows * rows * wide, bytes_accessed=8 * rows * wide, transcendentals=0
        ),
        name="arrange_rows",
    )(jnp.asarray(row_order(rows)), values, taps)


def convolve_kernel(
    streams_hbm, forward_hbm, turns_hbm, backward_hbm, out_hbm,
    streams, forward_ref, turns_ref, backward_ref,
    raw_even, raw_odd, columns, mixed, halves_even, halves_odd, signals, sems,
):
    blocks, rows, _ = streams.shape
    chunk = rows // RADIX
    inner = blocks * chunk
    group = rows // 4
    raws = (raw_even, raw_odd)
    halves = (halves_even, halves_odd)
    load_forward = pltpu.make_async_copy(forward_hbm, forward_ref, sems.at[0])
    load_backward = pltpu.make_async_copy(backward_hbm, backward_ref, sems.at[1])
    load_streams, load_turns, stores = [], [], []
    for low in range(4):
        taken = pl.ds(low * group, group)
        load_streams.append(pltpu.make_async_copy(streams_hbm.at[:, taken], streams.at[:, taken], sems.at[2 + low]))
        four = pl.ds(4 * low, 4)
        load_turns.append(pltpu.make_async_copy(turns_hbm.at[four], turns_ref.at[four], sems.at[6 + low]))
        stores.append(pltpu.make_async_copy(signals.at[:, taken], out_hbm.at[:, taken], sems.at[10 + low]))
    load_forward.start()
    load_streams[0].start()
    load_streams[1].start()
    load_turns[0].start()
    load_streams[2].start()
    load_turns[1].start()
    load_streams[3].start()
    load_turns[2].start()
    load_turns[3].start()
    load_backward.start()

    def transform(low, pair):
        streams_of = []
        for part in range(2):
            taken = pl.ds(pl.multiple_of(low * group + (2 * pair + part) * chunk, chunk), chunk)
            streams_of.append(streams[:, taken].reshape(inner, 2 * LANES))
        both = jnp.concatenate(streams_of, axis=1)
        result = jnp.dot(
            forward_ref[...], jnp.concatenate([both, both], axis=0), preferred_element_type=jnp.float32
        )
        raws[low % 2][2 * pair] = result[:, : 2 * LANES]
        raws[low % 2][2 * pair + 1] = result[:, 2 * LANES :]

    def first_pass(low, start):
        raw = raws[low % 2]
        upper, lower = pl.ds(start, 8), pl.ds(inner + start, 8)
        for side in range(2):
            lanes = pl.ds(side * LANES, LANES)
            points = []
            for high in range(4):
                point = (raw[high, upper, lanes], raw[high, lower, lanes])
                if low + high:
                    turns = [turns_ref[4 * low + high, part, upper] for part in range(2)]
                    point = turned(point, *turns, -1)
                points.append(point)
            for k, point in enumerate(four_points(points, -1)):
                point = turn(point, low * k, -1)
                columns[4 * low + k, upper, lanes] = point[0]
                columns[4 * low + k, lower, lanes] = point[1]

    def first_rows(low, start, count):
        for part in range(count):
            first_pass(low, pl.multiple_of(start + 8 * part, 8))

    steps = inner // 2

    load_forward.wait()
    load_streams[0].wait()

    def alone(pair, carry):
        transform(0, pair)
        return carry

    lax.fori_loop(0, 2, alone, 0)
    for low in range(1, 4):
        load_streams[low].wait()
        load_turns[low - 1].wait()

        def beside(pair, carry, low=low):
            transform(low, pair)
            first_rows(low - 1, pair * steps, steps // 8)
            return carry

        lax.fori_loop(0, 2, beside, 0)
    load_turns[3].wait()

    def middle(index, carry):
        start = pl.multiple_of(index * 8, 8)
        first_pass(3, start)
        upper, lower = pl.ds(start, 8), pl.ds(inner + start, 8)
        for k in range(4):
            sides = []
            for side in range(2):
                lanes = pl.ds(side * LANES, LANES)
                points = [(columns[4 * low + k, upper, lanes], columns[4 * low + k, lower, lanes]) for low in range(4)]
                sides.append(four_points(points, -1))
            product = [
                (a[0] * b[0] - a[1] * b[1], a[0] * b[1] + a[1] * b[0]) for a, b in zip(*sides)
            ]
            for part, point in enumerate(four_points(product, 1)):
                point = turn(point, k * part, 1)
                mixed[4 * part + k, upper] = point[0]
                mixed[4 * part + k, lower] = point[1]
        return carry

    lax.fori_loop(0, inner // 8, middle, 0)

    def last_pass(low, start):
        target = halves[low % 2]
        upper, lower = pl.ds(start, 16), pl.ds(inner + start, 16)
        points = [(mixed[4 * low + k, upper], mixed[4 * low + k, lower]) for k in range(4)]
        for high, point in enumerate(four_points(points, 1)):
            if low + high:
                turns = [turns_ref[4 * low + high, part, upper] for part in range(2)]
                point = turned(point, *turns, 1)
            for part, taken in zip(point, (upper, lower)):
                rounded = part.astype(jnp.bfloat16)
                target[high, taken, pl.ds(0, LANES)] = rounded
                target[high, taken, pl.ds(LANES, LANES)] = (part - rounded.astype(jnp.float32)).astype(jnp.bfloat16)

    def last_rows(low, start, count):
        for part in range(count):
            last_pass(low, pl.multiple_of(start + 16 * part, 16))

    def restore(low, pair):
        both = jnp.concatenate([halves[low % 2][2 * pair], halves[low % 2][2 * pair + 1]], axis=1)
        terms = jnp.dot(backward_ref[...], both, preferred_element_type=jnp.float32)
        for part in range(2):
            first, second = [slice((2 * part + i) * LANES, (2 * part + i + 1) * LANES) for i in range(2)]
            signal = terms[:inner, first] + terms[:inner, second] + terms[inner:, first]
            taken = pl.ds(pl.multiple_of(low * group + (2 * pair + part) * chunk, chunk), chunk)
            signals[:, taken] = signal.astype(jnp.bfloat16).reshape(blocks, chunk, LANES)

    def prepare(index, carry):
        last_rows(0, index * steps, steps // 16)
        return carry

    lax.fori_loop(0, 2, prepare, 0)
    load_backward.wait()
    for low in range(4):

        def back(pair, carry, low=low):
            restore(low, pair)
            if low < 3:
                last_rows(low + 1, pair * steps, steps // 16)
            return carry

        lax.fori_loop(0, 2, back, 0)
        stores[low].start()
    for store in stores:
        store.wait()


def convolve(streams):
    blocks, rows, lanes = streams.shape
    length = blocks * rows
    inner = length // RADIX
    return pl.pallas_call(
        convolve_kernel,
        in_specs=[pl.BlockSpec(memory_space=pl.ANY)] * 4,
        out_specs=pl.BlockSpec(memory_space=pl.ANY),
        out_shape=jax.ShapeDtypeStruct((blocks, rows, LANES), jnp.bfloat16),
        scratch_shapes=[
            pltpu.VMEM(streams.shape, jnp.bfloat16),
            pltpu.VMEM((2 * inner, 2 * inner), jnp.bfloat16),
            pltpu.VMEM((RADIX, 2, inner, LANES), jnp.float32),
            pltpu.VMEM((2 * inner, 2 * inner), jnp.bfloat16),
            pltpu.VMEM((4, 2 * inner, lanes), jnp.float32),
            pltpu.VMEM((4, 2 * inner, lanes), jnp.float32),
            pltpu.VMEM((RADIX, 2 * inner, lanes), jnp.float32),
            pltpu.VMEM((RADIX, 2 * inner, LANES), jnp.float32),
            pltpu.VMEM((4, 2 * inner, lanes), jnp.bfloat16),
            pltpu.VMEM((4, 2 * inner, lanes), jnp.bfloat16),
            pltpu.VMEM((blocks, rows, LANES), jnp.bfloat16),
            pltpu.SemaphoreType.DMA((14,)),
        ],
        compiler_params=pltpu.CompilerParams(vmem_limit_bytes=VMEM_BYTES),
        cost_estimate=pl.CostEstimate(flops=9 * 10**9, bytes_accessed=9 * 10**6, transcendentals=0),
        name="long_convolution",
    )(streams, *(jnp.asarray(table) for table in transform_tables(length)))


def stage_kernel(half_ref, after_ref, weight_hbm, gates_hbm, values_hbm, sent_ref, kept_ref, gates_ref, values_ref, sems):
    del after_ref
    features = sent_ref.shape[1]
    half = half_ref[0]
    sides = [pl.ds(pl.multiple_of(side * features, features), features) for side in (1 - half, half)]
    copies = [
        pltpu.make_async_copy(weight_hbm.at[:, sides[0]], sent_ref, sems.at[0]),
        pltpu.make_async_copy(weight_hbm.at[:, sides[1]], kept_ref, sems.at[1]),
        pltpu.make_async_copy(gates_hbm, gates_ref, sems.at[2]),
        pltpu.make_async_copy(values_hbm, values_ref, sems.at[3]),
    ]
    for copy in copies:
        copy.start()
    for copy in copies:
        copy.wait()


def stage(half, after, out_weight, gates, values):
    width, features = out_weight.shape
    share = jax.ShapeDtypeStruct((width, features // 2), out_weight.dtype)
    stream = jax.ShapeDtypeStruct(gates.shape, gates.dtype)
    return pl.pallas_call(
        stage_kernel,
        in_specs=[pl.BlockSpec(memory_space=pltpu.SMEM)] + [pl.BlockSpec(memory_space=pl.ANY)] * 4,
        out_specs=[pl.BlockSpec(memory_space=pl.ANY)] * 4,
        out_shape=[share, share, stream, stream],
        scratch_shapes=[pltpu.SemaphoreType.DMA((4,))],
        compiler_params=pltpu.CompilerParams(vmem_limit_bytes=STAGE_BYTES),
        cost_estimate=pl.CostEstimate(
            flops=0, bytes_accessed=4 * width * features + 8 * gates.size, transcendentals=0
        ),
        name="stage_tail",
    )(half, after, out_weight, gates, values)


def gate_kernel(group, order_ref, conv_ref, gates_ref, values_ref, skip_ref, weight_ref, gated_ref, out_ref):
    blocks, _, lanes = conv_ref.shape
    for step in range(blocks // group):
        taken = pl.ds(step * group * lanes, group * lanes)
        conv = jnp.concatenate([conv_ref[step * group + part] for part in range(group)], axis=1)
        conv = jnp.dot(order_ref[...], conv, preferred_element_type=jnp.float32)
        direct = skip_ref[:, taken] * values_ref[:, taken].astype(jnp.float32)
        gated_ref[:, taken] = (gates_ref[:, taken].astype(jnp.float32) * (conv + direct)).astype(jnp.bfloat16)
    out_ref[...] = jnp.dot(gated_ref[...], weight_ref[...], preferred_element_type=jnp.float32)


def gate_and_project(conv, gates, values, skip_gain, weight):
    rows, width = gates.shape
    features = weight.shape[1]
    return pl.pallas_call(
        functools.partial(gate_kernel, 4),
        in_specs=[pl.BlockSpec(memory_space=pltpu.VMEM)] * 6,
        out_specs=[pl.BlockSpec(memory_space=pltpu.VMEM)] * 2,
        out_shape=[
            jax.ShapeDtypeStruct((rows, width), jnp.bfloat16),
            jax.ShapeDtypeStruct((rows, features), jnp.float32),
        ],
        compiler_params=pltpu.CompilerParams(vmem_limit_bytes=TAIL_BYTES),
        cost_estimate=pl.CostEstimate(
            flops=2 * rows * width * features, bytes_accessed=2 * width * features, transcendentals=0
        ),
        name="gate_project_sent",
    )(jnp.asarray(row_order(rows).T), conv, gates, values, skip_gain[None, :], weight)


def kept_kernel(gated_ref, weight_ref, out_ref):
    out_ref[...] = jnp.dot(gated_ref[...], weight_ref[...], preferred_element_type=jnp.float32)


def project_kept(gated, weight):
    rows, width = gated.shape
    features = weight.shape[1]
    return pl.pallas_call(
        kept_kernel,
        in_specs=[pl.BlockSpec(memory_space=pltpu.VMEM)] * 2,
        out_specs=pl.BlockSpec(memory_space=pltpu.VMEM),
        out_shape=jax.ShapeDtypeStruct((rows, features), jnp.float32),
        compiler_params=pltpu.CompilerParams(vmem_limit_bytes=TAIL_BYTES),
        cost_estimate=pl.CostEstimate(
            flops=2 * rows * width * features, bytes_accessed=2 * width * features, transcendentals=0
        ),
        name="project_kept",
    )(gated, weight)


def join_kernel(kept_ref, came_ref, out_ref):
    out_ref[...] = (kept_ref[...] + came_ref[...]).astype(jnp.bfloat16).T


def join(kept, came):
    rows, features = kept.shape
    wide = features // 4
    return pl.pallas_call(
        join_kernel,
        grid=(4,),
        in_specs=[pl.BlockSpec((rows, wide), lambda i: (0, i))] * 2,
        out_specs=pl.BlockSpec((wide, rows), lambda i: (i, 0)),
        out_shape=jax.ShapeDtypeStruct((features, rows), jnp.bfloat16),
        compiler_params=pltpu.CompilerParams(vmem_limit_bytes=TAIL_BYTES),
        name="join_halves",
    )(kept, came)


def swap_blocks(array):
    return lax.all_to_all(array, "seq", split_axis=0, concat_axis=0, tiled=True)


def kernel_local(values, gates, filter_taps, skip_gain, out_weight):
    blocks = lax.axis_size("seq")
    conv = convolve(swap_blocks(arrange(values, filter_taps, blocks)))
    half = lax.axis_index("chan").astype(jnp.int32)[None]
    weight_sent, weight_kept, gates, values = stage(half, conv, out_weight, gates, values)
    gated, sent = gate_and_project(swap_blocks(conv), gates, values, skip_gain, weight_sent)
    other = lax.ppermute(sent, "chan", [(0, 1), (1, 0)])
    kept = project_kept(gated, weight_kept)
    return join(kept, other)


def takes_kernels(mesh, values, out_weight):
    blocks, halves = mesh.shape["seq"], mesh.shape["chan"]
    rows = values.shape[0] // blocks
    return (
        halves == 2
        and blocks == 16
        and rows == 256
        and values.shape[1] == halves * blocks * LANES
        and out_weight.shape[1] % (8 * LANES) == 0
    )


def solution(mesh):
    placed = (P("seq", "chan"), P("seq", "chan"), P("seq", "chan"), P("chan"), P("chan", None))

    def whole(values, gates, filter_taps, skip_gain, out_weight):
        local = kernel_local if takes_kernels(mesh, values, out_weight) else general_local
        return jax.shard_map(
            local, mesh=mesh, in_specs=placed, out_specs=P("chan", "seq"), check_vma=False
        )(values, gates, filter_taps, skip_gain, out_weight)

    return whole
```

```python
import functools
import math

import jax
import jax.numpy as jnp
import ml_dtypes
import numpy as np
from jax import lax
from jax.experimental import pallas as pl
from jax.experimental.pallas import tpu as pltpu
from jax.sharding import PartitionSpec as P

TWO_PI = 2.0 * math.pi
HIGH = lax.Precision.HIGHEST
RADIX = 16
LANES = 128
Q_ORDER = [low + 4 * high for low in range(4) for high in range(4)]
VMEM_BYTES = 60 * 1024 * 1024
CONV_BYTES = 49 * 1024 * 1024
TAIL_BYTES = 16 * 1024 * 1024


def angle_table(first, second, period):
    product = first[:, None] * second[None, :] % period
    angles = product.astype(jnp.float32) * (TWO_PI / period)
    return (jnp.cos(angles), jnp.sin(angles))


def mix(equation, left, right):
    return jnp.einsum(equation, left, right, precision=HIGH)


def outer_forward(data, outer_cos, outer_sin, twist_cos, twist_sin, equation):
    source = data.astype(jnp.float32)
    real = mix(equation, outer_cos, source)
    imag = -mix(equation, outer_sin, source)
    cos_part = twist_cos[:, :, None]
    sin_part = twist_sin[:, :, None]
    return (real * cos_part + imag * sin_part, imag * cos_part - real * sin_part)


def inner_filter(spectra, inner_cos, inner_sin):
    value_re, value_im, taps_re, taps_im = spectra

    def forward(real, imag):
        out_re = mix("kr,jrc->jkc", inner_cos, real) + mix("kr,jrc->jkc", inner_sin, imag)
        out_im = mix("kr,jrc->jkc", inner_cos, imag) - mix("kr,jrc->jkc", inner_sin, real)
        return (out_re, out_im)

    value_fre, value_fim = forward(value_re, value_im)
    taps_fre, taps_fim = forward(taps_re, taps_im)
    prod_re = value_fre * taps_fre - value_fim * taps_fim
    prod_im = value_fre * taps_fim + value_fim * taps_fre
    back_re = mix("rk,jkc->jrc", inner_cos, prod_re) - mix("rk,jkc->jrc", inner_sin, prod_im)
    back_im = mix("rk,jkc->jrc", inner_cos, prod_im) + mix("rk,jkc->jrc", inner_sin, prod_re)
    return (back_re, back_im)


def untwist(real, imag, twist_cos, twist_sin):
    cos_part = twist_cos[:, :, None]
    sin_part = twist_sin[:, :, None]
    return (real * cos_part - imag * sin_part, imag * cos_part + real * sin_part)


def channels_plan(values, filter_taps):
    rows, width = values.shape
    blocks = lax.axis_size("seq")
    length = 2 * blocks * rows
    narrow = width // blocks
    whole_values, whole_taps = (
        lax.all_to_all(values, "seq", split_axis=1, concat_axis=0, tiled=True),
        lax.all_to_all(filter_taps, "seq", split_axis=1, concat_axis=0, tiled=True),
    )
    freq_ids = jnp.arange(2 * blocks, dtype=jnp.int32)
    block_ids = jnp.arange(blocks, dtype=jnp.int32)
    all_rows = jnp.arange(rows, dtype=jnp.int32)
    outer_cos, outer_sin = angle_table(freq_ids, block_ids, 2 * blocks)
    twist_cos, twist_sin = angle_table(freq_ids, all_rows, length)
    tables = (outer_cos, outer_sin, twist_cos, twist_sin, "ka,arc->krc")
    value_re, value_im = outer_forward(whole_values.reshape(blocks, rows, narrow), *tables)
    taps_re, taps_im = outer_forward(whole_taps.reshape(blocks, rows, narrow), *tables)
    inner_cos, inner_sin = angle_table(all_rows, all_rows, rows)
    back_re, back_im = inner_filter((value_re, value_im, taps_re, taps_im), inner_cos, inner_sin)
    turned_re, turned_im = untwist(back_re, back_im, twist_cos, twist_sin)
    final_cos, final_sin = angle_table(block_ids, freq_ids, 2 * blocks)
    signal = (
        mix("ak,krc->arc", final_cos, turned_re) - mix("ak,krc->arc", final_sin, turned_im)
    ) / length
    returned = lax.all_to_all(signal, "seq", split_axis=0, concat_axis=2, tiled=True)
    return returned[0]


def general_local(values, gates, filter_taps, skip_gain, out_weight):
    conv = channels_plan(values, filter_taps)
    gated = (
        gates.astype(jnp.float32) * (conv + skip_gain[None, :] * values.astype(jnp.float32))
    ).astype(jnp.bfloat16)
    projected = lax.psum_scatter(
        lax.dot_general(
            out_weight, gated, (((0,), (1,)), ((), ())), preferred_element_type=jnp.float32
        ),
        "chan",
        scatter_dimension=0,
        tiled=True,
    )
    return projected.astype(jnp.bfloat16)


def split_table(table):
    high = table.astype(ml_dtypes.bfloat16)
    low = (table - high.astype(np.float64)).astype(ml_dtypes.bfloat16)
    return high, low


@functools.lru_cache(maxsize=None)
def transform_tables(length):
    inner = length // RADIX
    k = np.arange(inner)[:, None]
    m = np.arange(inner)[None, :]
    angles = (RADIX * m * (4 * k + 1)) % (4 * length) * (TWO_PI / (4 * length))
    table = np.concatenate([np.cos(angles), -np.sin(angles)], axis=0)
    forward = np.concatenate(split_table(table), axis=1)
    backward = np.concatenate(split_table(table.T / length), axis=0)
    turns = (np.array(Q_ORDER)[:, None] * (4 * k.T + 1)) % (4 * length) * (TWO_PI / (4 * length))
    turns = np.stack([np.cos(turns), np.sin(turns)], axis=1).astype(np.float32)
    turns = np.ascontiguousarray(np.broadcast_to(turns[..., None], (*turns.shape, LANES)))
    return forward, turns, backward


@functools.lru_cache(maxsize=None)
def row_order(rows):
    chunk = rows // RADIX
    order = np.zeros((rows, rows), np.float32)
    for i, q in enumerate(Q_ORDER):
        for j in range(chunk):
            order[i * chunk + j, RADIX * j + q] = 1.0
    return order.astype(ml_dtypes.bfloat16)


def turn(point, index, sign):
    re, im = point
    index %= 16
    if index == 0:
        return point
    if index == 4:
        return (-im, re) if sign > 0 else (im, -re)
    if index == 8:
        return (-re, -im)
    half = math.sqrt(0.5)
    if index == 2:
        return ((re - im) * half, (re + im) * half) if sign > 0 else ((re + im) * half, (im - re) * half)
    if index == 6:
        return ((-re - im) * half, (re - im) * half) if sign > 0 else ((im - re) * half, (-re - im) * half)
    cos = math.cos(TWO_PI * index / 16)
    sin = sign * math.sin(TWO_PI * index / 16)
    return (re * cos - im * sin, re * sin + im * cos)


def four_points(points, sign):
    a, b, c, d = points
    ac = (a[0] + c[0], a[1] + c[1])
    am = (a[0] - c[0], a[1] - c[1])
    bd = (b[0] + d[0], b[1] + d[1])
    bm = (b[0] - d[0], b[1] - d[1])
    if sign < 0:
        side = (bm[1], -bm[0])
    else:
        side = (-bm[1], bm[0])
    return (
        (ac[0] + bd[0], ac[1] + bd[1]),
        (am[0] + side[0], am[1] + side[1]),
        (ac[0] - bd[0], ac[1] - bd[1]),
        (am[0] - side[0], am[1] - side[1]),
    )


def turned(point, cos, sin, sign):
    re, im = point
    if sign < 0:
        return (re * cos + im * sin, im * cos - re * sin)
    return (re * cos - im * sin, im * cos + re * sin)


def slot_order(blocks):
    half = blocks // 2
    across = [half + (i // 2 if i % 2 == 0 else half // 2 + i // 2) for i in range(half)]
    near = list(range(1, half)) + [0]
    return [slot for pair in zip(across, near) for slot in pair]


def arrange_kernel(pieces, blocks, me_ref, order_hbm, values_hbm, taps_hbm, *rest):
    outs = rest[:blocks]
    order_ref, values_ref, taps_ref, packed, sems = rest[blocks:]
    piece = values_ref.shape[1] // pieces
    loads = [pltpu.make_async_copy(order_hbm, order_ref, sems.at[2 * pieces])]
    for part in range(pieces):
        lanes = pl.ds(part * piece, piece)
        loads.append(pltpu.make_async_copy(values_hbm.at[:, lanes], values_ref.at[:, lanes], sems.at[2 * part]))
        loads.append(pltpu.make_async_copy(taps_hbm.at[:, lanes], taps_ref.at[:, lanes], sems.at[2 * part + 1]))
    for load in loads:
        load.start()
    loads[0].wait()
    for part in range(pieces):
        loads[2 * part + 1].wait()
        loads[2 * part + 2].wait()
        lanes = pl.ds(part * piece, piece)
        both = jnp.concatenate([values_ref[:, lanes], taps_ref[:, lanes]], axis=1)
        moved = jnp.dot(order_ref[...], both, preferred_element_type=jnp.float32).astype(jnp.bfloat16)
        for block in range(piece // LANES):
            for side in range(2):
                start = side * piece + block * LANES
                packed[part * piece // LANES + block, :, pl.ds(side * LANES, LANES)] = moved[:, start : start + LANES]
    for out, slot in zip(outs, slot_order(blocks)):
        out[...] = packed[me_ref[0] ^ slot]


def arrange(me, values, taps, blocks):
    rows, wide = values.shape
    pieces = 4
    return pl.pallas_call(
        functools.partial(arrange_kernel, pieces, blocks),
        in_specs=[pl.BlockSpec(memory_space=pltpu.SMEM)] + [pl.BlockSpec(memory_space=pl.ANY)] * 3,
        out_specs=[pl.BlockSpec(memory_space=pltpu.VMEM)] * blocks,
        out_shape=[jax.ShapeDtypeStruct((rows, 2 * LANES), jnp.bfloat16)] * blocks,
        scratch_shapes=[
            pltpu.VMEM((rows, rows), jnp.bfloat16),
            pltpu.VMEM((rows, wide), jnp.bfloat16),
            pltpu.VMEM((rows, wide), jnp.bfloat16),
            pltpu.VMEM((blocks, rows, 2 * LANES), jnp.bfloat16),
            pltpu.SemaphoreType.DMA((2 * pieces + 1,)),
        ],
        compiler_params=pltpu.CompilerParams(vmem_limit_bytes=VMEM_BYTES),
        cost_estimate=pl.CostEstimate(
            flops=4 * rows * rows * wide, bytes_accessed=8 * rows * wide, transcendentals=0
        ),
        name="arrange_rows",
    )(me, jnp.asarray(row_order(rows)), values, taps)


def convolve_kernel(blocks, me_ref, *rest):
    slots = rest[:blocks]
    convolve_blocks(me_ref, slots, *rest[blocks:])


def convolve_blocks(
    me_ref, slots, forward_hbm, turns_hbm, backward_hbm, out_hbm,
    streams, forward_ref, turns_ref, backward_ref,
    raw_even, raw_odd, columns, mixed, halves_even, halves_odd, signals, sems,
):
    blocks, rows, _ = streams.shape
    chunk = rows // RADIX
    inner = blocks * chunk
    group = rows // 4
    raws = (raw_even, raw_odd)
    halves = (halves_even, halves_odd)
    load_forward = pltpu.make_async_copy(forward_hbm, forward_ref, sems.at[0])
    load_backward = pltpu.make_async_copy(backward_hbm, backward_ref, sems.at[1])
    load_turns, stores = [], []
    for low in range(4):
        taken = pl.ds(low * group, group)
        four = pl.ds(4 * low, 4)
        load_turns.append(pltpu.make_async_copy(turns_hbm.at[four], turns_ref.at[four], sems.at[6 + low]))
        stores.append(pltpu.make_async_copy(signals.at[:, taken], out_hbm.at[:, taken], sems.at[10 + low]))
    load_forward.start()
    for load in load_turns:
        load.start()
    load_backward.start()
    for slot, source in zip(slot_order(blocks), slots):
        streams[me_ref[0] ^ slot] = source[...]

    def transform(low, pair):
        streams_of = []
        for part in range(2):
            taken = pl.ds(pl.multiple_of(low * group + (2 * pair + part) * chunk, chunk), chunk)
            streams_of.append(streams[:, taken].reshape(inner, 2 * LANES))
        both = jnp.concatenate(streams_of, axis=1)
        result = jnp.dot(
            forward_ref[...], jnp.concatenate([both, both], axis=0), preferred_element_type=jnp.float32
        )
        raws[low % 2][2 * pair] = result[:, : 2 * LANES]
        raws[low % 2][2 * pair + 1] = result[:, 2 * LANES :]

    def first_pass(low, start):
        raw = raws[low % 2]
        upper, lower = pl.ds(start, 8), pl.ds(inner + start, 8)
        for side in range(2):
            lanes = pl.ds(side * LANES, LANES)
            points = []
            for high in range(4):
                point = (raw[high, upper, lanes], raw[high, lower, lanes])
                if low + high:
                    turns = [turns_ref[4 * low + high, part, upper] for part in range(2)]
                    point = turned(point, *turns, -1)
                points.append(point)
            for k, point in enumerate(four_points(points, -1)):
                point = turn(point, low * k, -1)
                columns[4 * low + k, upper, lanes] = point[0]
                columns[4 * low + k, lower, lanes] = point[1]

    def first_rows(low, start, count):
        for part in range(count):
            first_pass(low, pl.multiple_of(start + 8 * part, 8))

    steps = inner // 2

    load_forward.wait()

    def alone(pair, carry):
        transform(0, pair)
        return carry

    lax.fori_loop(0, 2, alone, 0)
    for low in range(1, 4):
        load_turns[low - 1].wait()

        def beside(pair, carry, low=low):
            transform(low, pair)
            first_rows(low - 1, pair * steps, steps // 8)
            return carry

        lax.fori_loop(0, 2, beside, 0)
    load_turns[3].wait()

    def middle(index, carry):
        start = pl.multiple_of(index * 8, 8)
        first_pass(3, start)
        upper, lower = pl.ds(start, 8), pl.ds(inner + start, 8)
        for k in range(4):
            sides = []
            for side in range(2):
                lanes = pl.ds(side * LANES, LANES)
                points = [(columns[4 * low + k, upper, lanes], columns[4 * low + k, lower, lanes]) for low in range(4)]
                sides.append(four_points(points, -1))
            product = [
                (a[0] * b[0] - a[1] * b[1], a[0] * b[1] + a[1] * b[0]) for a, b in zip(*sides)
            ]
            for part, point in enumerate(four_points(product, 1)):
                point = turn(point, k * part, 1)
                mixed[4 * part + k, upper] = point[0]
                mixed[4 * part + k, lower] = point[1]
        return carry

    lax.fori_loop(0, inner // 8, middle, 0)

    def last_pass(low, start):
        target = halves[low % 2]
        upper, lower = pl.ds(start, 16), pl.ds(inner + start, 16)
        points = [(mixed[4 * low + k, upper], mixed[4 * low + k, lower]) for k in range(4)]
        for high, point in enumerate(four_points(points, 1)):
            if low + high:
                turns = [turns_ref[4 * low + high, part, upper] for part in range(2)]
                point = turned(point, *turns, 1)
            for part, taken in zip(point, (upper, lower)):
                rounded = part.astype(jnp.bfloat16)
                target[high, taken, pl.ds(0, LANES)] = rounded
                target[high, taken, pl.ds(LANES, LANES)] = (part - rounded.astype(jnp.float32)).astype(jnp.bfloat16)

    def last_rows(low, start, count):
        for part in range(count):
            last_pass(low, pl.multiple_of(start + 16 * part, 16))

    def restore(low, pair):
        both = jnp.concatenate([halves[low % 2][2 * pair], halves[low % 2][2 * pair + 1]], axis=1)
        terms = jnp.dot(backward_ref[...], both, preferred_element_type=jnp.float32)
        for part in range(2):
            first, second = [slice((2 * part + i) * LANES, (2 * part + i + 1) * LANES) for i in range(2)]
            signal = terms[:inner, first] + terms[:inner, second] + terms[inner:, first]
            taken = pl.ds(pl.multiple_of(low * group + (2 * pair + part) * chunk, chunk), chunk)
            signals[:, taken] = signal.astype(jnp.bfloat16).reshape(blocks, chunk, LANES)

    def prepare(index, carry):
        last_rows(0, index * steps, steps // 16)
        return carry

    lax.fori_loop(0, 2, prepare, 0)
    load_backward.wait()
    for low in range(4):

        def back(pair, carry, low=low):
            restore(low, pair)
            if low < 3:
                last_rows(low + 1, pair * steps, steps // 16)
            return carry

        lax.fori_loop(0, 2, back, 0)
        stores[low].start()
    for store in stores:
        store.wait()


def convolve(me, slots):
    blocks = len(slots)
    rows, lanes = slots[0].shape
    length = blocks * rows
    inner = length // RADIX
    return pl.pallas_call(
        functools.partial(convolve_kernel, blocks),
        in_specs=[pl.BlockSpec(memory_space=pltpu.SMEM)]
        + [pl.BlockSpec(memory_space=pltpu.VMEM)] * blocks
        + [pl.BlockSpec(memory_space=pl.ANY)] * 3,
        out_specs=pl.BlockSpec(memory_space=pl.ANY),
        out_shape=jax.ShapeDtypeStruct((blocks, rows, LANES), jnp.bfloat16),
        scratch_shapes=[
            pltpu.VMEM((blocks, rows, lanes), jnp.bfloat16),
            pltpu.VMEM((2 * inner, 2 * inner), jnp.bfloat16),
            pltpu.VMEM((RADIX, 2, inner, LANES), jnp.float32),
            pltpu.VMEM((2 * inner, 2 * inner), jnp.bfloat16),
            pltpu.VMEM((4, 2 * inner, lanes), jnp.float32),
            pltpu.VMEM((4, 2 * inner, lanes), jnp.float32),
            pltpu.VMEM((RADIX, 2 * inner, lanes), jnp.float32),
            pltpu.VMEM((RADIX, 2 * inner, LANES), jnp.float32),
            pltpu.VMEM((4, 2 * inner, lanes), jnp.bfloat16),
            pltpu.VMEM((4, 2 * inner, lanes), jnp.bfloat16),
            pltpu.VMEM((blocks, rows, LANES), jnp.bfloat16),
            pltpu.SemaphoreType.DMA((14,)),
        ],
        compiler_params=pltpu.CompilerParams(vmem_limit_bytes=CONV_BYTES),
        cost_estimate=pl.CostEstimate(flops=9 * 10**9, bytes_accessed=9 * 10**6, transcendentals=0),
        name="long_convolution",
    )(me, *slots, *(jnp.asarray(table) for table in transform_tables(length)))


def stage_kernel(half_ref, after_ref, weight_hbm, gates_hbm, values_hbm, sent_ref, kept_ref, gates_ref, values_ref, sems):
    del after_ref
    features = sent_ref.shape[1]
    half = half_ref[0]
    sides = [pl.ds(pl.multiple_of(side * features, features), features) for side in (1 - half, half)]
    copies = [
        pltpu.make_async_copy(weight_hbm.at[:, sides[0]], sent_ref, sems.at[0]),
        pltpu.make_async_copy(weight_hbm.at[:, sides[1]], kept_ref, sems.at[1]),
        pltpu.make_async_copy(gates_hbm, gates_ref, sems.at[2]),
        pltpu.make_async_copy(values_hbm, values_ref, sems.at[3]),
    ]
    for copy in copies:
        copy.start()
    for copy in copies:
        copy.wait()


def stage(half, after, out_weight, gates, values):
    width, features = out_weight.shape
    share = jax.ShapeDtypeStruct((width, features // 2), out_weight.dtype)
    stream = jax.ShapeDtypeStruct(gates.shape, gates.dtype)
    return pl.pallas_call(
        stage_kernel,
        in_specs=[pl.BlockSpec(memory_space=pltpu.SMEM)] + [pl.BlockSpec(memory_space=pl.ANY)] * 4,
        out_specs=[pl.BlockSpec(memory_space=pltpu.VMEM)] * 4,
        out_shape=[share, share, stream, stream],
        scratch_shapes=[pltpu.SemaphoreType.DMA((4,))],
        compiler_params=pltpu.CompilerParams(vmem_limit_bytes=TAIL_BYTES),
        cost_estimate=pl.CostEstimate(
            flops=0, bytes_accessed=4 * width * features + 8 * gates.size, transcendentals=0
        ),
        name="stage_tail",
    )(half, after, out_weight, gates, values)


def gate_kernel(group, order_ref, conv_ref, gates_ref, values_ref, skip_ref, weight_ref, gated_ref, out_ref):
    blocks, _, lanes = conv_ref.shape
    for step in range(blocks // group):
        taken = pl.ds(step * group * lanes, group * lanes)
        conv = jnp.concatenate([conv_ref[step * group + part] for part in range(group)], axis=1)
        conv = jnp.dot(order_ref[...], conv, preferred_element_type=jnp.float32)
        direct = skip_ref[:, taken] * values_ref[:, taken].astype(jnp.float32)
        gated_ref[:, taken] = (gates_ref[:, taken].astype(jnp.float32) * (conv + direct)).astype(jnp.bfloat16)
    out_ref[...] = jnp.dot(gated_ref[...], weight_ref[...], preferred_element_type=jnp.float32)


def gate_and_project(conv, gates, values, skip_gain, weight):
    rows, width = gates.shape
    features = weight.shape[1]
    return pl.pallas_call(
        functools.partial(gate_kernel, 4),
        in_specs=[pl.BlockSpec(memory_space=pltpu.VMEM)] * 6,
        out_specs=[pl.BlockSpec(memory_space=pltpu.VMEM)] * 2,
        out_shape=[
            jax.ShapeDtypeStruct((rows, width), jnp.bfloat16),
            jax.ShapeDtypeStruct((rows, features), jnp.float32),
        ],
        compiler_params=pltpu.CompilerParams(vmem_limit_bytes=TAIL_BYTES),
        cost_estimate=pl.CostEstimate(
            flops=2 * rows * width * features, bytes_accessed=2 * width * features, transcendentals=0
        ),
        name="gate_project_sent",
    )(jnp.asarray(row_order(rows).T), conv, gates, values, skip_gain[None, :], weight)


def kept_kernel(gated_ref, weight_ref, out_ref):
    out_ref[...] = jnp.dot(gated_ref[...], weight_ref[...], preferred_element_type=jnp.float32)


def project_kept(gated, weight):
    rows, width = gated.shape
    features = weight.shape[1]
    return pl.pallas_call(
        kept_kernel,
        in_specs=[pl.BlockSpec(memory_space=pltpu.VMEM)] * 2,
        out_specs=pl.BlockSpec(memory_space=pltpu.VMEM),
        out_shape=jax.ShapeDtypeStruct((rows, features), jnp.float32),
        compiler_params=pltpu.CompilerParams(vmem_limit_bytes=TAIL_BYTES),
        cost_estimate=pl.CostEstimate(
            flops=2 * rows * width * features, bytes_accessed=2 * width * features, transcendentals=0
        ),
        name="project_kept",
    )(gated, weight)


def join_kernel(kept_ref, came_ref, out_ref):
    out_ref[...] = (kept_ref[...] + came_ref[...]).astype(jnp.bfloat16).T


def join(kept, came):
    rows, features = kept.shape
    wide = features // 4
    return pl.pallas_call(
        join_kernel,
        grid=(4,),
        in_specs=[pl.BlockSpec((rows, wide), lambda i: (0, i))] * 2,
        out_specs=pl.BlockSpec((wide, rows), lambda i: (i, 0)),
        out_shape=jax.ShapeDtypeStruct((features, rows), jnp.bfloat16),
        compiler_params=pltpu.CompilerParams(vmem_limit_bytes=TAIL_BYTES),
        name="join_halves",
    )(kept, came)


def swap_blocks(array):
    return lax.all_to_all(array, "seq", split_axis=0, concat_axis=0, tiled=True)


def exchange(slots):
    blocks = len(slots)
    return [
        lax.ppermute(source, "seq", [(j, j ^ slot) for j in range(blocks)]) if slot else source
        for slot, source in zip(slot_order(blocks), slots)
    ]


def kernel_local(values, gates, filter_taps, skip_gain, out_weight):
    blocks = lax.axis_size("seq")
    me = lax.axis_index("seq").astype(jnp.int32)[None]
    half = lax.axis_index("chan").astype(jnp.int32)[None]
    conv = convolve(me, exchange(arrange(me, values, filter_taps, blocks)))
    weight_sent, weight_kept, gates, values = stage(half, conv, out_weight, gates, values)
    gated, sent = gate_and_project(swap_blocks(conv), gates, values, skip_gain, weight_sent)
    other = lax.ppermute(sent, "chan", [(0, 1), (1, 0)])
    kept = project_kept(gated, weight_kept)
    return join(kept, other)


def takes_kernels(mesh, values, out_weight):
    blocks, halves = mesh.shape["seq"], mesh.shape["chan"]
    rows = values.shape[0] // blocks
    return (
        halves == 2
        and blocks == 16
        and rows == 256
        and values.shape[1] == halves * blocks * LANES
        and out_weight.shape[1] % (8 * LANES) == 0
    )


def solution(mesh):
    placed = (P("seq", "chan"), P("seq", "chan"), P("seq", "chan"), P("chan"), P("chan", None))

    def whole(values, gates, filter_taps, skip_gain, out_weight):
        local = kernel_local if takes_kernels(mesh, values, out_weight) else general_local
        return jax.shard_map(
            local, mesh=mesh, in_specs=placed, out_specs=P("chan", "seq"), check_vma=False
        )(values, gates, filter_taps, skip_gain, out_weight)

    return whole
```

```python
import functools
import math

import jax
import jax.numpy as jnp
import ml_dtypes
import numpy as np
from jax import lax
from jax.experimental import pallas as pl
from jax.experimental.pallas import tpu as pltpu
from jax.sharding import PartitionSpec as P

TWO_PI = 2.0 * math.pi
HIGH = lax.Precision.HIGHEST
RADIX = 16
LANES = 128
Q_ORDER = [low + 4 * high for low in range(4) for high in range(4)]
VMEM_BYTES = 60 * 1024 * 1024
CONV_BYTES = 49 * 1024 * 1024
TAIL_BYTES = 49 * 1024 * 1024


def angle_table(first, second, period):
    product = first[:, None] * second[None, :] % period
    angles = product.astype(jnp.float32) * (TWO_PI / period)
    return (jnp.cos(angles), jnp.sin(angles))


def mix(equation, left, right):
    return jnp.einsum(equation, left, right, precision=HIGH)


def outer_forward(data, outer_cos, outer_sin, twist_cos, twist_sin, equation):
    source = data.astype(jnp.float32)
    real = mix(equation, outer_cos, source)
    imag = -mix(equation, outer_sin, source)
    cos_part = twist_cos[:, :, None]
    sin_part = twist_sin[:, :, None]
    return (real * cos_part + imag * sin_part, imag * cos_part - real * sin_part)


def inner_filter(spectra, inner_cos, inner_sin):
    value_re, value_im, taps_re, taps_im = spectra

    def forward(real, imag):
        out_re = mix("kr,jrc->jkc", inner_cos, real) + mix("kr,jrc->jkc", inner_sin, imag)
        out_im = mix("kr,jrc->jkc", inner_cos, imag) - mix("kr,jrc->jkc", inner_sin, real)
        return (out_re, out_im)

    value_fre, value_fim = forward(value_re, value_im)
    taps_fre, taps_fim = forward(taps_re, taps_im)
    prod_re = value_fre * taps_fre - value_fim * taps_fim
    prod_im = value_fre * taps_fim + value_fim * taps_fre
    back_re = mix("rk,jkc->jrc", inner_cos, prod_re) - mix("rk,jkc->jrc", inner_sin, prod_im)
    back_im = mix("rk,jkc->jrc", inner_cos, prod_im) + mix("rk,jkc->jrc", inner_sin, prod_re)
    return (back_re, back_im)


def untwist(real, imag, twist_cos, twist_sin):
    cos_part = twist_cos[:, :, None]
    sin_part = twist_sin[:, :, None]
    return (real * cos_part - imag * sin_part, imag * cos_part + real * sin_part)


def channels_plan(values, filter_taps):
    rows, width = values.shape
    blocks = lax.axis_size("seq")
    length = 2 * blocks * rows
    narrow = width // blocks
    whole_values, whole_taps = (
        lax.all_to_all(values, "seq", split_axis=1, concat_axis=0, tiled=True),
        lax.all_to_all(filter_taps, "seq", split_axis=1, concat_axis=0, tiled=True),
    )
    freq_ids = jnp.arange(2 * blocks, dtype=jnp.int32)
    block_ids = jnp.arange(blocks, dtype=jnp.int32)
    all_rows = jnp.arange(rows, dtype=jnp.int32)
    outer_cos, outer_sin = angle_table(freq_ids, block_ids, 2 * blocks)
    twist_cos, twist_sin = angle_table(freq_ids, all_rows, length)
    tables = (outer_cos, outer_sin, twist_cos, twist_sin, "ka,arc->krc")
    value_re, value_im = outer_forward(whole_values.reshape(blocks, rows, narrow), *tables)
    taps_re, taps_im = outer_forward(whole_taps.reshape(blocks, rows, narrow), *tables)
    inner_cos, inner_sin = angle_table(all_rows, all_rows, rows)
    back_re, back_im = inner_filter((value_re, value_im, taps_re, taps_im), inner_cos, inner_sin)
    turned_re, turned_im = untwist(back_re, back_im, twist_cos, twist_sin)
    final_cos, final_sin = angle_table(block_ids, freq_ids, 2 * blocks)
    signal = (
        mix("ak,krc->arc", final_cos, turned_re) - mix("ak,krc->arc", final_sin, turned_im)
    ) / length
    returned = lax.all_to_all(signal, "seq", split_axis=0, concat_axis=2, tiled=True)
    return returned[0]


def general_local(values, gates, filter_taps, skip_gain, out_weight):
    conv = channels_plan(values, filter_taps)
    gated = (
        gates.astype(jnp.float32) * (conv + skip_gain[None, :] * values.astype(jnp.float32))
    ).astype(jnp.bfloat16)
    projected = lax.psum_scatter(
        lax.dot_general(
            out_weight, gated, (((0,), (1,)), ((), ())), preferred_element_type=jnp.float32
        ),
        "chan",
        scatter_dimension=0,
        tiled=True,
    )
    return projected.astype(jnp.bfloat16)


def split_table(table):
    high = table.astype(ml_dtypes.bfloat16)
    low = (table - high.astype(np.float64)).astype(ml_dtypes.bfloat16)
    return high, low


@functools.lru_cache(maxsize=None)
def transform_tables(length):
    inner = length // RADIX
    k = np.arange(inner)[:, None]
    unit = TWO_PI / (4 * length)
    turns = (np.array(Q_ORDER)[:, None] * (4 * k.T + 1)) % (4 * length) * unit
    turns = np.stack([np.cos(turns), np.sin(turns)], axis=1).reshape(2 * RADIX, inner, 1)
    blocks = [np.broadcast_to(turns, (2 * RADIX, inner, LANES))]
    forward, backward = [], []
    for odd in range(2):
        m = 2 * np.arange(inner // 2)[None, :] + odd
        angles = (RADIX * m * (4 * k[: inner // 2] + 1)) % (4 * length) * unit
        table = np.concatenate([np.cos(angles), -np.sin(angles)], axis=0)
        forward.append(np.concatenate(split_table(table), axis=1))
        backward.append(np.concatenate(split_table(table.T / length), axis=0))
    for table in forward + backward:
        blocks.append(table.astype(np.float32).reshape(inner, -1, LANES).swapaxes(0, 1))
    return np.concatenate(blocks, axis=0).astype(np.float32)


@functools.lru_cache(maxsize=None)
def row_order(rows):
    chunk = rows // RADIX
    order = np.zeros((rows, rows), np.float32)
    for i, q in enumerate(Q_ORDER):
        for odd in range(2):
            for j in range(chunk // 2):
                order[i * chunk + odd * (chunk // 2) + j, RADIX * (2 * j + odd) + q] = 1.0
    return order.astype(ml_dtypes.bfloat16)


def turn(point, index, sign):
    re, im = point
    index %= 16
    if index == 0:
        return point
    if index == 4:
        return (-im, re) if sign > 0 else (im, -re)
    if index == 8:
        return (-re, -im)
    half = math.sqrt(0.5)
    if index == 2:
        return ((re - im) * half, (re + im) * half) if sign > 0 else ((re + im) * half, (im - re) * half)
    if index == 6:
        return ((-re - im) * half, (re - im) * half) if sign > 0 else ((im - re) * half, (-re - im) * half)
    cos = math.cos(TWO_PI * index / 16)
    sin = sign * math.sin(TWO_PI * index / 16)
    return (re * cos - im * sin, re * sin + im * cos)


def four_points(points, sign):
    a, b, c, d = points
    ac = (a[0] + c[0], a[1] + c[1])
    am = (a[0] - c[0], a[1] - c[1])
    bd = (b[0] + d[0], b[1] + d[1])
    bm = (b[0] - d[0], b[1] - d[1])
    if sign < 0:
        side = (bm[1], -bm[0])
    else:
        side = (-bm[1], bm[0])
    return (
        (ac[0] + bd[0], ac[1] + bd[1]),
        (am[0] + side[0], am[1] + side[1]),
        (ac[0] - bd[0], ac[1] - bd[1]),
        (am[0] - side[0], am[1] - side[1]),
    )


def turned(point, cos, sin, sign):
    re, im = point
    if sign < 0:
        return (re * cos + im * sin, im * cos - re * sin)
    return (re * cos - im * sin, im * cos + re * sin)


def slot_order(blocks):
    half = blocks // 2
    across = [half + (i // 2 if i % 2 == 0 else half // 2 + i // 2) for i in range(half)]
    near = list(range(1, half)) + [0]
    lead = 2
    mixed = [slot for pair in zip(across[lead:], near) for slot in pair]
    return across[:lead] + mixed + near[half - lead :]


def arrange_kernel(pieces, blocks, me_ref, order_hbm, values_hbm, taps_hbm, *rest):
    outs = rest[:blocks]
    order_ref, values_ref, taps_ref, packed, sems = rest[blocks:]
    piece = values_ref.shape[1] // pieces
    loads = [pltpu.make_async_copy(order_hbm, order_ref, sems.at[2 * pieces])]
    for part in range(pieces):
        lanes = pl.ds(part * piece, piece)
        loads.append(pltpu.make_async_copy(values_hbm.at[:, lanes], values_ref.at[:, lanes], sems.at[2 * part]))
        loads.append(pltpu.make_async_copy(taps_hbm.at[:, lanes], taps_ref.at[:, lanes], sems.at[2 * part + 1]))
    for load in loads:
        load.start()
    loads[0].wait()
    for part in range(pieces):
        loads[2 * part + 1].wait()
        loads[2 * part + 2].wait()
        lanes = pl.ds(part * piece, piece)
        both = jnp.concatenate([values_ref[:, lanes], taps_ref[:, lanes]], axis=1)
        moved = jnp.dot(order_ref[...], both, preferred_element_type=jnp.float32).astype(jnp.bfloat16)
        for block in range(piece // LANES):
            for side in range(2):
                start = side * piece + block * LANES
                packed[part * piece // LANES + block, :, pl.ds(side * LANES, LANES)] = moved[:, start : start + LANES]
    for out, slot in zip(outs, slot_order(blocks)):
        out[...] = packed[me_ref[0] ^ slot]


def arrange(me, values, taps, blocks):
    rows, wide = values.shape
    pieces = 4
    return pl.pallas_call(
        functools.partial(arrange_kernel, pieces, blocks),
        in_specs=[pl.BlockSpec(memory_space=pltpu.SMEM)] + [pl.BlockSpec(memory_space=pl.ANY)] * 3,
        out_specs=[pl.BlockSpec(memory_space=pltpu.VMEM)] * blocks,
        out_shape=[jax.ShapeDtypeStruct((rows, 2 * LANES), jnp.bfloat16)] * blocks,
        scratch_shapes=[
            pltpu.VMEM((rows, rows), jnp.bfloat16),
            pltpu.VMEM((rows, wide), jnp.bfloat16),
            pltpu.VMEM((rows, wide), jnp.bfloat16),
            pltpu.VMEM((blocks, rows, 2 * LANES), jnp.bfloat16),
            pltpu.SemaphoreType.DMA((2 * pieces + 1,)),
        ],
        compiler_params=pltpu.CompilerParams(vmem_limit_bytes=VMEM_BYTES),
        cost_estimate=pl.CostEstimate(
            flops=4 * rows * rows * wide, bytes_accessed=8 * rows * wide, transcendentals=0
        ),
        name="arrange_rows",
    )(me, jnp.asarray(row_order(rows)), values, taps)


def convolve_kernel(blocks, me_ref, *rest):
    slots = rest[:blocks]
    convolve_blocks(me_ref, slots, *rest[blocks:])


def convolve_blocks(
    me_ref, slots, tables_hbm, out_hbm,
    streams, turns_ref, fixed, stages, raw_even, raw_odd, columns, mixed, halves_even, halves_odd, signals, sems,
):
    blocks, rows, _ = streams.shape
    chunk = rows // RADIX
    inner = blocks * chunk
    part_rows = inner // 2
    group = rows // 4
    raws = (raw_even, raw_odd)
    halves = (halves_even, halves_odd)
    count = fixed.shape[0]
    load_fixed = pltpu.make_async_copy(tables_hbm.at[pl.ds(2 * RADIX, count)], fixed, sems.at[0])
    load_turns, stores = [], []
    for low in range(4):
        taken = pl.ds(low * group, group)
        eight = pl.ds(8 * low, 8)
        load_turns.append(pltpu.make_async_copy(tables_hbm.at[eight], turns_ref.at[eight], sems.at[1 + low]))
        stores.append(pltpu.make_async_copy(signals.at[:, taken], out_hbm.at[:, taken], sems.at[5 + low]))
    load_fixed.start()
    for load in load_turns:
        load.start()
    for slot, source in zip(slot_order(blocks), slots):
        streams[me_ref[0] ^ slot] = source[...]
    load_fixed.wait()
    width = inner // LANES
    for table in range(4):
        for block in range(width):
            stages[table, :, pl.ds(block * LANES, LANES)] = fixed[table * width + block].astype(jnp.bfloat16)

    def transform(low, pair):
        sides = [[], []]
        for part in range(2):
            taken = pl.ds(pl.multiple_of(low * group + (2 * pair + part) * chunk, chunk), chunk)
            stream = streams[:, taken].astype(jnp.float32).reshape(blocks, 2, chunk // 2, 2 * LANES)
            for odd in range(2):
                sides[odd].append(stream[:, odd].reshape(part_rows, 2 * LANES).astype(jnp.bfloat16))
        for odd in range(2):
            both = jnp.concatenate(sides[odd], axis=1)
            result = jnp.dot(
                stages[odd], jnp.concatenate([both, both], axis=0), preferred_element_type=jnp.float32
            )
            for part in range(2):
                raws[low % 2][2 * pair + part, odd] = result[:, 2 * part * LANES : 2 * (part + 1) * LANES]

    def first_pass(low, start):
        raw = raws[low % 2]
        real, imaginary = pl.ds(start, 8), pl.ds(part_rows + start, 8)
        for side in range(2):
            lanes = pl.ds(side * LANES, LANES)
            points = [[], []]
            for high in range(4):
                even = (raw[high, 0, real, lanes], raw[high, 0, imaginary, lanes])
                odd = (raw[high, 1, real, lanes], raw[high, 1, imaginary, lanes])
                points[0].append((even[0] + odd[0], even[1] + odd[1]))
                points[1].append((even[0] - odd[0], even[1] - odd[1]))
            for part in range(2):
                upper, lower = pl.ds(part * part_rows + start, 8), pl.ds(inner + part * part_rows + start, 8)
                for high in range(4):
                    if low + high:
                        turns = [turns_ref[2 * (4 * low + high) + i, upper] for i in range(2)]
                        points[part][high] = turned(points[part][high], *turns, -1)
                for k, point in enumerate(four_points(points[part], -1)):
                    point = turn(point, low * k, -1)
                    columns[4 * low + k, upper, lanes] = point[0]
                    columns[4 * low + k, lower, lanes] = point[1]

    def first_rows(low, start, count):
        for part in range(count):
            first_pass(low, pl.multiple_of(start + 8 * part, 8))

    steps = part_rows // 2

    def alone(pair, carry):
        transform(0, pair)
        return carry

    lax.fori_loop(0, 2, alone, 0)
    for low in range(1, 4):
        load_turns[low - 1].wait()

        def beside(pair, carry, low=low):
            transform(low, pair)
            first_rows(low - 1, pair * steps, steps // 8)
            return carry

        lax.fori_loop(0, 2, beside, 0)
    load_turns[3].wait()

    def middle(index, carry):
        start = pl.multiple_of(index * 8, 8)
        first_pass(3, start)
        for part in range(2):
            upper, lower = pl.ds(part * part_rows + start, 8), pl.ds(inner + part * part_rows + start, 8)
            for k in range(4):
                sides = []
                for side in range(2):
                    lanes = pl.ds(side * LANES, LANES)
                    points = [
                        (columns[4 * low + k, upper, lanes], columns[4 * low + k, lower, lanes]) for low in range(4)
                    ]
                    sides.append(four_points(points, -1))
                product = [
                    (a[0] * b[0] - a[1] * b[1], a[0] * b[1] + a[1] * b[0]) for a, b in zip(*sides)
                ]
                for high, point in enumerate(four_points(product, 1)):
                    point = turn(point, k * high, 1)
                    mixed[4 * high + k, upper] = point[0]
                    mixed[4 * high + k, lower] = point[1]
        return carry

    lax.fori_loop(0, part_rows // 8, middle, 0)

    def last_pass(low, start):
        target = halves[low % 2]
        found = []
        for part in range(2):
            upper, lower = pl.ds(part * part_rows + start, 16), pl.ds(inner + part * part_rows + start, 16)
            points = list(four_points([(mixed[4 * low + k, upper], mixed[4 * low + k, lower]) for k in range(4)], 1))
            for high in range(4):
                if low + high:
                    turns = [turns_ref[2 * (4 * low + high) + i, upper] for i in range(2)]
                    points[high] = turned(points[high], *turns, 1)
            found.append(points)
        for high in range(4):
            for i in range(2):
                taken = pl.ds(i * part_rows + start, 16)
                first, second = found[0][high][i], found[1][high][i]
                for odd, value in enumerate((first + second, first - second)):
                    rounded = value.astype(jnp.bfloat16)
                    target[high, odd, taken, pl.ds(0, LANES)] = rounded
                    target[high, odd, taken, pl.ds(LANES, LANES)] = (value - rounded.astype(jnp.float32)).astype(
                        jnp.bfloat16
                    )

    def last_rows(low, start, count):
        for part in range(count):
            last_pass(low, pl.multiple_of(start + 16 * part, 16))

    def restore(low, pair):
        sides = []
        for odd in range(2):
            both = jnp.concatenate([halves[low % 2][2 * pair + part, odd] for part in range(2)], axis=1)
            terms = jnp.dot(stages[2 + odd], both, preferred_element_type=jnp.float32)
            found = []
            for part in range(2):
                first, second = [slice((2 * part + i) * LANES, (2 * part + i + 1) * LANES) for i in range(2)]
                signal = terms[:part_rows, first] + terms[:part_rows, second] + terms[part_rows:, first]
                found.append(signal.reshape(blocks, 1, chunk // 2, LANES))
            sides.append(found)
        for part in range(2):
            signal = jnp.concatenate([sides[0][part], sides[1][part]], axis=1).reshape(blocks, chunk, LANES)
            taken = pl.ds(pl.multiple_of(low * group + (2 * pair + part) * chunk, chunk), chunk)
            signals[:, taken] = signal.astype(jnp.bfloat16)

    def prepare(index, carry):
        last_rows(0, index * steps, steps // 16)
        return carry

    lax.fori_loop(0, 2, prepare, 0)
    for low in range(4):

        def back(pair, carry, low=low):
            restore(low, pair)
            if low < 3:
                last_rows(low + 1, pair * steps, steps // 16)
            return carry

        lax.fori_loop(0, 2, back, 0)
        stores[low].start()
    for store in stores:
        store.wait()


def convolve(me, slots):
    blocks = len(slots)
    rows, lanes = slots[0].shape
    length = blocks * rows
    inner = length // RADIX
    tables = transform_tables(length)
    return pl.pallas_call(
        functools.partial(convolve_kernel, blocks),
        in_specs=[pl.BlockSpec(memory_space=pltpu.SMEM)]
        + [pl.BlockSpec(memory_space=pltpu.VMEM)] * blocks
        + [pl.BlockSpec(memory_space=pl.ANY)],
        out_specs=pl.BlockSpec(memory_space=pl.ANY),
        out_shape=jax.ShapeDtypeStruct((blocks, rows, LANES), jnp.bfloat16),
        scratch_shapes=[
            pltpu.VMEM((blocks, rows, lanes), jnp.bfloat16),
            pltpu.VMEM((2 * RADIX, inner, LANES), jnp.float32),
            pltpu.VMEM((tables.shape[0] - 2 * RADIX, inner, LANES), jnp.float32),
            pltpu.VMEM((4, inner, inner), jnp.bfloat16),
            pltpu.VMEM((4, 2, inner, lanes), jnp.float32),
            pltpu.VMEM((4, 2, inner, lanes), jnp.float32),
            pltpu.VMEM((RADIX, 2 * inner, lanes), jnp.float32),
            pltpu.VMEM((RADIX, 2 * inner, LANES), jnp.float32),
            pltpu.VMEM((4, 2, inner, lanes), jnp.bfloat16),
            pltpu.VMEM((4, 2, inner, lanes), jnp.bfloat16),
            pltpu.VMEM((blocks, rows, LANES), jnp.bfloat16),
            pltpu.SemaphoreType.DMA((9,)),
        ],
        compiler_params=pltpu.CompilerParams(vmem_limit_bytes=CONV_BYTES),
        cost_estimate=pl.CostEstimate(flops=5 * 10**9, bytes_accessed=9 * 10**6, transcendentals=0),
        name="long_convolution",
    )(me, *slots, jnp.asarray(tables))


def gate_kernel(
    group, half_ref, order_hbm, conv_ref, gates_hbm, values_hbm, skip_ref, weight_hbm, gated_ref, out_ref,
    order_ref, gates_ref, values_ref, weight_ref, sems,
):
    blocks, _, lanes = conv_ref.shape
    width, features = weight_ref.shape
    columns = pl.ds(pl.multiple_of((1 - half_ref[0]) * features, features), features)
    loads = [
        pltpu.make_async_copy(order_hbm, order_ref, sems.at[0]),
        pltpu.make_async_copy(gates_hbm, gates_ref, sems.at[1]),
        pltpu.make_async_copy(values_hbm, values_ref, sems.at[2]),
    ]
    deep = width // 2
    for part in range(2):
        rows = pl.ds(part * deep, deep)
        loads.append(pltpu.make_async_copy(weight_hbm.at[rows, columns], weight_ref.at[rows], sems.at[3 + part]))
    for load in loads:
        load.start()
    for load in loads[:3]:
        load.wait()
    for step in range(blocks // group):
        taken = pl.ds(step * group * lanes, group * lanes)
        conv = jnp.concatenate([conv_ref[step * group + part] for part in range(group)], axis=1)
        conv = jnp.dot(order_ref[...], conv, preferred_element_type=jnp.float32)
        direct = skip_ref[:, taken] * values_ref[:, taken].astype(jnp.float32)
        gated_ref[:, taken] = (gates_ref[:, taken].astype(jnp.float32) * (conv + direct)).astype(jnp.bfloat16)
    loads[3].wait()
    first = jnp.dot(gated_ref[:, :deep], weight_ref[:deep], preferred_element_type=jnp.float32)
    loads[4].wait()
    out_ref[...] = first + jnp.dot(gated_ref[:, deep:], weight_ref[deep:], preferred_element_type=jnp.float32)


def gate_and_project(half, conv, gates, values, skip_gain, weight):
    rows, width = gates.shape
    features = weight.shape[1] // 2
    anywhere, inside = pl.BlockSpec(memory_space=pl.ANY), pl.BlockSpec(memory_space=pltpu.VMEM)
    return pl.pallas_call(
        functools.partial(gate_kernel, 4),
        in_specs=[pl.BlockSpec(memory_space=pltpu.SMEM), anywhere, inside, anywhere, anywhere, inside, anywhere],
        out_specs=[inside] * 2,
        out_shape=[
            jax.ShapeDtypeStruct((rows, width), jnp.bfloat16),
            jax.ShapeDtypeStruct((rows, features), jnp.float32),
        ],
        scratch_shapes=[
            pltpu.VMEM((rows, rows), jnp.bfloat16),
            pltpu.VMEM((rows, width), jnp.bfloat16),
            pltpu.VMEM((rows, width), jnp.bfloat16),
            pltpu.VMEM((width, features), jnp.bfloat16),
            pltpu.SemaphoreType.DMA((5,)),
        ],
        compiler_params=pltpu.CompilerParams(vmem_limit_bytes=TAIL_BYTES),
        cost_estimate=pl.CostEstimate(
            flops=2 * rows * width * features, bytes_accessed=2 * width * features, transcendentals=0
        ),
        name="gate_project_sent",
    )(half, jnp.asarray(row_order(rows).T), conv, gates, values, skip_gain[None, :], weight)


def kept_kernel(half_ref, gated_ref, weight_hbm, out_ref, weight_ref, sems):
    width, features = weight_ref.shape
    columns = pl.ds(pl.multiple_of(half_ref[0] * features, features), features)
    deep = width // 2
    loads = []
    for part in range(2):
        rows = pl.ds(part * deep, deep)
        loads.append(pltpu.make_async_copy(weight_hbm.at[rows, columns], weight_ref.at[rows], sems.at[part]))
        loads[part].start()
    loads[0].wait()
    first = jnp.dot(gated_ref[:, :deep], weight_ref[:deep], preferred_element_type=jnp.float32)
    loads[1].wait()
    out_ref[...] = first + jnp.dot(gated_ref[:, deep:], weight_ref[deep:], preferred_element_type=jnp.float32)


def project_kept(half, gated, weight):
    rows, width = gated.shape
    features = weight.shape[1] // 2
    anywhere, inside = pl.BlockSpec(memory_space=pl.ANY), pl.BlockSpec(memory_space=pltpu.VMEM)
    return pl.pallas_call(
        kept_kernel,
        in_specs=[pl.BlockSpec(memory_space=pltpu.SMEM), inside, anywhere],
        out_specs=inside,
        out_shape=jax.ShapeDtypeStruct((rows, features), jnp.float32),
        scratch_shapes=[pltpu.VMEM((width, features), jnp.bfloat16), pltpu.SemaphoreType.DMA((2,))],
        compiler_params=pltpu.CompilerParams(vmem_limit_bytes=TAIL_BYTES),
        cost_estimate=pl.CostEstimate(
            flops=2 * rows * width * features, bytes_accessed=2 * width * features, transcendentals=0
        ),
        name="project_kept",
    )(half, gated, weight)


def join_kernel(kept_ref, came_ref, out_ref):
    out_ref[...] = (kept_ref[...] + came_ref[...]).astype(jnp.bfloat16).T


def join(kept, came):
    rows, features = kept.shape
    wide = features // 4
    return pl.pallas_call(
        join_kernel,
        grid=(4,),
        in_specs=[pl.BlockSpec((rows, wide), lambda i: (0, i))] * 2,
        out_specs=pl.BlockSpec((wide, rows), lambda i: (i, 0)),
        out_shape=jax.ShapeDtypeStruct((features, rows), jnp.bfloat16),
        compiler_params=pltpu.CompilerParams(vmem_limit_bytes=TAIL_BYTES),
        name="join_halves",
    )(kept, came)


def swap_blocks(array):
    return lax.all_to_all(array, "seq", split_axis=0, concat_axis=0, tiled=True)


def exchange(slots):
    blocks = len(slots)
    return [
        lax.ppermute(source, "seq", [(j, j ^ slot) for j in range(blocks)]) if slot else source
        for slot, source in zip(slot_order(blocks), slots)
    ]


def kernel_local(values, gates, filter_taps, skip_gain, out_weight):
    blocks = lax.axis_size("seq")
    me = lax.axis_index("seq").astype(jnp.int32)[None]
    half = lax.axis_index("chan").astype(jnp.int32)[None]
    conv = convolve(me, exchange(arrange(me, values, filter_taps, blocks)))
    gated, sent = gate_and_project(half, swap_blocks(conv), gates, values, skip_gain, out_weight)
    other = lax.ppermute(sent, "chan", [(0, 1), (1, 0)])
    kept = project_kept(half, gated, out_weight)
    return join(kept, other)


def takes_kernels(mesh, values, out_weight):
    blocks, halves = mesh.shape["seq"], mesh.shape["chan"]
    rows = values.shape[0] // blocks
    return (
        halves == 2
        and blocks == 16
        and rows == 256
        and values.shape[1] == halves * blocks * LANES
        and out_weight.shape[1] % (8 * LANES) == 0
    )


def solution(mesh):
    placed = (P("seq", "chan"), P("seq", "chan"), P("seq", "chan"), P("chan"), P("chan", None))

    def whole(values, gates, filter_taps, skip_gain, out_weight):
        local = kernel_local if takes_kernels(mesh, values, out_weight) else general_local
        return jax.shard_map(
            local, mesh=mesh, in_specs=placed, out_specs=P("chan", "seq"), check_vma=False
        )(values, gates, filter_taps, skip_gain, out_weight)

    return whole
```

```python
import functools
import math

import jax
import jax.numpy as jnp
import ml_dtypes
import numpy as np
from jax import lax
from jax.experimental import pallas as pl
from jax.experimental.pallas import tpu as pltpu
from jax.sharding import PartitionSpec as P

TWO_PI = 2.0 * math.pi
HIGH = lax.Precision.HIGHEST
RADIX = 16
LANES = 128
Q_ORDER = [low + 4 * high for low in range(4) for high in range(4)]
ARRANGE_BYTES = 60 * 1024 * 1024
CONV_BYTES = 50 * 1024 * 1024
TAIL_BYTES = 16 * 1024 * 1024


def angle_table(first, second, period):
    product = first[:, None] * second[None, :] % period
    angles = product.astype(jnp.float32) * (TWO_PI / period)
    return (jnp.cos(angles), jnp.sin(angles))


def mix(equation, left, right):
    return jnp.einsum(equation, left, right, precision=HIGH)


def outer_forward(data, outer_cos, outer_sin, twist_cos, twist_sin, equation):
    source = data.astype(jnp.float32)
    real = mix(equation, outer_cos, source)
    imag = -mix(equation, outer_sin, source)
    cos_part = twist_cos[:, :, None]
    sin_part = twist_sin[:, :, None]
    return (real * cos_part + imag * sin_part, imag * cos_part - real * sin_part)


def inner_filter(spectra, inner_cos, inner_sin):
    value_re, value_im, taps_re, taps_im = spectra

    def forward(real, imag):
        out_re = mix("kr,jrc->jkc", inner_cos, real) + mix("kr,jrc->jkc", inner_sin, imag)
        out_im = mix("kr,jrc->jkc", inner_cos, imag) - mix("kr,jrc->jkc", inner_sin, real)
        return (out_re, out_im)

    value_fre, value_fim = forward(value_re, value_im)
    taps_fre, taps_fim = forward(taps_re, taps_im)
    prod_re = value_fre * taps_fre - value_fim * taps_fim
    prod_im = value_fre * taps_fim + value_fim * taps_fre
    back_re = mix("rk,jkc->jrc", inner_cos, prod_re) - mix("rk,jkc->jrc", inner_sin, prod_im)
    back_im = mix("rk,jkc->jrc", inner_cos, prod_im) + mix("rk,jkc->jrc", inner_sin, prod_re)
    return (back_re, back_im)


def untwist(real, imag, twist_cos, twist_sin):
    cos_part = twist_cos[:, :, None]
    sin_part = twist_sin[:, :, None]
    return (real * cos_part - imag * sin_part, imag * cos_part + real * sin_part)


def channels_plan(values, filter_taps):
    rows, width = values.shape
    blocks = lax.axis_size("seq")
    length = 2 * blocks * rows
    narrow = width // blocks
    whole_values, whole_taps = (
        lax.all_to_all(values, "seq", split_axis=1, concat_axis=0, tiled=True),
        lax.all_to_all(filter_taps, "seq", split_axis=1, concat_axis=0, tiled=True),
    )
    freq_ids = jnp.arange(2 * blocks, dtype=jnp.int32)
    block_ids = jnp.arange(blocks, dtype=jnp.int32)
    all_rows = jnp.arange(rows, dtype=jnp.int32)
    outer_cos, outer_sin = angle_table(freq_ids, block_ids, 2 * blocks)
    twist_cos, twist_sin = angle_table(freq_ids, all_rows, length)
    tables = (outer_cos, outer_sin, twist_cos, twist_sin, "ka,arc->krc")
    value_re, value_im = outer_forward(whole_values.reshape(blocks, rows, narrow), *tables)
    taps_re, taps_im = outer_forward(whole_taps.reshape(blocks, rows, narrow), *tables)
    inner_cos, inner_sin = angle_table(all_rows, all_rows, rows)
    back_re, back_im = inner_filter((value_re, value_im, taps_re, taps_im), inner_cos, inner_sin)
    turned_re, turned_im = untwist(back_re, back_im, twist_cos, twist_sin)
    final_cos, final_sin = angle_table(block_ids, freq_ids, 2 * blocks)
    signal = (
        mix("ak,krc->arc", final_cos, turned_re) - mix("ak,krc->arc", final_sin, turned_im)
    ) / length
    returned = lax.all_to_all(signal, "seq", split_axis=0, concat_axis=2, tiled=True)
    return returned[0]


def general_local(values, gates, filter_taps, skip_gain, out_weight):
    conv = channels_plan(values, filter_taps)
    gated = (
        gates.astype(jnp.float32) * (conv + skip_gain[None, :] * values.astype(jnp.float32))
    ).astype(jnp.bfloat16)
    projected = lax.psum_scatter(
        lax.dot_general(
            out_weight, gated, (((0,), (1,)), ((), ())), preferred_element_type=jnp.float32
        ),
        "chan",
        scatter_dimension=0,
        tiled=True,
    )
    return projected.astype(jnp.bfloat16)


def split_table(table):
    high = table.astype(ml_dtypes.bfloat16)
    low = (table - high.astype(np.float64)).astype(ml_dtypes.bfloat16)
    return high, low


@functools.lru_cache(maxsize=None)
def transform_tables(length):
    inner = length // RADIX
    k = np.arange(inner)[:, None]
    unit = TWO_PI / (4 * length)
    turns = (np.array(Q_ORDER)[:, None] * (4 * k.T + 1)) % (4 * length) * unit
    turns = np.stack([np.cos(turns), np.sin(turns)], axis=1).reshape(2 * RADIX, inner, 1)
    blocks = [np.broadcast_to(turns, (2 * RADIX, inner, LANES))]
    forward, backward = [], []
    for odd in range(2):
        m = 2 * np.arange(inner // 2)[None, :] + odd
        angles = (RADIX * m * (4 * k[: inner // 2] + 1)) % (4 * length) * unit
        table = np.concatenate([np.cos(angles), -np.sin(angles)], axis=0)
        forward.append(np.concatenate(split_table(table), axis=1))
        backward.append(np.concatenate(split_table(table.T / length), axis=0))
    for table in forward + backward:
        blocks.append(table.astype(np.float32).reshape(inner, -1, LANES).swapaxes(0, 1))
    return np.concatenate(blocks, axis=0).astype(np.float32)


def row_order(rows, turned_over=False):
    place = lax.broadcasted_iota(jnp.int32, (rows, rows), 1 if turned_over else 0)
    source = lax.broadcasted_iota(jnp.int32, (rows, rows), 0 if turned_over else 1)
    chunk = rows // RADIX
    index, within = place // chunk, place % chunk
    odd, j = within // (chunk // 2), within % (chunk // 2)
    wanted = RADIX * (2 * j + odd) + index // 4 + 4 * (index % 4)
    return jnp.where(source == wanted, 1.0, 0.0).astype(jnp.bfloat16)


def turn(point, index, sign):
    re, im = point
    index %= 16
    if index == 0:
        return point
    if index == 4:
        return (-im, re) if sign > 0 else (im, -re)
    if index == 8:
        return (-re, -im)
    half = math.sqrt(0.5)
    if index == 2:
        return ((re - im) * half, (re + im) * half) if sign > 0 else ((re + im) * half, (im - re) * half)
    if index == 6:
        return ((-re - im) * half, (re - im) * half) if sign > 0 else ((im - re) * half, (-re - im) * half)
    cos = math.cos(TWO_PI * index / 16)
    sin = sign * math.sin(TWO_PI * index / 16)
    return (re * cos - im * sin, re * sin + im * cos)


def four_points(points, sign):
    a, b, c, d = points
    ac = (a[0] + c[0], a[1] + c[1])
    am = (a[0] - c[0], a[1] - c[1])
    bd = (b[0] + d[0], b[1] + d[1])
    bm = (b[0] - d[0], b[1] - d[1])
    if sign < 0:
        side = (bm[1], -bm[0])
    else:
        side = (-bm[1], bm[0])
    return (
        (ac[0] + bd[0], ac[1] + bd[1]),
        (am[0] + side[0], am[1] + side[1]),
        (ac[0] - bd[0], ac[1] - bd[1]),
        (am[0] - side[0], am[1] - side[1]),
    )


def turned(point, cos, sin, sign):
    re, im = point
    if sign < 0:
        return (re * cos + im * sin, im * cos - re * sin)
    return (re * cos - im * sin, im * cos + re * sin)


def slot_order(blocks):
    half = blocks // 2
    across = [half + (i // 2 if i % 2 == 0 else half // 2 + i // 2) for i in range(half)]
    near = list(range(1, half)) + [0]
    return [slot for pair in zip(across, near) for slot in pair]


def arrange_kernel(pieces, blocks, me_ref, values_hbm, taps_hbm, *rest):
    outs = rest[:blocks]
    values_ref, taps_ref, packed, sems = rest[blocks:]
    piece = values_ref.shape[1] // pieces
    loads = []
    for part in range(pieces):
        lanes = pl.ds(part * piece, piece)
        loads.append(pltpu.make_async_copy(values_hbm.at[:, lanes], values_ref.at[:, lanes], sems.at[2 * part]))
        loads.append(pltpu.make_async_copy(taps_hbm.at[:, lanes], taps_ref.at[:, lanes], sems.at[2 * part + 1]))
    for load in loads:
        load.start()
    order = row_order(values_ref.shape[0])
    for part in range(pieces):
        loads[2 * part].wait()
        loads[2 * part + 1].wait()
        lanes = pl.ds(part * piece, piece)
        both = jnp.concatenate([values_ref[:, lanes], taps_ref[:, lanes]], axis=1)
        moved = jnp.dot(order, both, preferred_element_type=jnp.float32).astype(jnp.bfloat16)
        for block in range(piece // LANES):
            for side in range(2):
                start = side * piece + block * LANES
                packed[part * piece // LANES + block, :, pl.ds(side * LANES, LANES)] = moved[:, start : start + LANES]
    for out, slot in zip(outs, slot_order(blocks)):
        out[...] = packed[me_ref[0] ^ slot]


def arrange(me, values, taps, blocks):
    rows, wide = values.shape
    pieces = 4
    return pl.pallas_call(
        functools.partial(arrange_kernel, pieces, blocks),
        in_specs=[pl.BlockSpec(memory_space=pltpu.SMEM)] + [pl.BlockSpec(memory_space=pl.ANY)] * 2,
        out_specs=[pl.BlockSpec(memory_space=pltpu.VMEM)] * blocks,
        out_shape=[jax.ShapeDtypeStruct((rows, 2 * LANES), jnp.bfloat16)] * blocks,
        scratch_shapes=[
            pltpu.VMEM((rows, wide), jnp.bfloat16),
            pltpu.VMEM((rows, wide), jnp.bfloat16),
            pltpu.VMEM((blocks, rows, 2 * LANES), jnp.bfloat16),
            pltpu.SemaphoreType.DMA((2 * pieces,)),
        ],
        compiler_params=pltpu.CompilerParams(vmem_limit_bytes=ARRANGE_BYTES),
        cost_estimate=pl.CostEstimate(
            flops=4 * rows * rows * wide, bytes_accessed=8 * rows * wide, transcendentals=0
        ),
        name="arrange_rows",
    )(me, values, taps)


def convolve_kernel(blocks, me_ref, *rest):
    slots = rest[:blocks]
    convolve_blocks(me_ref, slots, *rest[blocks:])


def convolve_blocks(
    me_ref, slots, tables_hbm, out_hbm,
    streams, turns_ref, fixed, stages, raw_even, raw_odd, columns, mixed, halves_even, halves_odd, signals, sems,
):
    blocks, rows, _ = streams.shape
    chunk = rows // RADIX
    inner = blocks * chunk
    part_rows = inner // 2
    group = rows // 4
    raws = (raw_even, raw_odd)
    halves = (halves_even, halves_odd)
    count = fixed.shape[0]
    load_fixed = pltpu.make_async_copy(tables_hbm.at[pl.ds(2 * RADIX, count)], fixed, sems.at[0])
    load_turns, stores = [], []
    for low in range(4):
        taken = pl.ds(low * group, group)
        eight = pl.ds(8 * low, 8)
        load_turns.append(pltpu.make_async_copy(tables_hbm.at[eight], turns_ref.at[eight], sems.at[1 + low]))
        stores.append(pltpu.make_async_copy(signals.at[:, taken], out_hbm.at[:, taken], sems.at[5 + low]))
    load_fixed.start()
    for load in load_turns:
        load.start()
    own = pltpu.make_async_copy(slots[-1], streams.at[me_ref[0]], sems.at[9])
    own.start()
    for slot, source in zip(slot_order(blocks)[:-1], slots[:-1]):
        streams[me_ref[0] ^ slot] = source[...]
    own.wait()
    load_fixed.wait()
    width = inner // LANES
    for table in range(4):
        for block in range(width):
            stages[table, :, pl.ds(block * LANES, LANES)] = fixed[table * width + block].astype(jnp.bfloat16)

    def transform(low, pair):
        sides = [[], []]
        for part in range(2):
            taken = pl.ds(pl.multiple_of(low * group + (2 * pair + part) * chunk, chunk), chunk)
            stream = streams[:, taken].astype(jnp.float32).reshape(blocks, 2, chunk // 2, 2 * LANES)
            for odd in range(2):
                sides[odd].append(stream[:, odd].reshape(part_rows, 2 * LANES).astype(jnp.bfloat16))
        for odd in range(2):
            both = jnp.concatenate(sides[odd], axis=1)
            result = jnp.dot(
                stages[odd], jnp.concatenate([both, both], axis=0), preferred_element_type=jnp.float32
            )
            for part in range(2):
                raws[low % 2][2 * pair + part, odd] = result[:, 2 * part * LANES : 2 * (part + 1) * LANES]

    def first_pass(low, start):
        raw = raws[low % 2]
        real, imaginary = pl.ds(start, 8), pl.ds(part_rows + start, 8)
        for side in range(2):
            lanes = pl.ds(side * LANES, LANES)
            points = [[], []]
            for high in range(4):
                even = (raw[high, 0, real, lanes], raw[high, 0, imaginary, lanes])
                odd = (raw[high, 1, real, lanes], raw[high, 1, imaginary, lanes])
                points[0].append((even[0] + odd[0], even[1] + odd[1]))
                points[1].append((even[0] - odd[0], even[1] - odd[1]))
            for part in range(2):
                upper, lower = pl.ds(part * part_rows + start, 8), pl.ds(inner + part * part_rows + start, 8)
                for high in range(4):
                    if low + high:
                        turns = [turns_ref[2 * (4 * low + high) + i, upper] for i in range(2)]
                        points[part][high] = turned(points[part][high], *turns, -1)
                for k, point in enumerate(four_points(points[part], -1)):
                    point = turn(point, low * k, -1)
                    columns[4 * low + k, upper, lanes] = point[0]
                    columns[4 * low + k, lower, lanes] = point[1]

    def first_rows(low, start, count):
        for part in range(count):
            first_pass(low, pl.multiple_of(start + 8 * part, 8))

    steps = part_rows // 2

    def alone(pair, carry):
        transform(0, pair)
        return carry

    lax.fori_loop(0, 2, alone, 0)
    for low in range(1, 4):
        load_turns[low - 1].wait()

        def beside(pair, carry, low=low):
            transform(low, pair)
            first_rows(low - 1, pair * steps, steps // 8)
            return carry

        lax.fori_loop(0, 2, beside, 0)
    load_turns[3].wait()

    def middle(index, carry):
        start = pl.multiple_of(index * 8, 8)
        first_pass(3, start)
        for part in range(2):
            upper, lower = pl.ds(part * part_rows + start, 8), pl.ds(inner + part * part_rows + start, 8)
            for k in range(4):
                sides = []
                for side in range(2):
                    lanes = pl.ds(side * LANES, LANES)
                    points = [
                        (columns[4 * low + k, upper, lanes], columns[4 * low + k, lower, lanes]) for low in range(4)
                    ]
                    sides.append(four_points(points, -1))
                product = [
                    (a[0] * b[0] - a[1] * b[1], a[0] * b[1] + a[1] * b[0]) for a, b in zip(*sides)
                ]
                for high, point in enumerate(four_points(product, 1)):
                    point = turn(point, k * high, 1)
                    mixed[4 * high + k, upper] = point[0]
                    mixed[4 * high + k, lower] = point[1]
        return carry

    lax.fori_loop(0, part_rows // 8, middle, 0)

    def last_pass(low, start):
        target = halves[low % 2]
        found = []
        for part in range(2):
            upper, lower = pl.ds(part * part_rows + start, 16), pl.ds(inner + part * part_rows + start, 16)
            points = list(four_points([(mixed[4 * low + k, upper], mixed[4 * low + k, lower]) for k in range(4)], 1))
            for high in range(4):
                if low + high:
                    turns = [turns_ref[2 * (4 * low + high) + i, upper] for i in range(2)]
                    points[high] = turned(points[high], *turns, 1)
            found.append(points)
        for high in range(4):
            for i in range(2):
                taken = pl.ds(i * part_rows + start, 16)
                first, second = found[0][high][i], found[1][high][i]
                for odd, value in enumerate((first + second, first - second)):
                    rounded = value.astype(jnp.bfloat16)
                    target[high, odd, taken, pl.ds(0, LANES)] = rounded
                    target[high, odd, taken, pl.ds(LANES, LANES)] = (value - rounded.astype(jnp.float32)).astype(
                        jnp.bfloat16
                    )

    def last_rows(low, start, count):
        for part in range(count):
            last_pass(low, pl.multiple_of(start + 16 * part, 16))

    def restore(low, pair):
        sides = []
        for odd in range(2):
            both = jnp.concatenate([halves[low % 2][2 * pair + part, odd] for part in range(2)], axis=1)
            terms = jnp.dot(stages[2 + odd], both, preferred_element_type=jnp.float32)
            found = []
            for part in range(2):
                first, second = [slice((2 * part + i) * LANES, (2 * part + i + 1) * LANES) for i in range(2)]
                signal = terms[:part_rows, first] + terms[:part_rows, second] + terms[part_rows:, first]
                found.append(signal.reshape(blocks, 1, chunk // 2, LANES))
            sides.append(found)
        for part in range(2):
            signal = jnp.concatenate([sides[0][part], sides[1][part]], axis=1).reshape(blocks, chunk, LANES)
            taken = pl.ds(pl.multiple_of(low * group + (2 * pair + part) * chunk, chunk), chunk)
            signals[:, taken] = signal.astype(jnp.bfloat16)

    def prepare(index, carry):
        last_rows(0, index * steps, steps // 16)
        return carry

    lax.fori_loop(0, 2, prepare, 0)
    for low in range(4):

        def back(pair, carry, low=low):
            restore(low, pair)
            if low < 3:
                last_rows(low + 1, pair * steps, steps // 16)
            return carry

        lax.fori_loop(0, 2, back, 0)
        stores[low].start()
    for store in stores:
        store.wait()


def convolve(me, slots):
    blocks = len(slots)
    rows, lanes = slots[0].shape
    length = blocks * rows
    inner = length // RADIX
    tables = transform_tables(length)
    return pl.pallas_call(
        functools.partial(convolve_kernel, blocks),
        in_specs=[pl.BlockSpec(memory_space=pltpu.SMEM)]
        + [pl.BlockSpec(memory_space=pltpu.VMEM)] * (blocks - 1)
        + [pl.BlockSpec(memory_space=pl.ANY)] * 2,
        out_specs=pl.BlockSpec(memory_space=pl.ANY),
        out_shape=jax.ShapeDtypeStruct((blocks, rows, LANES), jnp.bfloat16),
        scratch_shapes=[
            pltpu.VMEM((blocks, rows, lanes), jnp.bfloat16),
            pltpu.VMEM((2 * RADIX, inner, LANES), jnp.float32),
            pltpu.VMEM((tables.shape[0] - 2 * RADIX, inner, LANES), jnp.float32),
            pltpu.VMEM((4, inner, inner), jnp.bfloat16),
            pltpu.VMEM((4, 2, inner, lanes), jnp.float32),
            pltpu.VMEM((4, 2, inner, lanes), jnp.float32),
            pltpu.VMEM((RADIX, 2 * inner, lanes), jnp.float32),
            pltpu.VMEM((RADIX, 2 * inner, LANES), jnp.float32),
            pltpu.VMEM((4, 2, inner, lanes), jnp.bfloat16),
            pltpu.VMEM((4, 2, inner, lanes), jnp.bfloat16),
            pltpu.VMEM((blocks, rows, LANES), jnp.bfloat16),
            pltpu.SemaphoreType.DMA((10,)),
        ],
        compiler_params=pltpu.CompilerParams(vmem_limit_bytes=CONV_BYTES),
        cost_estimate=pl.CostEstimate(flops=5 * 10**9, bytes_accessed=9 * 10**6, transcendentals=0),
        name="long_convolution",
    )(me, *slots, jnp.asarray(tables))


def gate_kernel(group, half_ref, conv_ref, gates_ref, values_ref, skip_ref, weight_ref, gated_ref, out_ref):
    blocks, rows, lanes = conv_ref.shape
    features = out_ref.shape[1]
    order = row_order(rows, True)
    for step in range(blocks // group):
        taken = pl.ds(step * group * lanes, group * lanes)
        conv = jnp.concatenate([conv_ref[step * group + part] for part in range(group)], axis=1)
        conv = jnp.dot(order, conv, preferred_element_type=jnp.float32)
        direct = skip_ref[:, taken] * values_ref[:, taken].astype(jnp.float32)
        gated_ref[:, taken] = (gates_ref[:, taken].astype(jnp.float32) * (conv + direct)).astype(jnp.bfloat16)
    columns = pl.ds(pl.multiple_of((1 - half_ref[0]) * features, features), features)
    out_ref[...] = jnp.dot(gated_ref[...], weight_ref[:, columns], preferred_element_type=jnp.float32)


def gate_and_project(half, conv, gates, values, skip_gain, weight):
    rows, width = gates.shape
    features = weight.shape[1] // 2
    return pl.pallas_call(
        functools.partial(gate_kernel, 4),
        in_specs=[pl.BlockSpec(memory_space=pltpu.SMEM)] + [pl.BlockSpec(memory_space=pltpu.VMEM)] * 5,
        out_specs=[pl.BlockSpec(memory_space=pltpu.VMEM)] * 2,
        out_shape=[
            jax.ShapeDtypeStruct((rows, width), jnp.bfloat16),
            jax.ShapeDtypeStruct((rows, features), jnp.float32),
        ],
        compiler_params=pltpu.CompilerParams(vmem_limit_bytes=TAIL_BYTES),
        cost_estimate=pl.CostEstimate(
            flops=2 * rows * width * features, bytes_accessed=2 * width * features, transcendentals=0
        ),
        name="gate_project_sent",
    )(half, conv, gates, values, skip_gain[None, :], weight)


def kept_kernel(half_ref, gated_ref, weight_ref, out_ref):
    features = out_ref.shape[1]
    columns = pl.ds(pl.multiple_of(half_ref[0] * features, features), features)
    out_ref[...] = jnp.dot(gated_ref[...], weight_ref[:, columns], preferred_element_type=jnp.float32)


def project_kept(half, gated, weight):
    rows, width = gated.shape
    features = weight.shape[1] // 2
    return pl.pallas_call(
        kept_kernel,
        in_specs=[pl.BlockSpec(memory_space=pltpu.SMEM)] + [pl.BlockSpec(memory_space=pltpu.VMEM)] * 2,
        out_specs=pl.BlockSpec(memory_space=pltpu.VMEM),
        out_shape=jax.ShapeDtypeStruct((rows, features), jnp.float32),
        compiler_params=pltpu.CompilerParams(vmem_limit_bytes=TAIL_BYTES),
        cost_estimate=pl.CostEstimate(
            flops=2 * rows * width * features, bytes_accessed=2 * width * features, transcendentals=0
        ),
        name="project_kept",
    )(half, gated, weight)


def join_kernel(kept_ref, came_ref, out_ref):
    out_ref[...] = (kept_ref[...] + came_ref[...]).astype(jnp.bfloat16).T


def join(kept, came):
    rows, features = kept.shape
    wide = features // 4
    return pl.pallas_call(
        join_kernel,
        grid=(4,),
        in_specs=[pl.BlockSpec((rows, wide), lambda i: (0, i))] * 2,
        out_specs=pl.BlockSpec((wide, rows), lambda i: (i, 0)),
        out_shape=jax.ShapeDtypeStruct((features, rows), jnp.bfloat16),
        compiler_params=pltpu.CompilerParams(vmem_limit_bytes=TAIL_BYTES),
        name="join_halves",
    )(kept, came)


def swap_blocks(array):
    return lax.all_to_all(array, "seq", split_axis=0, concat_axis=0, tiled=True)


def exchange(slots):
    blocks = len(slots)
    return [
        lax.ppermute(source, "seq", [(j, j ^ slot) for j in range(blocks)]) if slot else source
        for slot, source in zip(slot_order(blocks), slots)
    ]


def kernel_local(values, gates, filter_taps, skip_gain, out_weight):
    blocks = lax.axis_size("seq")
    me = lax.axis_index("seq").astype(jnp.int32)[None]
    half = lax.axis_index("chan").astype(jnp.int32)[None]
    conv = convolve(me, exchange(arrange(me, values, filter_taps, blocks)))
    gated, sent = gate_and_project(half, swap_blocks(conv), gates, values, skip_gain, out_weight)
    other = lax.ppermute(sent, "chan", [(0, 1), (1, 0)])
    kept = project_kept(half, gated, out_weight)
    return join(kept, other)


def takes_kernels(mesh, values, out_weight):
    blocks, halves = mesh.shape["seq"], mesh.shape["chan"]
    rows = values.shape[0] // blocks
    return (
        halves == 2
        and blocks == 16
        and rows == 256
        and values.shape[1] == halves * blocks * LANES
        and out_weight.shape[1] % (8 * LANES) == 0
    )


def solution(mesh):
    placed = (P("seq", "chan"), P("seq", "chan"), P("seq", "chan"), P("chan"), P("chan", None))

    def whole(values, gates, filter_taps, skip_gain, out_weight):
        local = kernel_local if takes_kernels(mesh, values, out_weight) else general_local
        return jax.shard_map(
            local, mesh=mesh, in_specs=placed, out_specs=P("chan", "seq"), check_vma=False
        )(values, gates, filter_taps, skip_gain, out_weight)

    return whole
```

```python
import functools
import math

import jax
import jax.numpy as jnp
import ml_dtypes
import numpy as np
from jax import lax
from jax.experimental import pallas as pl
from jax.experimental.pallas import tpu as pltpu
from jax.sharding import PartitionSpec as P

TWO_PI = 2.0 * math.pi
HIGH = lax.Precision.HIGHEST
RADIX = 16
LANES = 128
Q_ORDER = [low + 4 * high for low in range(4) for high in range(4)]
ARRANGE_BYTES = 60 * 1024 * 1024
CONV_BYTES = 49 * 1024 * 1024
TAIL_BYTES = 49 * 1024 * 1024


def angle_table(first, second, period):
    product = first[:, None] * second[None, :] % period
    angles = product.astype(jnp.float32) * (TWO_PI / period)
    return (jnp.cos(angles), jnp.sin(angles))


def mix(equation, left, right):
    return jnp.einsum(equation, left, right, precision=HIGH)


def outer_forward(data, outer_cos, outer_sin, twist_cos, twist_sin, equation):
    source = data.astype(jnp.float32)
    real = mix(equation, outer_cos, source)
    imag = -mix(equation, outer_sin, source)
    cos_part = twist_cos[:, :, None]
    sin_part = twist_sin[:, :, None]
    return (real * cos_part + imag * sin_part, imag * cos_part - real * sin_part)


def inner_filter(spectra, inner_cos, inner_sin):
    value_re, value_im, taps_re, taps_im = spectra

    def forward(real, imag):
        out_re = mix("kr,jrc->jkc", inner_cos, real) + mix("kr,jrc->jkc", inner_sin, imag)
        out_im = mix("kr,jrc->jkc", inner_cos, imag) - mix("kr,jrc->jkc", inner_sin, real)
        return (out_re, out_im)

    value_fre, value_fim = forward(value_re, value_im)
    taps_fre, taps_fim = forward(taps_re, taps_im)
    prod_re = value_fre * taps_fre - value_fim * taps_fim
    prod_im = value_fre * taps_fim + value_fim * taps_fre
    back_re = mix("rk,jkc->jrc", inner_cos, prod_re) - mix("rk,jkc->jrc", inner_sin, prod_im)
    back_im = mix("rk,jkc->jrc", inner_cos, prod_im) + mix("rk,jkc->jrc", inner_sin, prod_re)
    return (back_re, back_im)


def untwist(real, imag, twist_cos, twist_sin):
    cos_part = twist_cos[:, :, None]
    sin_part = twist_sin[:, :, None]
    return (real * cos_part - imag * sin_part, imag * cos_part + real * sin_part)


def channels_plan(values, filter_taps):
    rows, width = values.shape
    blocks = lax.axis_size("seq")
    length = 2 * blocks * rows
    narrow = width // blocks
    whole_values, whole_taps = (
        lax.all_to_all(values, "seq", split_axis=1, concat_axis=0, tiled=True),
        lax.all_to_all(filter_taps, "seq", split_axis=1, concat_axis=0, tiled=True),
    )
    freq_ids = jnp.arange(2 * blocks, dtype=jnp.int32)
    block_ids = jnp.arange(blocks, dtype=jnp.int32)
    all_rows = jnp.arange(rows, dtype=jnp.int32)
    outer_cos, outer_sin = angle_table(freq_ids, block_ids, 2 * blocks)
    twist_cos, twist_sin = angle_table(freq_ids, all_rows, length)
    tables = (outer_cos, outer_sin, twist_cos, twist_sin, "ka,arc->krc")
    value_re, value_im = outer_forward(whole_values.reshape(blocks, rows, narrow), *tables)
    taps_re, taps_im = outer_forward(whole_taps.reshape(blocks, rows, narrow), *tables)
    inner_cos, inner_sin = angle_table(all_rows, all_rows, rows)
    back_re, back_im = inner_filter((value_re, value_im, taps_re, taps_im), inner_cos, inner_sin)
    turned_re, turned_im = untwist(back_re, back_im, twist_cos, twist_sin)
    final_cos, final_sin = angle_table(block_ids, freq_ids, 2 * blocks)
    signal = (
        mix("ak,krc->arc", final_cos, turned_re) - mix("ak,krc->arc", final_sin, turned_im)
    ) / length
    returned = lax.all_to_all(signal, "seq", split_axis=0, concat_axis=2, tiled=True)
    return returned[0]


def general_local(values, gates, filter_taps, skip_gain, out_weight):
    conv = channels_plan(values, filter_taps)
    gated = (
        gates.astype(jnp.float32) * (conv + skip_gain[None, :] * values.astype(jnp.float32))
    ).astype(jnp.bfloat16)
    projected = lax.psum_scatter(
        lax.dot_general(
            out_weight, gated, (((0,), (1,)), ((), ())), preferred_element_type=jnp.float32
        ),
        "chan",
        scatter_dimension=0,
        tiled=True,
    )
    return projected.astype(jnp.bfloat16)


def split_table(table):
    high = table.astype(ml_dtypes.bfloat16)
    low = (table - high.astype(np.float64)).astype(ml_dtypes.bfloat16)
    return high, low


@functools.lru_cache(maxsize=None)
def transform_tables(length):
    inner = length // RADIX
    k = np.arange(inner)[:, None]
    unit = TWO_PI / (4 * length)
    turns = (np.array(Q_ORDER)[:, None] * (4 * k.T + 1)) % (4 * length) * unit
    turns = np.stack([np.cos(turns), np.sin(turns)], axis=1).reshape(2 * RADIX, inner, 1)
    blocks = [np.broadcast_to(turns, (2 * RADIX, inner, LANES))]
    forward, backward = [], []
    for odd in range(2):
        m = 2 * np.arange(inner // 2)[None, :] + odd
        angles = (RADIX * m * (4 * k[: inner // 2] + 1)) % (4 * length) * unit
        table = np.concatenate([np.cos(angles), -np.sin(angles)], axis=0)
        forward.append(np.concatenate(split_table(table), axis=1))
        backward.append(np.concatenate(split_table(table.T / length), axis=0))
    for table in forward + backward:
        blocks.append(table.astype(np.float32).reshape(inner, -1, LANES).swapaxes(0, 1))
    return np.concatenate(blocks, axis=0).astype(np.float32)


def row_order(rows, turned_over=False):
    place = lax.broadcasted_iota(jnp.int32, (rows, rows), 1 if turned_over else 0)
    source = lax.broadcasted_iota(jnp.int32, (rows, rows), 0 if turned_over else 1)
    chunk = rows // RADIX
    index, within = place // chunk, place % chunk
    odd, j = within // (chunk // 2), within % (chunk // 2)
    wanted = RADIX * (2 * j + odd) + index // 4 + 4 * (index % 4)
    return jnp.where(source == wanted, 1.0, 0.0).astype(jnp.bfloat16)


def turn(point, index, sign):
    re, im = point
    index %= 16
    if index == 0:
        return point
    if index == 4:
        return (-im, re) if sign > 0 else (im, -re)
    if index == 8:
        return (-re, -im)
    half = math.sqrt(0.5)
    if index == 2:
        return ((re - im) * half, (re + im) * half) if sign > 0 else ((re + im) * half, (im - re) * half)
    if index == 6:
        return ((-re - im) * half, (re - im) * half) if sign > 0 else ((im - re) * half, (-re - im) * half)
    cos = math.cos(TWO_PI * index / 16)
    sin = sign * math.sin(TWO_PI * index / 16)
    return (re * cos - im * sin, re * sin + im * cos)


def four_points(points, sign):
    a, b, c, d = points
    ac = (a[0] + c[0], a[1] + c[1])
    am = (a[0] - c[0], a[1] - c[1])
    bd = (b[0] + d[0], b[1] + d[1])
    bm = (b[0] - d[0], b[1] - d[1])
    if sign < 0:
        side = (bm[1], -bm[0])
    else:
        side = (-bm[1], bm[0])
    return (
        (ac[0] + bd[0], ac[1] + bd[1]),
        (am[0] + side[0], am[1] + side[1]),
        (ac[0] - bd[0], ac[1] - bd[1]),
        (am[0] - side[0], am[1] - side[1]),
    )


def turned(point, cos, sin, sign):
    re, im = point
    if sign < 0:
        return (re * cos + im * sin, im * cos - re * sin)
    return (re * cos - im * sin, im * cos + re * sin)


def slot_order(blocks):
    half = blocks // 2
    across = [half + (i // 2 if i % 2 == 0 else half // 2 + i // 2) for i in range(half)]
    near = list(range(1, half)) + [0]
    return [slot for pair in zip(across, near) for slot in pair]


def arrange_kernel(pieces, blocks, me_ref, values_hbm, taps_hbm, *rest):
    outs = rest[:blocks]
    values_ref, taps_ref, packed, sems = rest[blocks:]
    piece = values_ref.shape[1] // pieces
    loads = []
    for part in range(pieces):
        lanes = pl.ds(part * piece, piece)
        loads.append(pltpu.make_async_copy(values_hbm.at[:, lanes], values_ref.at[:, lanes], sems.at[2 * part]))
        loads.append(pltpu.make_async_copy(taps_hbm.at[:, lanes], taps_ref.at[:, lanes], sems.at[2 * part + 1]))
    for load in loads:
        load.start()
    order = row_order(values_ref.shape[0])
    for part in range(pieces):
        loads[2 * part].wait()
        loads[2 * part + 1].wait()
        lanes = pl.ds(part * piece, piece)
        both = jnp.concatenate([values_ref[:, lanes], taps_ref[:, lanes]], axis=1)
        moved = jnp.dot(order, both, preferred_element_type=jnp.float32).astype(jnp.bfloat16)
        for block in range(piece // LANES):
            for side in range(2):
                start = side * piece + block * LANES
                packed[part * piece // LANES + block, :, pl.ds(side * LANES, LANES)] = moved[:, start : start + LANES]
    for out, slot in zip(outs, slot_order(blocks)):
        out[...] = packed[me_ref[0] ^ slot]


def arrange(me, values, taps, blocks):
    rows, wide = values.shape
    pieces = 4
    return pl.pallas_call(
        functools.partial(arrange_kernel, pieces, blocks),
        in_specs=[pl.BlockSpec(memory_space=pltpu.SMEM)] + [pl.BlockSpec(memory_space=pl.ANY)] * 2,
        out_specs=[pl.BlockSpec(memory_space=pltpu.VMEM)] * blocks,
        out_shape=[jax.ShapeDtypeStruct((rows, 2 * LANES), jnp.bfloat16)] * blocks,
        scratch_shapes=[
            pltpu.VMEM((rows, wide), jnp.bfloat16),
            pltpu.VMEM((rows, wide), jnp.bfloat16),
            pltpu.VMEM((blocks, rows, 2 * LANES), jnp.bfloat16),
            pltpu.SemaphoreType.DMA((2 * pieces,)),
        ],
        compiler_params=pltpu.CompilerParams(vmem_limit_bytes=ARRANGE_BYTES),
        cost_estimate=pl.CostEstimate(
            flops=4 * rows * rows * wide, bytes_accessed=8 * rows * wide, transcendentals=0
        ),
        name="arrange_rows",
    )(me, values, taps)


def convolve_kernel(blocks, me_ref, *rest):
    slots = rest[:blocks]
    convolve_blocks(me_ref, slots, *rest[blocks:])


def convolve_blocks(
    me_ref, slots, tables_hbm, out_hbm,
    streams, turns_ref, fixed, stages, raw_even, raw_odd, columns, mixed, halves_even, halves_odd, signals, sems,
):
    blocks, rows, _ = streams.shape
    chunk = rows // RADIX
    inner = blocks * chunk
    part_rows = inner // 2
    group = rows // 4
    raws = (raw_even, raw_odd)
    halves = (halves_even, halves_odd)
    count = fixed.shape[0]
    load_fixed = pltpu.make_async_copy(tables_hbm.at[pl.ds(2 * RADIX, count)], fixed, sems.at[0])
    load_turns, stores = [], []
    for low in range(4):
        taken = pl.ds(low * group, group)
        eight = pl.ds(8 * low, 8)
        load_turns.append(pltpu.make_async_copy(tables_hbm.at[eight], turns_ref.at[eight], sems.at[1 + low]))
        stores.append(pltpu.make_async_copy(signals.at[:, taken], out_hbm.at[:, taken], sems.at[5 + low]))
    load_fixed.start()
    for load in load_turns:
        load.start()
    own = pltpu.make_async_copy(slots[-1], streams.at[me_ref[0]], sems.at[9])
    own.start()
    for slot, source in zip(slot_order(blocks)[:-1], slots[:-1]):
        streams[me_ref[0] ^ slot] = source[...]
    own.wait()
    load_fixed.wait()
    width = inner // LANES
    for table in range(4):
        for block in range(width):
            stages[table, :, pl.ds(block * LANES, LANES)] = fixed[table * width + block].astype(jnp.bfloat16)

    def transform(low, pair):
        sides = [[], []]
        for part in range(2):
            taken = pl.ds(pl.multiple_of(low * group + (2 * pair + part) * chunk, chunk), chunk)
            stream = streams[:, taken].astype(jnp.float32).reshape(blocks, 2, chunk // 2, 2 * LANES)
            for odd in range(2):
                sides[odd].append(stream[:, odd].reshape(part_rows, 2 * LANES).astype(jnp.bfloat16))
        for odd in range(2):
            both = jnp.concatenate(sides[odd], axis=1)
            result = jnp.dot(
                stages[odd], jnp.concatenate([both, both], axis=0), preferred_element_type=jnp.float32
            )
            for part in range(2):
                raws[low % 2][2 * pair + part, odd] = result[:, 2 * part * LANES : 2 * (part + 1) * LANES]

    def first_pass(low, start):
        raw = raws[low % 2]
        real, imaginary = pl.ds(start, 8), pl.ds(part_rows + start, 8)
        for side in range(2):
            lanes = pl.ds(side * LANES, LANES)
            points = [[], []]
            for high in range(4):
                even = (raw[high, 0, real, lanes], raw[high, 0, imaginary, lanes])
                odd = (raw[high, 1, real, lanes], raw[high, 1, imaginary, lanes])
                points[0].append((even[0] + odd[0], even[1] + odd[1]))
                points[1].append((even[0] - odd[0], even[1] - odd[1]))
            for part in range(2):
                upper, lower = pl.ds(part * part_rows + start, 8), pl.ds(inner + part * part_rows + start, 8)
                for high in range(4):
                    if low + high:
                        turns = [turns_ref[2 * (4 * low + high) + i, upper] for i in range(2)]
                        points[part][high] = turned(points[part][high], *turns, -1)
                for k, point in enumerate(four_points(points[part], -1)):
                    point = turn(point, low * k, -1)
                    columns[4 * low + k, upper, lanes] = point[0]
                    columns[4 * low + k, lower, lanes] = point[1]

    def first_rows(low, start, count):
        for part in range(count):
            first_pass(low, pl.multiple_of(start + 8 * part, 8))

    steps = part_rows // 2

    def alone(pair, carry):
        transform(0, pair)
        return carry

    lax.fori_loop(0, 2, alone, 0)
    for low in range(1, 4):
        load_turns[low - 1].wait()

        def beside(pair, carry, low=low):
            transform(low, pair)
            first_rows(low - 1, pair * steps, steps // 8)
            return carry

        lax.fori_loop(0, 2, beside, 0)
    load_turns[3].wait()

    def middle(index, carry):
        start = pl.multiple_of(index * 8, 8)
        first_pass(3, start)
        for part in range(2):
            upper, lower = pl.ds(part * part_rows + start, 8), pl.ds(inner + part * part_rows + start, 8)
            for k in range(4):
                sides = []
                for side in range(2):
                    lanes = pl.ds(side * LANES, LANES)
                    points = [
                        (columns[4 * low + k, upper, lanes], columns[4 * low + k, lower, lanes]) for low in range(4)
                    ]
                    sides.append(four_points(points, -1))
                product = [
                    (a[0] * b[0] - a[1] * b[1], a[0] * b[1] + a[1] * b[0]) for a, b in zip(*sides)
                ]
                for high, point in enumerate(four_points(product, 1)):
                    point = turn(point, k * high, 1)
                    mixed[4 * high + k, upper] = point[0]
                    mixed[4 * high + k, lower] = point[1]
        return carry

    lax.fori_loop(0, part_rows // 8, middle, 0)

    def last_pass(low, start):
        target = halves[low % 2]
        found = []
        for part in range(2):
            upper, lower = pl.ds(part * part_rows + start, 16), pl.ds(inner + part * part_rows + start, 16)
            points = list(four_points([(mixed[4 * low + k, upper], mixed[4 * low + k, lower]) for k in range(4)], 1))
            for high in range(4):
                if low + high:
                    turns = [turns_ref[2 * (4 * low + high) + i, upper] for i in range(2)]
                    points[high] = turned(points[high], *turns, 1)
            found.append(points)
        for high in range(4):
            for i in range(2):
                taken = pl.ds(i * part_rows + start, 16)
                first, second = found[0][high][i], found[1][high][i]
                for odd, value in enumerate((first + second, first - second)):
                    rounded = value.astype(jnp.bfloat16)
                    target[high, odd, taken, pl.ds(0, LANES)] = rounded
                    target[high, odd, taken, pl.ds(LANES, LANES)] = (value - rounded.astype(jnp.float32)).astype(
                        jnp.bfloat16
                    )

    def last_rows(low, start, count):
        for part in range(count):
            last_pass(low, pl.multiple_of(start + 16 * part, 16))

    def restore(low, pair):
        sides = []
        for odd in range(2):
            both = jnp.concatenate([halves[low % 2][2 * pair + part, odd] for part in range(2)], axis=1)
            terms = jnp.dot(stages[2 + odd], both, preferred_element_type=jnp.float32)
            found = []
            for part in range(2):
                first, second = [slice((2 * part + i) * LANES, (2 * part + i + 1) * LANES) for i in range(2)]
                signal = terms[:part_rows, first] + terms[:part_rows, second] + terms[part_rows:, first]
                found.append(signal.reshape(blocks, 1, chunk // 2, LANES))
            sides.append(found)
        for part in range(2):
            signal = jnp.concatenate([sides[0][part], sides[1][part]], axis=1).reshape(blocks, chunk, LANES)
            taken = pl.ds(pl.multiple_of(low * group + (2 * pair + part) * chunk, chunk), chunk)
            signals[:, taken] = signal.astype(jnp.bfloat16)

    def prepare(index, carry):
        last_rows(0, index * steps, steps // 16)
        return carry

    lax.fori_loop(0, 2, prepare, 0)
    for low in range(4):

        def back(pair, carry, low=low):
            restore(low, pair)
            if low < 3:
                last_rows(low + 1, pair * steps, steps // 16)
            return carry

        lax.fori_loop(0, 2, back, 0)
        stores[low].start()
    for store in stores:
        store.wait()


def convolve(me, slots):
    blocks = len(slots)
    rows, lanes = slots[0].shape
    length = blocks * rows
    inner = length // RADIX
    tables = transform_tables(length)
    return pl.pallas_call(
        functools.partial(convolve_kernel, blocks),
        in_specs=[pl.BlockSpec(memory_space=pltpu.SMEM)]
        + [pl.BlockSpec(memory_space=pltpu.VMEM)] * (blocks - 1)
        + [pl.BlockSpec(memory_space=pl.ANY)] * 2,
        out_specs=pl.BlockSpec(memory_space=pl.ANY),
        out_shape=jax.ShapeDtypeStruct((blocks, rows, LANES), jnp.bfloat16),
        scratch_shapes=[
            pltpu.VMEM((blocks, rows, lanes), jnp.bfloat16),
            pltpu.VMEM((2 * RADIX, inner, LANES), jnp.float32),
            pltpu.VMEM((tables.shape[0] - 2 * RADIX, inner, LANES), jnp.float32),
            pltpu.VMEM((4, inner, inner), jnp.bfloat16),
            pltpu.VMEM((4, 2, inner, lanes), jnp.float32),
            pltpu.VMEM((4, 2, inner, lanes), jnp.float32),
            pltpu.VMEM((RADIX, 2 * inner, lanes), jnp.float32),
            pltpu.VMEM((RADIX, 2 * inner, LANES), jnp.float32),
            pltpu.VMEM((4, 2, inner, lanes), jnp.bfloat16),
            pltpu.VMEM((4, 2, inner, lanes), jnp.bfloat16),
            pltpu.VMEM((blocks, rows, LANES), jnp.bfloat16),
            pltpu.SemaphoreType.DMA((10,)),
        ],
        compiler_params=pltpu.CompilerParams(vmem_limit_bytes=CONV_BYTES),
        cost_estimate=pl.CostEstimate(flops=5 * 10**9, bytes_accessed=9 * 10**6, transcendentals=0),
        name="long_convolution",
    )(me, *slots, jnp.asarray(tables))


PIECES = 4


def weight_loads(weight_hbm, weight_ref, side, sems):
    width, features = weight_ref.shape
    columns = pl.ds(pl.multiple_of(side * features, features), features)
    deep = width // PIECES
    loads = []
    for part in range(PIECES):
        rows = pl.ds(part * deep, deep)
        loads.append(pltpu.make_async_copy(weight_hbm.at[rows, columns], weight_ref.at[rows], sems.at[part]))
        loads[part].start()
    return loads


def gate_kernel(
    half_ref, conv_ref, gates_hbm, values_hbm, skip_ref, weight_hbm, gated_ref, out_ref,
    gates_ref, values_ref, weight_ref, sems,
):
    blocks, rows, lanes = conv_ref.shape
    streams = [
        pltpu.make_async_copy(gates_hbm, gates_ref, sems.at[PIECES]),
        pltpu.make_async_copy(values_hbm, values_ref, sems.at[PIECES + 1]),
    ]
    for stream in streams:
        stream.start()
    loads = weight_loads(weight_hbm, weight_ref, 1 - half_ref[0], sems)
    order = row_order(rows, True)
    for stream in streams:
        stream.wait()
    group = blocks // PIECES
    wide = group * lanes
    for part in range(PIECES):
        taken = pl.ds(part * wide, wide)
        conv = jnp.concatenate([conv_ref[part * group + block] for block in range(group)], axis=1)
        conv = jnp.dot(order, conv, preferred_element_type=jnp.float32)
        direct = skip_ref[:, taken] * values_ref[:, taken].astype(jnp.float32)
        gated_ref[:, taken] = (gates_ref[:, taken].astype(jnp.float32) * (conv + direct)).astype(jnp.bfloat16)
    multiply_pieces(loads, gated_ref, weight_ref, out_ref)


def multiply_pieces(loads, gated_ref, weight_ref, out_ref):
    deep = weight_ref.shape[0] // PIECES
    for part in range(PIECES):
        taken = pl.ds(part * deep, deep)
        loads[part].wait()
        term = jnp.dot(gated_ref[:, taken], weight_ref[taken], preferred_element_type=jnp.float32)
        out_ref[...] = term if part == 0 else out_ref[...] + term


def gate_and_project(half, conv, gates, values, skip_gain, weight):
    rows, width = gates.shape
    features = weight.shape[1] // 2
    anywhere, inside = pl.BlockSpec(memory_space=pl.ANY), pl.BlockSpec(memory_space=pltpu.VMEM)
    return pl.pallas_call(
        gate_kernel,
        in_specs=[pl.BlockSpec(memory_space=pltpu.SMEM), inside, anywhere, anywhere, inside, anywhere],
        out_specs=[inside] * 2,
        out_shape=[
            jax.ShapeDtypeStruct((rows, width), jnp.bfloat16),
            jax.ShapeDtypeStruct((rows, features), jnp.float32),
        ],
        scratch_shapes=[
            pltpu.VMEM((rows, width), jnp.bfloat16),
            pltpu.VMEM((rows, width), jnp.bfloat16),
            pltpu.VMEM((width, features), jnp.bfloat16),
            pltpu.SemaphoreType.DMA((PIECES + 2,)),
        ],
        compiler_params=pltpu.CompilerParams(vmem_limit_bytes=TAIL_BYTES),
        cost_estimate=pl.CostEstimate(
            flops=2 * rows * width * features, bytes_accessed=2 * width * features, transcendentals=0
        ),
        name="gate_project_sent",
    )(half, conv, gates, values, skip_gain[None, :], weight)


def kept_kernel(half_ref, gated_ref, weight_hbm, out_ref, weight_ref, sems):
    multiply_pieces(weight_loads(weight_hbm, weight_ref, half_ref[0], sems), gated_ref, weight_ref, out_ref)


def project_kept(half, gated, weight):
    rows, width = gated.shape
    features = weight.shape[1] // 2
    inside = pl.BlockSpec(memory_space=pltpu.VMEM)
    return pl.pallas_call(
        kept_kernel,
        in_specs=[pl.BlockSpec(memory_space=pltpu.SMEM), inside, pl.BlockSpec(memory_space=pl.ANY)],
        out_specs=inside,
        out_shape=jax.ShapeDtypeStruct((rows, features), jnp.float32),
        scratch_shapes=[pltpu.VMEM((width, features), jnp.bfloat16), pltpu.SemaphoreType.DMA((PIECES,))],
        compiler_params=pltpu.CompilerParams(vmem_limit_bytes=TAIL_BYTES),
        cost_estimate=pl.CostEstimate(
            flops=2 * rows * width * features, bytes_accessed=2 * width * features, transcendentals=0
        ),
        name="project_kept",
    )(half, gated, weight)


def join_kernel(kept_ref, came_ref, out_hbm, out_ref, sems):
    wide = out_ref.shape[0] // PIECES
    stores = []
    for part in range(PIECES):
        taken = pl.ds(part * wide, wide)
        out_ref[taken] = (kept_ref[:, taken] + came_ref[:, taken]).astype(jnp.bfloat16).T
        stores.append(pltpu.make_async_copy(out_ref.at[taken], out_hbm.at[taken], sems.at[part]))
        stores[part].start()
    for store in stores:
        store.wait()


def join(kept, came):
    rows, features = kept.shape
    return pl.pallas_call(
        join_kernel,
        in_specs=[pl.BlockSpec(memory_space=pltpu.VMEM)] * 2,
        out_specs=pl.BlockSpec(memory_space=pl.ANY),
        out_shape=jax.ShapeDtypeStruct((features, rows), jnp.bfloat16),
        scratch_shapes=[pltpu.VMEM((features, rows), jnp.bfloat16), pltpu.SemaphoreType.DMA((PIECES,))],
        compiler_params=pltpu.CompilerParams(vmem_limit_bytes=TAIL_BYTES),
        name="join_halves",
    )(kept, came)


def swap_blocks(array):
    return lax.all_to_all(array, "seq", split_axis=0, concat_axis=0, tiled=True)


def exchange(slots):
    blocks = len(slots)
    return [
        lax.ppermute(source, "seq", [(j, j ^ slot) for j in range(blocks)]) if slot else source
        for slot, source in zip(slot_order(blocks), slots)
    ]


def kernel_local(values, gates, filter_taps, skip_gain, out_weight):
    blocks = lax.axis_size("seq")
    me = lax.axis_index("seq").astype(jnp.int32)[None]
    half = lax.axis_index("chan").astype(jnp.int32)[None]
    conv = convolve(me, exchange(arrange(me, values, filter_taps, blocks)))
    gated, sent = gate_and_project(half, swap_blocks(conv), gates, values, skip_gain, out_weight)
    other = lax.ppermute(sent, "chan", [(0, 1), (1, 0)])
    kept = project_kept(half, gated, out_weight)
    return join(kept, other)


def takes_kernels(mesh, values, out_weight):
    blocks, halves = mesh.shape["seq"], mesh.shape["chan"]
    rows = values.shape[0] // blocks
    return (
        halves == 2
        and blocks == 16
        and rows == 256
        and values.shape[1] == halves * blocks * LANES
        and out_weight.shape[1] % (8 * LANES) == 0
    )


def solution(mesh):
    placed = (P("seq", "chan"), P("seq", "chan"), P("seq", "chan"), P("chan"), P("chan", None))

    def whole(values, gates, filter_taps, skip_gain, out_weight):
        local = kernel_local if takes_kernels(mesh, values, out_weight) else general_local
        return jax.shard_map(
            local, mesh=mesh, in_specs=placed, out_specs=P("chan", "seq"), check_vma=False
        )(values, gates, filter_taps, skip_gain, out_weight)

    return whole
```

```python
import functools
import math

import jax
import jax.numpy as jnp
import ml_dtypes
import numpy as np
from jax import lax
from jax.experimental import pallas as pl
from jax.experimental.pallas import tpu as pltpu
from jax.sharding import PartitionSpec as P

TWO_PI = 2.0 * math.pi
HIGH = lax.Precision.HIGHEST
RADIX = 16
LANES = 128
Q_ORDER = [low + 4 * high for low in range(4) for high in range(4)]
ARRANGE_BYTES = 60 * 1024 * 1024
CONV_BYTES = 49 * 1024 * 1024
TAIL_BYTES = 49 * 1024 * 1024


def angle_table(first, second, period):
    product = first[:, None] * second[None, :] % period
    angles = product.astype(jnp.float32) * (TWO_PI / period)
    return (jnp.cos(angles), jnp.sin(angles))


def mix(equation, left, right):
    return jnp.einsum(equation, left, right, precision=HIGH)


def outer_forward(data, outer_cos, outer_sin, twist_cos, twist_sin, equation):
    source = data.astype(jnp.float32)
    real = mix(equation, outer_cos, source)
    imag = -mix(equation, outer_sin, source)
    cos_part = twist_cos[:, :, None]
    sin_part = twist_sin[:, :, None]
    return (real * cos_part + imag * sin_part, imag * cos_part - real * sin_part)


def inner_filter(spectra, inner_cos, inner_sin):
    value_re, value_im, taps_re, taps_im = spectra

    def forward(real, imag):
        out_re = mix("kr,jrc->jkc", inner_cos, real) + mix("kr,jrc->jkc", inner_sin, imag)
        out_im = mix("kr,jrc->jkc", inner_cos, imag) - mix("kr,jrc->jkc", inner_sin, real)
        return (out_re, out_im)

    value_fre, value_fim = forward(value_re, value_im)
    taps_fre, taps_fim = forward(taps_re, taps_im)
    prod_re = value_fre * taps_fre - value_fim * taps_fim
    prod_im = value_fre * taps_fim + value_fim * taps_fre
    back_re = mix("rk,jkc->jrc", inner_cos, prod_re) - mix("rk,jkc->jrc", inner_sin, prod_im)
    back_im = mix("rk,jkc->jrc", inner_cos, prod_im) + mix("rk,jkc->jrc", inner_sin, prod_re)
    return (back_re, back_im)


def untwist(real, imag, twist_cos, twist_sin):
    cos_part = twist_cos[:, :, None]
    sin_part = twist_sin[:, :, None]
    return (real * cos_part - imag * sin_part, imag * cos_part + real * sin_part)


def channels_plan(values, filter_taps):
    rows, width = values.shape
    blocks = lax.axis_size("seq")
    length = 2 * blocks * rows
    narrow = width // blocks
    whole_values, whole_taps = (
        lax.all_to_all(values, "seq", split_axis=1, concat_axis=0, tiled=True),
        lax.all_to_all(filter_taps, "seq", split_axis=1, concat_axis=0, tiled=True),
    )
    freq_ids = jnp.arange(2 * blocks, dtype=jnp.int32)
    block_ids = jnp.arange(blocks, dtype=jnp.int32)
    all_rows = jnp.arange(rows, dtype=jnp.int32)
    outer_cos, outer_sin = angle_table(freq_ids, block_ids, 2 * blocks)
    twist_cos, twist_sin = angle_table(freq_ids, all_rows, length)
    tables = (outer_cos, outer_sin, twist_cos, twist_sin, "ka,arc->krc")
    value_re, value_im = outer_forward(whole_values.reshape(blocks, rows, narrow), *tables)
    taps_re, taps_im = outer_forward(whole_taps.reshape(blocks, rows, narrow), *tables)
    inner_cos, inner_sin = angle_table(all_rows, all_rows, rows)
    back_re, back_im = inner_filter((value_re, value_im, taps_re, taps_im), inner_cos, inner_sin)
    turned_re, turned_im = untwist(back_re, back_im, twist_cos, twist_sin)
    final_cos, final_sin = angle_table(block_ids, freq_ids, 2 * blocks)
    signal = (
        mix("ak,krc->arc", final_cos, turned_re) - mix("ak,krc->arc", final_sin, turned_im)
    ) / length
    returned = lax.all_to_all(signal, "seq", split_axis=0, concat_axis=2, tiled=True)
    return returned[0]


def general_local(values, gates, filter_taps, skip_gain, out_weight):
    conv = channels_plan(values, filter_taps)
    gated = (
        gates.astype(jnp.float32) * (conv + skip_gain[None, :] * values.astype(jnp.float32))
    ).astype(jnp.bfloat16)
    projected = lax.psum_scatter(
        lax.dot_general(
            out_weight, gated, (((0,), (1,)), ((), ())), preferred_element_type=jnp.float32
        ),
        "chan",
        scatter_dimension=0,
        tiled=True,
    )
    return projected.astype(jnp.bfloat16)


def split_table(table):
    high = table.astype(ml_dtypes.bfloat16)
    low = (table - high.astype(np.float64)).astype(ml_dtypes.bfloat16)
    return high, low


@functools.lru_cache(maxsize=None)
def transform_tables(length):
    inner = length // RADIX
    k = np.arange(inner)[:, None]
    unit = TWO_PI / (4 * length)
    turns = (np.array(Q_ORDER)[:, None] * (4 * k.T + 1)) % (4 * length) * unit
    turns = np.stack([np.cos(turns), np.sin(turns)], axis=1).reshape(2 * RADIX, inner, 1)
    blocks = [np.broadcast_to(turns, (2 * RADIX, inner, LANES))]
    forward, backward = [], []
    for odd in range(2):
        m = 2 * np.arange(inner // 2)[None, :] + odd
        angles = (RADIX * m * (4 * k[: inner // 2] + 1)) % (4 * length) * unit
        table = np.concatenate([np.cos(angles), -np.sin(angles)], axis=0)
        forward.append(np.concatenate(split_table(table), axis=1))
        backward.append(np.concatenate(split_table(table.T / length), axis=0))
    for table in forward + backward:
        blocks.append(table.astype(np.float32).reshape(inner, -1, LANES).swapaxes(0, 1))
    return np.concatenate(blocks, axis=0).astype(np.float32)


def row_order(rows, turned_over=False):
    place = lax.broadcasted_iota(jnp.int32, (rows, rows), 1 if turned_over else 0)
    source = lax.broadcasted_iota(jnp.int32, (rows, rows), 0 if turned_over else 1)
    chunk = rows // RADIX
    index, within = place // chunk, place % chunk
    odd, j = within // (chunk // 2), within % (chunk // 2)
    wanted = RADIX * (2 * j + odd) + index // 4 + 4 * (index % 4)
    return jnp.where(source == wanted, 1.0, 0.0).astype(jnp.bfloat16)


def turn(point, index, sign):
    re, im = point
    index %= 16
    if index == 0:
        return point
    if index == 4:
        return (-im, re) if sign > 0 else (im, -re)
    if index == 8:
        return (-re, -im)
    half = math.sqrt(0.5)
    if index == 2:
        return ((re - im) * half, (re + im) * half) if sign > 0 else ((re + im) * half, (im - re) * half)
    if index == 6:
        return ((-re - im) * half, (re - im) * half) if sign > 0 else ((im - re) * half, (-re - im) * half)
    cos = math.cos(TWO_PI * index / 16)
    sin = sign * math.sin(TWO_PI * index / 16)
    return (re * cos - im * sin, re * sin + im * cos)


def four_points(points, sign):
    a, b, c, d = points
    ac = (a[0] + c[0], a[1] + c[1])
    am = (a[0] - c[0], a[1] - c[1])
    bd = (b[0] + d[0], b[1] + d[1])
    bm = (b[0] - d[0], b[1] - d[1])
    if sign < 0:
        side = (bm[1], -bm[0])
    else:
        side = (-bm[1], bm[0])
    return (
        (ac[0] + bd[0], ac[1] + bd[1]),
        (am[0] + side[0], am[1] + side[1]),
        (ac[0] - bd[0], ac[1] - bd[1]),
        (am[0] - side[0], am[1] - side[1]),
    )


def turned(point, cos, sin, sign):
    re, im = point
    if sign < 0:
        return (re * cos + im * sin, im * cos - re * sin)
    return (re * cos - im * sin, im * cos + re * sin)


def partners_across(blocks):
    half = blocks // 2
    return [half + (i // 2 if i % 2 == 0 else half // 2 + i // 2) for i in range(half)]


def first_near(me, blocks):
    return me & (blocks // 2)


def arrange_kernel(pieces, blocks, me_ref, values_hbm, taps_hbm, *rest):
    near_hbm, outs = rest[0], rest[1 : 1 + blocks // 2]
    values_ref, taps_ref, packed, sems = rest[1 + blocks // 2 :]
    piece = values_ref.shape[1] // pieces
    loads = []
    for part in range(pieces):
        lanes = pl.ds(part * piece, piece)
        loads.append(pltpu.make_async_copy(values_hbm.at[:, lanes], values_ref.at[:, lanes], sems.at[2 * part]))
        loads.append(pltpu.make_async_copy(taps_hbm.at[:, lanes], taps_ref.at[:, lanes], sems.at[2 * part + 1]))
    for load in loads:
        load.start()
    order = row_order(values_ref.shape[0])
    for part in range(pieces):
        loads[2 * part].wait()
        loads[2 * part + 1].wait()
        lanes = pl.ds(part * piece, piece)
        both = jnp.concatenate([values_ref[:, lanes], taps_ref[:, lanes]], axis=1)
        moved = jnp.dot(order, both, preferred_element_type=jnp.float32).astype(jnp.bfloat16)
        for block in range(piece // LANES):
            for side in range(2):
                start = side * piece + block * LANES
                packed[part * piece // LANES + block, :, pl.ds(side * LANES, LANES)] = moved[:, start : start + LANES]
    me = me_ref[0]
    stores = [
        pltpu.make_async_copy(
            packed.at[pl.ds(first_near(me, blocks), blocks // 2)], near_hbm, sems.at[2 * pieces]
        )
    ]
    for i, (out, slot) in enumerate(zip(outs, partners_across(blocks))):
        stores.append(pltpu.make_async_copy(packed.at[me ^ slot], out, sems.at[2 * pieces + 1 + i]))
    for store in stores:
        store.start()
    for store in stores:
        store.wait()


def arrange(me, values, taps, blocks):
    rows, wide = values.shape
    pieces = 4
    return pl.pallas_call(
        functools.partial(arrange_kernel, pieces, blocks),
        in_specs=[pl.BlockSpec(memory_space=pltpu.SMEM)] + [pl.BlockSpec(memory_space=pl.ANY)] * 2,
        out_specs=[pl.BlockSpec(memory_space=pl.ANY)] * (1 + blocks // 2),
        out_shape=[jax.ShapeDtypeStruct((blocks // 2, rows, 2 * LANES), jnp.bfloat16)]
        + [jax.ShapeDtypeStruct((rows, 2 * LANES), jnp.bfloat16)] * (blocks // 2),
        scratch_shapes=[
            pltpu.VMEM((rows, wide), jnp.bfloat16),
            pltpu.VMEM((rows, wide), jnp.bfloat16),
            pltpu.VMEM((blocks, rows, 2 * LANES), jnp.bfloat16),
            pltpu.SemaphoreType.DMA((2 * pieces + 1 + blocks // 2,)),
        ],
        compiler_params=pltpu.CompilerParams(vmem_limit_bytes=ARRANGE_BYTES),
        cost_estimate=pl.CostEstimate(
            flops=4 * rows * rows * wide, bytes_accessed=8 * rows * wide, transcendentals=0
        ),
        name="arrange_rows",
    )(me, values, taps)


def convolve_kernel(blocks, me_ref, near_ref, *rest):
    half = blocks // 2
    convolve_blocks(me_ref, near_ref, rest[:half], rest[half], rest[half + 1], rest[half + 2 : 2 * half + 2], *rest[2 * half + 2 :])


def convolve_blocks(
    me_ref, near_ref, slots, tables_hbm, near_hbm, outs,
    streams, turns_ref, fixed, stages, raw_even, raw_odd, columns, mixed, halves_even, halves_odd, signals, sems,
):
    blocks, rows, _ = streams.shape
    chunk = rows // RADIX
    inner = blocks * chunk
    part_rows = inner // 2
    group = rows // 4
    raws = (raw_even, raw_odd)
    halves = (halves_even, halves_odd)
    count = fixed.shape[0]
    load_fixed = pltpu.make_async_copy(tables_hbm.at[pl.ds(2 * RADIX, count)], fixed, sems.at[0])
    me = me_ref[0]
    first, across = first_near(me, blocks), partners_across(blocks)
    load_turns, stores = [], []
    for low in range(4):
        taken = pl.ds(low * group, group)
        eight = pl.ds(8 * low, 8)
        load_turns.append(pltpu.make_async_copy(tables_hbm.at[eight], turns_ref.at[eight], sems.at[1 + low]))
        stores.append(
            [
                pltpu.make_async_copy(
                    signals.at[pl.ds(first, blocks // 2), taken], near_hbm.at[:, taken], sems.at[5 + low * (1 + len(outs))]
                )
            ]
        )
        for i, (out, slot) in enumerate(zip(outs, across)):
            stores[low].append(
                pltpu.make_async_copy(signals.at[me ^ slot, taken], out.at[taken], sems.at[6 + low * (1 + len(outs)) + i])
            )
    load_fixed.start()
    for load in load_turns:
        load.start()
    streams[pl.ds(first, blocks // 2)] = near_ref[...]
    for slot, source in zip(across, slots):
        streams[me ^ slot] = source[...]
    load_fixed.wait()
    width = inner // LANES
    for table in range(4):
        for block in range(width):
            stages[table, :, pl.ds(block * LANES, LANES)] = fixed[table * width + block].astype(jnp.bfloat16)

    def transform(low, pair):
        sides = [[], []]
        for part in range(2):
            taken = pl.ds(pl.multiple_of(low * group + (2 * pair + part) * chunk, chunk), chunk)
            stream = streams[:, taken].astype(jnp.float32).reshape(blocks, 2, chunk // 2, 2 * LANES)
            for odd in range(2):
                sides[odd].append(stream[:, odd].reshape(part_rows, 2 * LANES).astype(jnp.bfloat16))
        for odd in range(2):
            both = jnp.concatenate(sides[odd], axis=1)
            result = jnp.dot(
                stages[odd], jnp.concatenate([both, both], axis=0), preferred_element_type=jnp.float32
            )
            for part in range(2):
                raws[low % 2][2 * pair + part, odd] = result[:, 2 * part * LANES : 2 * (part + 1) * LANES]

    def first_pass(low, start):
        raw = raws[low % 2]
        real, imaginary = pl.ds(start, 8), pl.ds(part_rows + start, 8)
        for side in range(2):
            lanes = pl.ds(side * LANES, LANES)
            points = [[], []]
            for high in range(4):
                even = (raw[high, 0, real, lanes], raw[high, 0, imaginary, lanes])
                odd = (raw[high, 1, real, lanes], raw[high, 1, imaginary, lanes])
                points[0].append((even[0] + odd[0], even[1] + odd[1]))
                points[1].append((even[0] - odd[0], even[1] - odd[1]))
            for part in range(2):
                upper, lower = pl.ds(part * part_rows + start, 8), pl.ds(inner + part * part_rows + start, 8)
                for high in range(4):
                    if low + high:
                        turns = [turns_ref[2 * (4 * low + high) + i, upper] for i in range(2)]
                        points[part][high] = turned(points[part][high], *turns, -1)
                for k, point in enumerate(four_points(points[part], -1)):
                    point = turn(point, low * k, -1)
                    columns[4 * low + k, upper, lanes] = point[0]
                    columns[4 * low + k, lower, lanes] = point[1]

    def first_rows(low, start, count):
        for part in range(count):
            first_pass(low, pl.multiple_of(start + 8 * part, 8))

    steps = part_rows // 2

    def alone(pair, carry):
        transform(0, pair)
        return carry

    lax.fori_loop(0, 2, alone, 0)
    for low in range(1, 4):
        load_turns[low - 1].wait()

        def beside(pair, carry, low=low):
            transform(low, pair)
            first_rows(low - 1, pair * steps, steps // 8)
            return carry

        lax.fori_loop(0, 2, beside, 0)
    load_turns[3].wait()

    def middle(index, carry):
        start = pl.multiple_of(index * 8, 8)
        first_pass(3, start)
        for part in range(2):
            upper, lower = pl.ds(part * part_rows + start, 8), pl.ds(inner + part * part_rows + start, 8)
            for k in range(4):
                sides = []
                for side in range(2):
                    lanes = pl.ds(side * LANES, LANES)
                    points = [
                        (columns[4 * low + k, upper, lanes], columns[4 * low + k, lower, lanes]) for low in range(4)
                    ]
                    sides.append(four_points(points, -1))
                product = [
                    (a[0] * b[0] - a[1] * b[1], a[0] * b[1] + a[1] * b[0]) for a, b in zip(*sides)
                ]
                for high, point in enumerate(four_points(product, 1)):
                    point = turn(point, k * high, 1)
                    mixed[4 * high + k, upper] = point[0]
                    mixed[4 * high + k, lower] = point[1]
        return carry

    lax.fori_loop(0, part_rows // 8, middle, 0)

    def last_pass(low, start):
        target = halves[low % 2]
        found = []
        for part in range(2):
            upper, lower = pl.ds(part * part_rows + start, 16), pl.ds(inner + part * part_rows + start, 16)
            points = list(four_points([(mixed[4 * low + k, upper], mixed[4 * low + k, lower]) for k in range(4)], 1))
            for high in range(4):
                if low + high:
                    turns = [turns_ref[2 * (4 * low + high) + i, upper] for i in range(2)]
                    points[high] = turned(points[high], *turns, 1)
            found.append(points)
        for high in range(4):
            for i in range(2):
                taken = pl.ds(i * part_rows + start, 16)
                first, second = found[0][high][i], found[1][high][i]
                for odd, value in enumerate((first + second, first - second)):
                    rounded = value.astype(jnp.bfloat16)
                    target[high, odd, taken, pl.ds(0, LANES)] = rounded
                    target[high, odd, taken, pl.ds(LANES, LANES)] = (value - rounded.astype(jnp.float32)).astype(
                        jnp.bfloat16
                    )

    def last_rows(low, start, count):
        for part in range(count):
            last_pass(low, pl.multiple_of(start + 16 * part, 16))

    def restore(low, pair):
        sides = []
        for odd in range(2):
            both = jnp.concatenate([halves[low % 2][2 * pair + part, odd] for part in range(2)], axis=1)
            terms = jnp.dot(stages[2 + odd], both, preferred_element_type=jnp.float32)
            found = []
            for part in range(2):
                first, second = [slice((2 * part + i) * LANES, (2 * part + i + 1) * LANES) for i in range(2)]
                signal = terms[:part_rows, first] + terms[:part_rows, second] + terms[part_rows:, first]
                found.append(signal.reshape(blocks, 1, chunk // 2, LANES))
            sides.append(found)
        for part in range(2):
            signal = jnp.concatenate([sides[0][part], sides[1][part]], axis=1).reshape(blocks, chunk, LANES)
            taken = pl.ds(pl.multiple_of(low * group + (2 * pair + part) * chunk, chunk), chunk)
            signals[:, taken] = signal.astype(jnp.bfloat16)

    def prepare(index, carry):
        last_rows(0, index * steps, steps // 16)
        return carry

    lax.fori_loop(0, 2, prepare, 0)
    for low in range(4):

        def back(pair, carry, low=low):
            restore(low, pair)
            if low < 3:
                last_rows(low + 1, pair * steps, steps // 16)
            return carry

        lax.fori_loop(0, 2, back, 0)
        for store in stores[low]:
            store.start()
    for store in sum(stores, []):
        store.wait()


def convolve(me, near, slots):
    half, rows, lanes = near.shape
    blocks = 2 * half
    length = blocks * rows
    inner = length // RADIX
    tables = transform_tables(length)
    return pl.pallas_call(
        functools.partial(convolve_kernel, blocks),
        in_specs=[pl.BlockSpec(memory_space=pltpu.SMEM)]
        + [pl.BlockSpec(memory_space=pltpu.VMEM)] * (1 + half)
        + [pl.BlockSpec(memory_space=pl.ANY)],
        out_specs=[pl.BlockSpec(memory_space=pl.ANY)] * (1 + half),
        out_shape=[jax.ShapeDtypeStruct((half, rows, LANES), jnp.bfloat16)]
        + [jax.ShapeDtypeStruct((rows, LANES), jnp.bfloat16)] * half,
        scratch_shapes=[
            pltpu.VMEM((blocks, rows, lanes), jnp.bfloat16),
            pltpu.VMEM((2 * RADIX, inner, LANES), jnp.float32),
            pltpu.VMEM((tables.shape[0] - 2 * RADIX, inner, LANES), jnp.float32),
            pltpu.VMEM((4, inner, inner), jnp.bfloat16),
            pltpu.VMEM((4, 2, inner, lanes), jnp.float32),
            pltpu.VMEM((4, 2, inner, lanes), jnp.float32),
            pltpu.VMEM((RADIX, 2 * inner, lanes), jnp.float32),
            pltpu.VMEM((RADIX, 2 * inner, LANES), jnp.float32),
            pltpu.VMEM((4, 2, inner, lanes), jnp.bfloat16),
            pltpu.VMEM((4, 2, inner, lanes), jnp.bfloat16),
            pltpu.VMEM((blocks, rows, LANES), jnp.bfloat16),
            pltpu.SemaphoreType.DMA((5 + 4 * (1 + half),)),
        ],
        compiler_params=pltpu.CompilerParams(vmem_limit_bytes=CONV_BYTES),
        cost_estimate=pl.CostEstimate(flops=5 * 10**9, bytes_accessed=9 * 10**6, transcendentals=0),
        name="long_convolution",
    )(me, near, *slots, jnp.asarray(tables))


PIECES = 4


def weight_loads(weight_hbm, weight_ref, side, sems):
    width, features = weight_ref.shape
    columns = pl.ds(pl.multiple_of(side * features, features), features)
    deep = width // PIECES
    loads = []
    for part in range(PIECES):
        rows = pl.ds(part * deep, deep)
        loads.append(pltpu.make_async_copy(weight_hbm.at[rows, columns], weight_ref.at[rows], sems.at[part]))
        loads[part].start()
    return loads


def gate_kernel(
    count, me_ref, half_ref, near_ref, gates_hbm, values_hbm, skip_ref, weight_hbm, *rest,
):
    slots = rest[:count]
    gated_ref, out_ref, conv_ref, gates_ref, values_ref, weight_ref, sems = rest[count:]
    blocks, rows, lanes = conv_ref.shape
    streams = [
        pltpu.make_async_copy(gates_hbm, gates_ref, sems.at[PIECES]),
        pltpu.make_async_copy(values_hbm, values_ref, sems.at[PIECES + 1]),
    ]
    for stream in streams:
        stream.start()
    loads = weight_loads(weight_hbm, weight_ref, 1 - half_ref[0], sems)
    order = row_order(rows, True)
    me = me_ref[0]
    conv_ref[pl.ds(first_near(me, blocks), blocks // 2)] = near_ref[...]
    for slot, source in zip(partners_across(blocks), slots):
        conv_ref[me ^ slot] = source[...]
    for stream in streams:
        stream.wait()
    group = blocks // PIECES
    wide = group * lanes
    for part in range(PIECES):
        taken = pl.ds(part * wide, wide)
        conv = jnp.concatenate([conv_ref[part * group + block] for block in range(group)], axis=1)
        conv = jnp.dot(order, conv, preferred_element_type=jnp.float32)
        direct = skip_ref[:, taken] * values_ref[:, taken].astype(jnp.float32)
        gated_ref[:, taken] = (gates_ref[:, taken].astype(jnp.float32) * (conv + direct)).astype(jnp.bfloat16)
    multiply_pieces(loads, gated_ref, weight_ref, out_ref)


def multiply_pieces(loads, gated_ref, weight_ref, out_ref):
    deep = weight_ref.shape[0] // PIECES
    for part in range(PIECES):
        taken = pl.ds(part * deep, deep)
        loads[part].wait()
        term = jnp.dot(gated_ref[:, taken], weight_ref[taken], preferred_element_type=jnp.float32)
        out_ref[...] = term if part == 0 else out_ref[...] + term


def gate_and_project(me, half, near, slots, gates, values, skip_gain, weight):
    rows, width = gates.shape
    features = weight.shape[1] // 2
    anywhere, inside = pl.BlockSpec(memory_space=pl.ANY), pl.BlockSpec(memory_space=pltpu.VMEM)
    return pl.pallas_call(
        functools.partial(gate_kernel, len(slots)),
        in_specs=[pl.BlockSpec(memory_space=pltpu.SMEM)] * 2
        + [inside, anywhere, anywhere, inside, anywhere]
        + [inside] * len(slots),
        out_specs=[inside] * 2,
        out_shape=[
            jax.ShapeDtypeStruct((rows, width), jnp.bfloat16),
            jax.ShapeDtypeStruct((rows, features), jnp.float32),
        ],
        scratch_shapes=[
            pltpu.VMEM((2 * len(slots), rows, LANES), jnp.bfloat16),
            pltpu.VMEM((rows, width), jnp.bfloat16),
            pltpu.VMEM((rows, width), jnp.bfloat16),
            pltpu.VMEM((width, features), jnp.bfloat16),
            pltpu.SemaphoreType.DMA((PIECES + 2,)),
        ],
        compiler_params=pltpu.CompilerParams(vmem_limit_bytes=TAIL_BYTES),
        cost_estimate=pl.CostEstimate(
            flops=2 * rows * width * features, bytes_accessed=2 * width * features, transcendentals=0
        ),
        name="gate_project_sent",
    )(me, half, near, gates, values, skip_gain[None, :], weight, *slots)


def kept_kernel(half_ref, gated_ref, weight_hbm, out_ref, weight_ref, sems):
    multiply_pieces(weight_loads(weight_hbm, weight_ref, half_ref[0], sems), gated_ref, weight_ref, out_ref)


def project_kept(half, gated, weight):
    rows, width = gated.shape
    features = weight.shape[1] // 2
    inside = pl.BlockSpec(memory_space=pltpu.VMEM)
    return pl.pallas_call(
        kept_kernel,
        in_specs=[pl.BlockSpec(memory_space=pltpu.SMEM), inside, pl.BlockSpec(memory_space=pl.ANY)],
        out_specs=inside,
        out_shape=jax.ShapeDtypeStruct((rows, features), jnp.float32),
        scratch_shapes=[pltpu.VMEM((width, features), jnp.bfloat16), pltpu.SemaphoreType.DMA((PIECES,))],
        compiler_params=pltpu.CompilerParams(vmem_limit_bytes=TAIL_BYTES),
        cost_estimate=pl.CostEstimate(
            flops=2 * rows * width * features, bytes_accessed=2 * width * features, transcendentals=0
        ),
        name="project_kept",
    )(half, gated, weight)


def join_kernel(kept_ref, came_ref, out_hbm, out_ref, sems):
    wide = out_ref.shape[0] // PIECES
    stores = []
    for part in range(PIECES):
        taken = pl.ds(part * wide, wide)
        out_ref[taken] = (kept_ref[:, taken] + came_ref[:, taken]).astype(jnp.bfloat16).T
        stores.append(pltpu.make_async_copy(out_ref.at[taken], out_hbm.at[taken], sems.at[part]))
        stores[part].start()
    for store in stores:
        store.wait()


def join(kept, came):
    rows, features = kept.shape
    return pl.pallas_call(
        join_kernel,
        in_specs=[pl.BlockSpec(memory_space=pltpu.VMEM)] * 2,
        out_specs=pl.BlockSpec(memory_space=pl.ANY),
        out_shape=jax.ShapeDtypeStruct((features, rows), jnp.bfloat16),
        scratch_shapes=[pltpu.VMEM((features, rows), jnp.bfloat16), pltpu.SemaphoreType.DMA((PIECES,))],
        compiler_params=pltpu.CompilerParams(vmem_limit_bytes=TAIL_BYTES),
        name="join_halves",
    )(kept, came)


def exchange(near, across):
    half = near.shape[0]
    groups = [list(range(half)), list(range(half, 2 * half))]
    near = lax.all_to_all(near, "seq", split_axis=0, concat_axis=0, axis_index_groups=groups, tiled=True)
    came = [
        lax.ppermute(source, "seq", [(j, j ^ slot) for j in range(2 * half)])
        for slot, source in zip(partners_across(2 * half), across)
    ]
    return near, came


def kernel_local(values, gates, filter_taps, skip_gain, out_weight):
    blocks = lax.axis_size("seq")
    me = lax.axis_index("seq").astype(jnp.int32)[None]
    half = lax.axis_index("chan").astype(jnp.int32)[None]
    near, *across = arrange(me, values, filter_taps, blocks)
    near, *across = convolve(me, *exchange(near, across))
    gated, sent = gate_and_project(me, half, *exchange(near, across), gates, values, skip_gain, out_weight)
    other = lax.ppermute(sent, "chan", [(0, 1), (1, 0)])
    kept = project_kept(half, gated, out_weight)
    return join(kept, other)


def takes_kernels(mesh, values, out_weight):
    blocks, halves = mesh.shape["seq"], mesh.shape["chan"]
    rows = values.shape[0] // blocks
    return (
        halves == 2
        and blocks == 16
        and rows == 256
        and values.shape[1] == halves * blocks * LANES
        and out_weight.shape[1] % (8 * LANES) == 0
    )


def solution(mesh):
    placed = (P("seq", "chan"), P("seq", "chan"), P("seq", "chan"), P("chan"), P("chan", None))

    def whole(values, gates, filter_taps, skip_gain, out_weight):
        local = kernel_local if takes_kernels(mesh, values, out_weight) else general_local
        return jax.shard_map(
            local, mesh=mesh, in_specs=placed, out_specs=P("chan", "seq"), check_vma=False
        )(values, gates, filter_taps, skip_gain, out_weight)

    return whole
```

```python
import functools
import math

import jax
import jax.numpy as jnp
import ml_dtypes
import numpy as np
from jax import lax
from jax.experimental import pallas as pl
from jax.experimental.pallas import tpu as pltpu
from jax.sharding import PartitionSpec as P

TWO_PI = 2.0 * math.pi
HIGH = lax.Precision.HIGHEST
RADIX = 16
LANES = 128
Q_ORDER = [low + 4 * high for low in range(4) for high in range(4)]
ARRANGE_BYTES = 12 * 1024 * 1024
CONV_BYTES = 49 * 1024 * 1024
TAIL_BYTES = 49 * 1024 * 1024


def angle_table(first, second, period):
    product = first[:, None] * second[None, :] % period
    angles = product.astype(jnp.float32) * (TWO_PI / period)
    return (jnp.cos(angles), jnp.sin(angles))


def mix(equation, left, right):
    return jnp.einsum(equation, left, right, precision=HIGH)


def outer_forward(data, outer_cos, outer_sin, twist_cos, twist_sin, equation):
    source = data.astype(jnp.float32)
    real = mix(equation, outer_cos, source)
    imag = -mix(equation, outer_sin, source)
    cos_part = twist_cos[:, :, None]
    sin_part = twist_sin[:, :, None]
    return (real * cos_part + imag * sin_part, imag * cos_part - real * sin_part)


def inner_filter(spectra, inner_cos, inner_sin):
    value_re, value_im, taps_re, taps_im = spectra

    def forward(real, imag):
        out_re = mix("kr,jrc->jkc", inner_cos, real) + mix("kr,jrc->jkc", inner_sin, imag)
        out_im = mix("kr,jrc->jkc", inner_cos, imag) - mix("kr,jrc->jkc", inner_sin, real)
        return (out_re, out_im)

    value_fre, value_fim = forward(value_re, value_im)
    taps_fre, taps_fim = forward(taps_re, taps_im)
    prod_re = value_fre * taps_fre - value_fim * taps_fim
    prod_im = value_fre * taps_fim + value_fim * taps_fre
    back_re = mix("rk,jkc->jrc", inner_cos, prod_re) - mix("rk,jkc->jrc", inner_sin, prod_im)
    back_im = mix("rk,jkc->jrc", inner_cos, prod_im) + mix("rk,jkc->jrc", inner_sin, prod_re)
    return (back_re, back_im)


def untwist(real, imag, twist_cos, twist_sin):
    cos_part = twist_cos[:, :, None]
    sin_part = twist_sin[:, :, None]
    return (real * cos_part - imag * sin_part, imag * cos_part + real * sin_part)


def channels_plan(values, filter_taps):
    rows, width = values.shape
    blocks = lax.axis_size("seq")
    length = 2 * blocks * rows
    narrow = width // blocks
    whole_values, whole_taps = (
        lax.all_to_all(values, "seq", split_axis=1, concat_axis=0, tiled=True),
        lax.all_to_all(filter_taps, "seq", split_axis=1, concat_axis=0, tiled=True),
    )
    freq_ids = jnp.arange(2 * blocks, dtype=jnp.int32)
    block_ids = jnp.arange(blocks, dtype=jnp.int32)
    all_rows = jnp.arange(rows, dtype=jnp.int32)
    outer_cos, outer_sin = angle_table(freq_ids, block_ids, 2 * blocks)
    twist_cos, twist_sin = angle_table(freq_ids, all_rows, length)
    tables = (outer_cos, outer_sin, twist_cos, twist_sin, "ka,arc->krc")
    value_re, value_im = outer_forward(whole_values.reshape(blocks, rows, narrow), *tables)
    taps_re, taps_im = outer_forward(whole_taps.reshape(blocks, rows, narrow), *tables)
    inner_cos, inner_sin = angle_table(all_rows, all_rows, rows)
    back_re, back_im = inner_filter((value_re, value_im, taps_re, taps_im), inner_cos, inner_sin)
    turned_re, turned_im = untwist(back_re, back_im, twist_cos, twist_sin)
    final_cos, final_sin = angle_table(block_ids, freq_ids, 2 * blocks)
    signal = (
        mix("ak,krc->arc", final_cos, turned_re) - mix("ak,krc->arc", final_sin, turned_im)
    ) / length
    returned = lax.all_to_all(signal, "seq", split_axis=0, concat_axis=2, tiled=True)
    return returned[0]


def general_local(values, gates, filter_taps, skip_gain, out_weight):
    conv = channels_plan(values, filter_taps)
    gated = (
        gates.astype(jnp.float32) * (conv + skip_gain[None, :] * values.astype(jnp.float32))
    ).astype(jnp.bfloat16)
    projected = lax.psum_scatter(
        lax.dot_general(
            out_weight, gated, (((0,), (1,)), ((), ())), preferred_element_type=jnp.float32
        ),
        "chan",
        scatter_dimension=0,
        tiled=True,
    )
    return projected.astype(jnp.bfloat16)


def split_table(table):
    high = table.astype(ml_dtypes.bfloat16)
    low = (table - high.astype(np.float64)).astype(ml_dtypes.bfloat16)
    return high, low


@functools.lru_cache(maxsize=None)
def transform_tables(length):
    inner = length // RADIX
    k = np.arange(inner)[:, None]
    unit = TWO_PI / (4 * length)
    turns = (np.array(Q_ORDER)[:, None] * (4 * k.T + 1)) % (4 * length) * unit
    turns = np.stack([np.cos(turns), np.sin(turns)], axis=1).reshape(2 * RADIX, inner, 1)
    blocks = [np.broadcast_to(turns, (2 * RADIX, inner, LANES))]
    forward, backward = [], []
    for odd in range(2):
        m = 2 * np.arange(inner // 2)[None, :] + odd
        angles = (RADIX * m * (4 * k[: inner // 2] + 1)) % (4 * length) * unit
        table = np.concatenate([np.cos(angles), -np.sin(angles)], axis=0)
        forward.append(np.concatenate(split_table(table), axis=1))
        backward.append(np.concatenate(split_table(table.T / length), axis=0))
    for table in forward + backward:
        blocks.append(table.astype(np.float32).reshape(inner, -1, LANES).swapaxes(0, 1))
    return np.concatenate(blocks, axis=0).astype(np.float32)


def row_order(rows, turned_over=False):
    place = lax.broadcasted_iota(jnp.int32, (rows, rows), 1 if turned_over else 0)
    source = lax.broadcasted_iota(jnp.int32, (rows, rows), 0 if turned_over else 1)
    chunk = rows // RADIX
    index, within = place // chunk, place % chunk
    odd, j = within // (chunk // 2), within % (chunk // 2)
    wanted = RADIX * (2 * j + odd) + index // 4 + 4 * (index % 4)
    return jnp.where(source == wanted, 1.0, 0.0).astype(jnp.bfloat16)


def turn(point, index, sign):
    re, im = point
    index %= 16
    if index == 0:
        return point
    if index == 4:
        return (-im, re) if sign > 0 else (im, -re)
    if index == 8:
        return (-re, -im)
    half = math.sqrt(0.5)
    if index == 2:
        return ((re - im) * half, (re + im) * half) if sign > 0 else ((re + im) * half, (im - re) * half)
    if index == 6:
        return ((-re - im) * half, (re - im) * half) if sign > 0 else ((im - re) * half, (-re - im) * half)
    cos = math.cos(TWO_PI * index / 16)
    sin = sign * math.sin(TWO_PI * index / 16)
    return (re * cos - im * sin, re * sin + im * cos)


def four_points(points, sign):
    a, b, c, d = points
    ac = (a[0] + c[0], a[1] + c[1])
    am = (a[0] - c[0], a[1] - c[1])
    bd = (b[0] + d[0], b[1] + d[1])
    bm = (b[0] - d[0], b[1] - d[1])
    if sign < 0:
        side = (bm[1], -bm[0])
    else:
        side = (-bm[1], bm[0])
    return (
        (ac[0] + bd[0], ac[1] + bd[1]),
        (am[0] + side[0], am[1] + side[1]),
        (ac[0] - bd[0], ac[1] - bd[1]),
        (am[0] - side[0], am[1] - side[1]),
    )


def turned(point, cos, sin, sign):
    re, im = point
    if sign < 0:
        return (re * cos + im * sin, im * cos - re * sin)
    return (re * cos - im * sin, im * cos + re * sin)


def slot_order(blocks):
    half = blocks // 2
    across = [half + (i // 2 if i % 2 == 0 else half // 2 + i // 2) for i in range(half)]
    near = list(range(1, half)) + [0]
    return [slot for pair in zip(across, near) for slot in pair]


def arrange_kernel(pieces, blocks, me_ref, values_hbm, taps_hbm, *rest):
    outs = rest[:blocks]
    values_ref, taps_ref, packed, sems = rest[blocks:]
    piece = values_ref.shape[1] // pieces
    loads = []
    for part in range(pieces):
        lanes = pl.ds(part * piece, piece)
        loads.append(pltpu.make_async_copy(values_hbm.at[:, lanes], values_ref.at[:, lanes], sems.at[2 * part]))
        loads.append(pltpu.make_async_copy(taps_hbm.at[:, lanes], taps_ref.at[:, lanes], sems.at[2 * part + 1]))
    for load in loads:
        load.start()
    order = row_order(values_ref.shape[0])
    for part in range(pieces):
        loads[2 * part].wait()
        loads[2 * part + 1].wait()
        lanes = pl.ds(part * piece, piece)
        both = jnp.concatenate([values_ref[:, lanes], taps_ref[:, lanes]], axis=1)
        moved = jnp.dot(order, both, preferred_element_type=jnp.float32).astype(jnp.bfloat16)
        for block in range(piece // LANES):
            for side in range(2):
                start = side * piece + block * LANES
                packed[part * piece // LANES + block, :, pl.ds(side * LANES, LANES)] = moved[:, start : start + LANES]
    for out, slot in zip(outs, slot_order(blocks)):
        out[...] = packed[me_ref[0] ^ slot]


def arrange(me, values, taps, blocks):
    rows, wide = values.shape
    pieces = 4
    return pl.pallas_call(
        functools.partial(arrange_kernel, pieces, blocks),
        in_specs=[pl.BlockSpec(memory_space=pltpu.SMEM)] + [pl.BlockSpec(memory_space=pl.ANY)] * 2,
        out_specs=[pl.BlockSpec(memory_space=pltpu.VMEM)] * blocks,
        out_shape=[jax.ShapeDtypeStruct((rows, 2 * LANES), jnp.bfloat16)] * blocks,
        scratch_shapes=[
            pltpu.VMEM((rows, wide), jnp.bfloat16),
            pltpu.VMEM((rows, wide), jnp.bfloat16),
            pltpu.VMEM((blocks, rows, 2 * LANES), jnp.bfloat16),
            pltpu.SemaphoreType.DMA((2 * pieces,)),
        ],
        compiler_params=pltpu.CompilerParams(vmem_limit_bytes=ARRANGE_BYTES),
        cost_estimate=pl.CostEstimate(
            flops=4 * rows * rows * wide, bytes_accessed=8 * rows * wide, transcendentals=0
        ),
        name="arrange_rows",
    )(me, values, taps)


def convolve_kernel(blocks, me_ref, *rest):
    convolve_blocks(me_ref, rest[:blocks], rest[blocks], rest[blocks + 1 : 2 * blocks + 1], *rest[2 * blocks + 1 :])


def convolve_blocks(
    me_ref, slots, tables_hbm, outs,
    streams, turns_ref, fixed, stages, raw_even, raw_odd, columns, mixed, halves_even, halves_odd, signals, sems,
):
    blocks, rows, _ = streams.shape
    chunk = rows // RADIX
    inner = blocks * chunk
    part_rows = inner // 2
    group = rows // 4
    raws = (raw_even, raw_odd)
    halves = (halves_even, halves_odd)
    count = fixed.shape[0]
    load_fixed = pltpu.make_async_copy(tables_hbm.at[pl.ds(2 * RADIX, count)], fixed, sems.at[0])
    load_turns, stores = [], []
    for low in range(4):
        eight = pl.ds(8 * low, 8)
        load_turns.append(pltpu.make_async_copy(tables_hbm.at[eight], turns_ref.at[eight], sems.at[1 + low]))
    for part in range(2):
        taken = pl.ds(2 * part * group, 2 * group)
        stores.append(
            [
                pltpu.make_async_copy(
                    signals.at[me_ref[0] ^ slot, taken], out.at[taken], sems.at[6 + part * blocks + i]
                )
                for i, (out, slot) in enumerate(zip(outs, slot_order(blocks)))
            ]
        )
    load_fixed.start()
    for load in load_turns:
        load.start()
    own = pltpu.make_async_copy(slots[-1], streams.at[me_ref[0]], sems.at[5])
    own.start()
    for slot, source in zip(slot_order(blocks)[:-1], slots[:-1]):
        streams[me_ref[0] ^ slot] = source[...]
    own.wait()
    load_fixed.wait()
    width = inner // LANES
    for table in range(4):
        for block in range(width):
            stages[table, :, pl.ds(block * LANES, LANES)] = fixed[table * width + block].astype(jnp.bfloat16)

    def transform(low, pair):
        sides = [[], []]
        for part in range(2):
            taken = pl.ds(pl.multiple_of(low * group + (2 * pair + part) * chunk, chunk), chunk)
            stream = streams[:, taken].astype(jnp.float32).reshape(blocks, 2, chunk // 2, 2 * LANES)
            for odd in range(2):
                sides[odd].append(stream[:, odd].reshape(part_rows, 2 * LANES).astype(jnp.bfloat16))
        for odd in range(2):
            both = jnp.concatenate(sides[odd], axis=1)
            result = jnp.dot(
                stages[odd], jnp.concatenate([both, both], axis=0), preferred_element_type=jnp.float32
            )
            for part in range(2):
                raws[low % 2][2 * pair + part, odd] = result[:, 2 * part * LANES : 2 * (part + 1) * LANES]

    def first_pass(low, start):
        raw = raws[low % 2]
        real, imaginary = pl.ds(start, 8), pl.ds(part_rows + start, 8)
        for side in range(2):
            lanes = pl.ds(side * LANES, LANES)
            points = [[], []]
            for high in range(4):
                even = (raw[high, 0, real, lanes], raw[high, 0, imaginary, lanes])
                odd = (raw[high, 1, real, lanes], raw[high, 1, imaginary, lanes])
                points[0].append((even[0] + odd[0], even[1] + odd[1]))
                points[1].append((even[0] - odd[0], even[1] - odd[1]))
            for part in range(2):
                upper, lower = pl.ds(part * part_rows + start, 8), pl.ds(inner + part * part_rows + start, 8)
                for high in range(4):
                    if low + high:
                        turns = [turns_ref[2 * (4 * low + high) + i, upper] for i in range(2)]
                        points[part][high] = turned(points[part][high], *turns, -1)
                for k, point in enumerate(four_points(points[part], -1)):
                    point = turn(point, low * k, -1)
                    columns[4 * low + k, upper, lanes] = point[0]
                    columns[4 * low + k, lower, lanes] = point[1]

    def first_rows(low, start, count):
        for part in range(count):
            first_pass(low, pl.multiple_of(start + 8 * part, 8))

    steps = part_rows // 2

    def alone(pair, carry):
        transform(0, pair)
        return carry

    lax.fori_loop(0, 2, alone, 0)
    for low in range(1, 4):
        load_turns[low - 1].wait()

        def beside(pair, carry, low=low):
            transform(low, pair)
            first_rows(low - 1, pair * steps, steps // 8)
            return carry

        lax.fori_loop(0, 2, beside, 0)
    load_turns[3].wait()

    def middle(index, carry):
        start = pl.multiple_of(index * 8, 8)
        first_pass(3, start)
        for part in range(2):
            upper, lower = pl.ds(part * part_rows + start, 8), pl.ds(inner + part * part_rows + start, 8)
            for k in range(4):
                sides = []
                for side in range(2):
                    lanes = pl.ds(side * LANES, LANES)
                    points = [
                        (columns[4 * low + k, upper, lanes], columns[4 * low + k, lower, lanes]) for low in range(4)
                    ]
                    sides.append(four_points(points, -1))
                product = [
                    (a[0] * b[0] - a[1] * b[1], a[0] * b[1] + a[1] * b[0]) for a, b in zip(*sides)
                ]
                for high, point in enumerate(four_points(product, 1)):
                    point = turn(point, k * high, 1)
                    mixed[4 * high + k, upper] = point[0]
                    mixed[4 * high + k, lower] = point[1]
        return carry

    lax.fori_loop(0, part_rows // 8, middle, 0)

    def last_pass(low, start):
        target = halves[low % 2]
        found = []
        for part in range(2):
            upper, lower = pl.ds(part * part_rows + start, 16), pl.ds(inner + part * part_rows + start, 16)
            points = list(four_points([(mixed[4 * low + k, upper], mixed[4 * low + k, lower]) for k in range(4)], 1))
            for high in range(4):
                if low + high:
                    turns = [turns_ref[2 * (4 * low + high) + i, upper] for i in range(2)]
                    points[high] = turned(points[high], *turns, 1)
            found.append(points)
        for high in range(4):
            for i in range(2):
                taken = pl.ds(i * part_rows + start, 16)
                first, second = found[0][high][i], found[1][high][i]
                for odd, value in enumerate((first + second, first - second)):
                    rounded = value.astype(jnp.bfloat16)
                    target[high, odd, taken, pl.ds(0, LANES)] = rounded
                    target[high, odd, taken, pl.ds(LANES, LANES)] = (value - rounded.astype(jnp.float32)).astype(
                        jnp.bfloat16
                    )

    def last_rows(low, start, count):
        for part in range(count):
            last_pass(low, pl.multiple_of(start + 16 * part, 16))

    def restore(low, pair):
        sides = []
        for odd in range(2):
            both = jnp.concatenate([halves[low % 2][2 * pair + part, odd] for part in range(2)], axis=1)
            terms = jnp.dot(stages[2 + odd], both, preferred_element_type=jnp.float32)
            found = []
            for part in range(2):
                first, second = [slice((2 * part + i) * LANES, (2 * part + i + 1) * LANES) for i in range(2)]
                signal = terms[:part_rows, first] + terms[:part_rows, second] + terms[part_rows:, first]
                found.append(signal.reshape(blocks, 1, chunk // 2, LANES))
            sides.append(found)
        for part in range(2):
            signal = jnp.concatenate([sides[0][part], sides[1][part]], axis=1).reshape(blocks, chunk, LANES)
            taken = pl.ds(pl.multiple_of(low * group + (2 * pair + part) * chunk, chunk), chunk)
            signals[:, taken] = signal.astype(jnp.bfloat16)

    def prepare(index, carry):
        last_rows(0, index * steps, steps // 16)
        return carry

    lax.fori_loop(0, 2, prepare, 0)
    for low in range(4):

        def back(pair, carry, low=low):
            restore(low, pair)
            if low < 3:
                last_rows(low + 1, pair * steps, steps // 16)
            return carry

        lax.fori_loop(0, 2, back, 0)
        if low % 2:
            for store in stores[low // 2]:
                store.start()
    for store in stores[0] + stores[1]:
        store.wait()


def convolve(me, slots):
    blocks = len(slots)
    rows, lanes = slots[0].shape
    length = blocks * rows
    inner = length // RADIX
    tables = transform_tables(length)
    return pl.pallas_call(
        functools.partial(convolve_kernel, blocks),
        in_specs=[pl.BlockSpec(memory_space=pltpu.SMEM)]
        + [pl.BlockSpec(memory_space=pltpu.VMEM)] * (blocks - 1)
        + [pl.BlockSpec(memory_space=pl.ANY)] * 2,
        out_specs=[pl.BlockSpec(memory_space=pl.ANY)] * blocks,
        out_shape=[jax.ShapeDtypeStruct((rows, LANES), jnp.bfloat16)] * blocks,
        scratch_shapes=[
            pltpu.VMEM((blocks, rows, lanes), jnp.bfloat16),
            pltpu.VMEM((2 * RADIX, inner, LANES), jnp.float32),
            pltpu.VMEM((tables.shape[0] - 2 * RADIX, inner, LANES), jnp.float32),
            pltpu.VMEM((4, inner, inner), jnp.bfloat16),
            pltpu.VMEM((4, 2, inner, lanes), jnp.float32),
            pltpu.VMEM((4, 2, inner, lanes), jnp.float32),
            pltpu.VMEM((RADIX, 2 * inner, lanes), jnp.float32),
            pltpu.VMEM((RADIX, 2 * inner, LANES), jnp.float32),
            pltpu.VMEM((4, 2, inner, lanes), jnp.bfloat16),
            pltpu.VMEM((4, 2, inner, lanes), jnp.bfloat16),
            pltpu.VMEM((blocks, rows, LANES), jnp.bfloat16),
            pltpu.SemaphoreType.DMA((6 + 2 * blocks,)),
        ],
        compiler_params=pltpu.CompilerParams(vmem_limit_bytes=CONV_BYTES),
        cost_estimate=pl.CostEstimate(flops=5 * 10**9, bytes_accessed=9 * 10**6, transcendentals=0),
        name="long_convolution",
    )(me, *slots, jnp.asarray(tables))


PIECES = 4


def weight_loads(weight_hbm, weight_ref, side, sems):
    width, features = weight_ref.shape
    columns = pl.ds(pl.multiple_of(side * features, features), features)
    deep = width // PIECES
    loads = []
    for part in range(PIECES):
        rows = pl.ds(part * deep, deep)
        loads.append(pltpu.make_async_copy(weight_hbm.at[rows, columns], weight_ref.at[rows], sems.at[part]))
        loads[part].start()
    return loads


def gate_kernel(count, me_ref, half_ref, gates_hbm, values_hbm, skip_ref, weight_hbm, *rest):
    slots = rest[:count]
    gated_ref, out_ref, conv_ref, gates_ref, values_ref, weight_ref, sems = rest[count:]
    blocks, rows, lanes = conv_ref.shape
    me = me_ref[0]
    streams = [
        pltpu.make_async_copy(gates_hbm, gates_ref, sems.at[PIECES]),
        pltpu.make_async_copy(values_hbm, values_ref, sems.at[PIECES + 1]),
        pltpu.make_async_copy(slots[-1], conv_ref.at[me], sems.at[PIECES + 2]),
    ]
    for stream in streams:
        stream.start()
    loads = weight_loads(weight_hbm, weight_ref, 1 - half_ref[0], sems)
    order = row_order(rows, True)
    for slot, source in zip(slot_order(blocks)[:-1], slots[:-1]):
        conv_ref[me ^ slot] = source[...]
    for stream in streams:
        stream.wait()
    group = blocks // PIECES
    wide = group * lanes
    for part in range(PIECES):
        taken = pl.ds(part * wide, wide)
        conv = jnp.concatenate([conv_ref[part * group + block] for block in range(group)], axis=1)
        conv = jnp.dot(order, conv, preferred_element_type=jnp.float32)
        direct = skip_ref[:, taken] * values_ref[:, taken].astype(jnp.float32)
        gated_ref[:, taken] = (gates_ref[:, taken].astype(jnp.float32) * (conv + direct)).astype(jnp.bfloat16)
    multiply_pieces(loads, gated_ref, weight_ref, out_ref)


def multiply_pieces(loads, gated_ref, weight_ref, out_ref):
    deep = weight_ref.shape[0] // PIECES
    for part in range(PIECES):
        taken = pl.ds(part * deep, deep)
        loads[part].wait()
        term = jnp.dot(gated_ref[:, taken], weight_ref[taken], preferred_element_type=jnp.float32)
        out_ref[...] = term if part == 0 else out_ref[...] + term


def gate_and_project(me, half, slots, gates, values, skip_gain, weight):
    rows, width = gates.shape
    features = weight.shape[1] // 2
    anywhere, inside = pl.BlockSpec(memory_space=pl.ANY), pl.BlockSpec(memory_space=pltpu.VMEM)
    return pl.pallas_call(
        functools.partial(gate_kernel, len(slots)),
        in_specs=[pl.BlockSpec(memory_space=pltpu.SMEM)] * 2
        + [anywhere, anywhere, inside, anywhere]
        + [inside] * (len(slots) - 1)
        + [anywhere],
        out_specs=[inside] * 2,
        out_shape=[
            jax.ShapeDtypeStruct((rows, width), jnp.bfloat16),
            jax.ShapeDtypeStruct((rows, features), jnp.float32),
        ],
        scratch_shapes=[
            pltpu.VMEM((len(slots), rows, LANES), jnp.bfloat16),
            pltpu.VMEM((rows, width), jnp.bfloat16),
            pltpu.VMEM((rows, width), jnp.bfloat16),
            pltpu.VMEM((width, features), jnp.bfloat16),
            pltpu.SemaphoreType.DMA((PIECES + 3,)),
        ],
        compiler_params=pltpu.CompilerParams(vmem_limit_bytes=TAIL_BYTES),
        cost_estimate=pl.CostEstimate(
            flops=2 * rows * width * features, bytes_accessed=2 * width * features, transcendentals=0
        ),
        name="gate_project_sent",
    )(me, half, gates, values, skip_gain[None, :], weight, *slots)


def kept_kernel(half_ref, gated_ref, weight_hbm, out_ref, weight_ref, sems):
    multiply_pieces(weight_loads(weight_hbm, weight_ref, half_ref[0], sems), gated_ref, weight_ref, out_ref)


def project_kept(half, gated, weight):
    rows, width = gated.shape
    features = weight.shape[1] // 2
    inside = pl.BlockSpec(memory_space=pltpu.VMEM)
    return pl.pallas_call(
        kept_kernel,
        in_specs=[pl.BlockSpec(memory_space=pltpu.SMEM), inside, pl.BlockSpec(memory_space=pl.ANY)],
        out_specs=inside,
        out_shape=jax.ShapeDtypeStruct((rows, features), jnp.float32),
        scratch_shapes=[pltpu.VMEM((width, features), jnp.bfloat16), pltpu.SemaphoreType.DMA((PIECES,))],
        compiler_params=pltpu.CompilerParams(vmem_limit_bytes=TAIL_BYTES),
        cost_estimate=pl.CostEstimate(
            flops=2 * rows * width * features, bytes_accessed=2 * width * features, transcendentals=0
        ),
        name="project_kept",
    )(half, gated, weight)


def join_kernel(kept_ref, came_ref, out_hbm, out_ref, sems):
    wide = out_ref.shape[0] // PIECES
    stores = []
    for part in range(PIECES):
        taken = pl.ds(part * wide, wide)
        out_ref[taken] = (kept_ref[:, taken] + came_ref[:, taken]).astype(jnp.bfloat16).T
        stores.append(pltpu.make_async_copy(out_ref.at[taken], out_hbm.at[taken], sems.at[part]))
        stores[part].start()
    for store in stores:
        store.wait()


def join(kept, came):
    rows, features = kept.shape
    return pl.pallas_call(
        join_kernel,
        in_specs=[pl.BlockSpec(memory_space=pltpu.VMEM)] * 2,
        out_specs=pl.BlockSpec(memory_space=pl.ANY),
        out_shape=jax.ShapeDtypeStruct((features, rows), jnp.bfloat16),
        scratch_shapes=[pltpu.VMEM((features, rows), jnp.bfloat16), pltpu.SemaphoreType.DMA((PIECES,))],
        compiler_params=pltpu.CompilerParams(vmem_limit_bytes=TAIL_BYTES),
        name="join_halves",
    )(kept, came)


def exchange(slots):
    blocks = len(slots)
    return [
        lax.ppermute(source, "seq", [(j, j ^ slot) for j in range(blocks)]) if slot else source
        for slot, source in zip(slot_order(blocks), slots)
    ]


def kernel_local(values, gates, filter_taps, skip_gain, out_weight):
    blocks = lax.axis_size("seq")
    me = lax.axis_index("seq").astype(jnp.int32)[None]
    half = lax.axis_index("chan").astype(jnp.int32)[None]
    conv = convolve(me, exchange(arrange(me, values, filter_taps, blocks)))
    gated, sent = gate_and_project(me, half, exchange(conv), gates, values, skip_gain, out_weight)
    other = lax.ppermute(sent, "chan", [(0, 1), (1, 0)])
    kept = project_kept(half, gated, out_weight)
    return join(kept, other)


def takes_kernels(mesh, values, out_weight):
    blocks, halves = mesh.shape["seq"], mesh.shape["chan"]
    rows = values.shape[0] // blocks
    return (
        halves == 2
        and blocks == 16
        and rows == 256
        and values.shape[1] == halves * blocks * LANES
        and out_weight.shape[1] % (8 * LANES) == 0
    )


def solution(mesh):
    placed = (P("seq", "chan"), P("seq", "chan"), P("seq", "chan"), P("chan"), P("chan", None))

    def whole(values, gates, filter_taps, skip_gain, out_weight):
        local = kernel_local if takes_kernels(mesh, values, out_weight) else general_local
        return jax.shard_map(
            local, mesh=mesh, in_specs=placed, out_specs=P("chan", "seq"), check_vma=False
        )(values, gates, filter_taps, skip_gain, out_weight)

    return whole
```

```python
import functools
import math

import jax
import jax.numpy as jnp
import ml_dtypes
import numpy as np
from jax import lax
from jax.experimental import pallas as pl
from jax.experimental.pallas import tpu as pltpu
from jax.sharding import PartitionSpec as P

TWO_PI = 2.0 * math.pi
HIGH = lax.Precision.HIGHEST
RADIX = 16
LANES = 128
Q_ORDER = [low + 4 * high for low in range(4) for high in range(4)]
FIRST_BYTES = 60 * 1024 * 1024
ARRANGE_BYTES = 12 * 1024 * 1024
CONV_BYTES = 49 * 1024 * 1024
TAIL_BYTES = 49 * 1024 * 1024


def angle_table(first, second, period):
    product = first[:, None] * second[None, :] % period
    angles = product.astype(jnp.float32) * (TWO_PI / period)
    return (jnp.cos(angles), jnp.sin(angles))


def mix(equation, left, right):
    return jnp.einsum(equation, left, right, precision=HIGH)


def outer_forward(data, outer_cos, outer_sin, twist_cos, twist_sin, equation):
    source = data.astype(jnp.float32)
    real = mix(equation, outer_cos, source)
    imag = -mix(equation, outer_sin, source)
    cos_part = twist_cos[:, :, None]
    sin_part = twist_sin[:, :, None]
    return (real * cos_part + imag * sin_part, imag * cos_part - real * sin_part)


def inner_filter(spectra, inner_cos, inner_sin):
    value_re, value_im, taps_re, taps_im = spectra

    def forward(real, imag):
        out_re = mix("kr,jrc->jkc", inner_cos, real) + mix("kr,jrc->jkc", inner_sin, imag)
        out_im = mix("kr,jrc->jkc", inner_cos, imag) - mix("kr,jrc->jkc", inner_sin, real)
        return (out_re, out_im)

    value_fre, value_fim = forward(value_re, value_im)
    taps_fre, taps_fim = forward(taps_re, taps_im)
    prod_re = value_fre * taps_fre - value_fim * taps_fim
    prod_im = value_fre * taps_fim + value_fim * taps_fre
    back_re = mix("rk,jkc->jrc", inner_cos, prod_re) - mix("rk,jkc->jrc", inner_sin, prod_im)
    back_im = mix("rk,jkc->jrc", inner_cos, prod_im) + mix("rk,jkc->jrc", inner_sin, prod_re)
    return (back_re, back_im)


def untwist(real, imag, twist_cos, twist_sin):
    cos_part = twist_cos[:, :, None]
    sin_part = twist_sin[:, :, None]
    return (real * cos_part - imag * sin_part, imag * cos_part + real * sin_part)


def channels_plan(values, filter_taps):
    rows, width = values.shape
    blocks = lax.axis_size("seq")
    length = 2 * blocks * rows
    narrow = width // blocks
    whole_values, whole_taps = (
        lax.all_to_all(values, "seq", split_axis=1, concat_axis=0, tiled=True),
        lax.all_to_all(filter_taps, "seq", split_axis=1, concat_axis=0, tiled=True),
    )
    freq_ids = jnp.arange(2 * blocks, dtype=jnp.int32)
    block_ids = jnp.arange(blocks, dtype=jnp.int32)
    all_rows = jnp.arange(rows, dtype=jnp.int32)
    outer_cos, outer_sin = angle_table(freq_ids, block_ids, 2 * blocks)
    twist_cos, twist_sin = angle_table(freq_ids, all_rows, length)
    tables = (outer_cos, outer_sin, twist_cos, twist_sin, "ka,arc->krc")
    value_re, value_im = outer_forward(whole_values.reshape(blocks, rows, narrow), *tables)
    taps_re, taps_im = outer_forward(whole_taps.reshape(blocks, rows, narrow), *tables)
    inner_cos, inner_sin = angle_table(all_rows, all_rows, rows)
    back_re, back_im = inner_filter((value_re, value_im, taps_re, taps_im), inner_cos, inner_sin)
    turned_re, turned_im = untwist(back_re, back_im, twist_cos, twist_sin)
    final_cos, final_sin = angle_table(block_ids, freq_ids, 2 * blocks)
    signal = (
        mix("ak,krc->arc", final_cos, turned_re) - mix("ak,krc->arc", final_sin, turned_im)
    ) / length
    returned = lax.all_to_all(signal, "seq", split_axis=0, concat_axis=2, tiled=True)
    return returned[0]


def general_local(values, gates, filter_taps, skip_gain, out_weight):
    conv = channels_plan(values, filter_taps)
    gated = (
        gates.astype(jnp.float32) * (conv + skip_gain[None, :] * values.astype(jnp.float32))
    ).astype(jnp.bfloat16)
    projected = lax.psum_scatter(
        lax.dot_general(
            out_weight, gated, (((0,), (1,)), ((), ())), preferred_element_type=jnp.float32
        ),
        "chan",
        scatter_dimension=0,
        tiled=True,
    )
    return projected.astype(jnp.bfloat16)


def split_table(table):
    high = table.astype(ml_dtypes.bfloat16)
    low = (table - high.astype(np.float64)).astype(ml_dtypes.bfloat16)
    return high, low


@functools.lru_cache(maxsize=None)
def transform_tables(length):
    inner = length // RADIX
    k = np.arange(inner)[:, None]
    unit = TWO_PI / (4 * length)
    turns = (np.array(Q_ORDER)[:, None] * (4 * k.T + 1)) % (4 * length) * unit
    turns = np.stack([np.cos(turns), np.sin(turns)], axis=1).reshape(2 * RADIX, inner, 1)
    blocks = [np.broadcast_to(turns, (2 * RADIX, inner, LANES))]
    forward, backward = [], []
    for odd in range(2):
        m = 2 * np.arange(inner // 2)[None, :] + odd
        angles = (RADIX * m * (4 * k[: inner // 2] + 1)) % (4 * length) * unit
        table = np.concatenate([np.cos(angles), -np.sin(angles)], axis=0)
        forward.append(np.concatenate(split_table(table), axis=1))
        backward.append(np.concatenate(split_table(table.T / length), axis=0))
    for table in forward + backward:
        blocks.append(table.astype(np.float32).reshape(inner, -1, LANES).swapaxes(0, 1))
    return np.concatenate(blocks, axis=0).astype(np.float32)


def row_order(rows, turned_over=False):
    place = lax.broadcasted_iota(jnp.int32, (rows, rows), 1 if turned_over else 0)
    source = lax.broadcasted_iota(jnp.int32, (rows, rows), 0 if turned_over else 1)
    chunk = rows // RADIX
    index, within = place // chunk, place % chunk
    odd, j = within // (chunk // 2), within % (chunk // 2)
    wanted = RADIX * (2 * j + odd) + index // 4 + 4 * (index % 4)
    return jnp.where(source == wanted, 1.0, 0.0).astype(jnp.bfloat16)


def turn(point, index, sign):
    re, im = point
    index %= 16
    if index == 0:
        return point
    if index == 4:
        return (-im, re) if sign > 0 else (im, -re)
    if index == 8:
        return (-re, -im)
    half = math.sqrt(0.5)
    if index == 2:
        return ((re - im) * half, (re + im) * half) if sign > 0 else ((re + im) * half, (im - re) * half)
    if index == 6:
        return ((-re - im) * half, (re - im) * half) if sign > 0 else ((im - re) * half, (-re - im) * half)
    cos = math.cos(TWO_PI * index / 16)
    sin = sign * math.sin(TWO_PI * index / 16)
    return (re * cos - im * sin, re * sin + im * cos)


def four_points(points, sign):
    a, b, c, d = points
    ac = (a[0] + c[0], a[1] + c[1])
    am = (a[0] - c[0], a[1] - c[1])
    bd = (b[0] + d[0], b[1] + d[1])
    bm = (b[0] - d[0], b[1] - d[1])
    if sign < 0:
        side = (bm[1], -bm[0])
    else:
        side = (-bm[1], bm[0])
    return (
        (ac[0] + bd[0], ac[1] + bd[1]),
        (am[0] + side[0], am[1] + side[1]),
        (ac[0] - bd[0], ac[1] - bd[1]),
        (am[0] - side[0], am[1] - side[1]),
    )


def turned(point, cos, sin, sign):
    re, im = point
    if sign < 0:
        return (re * cos + im * sin, im * cos - re * sin)
    return (re * cos - im * sin, im * cos + re * sin)


def slot_order(blocks):
    half = blocks // 2
    across = [half + (i // 2 if i % 2 == 0 else half // 2 + i // 2) for i in range(half)]
    near = list(range(1, half)) + [0]
    return [slot for pair in zip(across, near) for slot in pair]


LEAD = 4


def lead_kernel(blocks, me_ref, values_hbm, taps_hbm, *rest):
    outs, (streams, sems) = rest[:LEAD], rest[LEAD:]
    loads = []
    for i, slot in enumerate(slot_order(blocks)[:LEAD]):
        lanes = pl.ds(pl.multiple_of((me_ref[0] ^ slot) * LANES, LANES), LANES)
        for side, source in enumerate((values_hbm, taps_hbm)):
            to = pl.ds((2 * i + side) * LANES, LANES)
            loads.append(pltpu.make_async_copy(source.at[:, lanes], streams.at[:, to], sems.at[2 * i + side]))
    for load in loads:
        load.start()
    order = row_order(streams.shape[0])
    for load in loads:
        load.wait()
    moved = jnp.dot(order, streams[...], preferred_element_type=jnp.float32).astype(jnp.bfloat16)
    for i, out in enumerate(outs):
        out[...] = moved[:, 2 * i * LANES : 2 * (i + 1) * LANES]


def arrange_kernel(pieces, blocks, me_ref, values_hbm, taps_hbm, *rest):
    outs, (values_ref, taps_ref, packed, sems) = rest[: blocks - LEAD], rest[blocks - LEAD :]
    piece = values_ref.shape[1] // pieces
    loads = []
    for part in range(pieces):
        lanes = pl.ds(part * piece, piece)
        loads.append(pltpu.make_async_copy(values_hbm.at[:, lanes], values_ref.at[:, lanes], sems.at[2 * part]))
        loads.append(pltpu.make_async_copy(taps_hbm.at[:, lanes], taps_ref.at[:, lanes], sems.at[2 * part + 1]))
    for load in loads:
        load.start()
    order = row_order(values_ref.shape[0])
    for part in range(pieces):
        loads[2 * part].wait()
        loads[2 * part + 1].wait()
        lanes = pl.ds(part * piece, piece)
        both = jnp.concatenate([values_ref[:, lanes], taps_ref[:, lanes]], axis=1)
        moved = jnp.dot(order, both, preferred_element_type=jnp.float32).astype(jnp.bfloat16)
        for block in range(piece // LANES):
            for side in range(2):
                start = side * piece + block * LANES
                packed[part * piece // LANES + block, :, pl.ds(side * LANES, LANES)] = moved[:, start : start + LANES]
    for out, slot in zip(outs, slot_order(blocks)[LEAD:]):
        out[...] = packed[me_ref[0] ^ slot]


def arrange(me, values, taps, blocks):
    rows, wide = values.shape
    pieces = 4
    block = jax.ShapeDtypeStruct((rows, 2 * LANES), jnp.bfloat16)
    in_specs = [pl.BlockSpec(memory_space=pltpu.SMEM)] + [pl.BlockSpec(memory_space=pl.ANY)] * 2
    lead = pl.pallas_call(
        functools.partial(lead_kernel, blocks),
        in_specs=in_specs,
        out_specs=[pl.BlockSpec(memory_space=pltpu.VMEM)] * LEAD,
        out_shape=[block] * LEAD,
        scratch_shapes=[
            pltpu.VMEM((rows, 2 * LEAD * LANES), jnp.bfloat16),
            pltpu.SemaphoreType.DMA((2 * LEAD,)),
        ],
        compiler_params=pltpu.CompilerParams(vmem_limit_bytes=FIRST_BYTES),
        cost_estimate=pl.CostEstimate(
            flops=4 * rows * rows * LEAD * LANES, bytes_accessed=8 * rows * LEAD * LANES, transcendentals=0
        ),
        name="arrange_lead",
    )(me, values, taps)
    others = pl.pallas_call(
        functools.partial(arrange_kernel, pieces, blocks),
        in_specs=in_specs,
        out_specs=[pl.BlockSpec(memory_space=pltpu.VMEM)] * (blocks - LEAD),
        out_shape=[block] * (blocks - LEAD),
        scratch_shapes=[
            pltpu.VMEM((rows, wide), jnp.bfloat16),
            pltpu.VMEM((rows, wide), jnp.bfloat16),
            pltpu.VMEM((blocks, rows, 2 * LANES), jnp.bfloat16),
            pltpu.SemaphoreType.DMA((2 * pieces,)),
        ],
        compiler_params=pltpu.CompilerParams(vmem_limit_bytes=ARRANGE_BYTES),
        cost_estimate=pl.CostEstimate(
            flops=4 * rows * rows * wide, bytes_accessed=8 * rows * wide, transcendentals=0
        ),
        name="arrange_others",
    )(me, values, taps)
    return [*lead, *others]


def convolve_kernel(blocks, me_ref, *rest):
    slots = rest[:blocks]
    convolve_blocks(me_ref, slots, *rest[blocks:])


def convolve_blocks(
    me_ref, slots, tables_hbm, out_hbm,
    streams, turns_ref, fixed, stages, raw_even, raw_odd, columns, mixed, halves_even, halves_odd, signals, sems,
):
    blocks, rows, _ = streams.shape
    chunk = rows // RADIX
    inner = blocks * chunk
    part_rows = inner // 2
    group = rows // 4
    raws = (raw_even, raw_odd)
    halves = (halves_even, halves_odd)
    count = fixed.shape[0]
    load_fixed = []
    for part in range(2):
        taken = pl.ds(part * count // 2, count // 2)
        source = tables_hbm.at[pl.ds(2 * RADIX + part * count // 2, count // 2)]
        load_fixed.append(pltpu.make_async_copy(source, fixed.at[taken], sems.at[10 * part]))
    load_turns, stores = [], []
    for low in range(4):
        taken = pl.ds(low * group, group)
        eight = pl.ds(8 * low, 8)
        load_turns.append(pltpu.make_async_copy(tables_hbm.at[eight], turns_ref.at[eight], sems.at[1 + low]))
        stores.append(pltpu.make_async_copy(signals.at[:, taken], out_hbm.at[:, taken], sems.at[5 + low]))
    load_fixed[0].start()
    for load in load_turns:
        load.start()
    load_fixed[1].start()
    own = pltpu.make_async_copy(slots[-1], streams.at[me_ref[0]], sems.at[9])
    own.start()
    for slot, source in zip(slot_order(blocks)[:-1], slots[:-1]):
        streams[me_ref[0] ^ slot] = source[...]
    own.wait()
    width = inner // LANES

    def take_stages(part):
        load_fixed[part].wait()
        for table in range(2 * part, 2 * part + 2):
            for block in range(width):
                stages[table, :, pl.ds(block * LANES, LANES)] = fixed[table * width + block].astype(jnp.bfloat16)

    take_stages(0)

    def transform(low, pair):
        sides = [[], []]
        for part in range(2):
            taken = pl.ds(pl.multiple_of(low * group + (2 * pair + part) * chunk, chunk), chunk)
            stream = streams[:, taken].astype(jnp.float32).reshape(blocks, 2, chunk // 2, 2 * LANES)
            for odd in range(2):
                sides[odd].append(stream[:, odd].reshape(part_rows, 2 * LANES).astype(jnp.bfloat16))
        for odd in range(2):
            both = jnp.concatenate(sides[odd], axis=1)
            result = jnp.dot(
                stages[odd], jnp.concatenate([both, both], axis=0), preferred_element_type=jnp.float32
            )
            for part in range(2):
                raws[low % 2][2 * pair + part, odd] = result[:, 2 * part * LANES : 2 * (part + 1) * LANES]

    def first_pass(low, start):
        raw = raws[low % 2]
        real, imaginary = pl.ds(start, 8), pl.ds(part_rows + start, 8)
        for side in range(2):
            lanes = pl.ds(side * LANES, LANES)
            points = [[], []]
            for high in range(4):
                even = (raw[high, 0, real, lanes], raw[high, 0, imaginary, lanes])
                odd = (raw[high, 1, real, lanes], raw[high, 1, imaginary, lanes])
                points[0].append((even[0] + odd[0], even[1] + odd[1]))
                points[1].append((even[0] - odd[0], even[1] - odd[1]))
            for part in range(2):
                upper, lower = pl.ds(part * part_rows + start, 8), pl.ds(inner + part * part_rows + start, 8)
                for high in range(4):
                    if low + high:
                        turns = [turns_ref[2 * (4 * low + high) + i, upper] for i in range(2)]
                        points[part][high] = turned(points[part][high], *turns, -1)
                for k, point in enumerate(four_points(points[part], -1)):
                    point = turn(point, low * k, -1)
                    columns[4 * low + k, upper, lanes] = point[0]
                    columns[4 * low + k, lower, lanes] = point[1]

    def first_rows(low, start, count):
        for part in range(count):
            first_pass(low, pl.multiple_of(start + 8 * part, 8))

    steps = part_rows // 2

    def alone(pair, carry):
        transform(0, pair)
        return carry

    lax.fori_loop(0, 2, alone, 0)
    for low in range(1, 4):
        load_turns[low - 1].wait()

        def beside(pair, carry, low=low):
            transform(low, pair)
            first_rows(low - 1, pair * steps, steps // 8)
            return carry

        lax.fori_loop(0, 2, beside, 0)
    load_turns[3].wait()

    def middle(index, carry):
        start = pl.multiple_of(index * 8, 8)
        first_pass(3, start)
        for part in range(2):
            upper, lower = pl.ds(part * part_rows + start, 8), pl.ds(inner + part * part_rows + start, 8)
            for k in range(4):
                sides = []
                for side in range(2):
                    lanes = pl.ds(side * LANES, LANES)
                    points = [
                        (columns[4 * low + k, upper, lanes], columns[4 * low + k, lower, lanes]) for low in range(4)
                    ]
                    sides.append(four_points(points, -1))
                product = [
                    (a[0] * b[0] - a[1] * b[1], a[0] * b[1] + a[1] * b[0]) for a, b in zip(*sides)
                ]
                for high, point in enumerate(four_points(product, 1)):
                    point = turn(point, k * high, 1)
                    mixed[4 * high + k, upper] = point[0]
                    mixed[4 * high + k, lower] = point[1]
        return carry

    lax.fori_loop(0, part_rows // 8, middle, 0)

    def last_pass(low, start):
        target = halves[low % 2]
        found = []
        for part in range(2):
            upper, lower = pl.ds(part * part_rows + start, 16), pl.ds(inner + part * part_rows + start, 16)
            points = list(four_points([(mixed[4 * low + k, upper], mixed[4 * low + k, lower]) for k in range(4)], 1))
            for high in range(4):
                if low + high:
                    turns = [turns_ref[2 * (4 * low + high) + i, upper] for i in range(2)]
                    points[high] = turned(points[high], *turns, 1)
            found.append(points)
        for high in range(4):
            for i in range(2):
                taken = pl.ds(i * part_rows + start, 16)
                first, second = found[0][high][i], found[1][high][i]
                for odd, value in enumerate((first + second, first - second)):
                    rounded = value.astype(jnp.bfloat16)
                    target[high, odd, taken, pl.ds(0, LANES)] = rounded
                    target[high, odd, taken, pl.ds(LANES, LANES)] = (value - rounded.astype(jnp.float32)).astype(
                        jnp.bfloat16
                    )

    def last_rows(low, start, count):
        for part in range(count):
            last_pass(low, pl.multiple_of(start + 16 * part, 16))

    def restore(low, pair):
        sides = []
        for odd in range(2):
            both = jnp.concatenate([halves[low % 2][2 * pair + part, odd] for part in range(2)], axis=1)
            terms = jnp.dot(stages[2 + odd], both, preferred_element_type=jnp.float32)
            found = []
            for part in range(2):
                first, second = [slice((2 * part + i) * LANES, (2 * part + i + 1) * LANES) for i in range(2)]
                signal = terms[:part_rows, first] + terms[:part_rows, second] + terms[part_rows:, first]
                found.append(signal.reshape(blocks, 1, chunk // 2, LANES))
            sides.append(found)
        for part in range(2):
            signal = jnp.concatenate([sides[0][part], sides[1][part]], axis=1).reshape(blocks, chunk, LANES)
            taken = pl.ds(pl.multiple_of(low * group + (2 * pair + part) * chunk, chunk), chunk)
            signals[:, taken] = signal.astype(jnp.bfloat16)

    def prepare(index, carry):
        last_rows(0, index * steps, steps // 16)
        return carry

    take_stages(1)
    lax.fori_loop(0, 2, prepare, 0)
    for low in range(4):

        def back(pair, carry, low=low):
            restore(low, pair)
            if low < 3:
                last_rows(low + 1, pair * steps, steps // 16)
            return carry

        lax.fori_loop(0, 2, back, 0)
        stores[low].start()
    for store in stores:
        store.wait()


def convolve(me, slots):
    blocks = len(slots)
    rows, lanes = slots[0].shape
    length = blocks * rows
    inner = length // RADIX
    tables = transform_tables(length)
    return pl.pallas_call(
        functools.partial(convolve_kernel, blocks),
        in_specs=[pl.BlockSpec(memory_space=pltpu.SMEM)]
        + [pl.BlockSpec(memory_space=pltpu.VMEM)] * (blocks - 1)
        + [pl.BlockSpec(memory_space=pl.ANY)] * 2,
        out_specs=pl.BlockSpec(memory_space=pl.ANY),
        out_shape=jax.ShapeDtypeStruct((blocks, rows, LANES), jnp.bfloat16),
        scratch_shapes=[
            pltpu.VMEM((blocks, rows, lanes), jnp.bfloat16),
            pltpu.VMEM((2 * RADIX, inner, LANES), jnp.float32),
            pltpu.VMEM((tables.shape[0] - 2 * RADIX, inner, LANES), jnp.float32),
            pltpu.VMEM((4, inner, inner), jnp.bfloat16),
            pltpu.VMEM((4, 2, inner, lanes), jnp.float32),
            pltpu.VMEM((4, 2, inner, lanes), jnp.float32),
            pltpu.VMEM((RADIX, 2 * inner, lanes), jnp.float32),
            pltpu.VMEM((RADIX, 2 * inner, LANES), jnp.float32),
            pltpu.VMEM((4, 2, inner, lanes), jnp.bfloat16),
            pltpu.VMEM((4, 2, inner, lanes), jnp.bfloat16),
            pltpu.VMEM((blocks, rows, LANES), jnp.bfloat16),
            pltpu.SemaphoreType.DMA((11,)),
        ],
        compiler_params=pltpu.CompilerParams(vmem_limit_bytes=CONV_BYTES),
        cost_estimate=pl.CostEstimate(flops=5 * 10**9, bytes_accessed=9 * 10**6, transcendentals=0),
        name="long_convolution",
    )(me, *slots, jnp.asarray(tables))


PIECES = 4


def weight_loads(weight_hbm, weight_ref, side, sems):
    width, features = weight_ref.shape
    columns = pl.ds(pl.multiple_of(side * features, features), features)
    deep = width // PIECES
    loads = []
    for part in range(PIECES):
        rows = pl.ds(part * deep, deep)
        loads.append(pltpu.make_async_copy(weight_hbm.at[rows, columns], weight_ref.at[rows], sems.at[part]))
        loads[part].start()
    return loads


def gate_kernel(
    half_ref, conv_ref, gates_hbm, values_hbm, skip_ref, weight_hbm, gated_ref, out_ref,
    gates_ref, values_ref, weight_ref, sems,
):
    blocks, rows, lanes = conv_ref.shape
    streams = [
        pltpu.make_async_copy(gates_hbm, gates_ref, sems.at[PIECES]),
        pltpu.make_async_copy(values_hbm, values_ref, sems.at[PIECES + 1]),
    ]
    for stream in streams:
        stream.start()
    loads = weight_loads(weight_hbm, weight_ref, 1 - half_ref[0], sems)
    order = row_order(rows, True)
    for stream in streams:
        stream.wait()
    group = blocks // PIECES
    wide = group * lanes
    for part in range(PIECES):
        taken = pl.ds(part * wide, wide)
        conv = jnp.concatenate([conv_ref[part * group + block] for block in range(group)], axis=1)
        conv = jnp.dot(order, conv, preferred_element_type=jnp.float32)
        direct = skip_ref[:, taken] * values_ref[:, taken].astype(jnp.float32)
        gated_ref[:, taken] = (gates_ref[:, taken].astype(jnp.float32) * (conv + direct)).astype(jnp.bfloat16)
    multiply_pieces(loads, gated_ref, weight_ref, out_ref)


def multiply_pieces(loads, gated_ref, weight_ref, out_ref):
    deep = weight_ref.shape[0] // PIECES
    for part in range(PIECES):
        taken = pl.ds(part * deep, deep)
        loads[part].wait()
        term = jnp.dot(gated_ref[:, taken], weight_ref[taken], preferred_element_type=jnp.float32)
        out_ref[...] = term if part == 0 else out_ref[...] + term


def gate_and_project(half, conv, gates, values, skip_gain, weight):
    rows, width = gates.shape
    features = weight.shape[1] // 2
    anywhere, inside = pl.BlockSpec(memory_space=pl.ANY), pl.BlockSpec(memory_space=pltpu.VMEM)
    return pl.pallas_call(
        gate_kernel,
        in_specs=[pl.BlockSpec(memory_space=pltpu.SMEM), inside, anywhere, anywhere, inside, anywhere],
        out_specs=[inside] * 2,
        out_shape=[
            jax.ShapeDtypeStruct((rows, width), jnp.bfloat16),
            jax.ShapeDtypeStruct((rows, features), jnp.float32),
        ],
        scratch_shapes=[
            pltpu.VMEM((rows, width), jnp.bfloat16),
            pltpu.VMEM((rows, width), jnp.bfloat16),
            pltpu.VMEM((width, features), jnp.bfloat16),
            pltpu.SemaphoreType.DMA((PIECES + 2,)),
        ],
        compiler_params=pltpu.CompilerParams(vmem_limit_bytes=TAIL_BYTES),
        cost_estimate=pl.CostEstimate(
            flops=2 * rows * width * features, bytes_accessed=2 * width * features, transcendentals=0
        ),
        name="gate_project_sent",
    )(half, conv, gates, values, skip_gain[None, :], weight)


def kept_kernel(half_ref, gated_ref, weight_hbm, out_ref, weight_ref, sems):
    multiply_pieces(weight_loads(weight_hbm, weight_ref, half_ref[0], sems), gated_ref, weight_ref, out_ref)


def project_kept(half, gated, weight):
    rows, width = gated.shape
    features = weight.shape[1] // 2
    inside = pl.BlockSpec(memory_space=pltpu.VMEM)
    return pl.pallas_call(
        kept_kernel,
        in_specs=[pl.BlockSpec(memory_space=pltpu.SMEM), inside, pl.BlockSpec(memory_space=pl.ANY)],
        out_specs=inside,
        out_shape=jax.ShapeDtypeStruct((rows, features), jnp.float32),
        scratch_shapes=[pltpu.VMEM((width, features), jnp.bfloat16), pltpu.SemaphoreType.DMA((PIECES,))],
        compiler_params=pltpu.CompilerParams(vmem_limit_bytes=TAIL_BYTES),
        cost_estimate=pl.CostEstimate(
            flops=2 * rows * width * features, bytes_accessed=2 * width * features, transcendentals=0
        ),
        name="project_kept",
    )(half, gated, weight)


def join_kernel(kept_ref, came_ref, out_hbm, out_ref, sems):
    wide = out_ref.shape[0] // PIECES
    stores = []
    for part in range(PIECES):
        taken = pl.ds(part * wide, wide)
        out_ref[taken] = (kept_ref[:, taken] + came_ref[:, taken]).astype(jnp.bfloat16).T
        stores.append(pltpu.make_async_copy(out_ref.at[taken], out_hbm.at[taken], sems.at[part]))
        stores[part].start()
    for store in stores:
        store.wait()


def join(kept, came):
    rows, features = kept.shape
    return pl.pallas_call(
        join_kernel,
        in_specs=[pl.BlockSpec(memory_space=pltpu.VMEM)] * 2,
        out_specs=pl.BlockSpec(memory_space=pl.ANY),
        out_shape=jax.ShapeDtypeStruct((features, rows), jnp.bfloat16),
        scratch_shapes=[pltpu.VMEM((features, rows), jnp.bfloat16), pltpu.SemaphoreType.DMA((PIECES,))],
        compiler_params=pltpu.CompilerParams(vmem_limit_bytes=TAIL_BYTES),
        name="join_halves",
    )(kept, came)


def swap_blocks(array):
    return lax.all_to_all(array, "seq", split_axis=0, concat_axis=0, tiled=True)


def exchange(slots):
    blocks = len(slots)
    return [
        lax.ppermute(source, "seq", [(j, j ^ slot) for j in range(blocks)]) if slot else source
        for slot, source in zip(slot_order(blocks), slots)
    ]


def kernel_local(values, gates, filter_taps, skip_gain, out_weight):
    blocks = lax.axis_size("seq")
    me = lax.axis_index("seq").astype(jnp.int32)[None]
    half = lax.axis_index("chan").astype(jnp.int32)[None]
    conv = convolve(me, exchange(arrange(me, values, filter_taps, blocks)))
    gated, sent = gate_and_project(half, swap_blocks(conv), gates, values, skip_gain, out_weight)
    other = lax.ppermute(sent, "chan", [(0, 1), (1, 0)])
    kept = project_kept(half, gated, out_weight)
    return join(kept, other)


def takes_kernels(mesh, values, out_weight):
    blocks, halves = mesh.shape["seq"], mesh.shape["chan"]
    rows = values.shape[0] // blocks
    return (
        halves == 2
        and blocks == 16
        and rows == 256
        and values.shape[1] == halves * blocks * LANES
        and out_weight.shape[1] % (8 * LANES) == 0
    )


def solution(mesh):
    placed = (P("seq", "chan"), P("seq", "chan"), P("seq", "chan"), P("chan"), P("chan", None))

    def whole(values, gates, filter_taps, skip_gain, out_weight):
        local = kernel_local if takes_kernels(mesh, values, out_weight) else general_local
        return jax.shard_map(
            local, mesh=mesh, in_specs=placed, out_specs=P("chan", "seq"), check_vma=False
        )(values, gates, filter_taps, skip_gain, out_weight)

    return whole
```

```python
import functools
import math

import jax
import jax.numpy as jnp
import ml_dtypes
import numpy as np
from jax import lax
from jax.experimental import pallas as pl
from jax.experimental.pallas import tpu as pltpu
from jax.sharding import PartitionSpec as P

TWO_PI = 2.0 * math.pi
HIGH = lax.Precision.HIGHEST
RADIX = 16
LANES = 128
Q_ORDER = [low + 4 * high for low in range(4) for high in range(4)]
FIRST_BYTES = 60 * 1024 * 1024
ARRANGE_BYTES = 12 * 1024 * 1024
CONV_BYTES = 49 * 1024 * 1024
TAIL_BYTES = 49 * 1024 * 1024


def angle_table(first, second, period):
    product = first[:, None] * second[None, :] % period
    angles = product.astype(jnp.float32) * (TWO_PI / period)
    return (jnp.cos(angles), jnp.sin(angles))


def mix(equation, left, right):
    return jnp.einsum(equation, left, right, precision=HIGH)


def outer_forward(data, outer_cos, outer_sin, twist_cos, twist_sin, equation):
    source = data.astype(jnp.float32)
    real = mix(equation, outer_cos, source)
    imag = -mix(equation, outer_sin, source)
    cos_part = twist_cos[:, :, None]
    sin_part = twist_sin[:, :, None]
    return (real * cos_part + imag * sin_part, imag * cos_part - real * sin_part)


def inner_filter(spectra, inner_cos, inner_sin):
    value_re, value_im, taps_re, taps_im = spectra

    def forward(real, imag):
        out_re = mix("kr,jrc->jkc", inner_cos, real) + mix("kr,jrc->jkc", inner_sin, imag)
        out_im = mix("kr,jrc->jkc", inner_cos, imag) - mix("kr,jrc->jkc", inner_sin, real)
        return (out_re, out_im)

    value_fre, value_fim = forward(value_re, value_im)
    taps_fre, taps_fim = forward(taps_re, taps_im)
    prod_re = value_fre * taps_fre - value_fim * taps_fim
    prod_im = value_fre * taps_fim + value_fim * taps_fre
    back_re = mix("rk,jkc->jrc", inner_cos, prod_re) - mix("rk,jkc->jrc", inner_sin, prod_im)
    back_im = mix("rk,jkc->jrc", inner_cos, prod_im) + mix("rk,jkc->jrc", inner_sin, prod_re)
    return (back_re, back_im)


def untwist(real, imag, twist_cos, twist_sin):
    cos_part = twist_cos[:, :, None]
    sin_part = twist_sin[:, :, None]
    return (real * cos_part - imag * sin_part, imag * cos_part + real * sin_part)


def channels_plan(values, filter_taps):
    rows, width = values.shape
    blocks = lax.axis_size("seq")
    length = 2 * blocks * rows
    narrow = width // blocks
    whole_values, whole_taps = (
        lax.all_to_all(values, "seq", split_axis=1, concat_axis=0, tiled=True),
        lax.all_to_all(filter_taps, "seq", split_axis=1, concat_axis=0, tiled=True),
    )
    freq_ids = jnp.arange(2 * blocks, dtype=jnp.int32)
    block_ids = jnp.arange(blocks, dtype=jnp.int32)
    all_rows = jnp.arange(rows, dtype=jnp.int32)
    outer_cos, outer_sin = angle_table(freq_ids, block_ids, 2 * blocks)
    twist_cos, twist_sin = angle_table(freq_ids, all_rows, length)
    tables = (outer_cos, outer_sin, twist_cos, twist_sin, "ka,arc->krc")
    value_re, value_im = outer_forward(whole_values.reshape(blocks, rows, narrow), *tables)
    taps_re, taps_im = outer_forward(whole_taps.reshape(blocks, rows, narrow), *tables)
    inner_cos, inner_sin = angle_table(all_rows, all_rows, rows)
    back_re, back_im = inner_filter((value_re, value_im, taps_re, taps_im), inner_cos, inner_sin)
    turned_re, turned_im = untwist(back_re, back_im, twist_cos, twist_sin)
    final_cos, final_sin = angle_table(block_ids, freq_ids, 2 * blocks)
    signal = (
        mix("ak,krc->arc", final_cos, turned_re) - mix("ak,krc->arc", final_sin, turned_im)
    ) / length
    returned = lax.all_to_all(signal, "seq", split_axis=0, concat_axis=2, tiled=True)
    return returned[0]


def general_local(values, gates, filter_taps, skip_gain, out_weight):
    conv = channels_plan(values, filter_taps)
    gated = (
        gates.astype(jnp.float32) * (conv + skip_gain[None, :] * values.astype(jnp.float32))
    ).astype(jnp.bfloat16)
    projected = lax.psum_scatter(
        lax.dot_general(
            out_weight, gated, (((0,), (1,)), ((), ())), preferred_element_type=jnp.float32
        ),
        "chan",
        scatter_dimension=0,
        tiled=True,
    )
    return projected.astype(jnp.bfloat16)


def split_table(table):
    high = table.astype(ml_dtypes.bfloat16)
    low = (table - high.astype(np.float64)).astype(ml_dtypes.bfloat16)
    return high, low


@functools.lru_cache(maxsize=None)
def transform_tables(length):
    inner = length // RADIX
    k = np.arange(inner)[:, None]
    unit = TWO_PI / (4 * length)
    turns = (np.array(Q_ORDER)[:, None] * (4 * k.T + 1)) % (4 * length) * unit
    turns = np.stack([np.cos(turns), np.sin(turns)], axis=1).reshape(2 * RADIX, inner, 1)
    blocks = [np.broadcast_to(turns, (2 * RADIX, inner, LANES))]
    forward, backward = [], []
    for odd in range(2):
        m = 2 * np.arange(inner // 2)[None, :] + odd
        angles = (RADIX * m * (4 * k[: inner // 2] + 1)) % (4 * length) * unit
        table = np.concatenate([np.cos(angles), -np.sin(angles)], axis=0)
        forward.append(np.concatenate(split_table(table), axis=1))
        backward.append(np.concatenate(split_table(table.T / length), axis=0))
    for table in forward + backward:
        blocks.append(table.astype(np.float32).reshape(inner, -1, LANES).swapaxes(0, 1))
    return np.concatenate(blocks, axis=0).astype(np.float32)


def row_order(rows, turned_over=False):
    place = lax.broadcasted_iota(jnp.int32, (rows, rows), 1 if turned_over else 0)
    source = lax.broadcasted_iota(jnp.int32, (rows, rows), 0 if turned_over else 1)
    chunk = rows // RADIX
    index, within = place // chunk, place % chunk
    odd, j = within // (chunk // 2), within % (chunk // 2)
    wanted = RADIX * (2 * j + odd) + index // 4 + 4 * (index % 4)
    return jnp.where(source == wanted, 1.0, 0.0).astype(jnp.bfloat16)


def turn(point, index, sign):
    re, im = point
    index %= 16
    if index == 0:
        return point
    if index == 4:
        return (-im, re) if sign > 0 else (im, -re)
    if index == 8:
        return (-re, -im)
    half = math.sqrt(0.5)
    if index == 2:
        return ((re - im) * half, (re + im) * half) if sign > 0 else ((re + im) * half, (im - re) * half)
    if index == 6:
        return ((-re - im) * half, (re - im) * half) if sign > 0 else ((im - re) * half, (-re - im) * half)
    cos = math.cos(TWO_PI * index / 16)
    sin = sign * math.sin(TWO_PI * index / 16)
    return (re * cos - im * sin, re * sin + im * cos)


def four_points(points, sign):
    a, b, c, d = points
    ac = (a[0] + c[0], a[1] + c[1])
    am = (a[0] - c[0], a[1] - c[1])
    bd = (b[0] + d[0], b[1] + d[1])
    bm = (b[0] - d[0], b[1] - d[1])
    if sign < 0:
        side = (bm[1], -bm[0])
    else:
        side = (-bm[1], bm[0])
    return (
        (ac[0] + bd[0], ac[1] + bd[1]),
        (am[0] + side[0], am[1] + side[1]),
        (ac[0] - bd[0], ac[1] - bd[1]),
        (am[0] - side[0], am[1] - side[1]),
    )


def turned(point, cos, sin, sign):
    re, im = point
    if sign < 0:
        return (re * cos + im * sin, im * cos - re * sin)
    return (re * cos - im * sin, im * cos + re * sin)


def slot_order(blocks):
    half = blocks // 2
    across = [half + (i // 2 if i % 2 == 0 else half // 2 + i // 2) for i in range(half)]
    near = list(range(1, half)) + [0]
    return [slot for pair in zip(across, near) for slot in pair]


LEAD = 5


def lead_kernel(blocks, me_ref, values_hbm, taps_hbm, *rest):
    outs, (streams, sems) = rest[:LEAD], rest[LEAD:]
    loads = []
    for i, slot in enumerate(slot_order(blocks)[:LEAD]):
        lanes = pl.ds(pl.multiple_of((me_ref[0] ^ slot) * LANES, LANES), LANES)
        for side, source in enumerate((values_hbm, taps_hbm)):
            to = pl.ds((2 * i + side) * LANES, LANES)
            loads.append(pltpu.make_async_copy(source.at[:, lanes], streams.at[:, to], sems.at[2 * i + side]))
    for load in loads:
        load.start()
    order = row_order(streams.shape[0])
    for load in loads:
        load.wait()
    moved = jnp.dot(order, streams[...], preferred_element_type=jnp.float32).astype(jnp.bfloat16)
    for i, out in enumerate(outs):
        out[...] = moved[:, 2 * i * LANES : 2 * (i + 1) * LANES]


def arrange_kernel(pieces, blocks, me_ref, values_hbm, taps_hbm, *rest):
    outs, (values_ref, taps_ref, packed, sems) = rest[: blocks - LEAD], rest[blocks - LEAD :]
    piece = values_ref.shape[1] // pieces
    loads = []
    for part in range(pieces):
        lanes = pl.ds(part * piece, piece)
        loads.append(pltpu.make_async_copy(values_hbm.at[:, lanes], values_ref.at[:, lanes], sems.at[2 * part]))
        loads.append(pltpu.make_async_copy(taps_hbm.at[:, lanes], taps_ref.at[:, lanes], sems.at[2 * part + 1]))
    for load in loads:
        load.start()
    order = row_order(values_ref.shape[0])
    for part in range(pieces):
        loads[2 * part].wait()
        loads[2 * part + 1].wait()
        lanes = pl.ds(part * piece, piece)
        both = jnp.concatenate([values_ref[:, lanes], taps_ref[:, lanes]], axis=1)
        moved = jnp.dot(order, both, preferred_element_type=jnp.float32).astype(jnp.bfloat16)
        for block in range(piece // LANES):
            for side in range(2):
                start = side * piece + block * LANES
                packed[part * piece // LANES + block, :, pl.ds(side * LANES, LANES)] = moved[:, start : start + LANES]
    for out, slot in zip(outs, slot_order(blocks)[LEAD:]):
        out[...] = packed[me_ref[0] ^ slot]


def arrange(me, values, taps, blocks):
    rows, wide = values.shape
    pieces = 4
    block = jax.ShapeDtypeStruct((rows, 2 * LANES), jnp.bfloat16)
    in_specs = [pl.BlockSpec(memory_space=pltpu.SMEM)] + [pl.BlockSpec(memory_space=pl.ANY)] * 2
    lead = pl.pallas_call(
        functools.partial(lead_kernel, blocks),
        in_specs=in_specs,
        out_specs=[pl.BlockSpec(memory_space=pltpu.VMEM)] * LEAD,
        out_shape=[block] * LEAD,
        scratch_shapes=[
            pltpu.VMEM((rows, 2 * LEAD * LANES), jnp.bfloat16),
            pltpu.SemaphoreType.DMA((2 * LEAD,)),
        ],
        compiler_params=pltpu.CompilerParams(vmem_limit_bytes=FIRST_BYTES),
        cost_estimate=pl.CostEstimate(
            flops=4 * rows * rows * LEAD * LANES, bytes_accessed=8 * rows * LEAD * LANES, transcendentals=0
        ),
        name="arrange_lead",
    )(me, values, taps)
    others = pl.pallas_call(
        functools.partial(arrange_kernel, pieces, blocks),
        in_specs=in_specs,
        out_specs=[pl.BlockSpec(memory_space=pltpu.VMEM)] * (blocks - LEAD),
        out_shape=[block] * (blocks - LEAD),
        scratch_shapes=[
            pltpu.VMEM((rows, wide), jnp.bfloat16),
            pltpu.VMEM((rows, wide), jnp.bfloat16),
            pltpu.VMEM((blocks, rows, 2 * LANES), jnp.bfloat16),
            pltpu.SemaphoreType.DMA((2 * pieces,)),
        ],
        compiler_params=pltpu.CompilerParams(vmem_limit_bytes=ARRANGE_BYTES),
        cost_estimate=pl.CostEstimate(
            flops=4 * rows * rows * wide, bytes_accessed=8 * rows * wide, transcendentals=0
        ),
        name="arrange_others",
    )(me, values, taps)
    return [*lead, *others]


def convolve_kernel(blocks, me_ref, *rest):
    slots = rest[:blocks]
    convolve_blocks(me_ref, slots, *rest[blocks:])


def convolve_blocks(
    me_ref, slots, tables_hbm, out_hbm,
    streams, turns_ref, fixed, stages, raw_even, raw_odd, columns, mixed, halves_even, halves_odd, signals, sems,
):
    blocks, rows, _ = streams.shape
    chunk = rows // RADIX
    inner = blocks * chunk
    part_rows = inner // 2
    group = rows // 4
    raws = (raw_even, raw_odd)
    halves = (halves_even, halves_odd)
    count = fixed.shape[0]
    load_fixed = []
    for part in range(2):
        taken = pl.ds(part * count // 2, count // 2)
        source = tables_hbm.at[pl.ds(2 * RADIX + part * count // 2, count // 2)]
        load_fixed.append(pltpu.make_async_copy(source, fixed.at[taken], sems.at[10 * part]))
    load_turns, stores = [], []
    for low in range(4):
        taken = pl.ds(low * group, group)
        eight = pl.ds(8 * low, 8)
        load_turns.append(pltpu.make_async_copy(tables_hbm.at[eight], turns_ref.at[eight], sems.at[1 + low]))
        stores.append(pltpu.make_async_copy(signals.at[:, taken], out_hbm.at[:, taken], sems.at[5 + low]))
    load_fixed[0].start()
    for load in load_turns:
        load.start()
    load_fixed[1].start()
    own = pltpu.make_async_copy(slots[-1], streams.at[me_ref[0]], sems.at[9])
    own.start()
    for slot, source in zip(slot_order(blocks)[:-1], slots[:-1]):
        streams[me_ref[0] ^ slot] = source[...]
    own.wait()
    width = inner // LANES

    def take_stages(part):
        load_fixed[part].wait()
        for table in range(2 * part, 2 * part + 2):
            for block in range(width):
                stages[table, :, pl.ds(block * LANES, LANES)] = fixed[table * width + block].astype(jnp.bfloat16)

    take_stages(0)

    def transform(low, pair):
        sides = [[], []]
        for part in range(2):
            taken = pl.ds(pl.multiple_of(low * group + (2 * pair + part) * chunk, chunk), chunk)
            stream = streams[:, taken].astype(jnp.float32).reshape(blocks, 2, chunk // 2, 2 * LANES)
            for odd in range(2):
                sides[odd].append(stream[:, odd].reshape(part_rows, 2 * LANES).astype(jnp.bfloat16))
        for odd in range(2):
            both = jnp.concatenate(sides[odd], axis=1)
            result = jnp.dot(
                stages[odd], jnp.concatenate([both, both], axis=0), preferred_element_type=jnp.float32
            )
            for part in range(2):
                raws[low % 2][2 * pair + part, odd] = result[:, 2 * part * LANES : 2 * (part + 1) * LANES]

    def first_pass(low, start):
        raw = raws[low % 2]
        real, imaginary = pl.ds(start, 8), pl.ds(part_rows + start, 8)
        for side in range(2):
            lanes = pl.ds(side * LANES, LANES)
            points = [[], []]
            for high in range(4):
                even = (raw[high, 0, real, lanes], raw[high, 0, imaginary, lanes])
                odd = (raw[high, 1, real, lanes], raw[high, 1, imaginary, lanes])
                points[0].append((even[0] + odd[0], even[1] + odd[1]))
                points[1].append((even[0] - odd[0], even[1] - odd[1]))
            for part in range(2):
                upper, lower = pl.ds(part * part_rows + start, 8), pl.ds(inner + part * part_rows + start, 8)
                for high in range(4):
                    if low + high:
                        turns = [turns_ref[2 * (4 * low + high) + i, upper] for i in range(2)]
                        points[part][high] = turned(points[part][high], *turns, -1)
                for k, point in enumerate(four_points(points[part], -1)):
                    point = turn(point, low * k, -1)
                    columns[4 * low + k, upper, lanes] = point[0]
                    columns[4 * low + k, lower, lanes] = point[1]

    def first_rows(low, start, count):
        for part in range(count):
            first_pass(low, pl.multiple_of(start + 8 * part, 8))

    steps = part_rows // 2

    def alone(pair, carry):
        transform(0, pair)
        return carry

    lax.fori_loop(0, 2, alone, 0)
    for low in range(1, 4):
        load_turns[low - 1].wait()

        def beside(pair, carry, low=low):
            transform(low, pair)
            first_rows(low - 1, pair * steps, steps // 8)
            return carry

        lax.fori_loop(0, 2, beside, 0)
    load_turns[3].wait()

    def middle(index, carry):
        start = pl.multiple_of(index * 8, 8)
        first_pass(3, start)
        for part in range(2):
            upper, lower = pl.ds(part * part_rows + start, 8), pl.ds(inner + part * part_rows + start, 8)
            for k in range(4):
                sides = []
                for side in range(2):
                    lanes = pl.ds(side * LANES, LANES)
                    points = [
                        (columns[4 * low + k, upper, lanes], columns[4 * low + k, lower, lanes]) for low in range(4)
                    ]
                    sides.append(four_points(points, -1))
                product = [
                    (a[0] * b[0] - a[1] * b[1], a[0] * b[1] + a[1] * b[0]) for a, b in zip(*sides)
                ]
                for high, point in enumerate(four_points(product, 1)):
                    point = turn(point, k * high, 1)
                    mixed[4 * high + k, upper] = point[0]
                    mixed[4 * high + k, lower] = point[1]
        return carry

    lax.fori_loop(0, part_rows // 8, middle, 0)

    def last_pass(low, start):
        target = halves[low % 2]
        found = []
        for part in range(2):
            upper, lower = pl.ds(part * part_rows + start, 16), pl.ds(inner + part * part_rows + start, 16)
            points = list(four_points([(mixed[4 * low + k, upper], mixed[4 * low + k, lower]) for k in range(4)], 1))
            for high in range(4):
                if low + high:
                    turns = [turns_ref[2 * (4 * low + high) + i, upper] for i in range(2)]
                    points[high] = turned(points[high], *turns, 1)
            found.append(points)
        for high in range(4):
            for i in range(2):
                taken = pl.ds(i * part_rows + start, 16)
                first, second = found[0][high][i], found[1][high][i]
                for odd, value in enumerate((first + second, first - second)):
                    rounded = value.astype(jnp.bfloat16)
                    target[high, odd, taken, pl.ds(0, LANES)] = rounded
                    target[high, odd, taken, pl.ds(LANES, LANES)] = (value - rounded.astype(jnp.float32)).astype(
                        jnp.bfloat16
                    )

    def last_rows(low, start, count):
        for part in range(count):
            last_pass(low, pl.multiple_of(start + 16 * part, 16))

    def restore(low, pair):
        sides = []
        for odd in range(2):
            both = jnp.concatenate([halves[low % 2][2 * pair + part, odd] for part in range(2)], axis=1)
            terms = jnp.dot(stages[2 + odd], both, preferred_element_type=jnp.float32)
            found = []
            for part in range(2):
                first, second = [slice((2 * part + i) * LANES, (2 * part + i + 1) * LANES) for i in range(2)]
                signal = terms[:part_rows, first] + terms[:part_rows, second] + terms[part_rows:, first]
                found.append(signal.reshape(blocks, 1, chunk // 2, LANES))
            sides.append(found)
        for part in range(2):
            signal = jnp.concatenate([sides[0][part], sides[1][part]], axis=1).reshape(blocks, chunk, LANES)
            taken = pl.ds(pl.multiple_of(low * group + (2 * pair + part) * chunk, chunk), chunk)
            signals[:, taken] = signal.astype(jnp.bfloat16)

    def prepare(index, carry):
        last_rows(0, index * steps, steps // 16)
        return carry

    take_stages(1)
    lax.fori_loop(0, 2, prepare, 0)
    for low in range(4):

        def back(pair, carry, low=low):
            restore(low, pair)
            if low < 3:
                last_rows(low + 1, pair * steps, steps // 16)
            return carry

        lax.fori_loop(0, 2, back, 0)
        stores[low].start()
    for store in stores:
        store.wait()


def convolve(me, slots):
    blocks = len(slots)
    rows, lanes = slots[0].shape
    length = blocks * rows
    inner = length // RADIX
    tables = transform_tables(length)
    return pl.pallas_call(
        functools.partial(convolve_kernel, blocks),
        in_specs=[pl.BlockSpec(memory_space=pltpu.SMEM)]
        + [pl.BlockSpec(memory_space=pltpu.VMEM)] * (blocks - 1)
        + [pl.BlockSpec(memory_space=pl.ANY)] * 2,
        out_specs=pl.BlockSpec(memory_space=pl.ANY),
        out_shape=jax.ShapeDtypeStruct((blocks, rows, LANES), jnp.bfloat16),
        scratch_shapes=[
            pltpu.VMEM((blocks, rows, lanes), jnp.bfloat16),
            pltpu.VMEM((2 * RADIX, inner, LANES), jnp.float32),
            pltpu.VMEM((tables.shape[0] - 2 * RADIX, inner, LANES), jnp.float32),
            pltpu.VMEM((4, inner, inner), jnp.bfloat16),
            pltpu.VMEM((4, 2, inner, lanes), jnp.float32),
            pltpu.VMEM((4, 2, inner, lanes), jnp.float32),
            pltpu.VMEM((RADIX, 2 * inner, lanes), jnp.float32),
            pltpu.VMEM((RADIX, 2 * inner, LANES), jnp.float32),
            pltpu.VMEM((4, 2, inner, lanes), jnp.bfloat16),
            pltpu.VMEM((4, 2, inner, lanes), jnp.bfloat16),
            pltpu.VMEM((blocks, rows, LANES), jnp.bfloat16),
            pltpu.SemaphoreType.DMA((11,)),
        ],
        compiler_params=pltpu.CompilerParams(vmem_limit_bytes=CONV_BYTES),
        cost_estimate=pl.CostEstimate(flops=5 * 10**9, bytes_accessed=9 * 10**6, transcendentals=0),
        name="long_convolution",
    )(me, *slots, jnp.asarray(tables))


PIECES = 4


def weight_loads(weight_hbm, weight_ref, side, sems):
    width, features = weight_ref.shape
    columns = pl.ds(pl.multiple_of(side * features, features), features)
    deep = width // PIECES
    loads = []
    for part in range(PIECES):
        rows = pl.ds(part * deep, deep)
        loads.append(pltpu.make_async_copy(weight_hbm.at[rows, columns], weight_ref.at[rows], sems.at[part]))
        loads[part].start()
    return loads


def gate_kernel(
    half_ref, conv_ref, gates_hbm, values_hbm, skip_ref, weight_hbm, gated_ref, out_ref,
    gates_ref, values_ref, weight_ref, sems,
):
    blocks, rows, lanes = conv_ref.shape
    streams = [
        pltpu.make_async_copy(gates_hbm, gates_ref, sems.at[PIECES]),
        pltpu.make_async_copy(values_hbm, values_ref, sems.at[PIECES + 1]),
    ]
    for stream in streams:
        stream.start()
    loads = weight_loads(weight_hbm, weight_ref, 1 - half_ref[0], sems)
    order = row_order(rows, True)
    for stream in streams:
        stream.wait()
    group = blocks // PIECES
    wide = group * lanes
    for part in range(PIECES):
        taken = pl.ds(part * wide, wide)
        conv = jnp.concatenate([conv_ref[part * group + block] for block in range(group)], axis=1)
        conv = jnp.dot(order, conv, preferred_element_type=jnp.float32)
        direct = skip_ref[:, taken] * values_ref[:, taken].astype(jnp.float32)
        gated_ref[:, taken] = (gates_ref[:, taken].astype(jnp.float32) * (conv + direct)).astype(jnp.bfloat16)
    multiply_pieces(loads, gated_ref, weight_ref, out_ref)


def multiply_pieces(loads, gated_ref, weight_ref, out_ref):
    deep = weight_ref.shape[0] // PIECES
    for part in range(PIECES):
        taken = pl.ds(part * deep, deep)
        loads[part].wait()
        term = jnp.dot(gated_ref[:, taken], weight_ref[taken], preferred_element_type=jnp.float32)
        out_ref[...] = term if part == 0 else out_ref[...] + term


def gate_and_project(half, conv, gates, values, skip_gain, weight):
    rows, width = gates.shape
    features = weight.shape[1] // 2
    anywhere, inside = pl.BlockSpec(memory_space=pl.ANY), pl.BlockSpec(memory_space=pltpu.VMEM)
    return pl.pallas_call(
        gate_kernel,
        in_specs=[pl.BlockSpec(memory_space=pltpu.SMEM), inside, anywhere, anywhere, inside, anywhere],
        out_specs=[inside] * 2,
        out_shape=[
            jax.ShapeDtypeStruct((rows, width), jnp.bfloat16),
            jax.ShapeDtypeStruct((rows, features), jnp.float32),
        ],
        scratch_shapes=[
            pltpu.VMEM((rows, width), jnp.bfloat16),
            pltpu.VMEM((rows, width), jnp.bfloat16),
            pltpu.VMEM((width, features), jnp.bfloat16),
            pltpu.SemaphoreType.DMA((PIECES + 2,)),
        ],
        compiler_params=pltpu.CompilerParams(vmem_limit_bytes=TAIL_BYTES),
        cost_estimate=pl.CostEstimate(
            flops=2 * rows * width * features, bytes_accessed=2 * width * features, transcendentals=0
        ),
        name="gate_project_sent",
    )(half, conv, gates, values, skip_gain[None, :], weight)


def kept_kernel(half_ref, gated_ref, weight_hbm, out_ref, weight_ref, sems):
    multiply_pieces(weight_loads(weight_hbm, weight_ref, half_ref[0], sems), gated_ref, weight_ref, out_ref)


def project_kept(half, gated, weight):
    rows, width = gated.shape
    features = weight.shape[1] // 2
    inside = pl.BlockSpec(memory_space=pltpu.VMEM)
    return pl.pallas_call(
        kept_kernel,
        in_specs=[pl.BlockSpec(memory_space=pltpu.SMEM), inside, pl.BlockSpec(memory_space=pl.ANY)],
        out_specs=inside,
        out_shape=jax.ShapeDtypeStruct((rows, features), jnp.float32),
        scratch_shapes=[pltpu.VMEM((width, features), jnp.bfloat16), pltpu.SemaphoreType.DMA((PIECES,))],
        compiler_params=pltpu.CompilerParams(vmem_limit_bytes=TAIL_BYTES),
        cost_estimate=pl.CostEstimate(
            flops=2 * rows * width * features, bytes_accessed=2 * width * features, transcendentals=0
        ),
        name="project_kept",
    )(half, gated, weight)


def join_kernel(kept_ref, came_ref, out_hbm, out_ref, sems):
    wide = out_ref.shape[0] // PIECES
    stores = []
    for part in range(PIECES):
        taken = pl.ds(part * wide, wide)
        out_ref[taken] = (kept_ref[:, taken] + came_ref[:, taken]).astype(jnp.bfloat16).T
        stores.append(pltpu.make_async_copy(out_ref.at[taken], out_hbm.at[taken], sems.at[part]))
        stores[part].start()
    for store in stores:
        store.wait()


def join(kept, came):
    rows, features = kept.shape
    return pl.pallas_call(
        join_kernel,
        in_specs=[pl.BlockSpec(memory_space=pltpu.VMEM)] * 2,
        out_specs=pl.BlockSpec(memory_space=pl.ANY),
        out_shape=jax.ShapeDtypeStruct((features, rows), jnp.bfloat16),
        scratch_shapes=[pltpu.VMEM((features, rows), jnp.bfloat16), pltpu.SemaphoreType.DMA((PIECES,))],
        compiler_params=pltpu.CompilerParams(vmem_limit_bytes=TAIL_BYTES),
        name="join_halves",
    )(kept, came)


def swap_blocks(array):
    return lax.all_to_all(array, "seq", split_axis=0, concat_axis=0, tiled=True)


def exchange(slots):
    blocks = len(slots)
    return [
        lax.ppermute(source, "seq", [(j, j ^ slot) for j in range(blocks)]) if slot else source
        for slot, source in zip(slot_order(blocks), slots)
    ]


def kernel_local(values, gates, filter_taps, skip_gain, out_weight):
    blocks = lax.axis_size("seq")
    me = lax.axis_index("seq").astype(jnp.int32)[None]
    half = lax.axis_index("chan").astype(jnp.int32)[None]
    conv = convolve(me, exchange(arrange(me, values, filter_taps, blocks)))
    gated, sent = gate_and_project(half, swap_blocks(conv), gates, values, skip_gain, out_weight)
    other = lax.ppermute(sent, "chan", [(0, 1), (1, 0)])
    kept = project_kept(half, gated, out_weight)
    return join(kept, other)


def takes_kernels(mesh, values, out_weight):
    blocks, halves = mesh.shape["seq"], mesh.shape["chan"]
    rows = values.shape[0] // blocks
    return (
        halves == 2
        and blocks == 16
        and rows == 256
        and values.shape[1] == halves * blocks * LANES
        and out_weight.shape[1] % (8 * LANES) == 0
    )


def solution(mesh):
    placed = (P("seq", "chan"), P("seq", "chan"), P("seq", "chan"), P("chan"), P("chan", None))

    def whole(values, gates, filter_taps, skip_gain, out_weight):
        local = kernel_local if takes_kernels(mesh, values, out_weight) else general_local
        return jax.shard_map(
            local, mesh=mesh, in_specs=placed, out_specs=P("chan", "seq"), check_vma=False
        )(values, gates, filter_taps, skip_gain, out_weight)

    return whole
```

```python
import functools
import math

import jax
import jax.numpy as jnp
import ml_dtypes
import numpy as np
from jax import lax
from jax.experimental import pallas as pl
from jax.experimental.pallas import tpu as pltpu
from jax.sharding import PartitionSpec as P

TWO_PI = 2.0 * math.pi
HIGH = lax.Precision.HIGHEST
RADIX = 16
LANES = 128
Q_ORDER = [low + 4 * high for low in range(4) for high in range(4)]
FIRST_BYTES = 60 * 1024 * 1024
ARRANGE_BYTES = 12 * 1024 * 1024
CONV_BYTES = 49 * 1024 * 1024
TAIL_BYTES = 49 * 1024 * 1024


def angle_table(first, second, period):
    product = first[:, None] * second[None, :] % period
    angles = product.astype(jnp.float32) * (TWO_PI / period)
    return (jnp.cos(angles), jnp.sin(angles))


def mix(equation, left, right):
    return jnp.einsum(equation, left, right, precision=HIGH)


def outer_forward(data, outer_cos, outer_sin, twist_cos, twist_sin, equation):
    source = data.astype(jnp.float32)
    real = mix(equation, outer_cos, source)
    imag = -mix(equation, outer_sin, source)
    cos_part = twist_cos[:, :, None]
    sin_part = twist_sin[:, :, None]
    return (real * cos_part + imag * sin_part, imag * cos_part - real * sin_part)


def inner_filter(spectra, inner_cos, inner_sin):
    value_re, value_im, taps_re, taps_im = spectra

    def forward(real, imag):
        out_re = mix("kr,jrc->jkc", inner_cos, real) + mix("kr,jrc->jkc", inner_sin, imag)
        out_im = mix("kr,jrc->jkc", inner_cos, imag) - mix("kr,jrc->jkc", inner_sin, real)
        return (out_re, out_im)

    value_fre, value_fim = forward(value_re, value_im)
    taps_fre, taps_fim = forward(taps_re, taps_im)
    prod_re = value_fre * taps_fre - value_fim * taps_fim
    prod_im = value_fre * taps_fim + value_fim * taps_fre
    back_re = mix("rk,jkc->jrc", inner_cos, prod_re) - mix("rk,jkc->jrc", inner_sin, prod_im)
    back_im = mix("rk,jkc->jrc", inner_cos, prod_im) + mix("rk,jkc->jrc", inner_sin, prod_re)
    return (back_re, back_im)


def untwist(real, imag, twist_cos, twist_sin):
    cos_part = twist_cos[:, :, None]
    sin_part = twist_sin[:, :, None]
    return (real * cos_part - imag * sin_part, imag * cos_part + real * sin_part)


def channels_plan(values, filter_taps):
    rows, width = values.shape
    blocks = lax.axis_size("seq")
    length = 2 * blocks * rows
    narrow = width // blocks
    whole_values, whole_taps = (
        lax.all_to_all(values, "seq", split_axis=1, concat_axis=0, tiled=True),
        lax.all_to_all(filter_taps, "seq", split_axis=1, concat_axis=0, tiled=True),
    )
    freq_ids = jnp.arange(2 * blocks, dtype=jnp.int32)
    block_ids = jnp.arange(blocks, dtype=jnp.int32)
    all_rows = jnp.arange(rows, dtype=jnp.int32)
    outer_cos, outer_sin = angle_table(freq_ids, block_ids, 2 * blocks)
    twist_cos, twist_sin = angle_table(freq_ids, all_rows, length)
    tables = (outer_cos, outer_sin, twist_cos, twist_sin, "ka,arc->krc")
    value_re, value_im = outer_forward(whole_values.reshape(blocks, rows, narrow), *tables)
    taps_re, taps_im = outer_forward(whole_taps.reshape(blocks, rows, narrow), *tables)
    inner_cos, inner_sin = angle_table(all_rows, all_rows, rows)
    back_re, back_im = inner_filter((value_re, value_im, taps_re, taps_im), inner_cos, inner_sin)
    turned_re, turned_im = untwist(back_re, back_im, twist_cos, twist_sin)
    final_cos, final_sin = angle_table(block_ids, freq_ids, 2 * blocks)
    signal = (
        mix("ak,krc->arc", final_cos, turned_re) - mix("ak,krc->arc", final_sin, turned_im)
    ) / length
    returned = lax.all_to_all(signal, "seq", split_axis=0, concat_axis=2, tiled=True)
    return returned[0]


def general_local(values, gates, filter_taps, skip_gain, out_weight):
    conv = channels_plan(values, filter_taps)
    gated = (
        gates.astype(jnp.float32) * (conv + skip_gain[None, :] * values.astype(jnp.float32))
    ).astype(jnp.bfloat16)
    projected = lax.psum_scatter(
        lax.dot_general(
            out_weight, gated, (((0,), (1,)), ((), ())), preferred_element_type=jnp.float32
        ),
        "chan",
        scatter_dimension=0,
        tiled=True,
    )
    return projected.astype(jnp.bfloat16)


def split_table(table):
    high = table.astype(ml_dtypes.bfloat16)
    low = (table - high.astype(np.float64)).astype(ml_dtypes.bfloat16)
    return high, low


@functools.lru_cache(maxsize=None)
def transform_tables(length):
    inner = length // RADIX
    k = np.arange(inner)[:, None]
    unit = TWO_PI / (4 * length)
    turns = (np.array(Q_ORDER)[:, None] * (4 * k.T + 1)) % (4 * length) * unit
    turns = np.stack([np.cos(turns), np.sin(turns)], axis=1).reshape(2 * RADIX, inner, 1)
    blocks = [np.broadcast_to(turns, (2 * RADIX, inner, LANES))]
    forward, backward = [], []
    for odd in range(2):
        m = 2 * np.arange(inner // 2)[None, :] + odd
        angles = (RADIX * m * (4 * k[: inner // 2] + 1)) % (4 * length) * unit
        table = np.concatenate([np.cos(angles), -np.sin(angles)], axis=0)
        forward.append(np.concatenate(split_table(table), axis=1))
        backward.append(np.concatenate(split_table(table.T / length), axis=0))
    for table in forward + backward:
        blocks.append(table.astype(np.float32).reshape(inner, -1, LANES).swapaxes(0, 1))
    return np.concatenate(blocks, axis=0).astype(np.float32)


def row_order(rows, turned_over=False):
    place = lax.broadcasted_iota(jnp.int32, (rows, rows), 1 if turned_over else 0)
    source = lax.broadcasted_iota(jnp.int32, (rows, rows), 0 if turned_over else 1)
    chunk = rows // RADIX
    index, within = place // chunk, place % chunk
    odd, j = within // (chunk // 2), within % (chunk // 2)
    wanted = RADIX * (2 * j + odd) + index // 4 + 4 * (index % 4)
    return jnp.where(source == wanted, 1.0, 0.0).astype(jnp.bfloat16)


def turn(point, index, sign):
    re, im = point
    index %= 16
    if index == 0:
        return point
    if index == 4:
        return (-im, re) if sign > 0 else (im, -re)
    if index == 8:
        return (-re, -im)
    half = math.sqrt(0.5)
    if index == 2:
        return ((re - im) * half, (re + im) * half) if sign > 0 else ((re + im) * half, (im - re) * half)
    if index == 6:
        return ((-re - im) * half, (re - im) * half) if sign > 0 else ((im - re) * half, (-re - im) * half)
    cos = math.cos(TWO_PI * index / 16)
    sin = sign * math.sin(TWO_PI * index / 16)
    return (re * cos - im * sin, re * sin + im * cos)


def four_points(points, sign):
    a, b, c, d = points
    ac = (a[0] + c[0], a[1] + c[1])
    am = (a[0] - c[0], a[1] - c[1])
    bd = (b[0] + d[0], b[1] + d[1])
    bm = (b[0] - d[0], b[1] - d[1])
    if sign < 0:
        side = (bm[1], -bm[0])
    else:
        side = (-bm[1], bm[0])
    return (
        (ac[0] + bd[0], ac[1] + bd[1]),
        (am[0] + side[0], am[1] + side[1]),
        (ac[0] - bd[0], ac[1] - bd[1]),
        (am[0] - side[0], am[1] - side[1]),
    )


def turned(point, cos, sin, sign):
    re, im = point
    if sign < 0:
        return (re * cos + im * sin, im * cos - re * sin)
    return (re * cos - im * sin, im * cos + re * sin)


def slot_order(blocks):
    half = blocks // 2
    across = [half + (i // 2 if i % 2 == 0 else half // 2 + i // 2) for i in range(half)]
    near = list(range(1, half)) + [0]
    lead = [across[0], near[0], across[1], near[1], across[2]]
    return lead + [slot for pair in zip(across[3:], near[2:]) for slot in pair] + near[half - 1 :]


LEAD = 5


def lead_kernel(blocks, me_ref, values_hbm, taps_hbm, *rest):
    outs, (streams, sems) = rest[:LEAD], rest[LEAD:]
    loads = []
    for i, slot in enumerate(slot_order(blocks)[:LEAD]):
        lanes = pl.ds(pl.multiple_of((me_ref[0] ^ slot) * LANES, LANES), LANES)
        for side, source in enumerate((values_hbm, taps_hbm)):
            to = pl.ds((2 * i + side) * LANES, LANES)
            loads.append(pltpu.make_async_copy(source.at[:, lanes], streams.at[:, to], sems.at[2 * i + side]))
    for load in loads:
        load.start()
    order = row_order(streams.shape[0])
    for load in loads:
        load.wait()
    moved = jnp.dot(order, streams[...], preferred_element_type=jnp.float32).astype(jnp.bfloat16)
    for i, out in enumerate(outs):
        out[...] = moved[:, 2 * i * LANES : 2 * (i + 1) * LANES]


def arrange_kernel(pieces, blocks, me_ref, values_hbm, taps_hbm, *rest):
    outs, (values_ref, taps_ref, packed, sems) = rest[: blocks - LEAD], rest[blocks - LEAD :]
    piece = values_ref.shape[1] // pieces
    loads = []
    for part in range(pieces):
        lanes = pl.ds(part * piece, piece)
        loads.append(pltpu.make_async_copy(values_hbm.at[:, lanes], values_ref.at[:, lanes], sems.at[2 * part]))
        loads.append(pltpu.make_async_copy(taps_hbm.at[:, lanes], taps_ref.at[:, lanes], sems.at[2 * part + 1]))
    for load in loads:
        load.start()
    order = row_order(values_ref.shape[0])
    for part in range(pieces):
        loads[2 * part].wait()
        loads[2 * part + 1].wait()
        lanes = pl.ds(part * piece, piece)
        both = jnp.concatenate([values_ref[:, lanes], taps_ref[:, lanes]], axis=1)
        moved = jnp.dot(order, both, preferred_element_type=jnp.float32).astype(jnp.bfloat16)
        for block in range(piece // LANES):
            for side in range(2):
                start = side * piece + block * LANES
                packed[part * piece // LANES + block, :, pl.ds(side * LANES, LANES)] = moved[:, start : start + LANES]
    for out, slot in zip(outs, slot_order(blocks)[LEAD:]):
        out[...] = packed[me_ref[0] ^ slot]


def arrange(me, values, taps, blocks):
    rows, wide = values.shape
    pieces = 4
    block = jax.ShapeDtypeStruct((rows, 2 * LANES), jnp.bfloat16)
    in_specs = [pl.BlockSpec(memory_space=pltpu.SMEM)] + [pl.BlockSpec(memory_space=pl.ANY)] * 2
    lead = pl.pallas_call(
        functools.partial(lead_kernel, blocks),
        in_specs=in_specs,
        out_specs=[pl.BlockSpec(memory_space=pltpu.VMEM)] * LEAD,
        out_shape=[block] * LEAD,
        scratch_shapes=[
            pltpu.VMEM((rows, 2 * LEAD * LANES), jnp.bfloat16),
            pltpu.SemaphoreType.DMA((2 * LEAD,)),
        ],
        compiler_params=pltpu.CompilerParams(vmem_limit_bytes=FIRST_BYTES),
        cost_estimate=pl.CostEstimate(
            flops=4 * rows * rows * LEAD * LANES, bytes_accessed=8 * rows * LEAD * LANES, transcendentals=0
        ),
        name="arrange_lead",
    )(me, values, taps)
    others = pl.pallas_call(
        functools.partial(arrange_kernel, pieces, blocks),
        in_specs=in_specs,
        out_specs=[pl.BlockSpec(memory_space=pltpu.VMEM)] * (blocks - LEAD),
        out_shape=[block] * (blocks - LEAD),
        scratch_shapes=[
            pltpu.VMEM((rows, wide), jnp.bfloat16),
            pltpu.VMEM((rows, wide), jnp.bfloat16),
            pltpu.VMEM((blocks, rows, 2 * LANES), jnp.bfloat16),
            pltpu.SemaphoreType.DMA((2 * pieces,)),
        ],
        compiler_params=pltpu.CompilerParams(vmem_limit_bytes=ARRANGE_BYTES),
        cost_estimate=pl.CostEstimate(
            flops=4 * rows * rows * wide, bytes_accessed=8 * rows * wide, transcendentals=0
        ),
        name="arrange_others",
    )(me, values, taps)
    return [*lead, *others]


def convolve_kernel(blocks, me_ref, *rest):
    slots = rest[:blocks]
    convolve_blocks(me_ref, slots, *rest[blocks:])


def convolve_blocks(
    me_ref, slots, tables_hbm, out_hbm,
    streams, turns_ref, fixed, stages, raw_even, raw_odd, columns, mixed, halves_even, halves_odd, signals, sems,
):
    blocks, rows, _ = streams.shape
    chunk = rows // RADIX
    inner = blocks * chunk
    part_rows = inner // 2
    group = rows // 4
    raws = (raw_even, raw_odd)
    halves = (halves_even, halves_odd)
    count = fixed.shape[0]
    load_fixed = []
    for part in range(2):
        taken = pl.ds(part * count // 2, count // 2)
        source = tables_hbm.at[pl.ds(2 * RADIX + part * count // 2, count // 2)]
        load_fixed.append(pltpu.make_async_copy(source, fixed.at[taken], sems.at[10 * part]))
    load_turns, stores = [], []
    for low in range(4):
        taken = pl.ds(low * group, group)
        eight = pl.ds(8 * low, 8)
        load_turns.append(pltpu.make_async_copy(tables_hbm.at[eight], turns_ref.at[eight], sems.at[1 + low]))
        stores.append(pltpu.make_async_copy(signals.at[:, taken], out_hbm.at[:, taken], sems.at[5 + low]))
    load_fixed[0].start()
    for load in load_turns:
        load.start()
    load_fixed[1].start()
    own = pltpu.make_async_copy(slots[-1], streams.at[me_ref[0]], sems.at[9])
    own.start()
    for slot, source in zip(slot_order(blocks)[:-1], slots[:-1]):
        streams[me_ref[0] ^ slot] = source[...]
    own.wait()
    width = inner // LANES

    def take_stages(part):
        load_fixed[part].wait()
        for table in range(2 * part, 2 * part + 2):
            for block in range(width):
                stages[table, :, pl.ds(block * LANES, LANES)] = fixed[table * width + block].astype(jnp.bfloat16)

    take_stages(0)

    def transform(low, pair):
        sides = [[], []]
        for part in range(2):
            taken = pl.ds(pl.multiple_of(low * group + (2 * pair + part) * chunk, chunk), chunk)
            stream = streams[:, taken].astype(jnp.float32).reshape(blocks, 2, chunk // 2, 2 * LANES)
            for odd in range(2):
                sides[odd].append(stream[:, odd].reshape(part_rows, 2 * LANES).astype(jnp.bfloat16))
        for odd in range(2):
            both = jnp.concatenate(sides[odd], axis=1)
            result = jnp.dot(
                stages[odd], jnp.concatenate([both, both], axis=0), preferred_element_type=jnp.float32
            )
            for part in range(2):
                raws[low % 2][2 * pair + part, odd] = result[:, 2 * part * LANES : 2 * (part + 1) * LANES]

    def first_pass(low, start):
        raw = raws[low % 2]
        real, imaginary = pl.ds(start, 8), pl.ds(part_rows + start, 8)
        for side in range(2):
            lanes = pl.ds(side * LANES, LANES)
            points = [[], []]
            for high in range(4):
                even = (raw[high, 0, real, lanes], raw[high, 0, imaginary, lanes])
                odd = (raw[high, 1, real, lanes], raw[high, 1, imaginary, lanes])
                points[0].append((even[0] + odd[0], even[1] + odd[1]))
                points[1].append((even[0] - odd[0], even[1] - odd[1]))
            for part in range(2):
                upper, lower = pl.ds(part * part_rows + start, 8), pl.ds(inner + part * part_rows + start, 8)
                for high in range(4):
                    if low + high:
                        turns = [turns_ref[2 * (4 * low + high) + i, upper] for i in range(2)]
                        points[part][high] = turned(points[part][high], *turns, -1)
                for k, point in enumerate(four_points(points[part], -1)):
                    point = turn(point, low * k, -1)
                    columns[4 * low + k, upper, lanes] = point[0]
                    columns[4 * low + k, lower, lanes] = point[1]

    def first_rows(low, start, count):
        for part in range(count):
            first_pass(low, pl.multiple_of(start + 8 * part, 8))

    steps = part_rows // 2

    def alone(pair, carry):
        transform(0, pair)
        return carry

    lax.fori_loop(0, 2, alone, 0)
    for low in range(1, 4):
        load_turns[low - 1].wait()

        def beside(pair, carry, low=low):
            transform(low, pair)
            first_rows(low - 1, pair * steps, steps // 8)
            return carry

        lax.fori_loop(0, 2, beside, 0)
    load_turns[3].wait()

    def middle(index, carry):
        start = pl.multiple_of(index * 8, 8)
        first_pass(3, start)
        for part in range(2):
            upper, lower = pl.ds(part * part_rows + start, 8), pl.ds(inner + part * part_rows + start, 8)
            for k in range(4):
                sides = []
                for side in range(2):
                    lanes = pl.ds(side * LANES, LANES)
                    points = [
                        (columns[4 * low + k, upper, lanes], columns[4 * low + k, lower, lanes]) for low in range(4)
                    ]
                    sides.append(four_points(points, -1))
                product = [
                    (a[0] * b[0] - a[1] * b[1], a[0] * b[1] + a[1] * b[0]) for a, b in zip(*sides)
                ]
                for high, point in enumerate(four_points(product, 1)):
                    point = turn(point, k * high, 1)
                    mixed[4 * high + k, upper] = point[0]
                    mixed[4 * high + k, lower] = point[1]
        return carry

    lax.fori_loop(0, part_rows // 8, middle, 0)

    def last_pass(low, start):
        target = halves[low % 2]
        found = []
        for part in range(2):
            upper, lower = pl.ds(part * part_rows + start, 16), pl.ds(inner + part * part_rows + start, 16)
            points = list(four_points([(mixed[4 * low + k, upper], mixed[4 * low + k, lower]) for k in range(4)], 1))
            for high in range(4):
                if low + high:
                    turns = [turns_ref[2 * (4 * low + high) + i, upper] for i in range(2)]
                    points[high] = turned(points[high], *turns, 1)
            found.append(points)
        for high in range(4):
            for i in range(2):
                taken = pl.ds(i * part_rows + start, 16)
                first, second = found[0][high][i], found[1][high][i]
                for odd, value in enumerate((first + second, first - second)):
                    rounded = value.astype(jnp.bfloat16)
                    target[high, odd, taken, pl.ds(0, LANES)] = rounded
                    target[high, odd, taken, pl.ds(LANES, LANES)] = (value - rounded.astype(jnp.float32)).astype(
                        jnp.bfloat16
                    )

    def last_rows(low, start, count):
        for part in range(count):
            last_pass(low, pl.multiple_of(start + 16 * part, 16))

    def restore(low, pair):
        sides = []
        for odd in range(2):
            both = jnp.concatenate([halves[low % 2][2 * pair + part, odd] for part in range(2)], axis=1)
            terms = jnp.dot(stages[2 + odd], both, preferred_element_type=jnp.float32)
            found = []
            for part in range(2):
                first, second = [slice((2 * part + i) * LANES, (2 * part + i + 1) * LANES) for i in range(2)]
                signal = terms[:part_rows, first] + terms[:part_rows, second] + terms[part_rows:, first]
                found.append(signal.reshape(blocks, 1, chunk // 2, LANES))
            sides.append(found)
        for part in range(2):
            signal = jnp.concatenate([sides[0][part], sides[1][part]], axis=1).reshape(blocks, chunk, LANES)
            taken = pl.ds(pl.multiple_of(low * group + (2 * pair + part) * chunk, chunk), chunk)
            signals[:, taken] = signal.astype(jnp.bfloat16)

    def prepare(index, carry):
        last_rows(0, index * steps, steps // 16)
        return carry

    take_stages(1)
    lax.fori_loop(0, 2, prepare, 0)
    for low in range(4):

        def back(pair, carry, low=low):
            restore(low, pair)
            if low < 3:
                last_rows(low + 1, pair * steps, steps // 16)
            return carry

        lax.fori_loop(0, 2, back, 0)
        stores[low].start()
    for store in stores:
        store.wait()


def convolve(me, slots):
    blocks = len(slots)
    rows, lanes = slots[0].shape
    length = blocks * rows
    inner = length // RADIX
    tables = transform_tables(length)
    return pl.pallas_call(
        functools.partial(convolve_kernel, blocks),
        in_specs=[pl.BlockSpec(memory_space=pltpu.SMEM)]
        + [pl.BlockSpec(memory_space=pltpu.VMEM)] * (blocks - 1)
        + [pl.BlockSpec(memory_space=pl.ANY)] * 2,
        out_specs=pl.BlockSpec(memory_space=pl.ANY),
        out_shape=jax.ShapeDtypeStruct((blocks, rows, LANES), jnp.bfloat16),
        scratch_shapes=[
            pltpu.VMEM((blocks, rows, lanes), jnp.bfloat16),
            pltpu.VMEM((2 * RADIX, inner, LANES), jnp.float32),
            pltpu.VMEM((tables.shape[0] - 2 * RADIX, inner, LANES), jnp.float32),
            pltpu.VMEM((4, inner, inner), jnp.bfloat16),
            pltpu.VMEM((4, 2, inner, lanes), jnp.float32),
            pltpu.VMEM((4, 2, inner, lanes), jnp.float32),
            pltpu.VMEM((RADIX, 2 * inner, lanes), jnp.float32),
            pltpu.VMEM((RADIX, 2 * inner, LANES), jnp.float32),
            pltpu.VMEM((4, 2, inner, lanes), jnp.bfloat16),
            pltpu.VMEM((4, 2, inner, lanes), jnp.bfloat16),
            pltpu.VMEM((blocks, rows, LANES), jnp.bfloat16),
            pltpu.SemaphoreType.DMA((11,)),
        ],
        compiler_params=pltpu.CompilerParams(vmem_limit_bytes=CONV_BYTES),
        cost_estimate=pl.CostEstimate(flops=5 * 10**9, bytes_accessed=9 * 10**6, transcendentals=0),
        name="long_convolution",
    )(me, *slots, jnp.asarray(tables))


PIECES = 4


def weight_loads(weight_hbm, weight_ref, side, sems):
    width, features = weight_ref.shape
    columns = pl.ds(pl.multiple_of(side * features, features), features)
    deep = width // PIECES
    loads = []
    for part in range(PIECES):
        rows = pl.ds(part * deep, deep)
        loads.append(pltpu.make_async_copy(weight_hbm.at[rows, columns], weight_ref.at[rows], sems.at[part]))
        loads[part].start()
    return loads


def gate_kernel(
    half_ref, conv_ref, gates_hbm, values_hbm, skip_ref, weight_hbm, gated_ref, out_ref,
    gates_ref, values_ref, weight_ref, sems,
):
    blocks, rows, lanes = conv_ref.shape
    streams = [
        pltpu.make_async_copy(gates_hbm, gates_ref, sems.at[PIECES]),
        pltpu.make_async_copy(values_hbm, values_ref, sems.at[PIECES + 1]),
    ]
    for stream in streams:
        stream.start()
    loads = weight_loads(weight_hbm, weight_ref, 1 - half_ref[0], sems)
    order = row_order(rows, True)
    for stream in streams:
        stream.wait()
    group = blocks // PIECES
    wide = group * lanes
    for part in range(PIECES):
        taken = pl.ds(part * wide, wide)
        conv = jnp.concatenate([conv_ref[part * group + block] for block in range(group)], axis=1)
        conv = jnp.dot(order, conv, preferred_element_type=jnp.float32)
        direct = skip_ref[:, taken] * values_ref[:, taken].astype(jnp.float32)
        gated_ref[:, taken] = (gates_ref[:, taken].astype(jnp.float32) * (conv + direct)).astype(jnp.bfloat16)
    multiply_pieces(loads, gated_ref, weight_ref, out_ref)


def multiply_pieces(loads, gated_ref, weight_ref, out_ref):
    deep = weight_ref.shape[0] // PIECES
    for part in range(PIECES):
        taken = pl.ds(part * deep, deep)
        loads[part].wait()
        term = jnp.dot(gated_ref[:, taken], weight_ref[taken], preferred_element_type=jnp.float32)
        out_ref[...] = term if part == 0 else out_ref[...] + term


def gate_and_project(half, conv, gates, values, skip_gain, weight):
    rows, width = gates.shape
    features = weight.shape[1] // 2
    anywhere, inside = pl.BlockSpec(memory_space=pl.ANY), pl.BlockSpec(memory_space=pltpu.VMEM)
    return pl.pallas_call(
        gate_kernel,
        in_specs=[pl.BlockSpec(memory_space=pltpu.SMEM), inside, anywhere, anywhere, inside, anywhere],
        out_specs=[inside] * 2,
        out_shape=[
            jax.ShapeDtypeStruct((rows, width), jnp.bfloat16),
            jax.ShapeDtypeStruct((rows, features), jnp.float32),
        ],
        scratch_shapes=[
            pltpu.VMEM((rows, width), jnp.bfloat16),
            pltpu.VMEM((rows, width), jnp.bfloat16),
            pltpu.VMEM((width, features), jnp.bfloat16),
            pltpu.SemaphoreType.DMA((PIECES + 2,)),
        ],
        compiler_params=pltpu.CompilerParams(vmem_limit_bytes=TAIL_BYTES),
        cost_estimate=pl.CostEstimate(
            flops=2 * rows * width * features, bytes_accessed=2 * width * features, transcendentals=0
        ),
        name="gate_project_sent",
    )(half, conv, gates, values, skip_gain[None, :], weight)


def kept_kernel(half_ref, gated_ref, weight_hbm, out_ref, weight_ref, sems):
    multiply_pieces(weight_loads(weight_hbm, weight_ref, half_ref[0], sems), gated_ref, weight_ref, out_ref)


def project_kept(half, gated, weight):
    rows, width = gated.shape
    features = weight.shape[1] // 2
    inside = pl.BlockSpec(memory_space=pltpu.VMEM)
    return pl.pallas_call(
        kept_kernel,
        in_specs=[pl.BlockSpec(memory_space=pltpu.SMEM), inside, pl.BlockSpec(memory_space=pl.ANY)],
        out_specs=inside,
        out_shape=jax.ShapeDtypeStruct((rows, features), jnp.float32),
        scratch_shapes=[pltpu.VMEM((width, features), jnp.bfloat16), pltpu.SemaphoreType.DMA((PIECES,))],
        compiler_params=pltpu.CompilerParams(vmem_limit_bytes=TAIL_BYTES),
        cost_estimate=pl.CostEstimate(
            flops=2 * rows * width * features, bytes_accessed=2 * width * features, transcendentals=0
        ),
        name="project_kept",
    )(half, gated, weight)


def join_kernel(kept_ref, came_ref, out_hbm, out_ref, sems):
    wide = out_ref.shape[0] // PIECES
    stores = []
    for part in range(PIECES):
        taken = pl.ds(part * wide, wide)
        out_ref[taken] = (kept_ref[:, taken] + came_ref[:, taken]).astype(jnp.bfloat16).T
        stores.append(pltpu.make_async_copy(out_ref.at[taken], out_hbm.at[taken], sems.at[part]))
        stores[part].start()
    for store in stores:
        store.wait()


def join(kept, came):
    rows, features = kept.shape
    return pl.pallas_call(
        join_kernel,
        in_specs=[pl.BlockSpec(memory_space=pltpu.VMEM)] * 2,
        out_specs=pl.BlockSpec(memory_space=pl.ANY),
        out_shape=jax.ShapeDtypeStruct((features, rows), jnp.bfloat16),
        scratch_shapes=[pltpu.VMEM((features, rows), jnp.bfloat16), pltpu.SemaphoreType.DMA((PIECES,))],
        compiler_params=pltpu.CompilerParams(vmem_limit_bytes=TAIL_BYTES),
        name="join_halves",
    )(kept, came)


def swap_blocks(array):
    return lax.all_to_all(array, "seq", split_axis=0, concat_axis=0, tiled=True)


def exchange(slots):
    blocks = len(slots)
    return [
        lax.ppermute(source, "seq", [(j, j ^ slot) for j in range(blocks)]) if slot else source
        for slot, source in zip(slot_order(blocks), slots)
    ]


def kernel_local(values, gates, filter_taps, skip_gain, out_weight):
    blocks = lax.axis_size("seq")
    me = lax.axis_index("seq").astype(jnp.int32)[None]
    half = lax.axis_index("chan").astype(jnp.int32)[None]
    conv = convolve(me, exchange(arrange(me, values, filter_taps, blocks)))
    gated, sent = gate_and_project(half, swap_blocks(conv), gates, values, skip_gain, out_weight)
    other = lax.ppermute(sent, "chan", [(0, 1), (1, 0)])
    kept = project_kept(half, gated, out_weight)
    return join(kept, other)


def takes_kernels(mesh, values, out_weight):
    blocks, halves = mesh.shape["seq"], mesh.shape["chan"]
    rows = values.shape[0] // blocks
    return (
        halves == 2
        and blocks == 16
        and rows == 256
        and values.shape[1] == halves * blocks * LANES
        and out_weight.shape[1] % (8 * LANES) == 0
    )


def solution(mesh):
    placed = (P("seq", "chan"), P("seq", "chan"), P("seq", "chan"), P("chan"), P("chan", None))

    def whole(values, gates, filter_taps, skip_gain, out_weight):
        local = kernel_local if takes_kernels(mesh, values, out_weight) else general_local
        return jax.shard_map(
            local, mesh=mesh, in_specs=placed, out_specs=P("chan", "seq"), check_vma=False
        )(values, gates, filter_taps, skip_gain, out_weight)

    return whole
```

```python
import functools
import math

import jax
import jax.numpy as jnp
import ml_dtypes
import numpy as np
from jax import lax
from jax.experimental import pallas as pl
from jax.experimental.pallas import tpu as pltpu
from jax.sharding import PartitionSpec as P

TWO_PI = 2.0 * math.pi
HIGH = lax.Precision.HIGHEST
RADIX = 16
LANES = 128
Q_ORDER = [low + 4 * high for low in range(4) for high in range(4)]
FIRST_BYTES = 60 * 1024 * 1024
ARRANGE_BYTES = 12 * 1024 * 1024
CONV_BYTES = 49 * 1024 * 1024
TAIL_BYTES = 46 * 1024 * 1024


def angle_table(first, second, period):
    product = first[:, None] * second[None, :] % period
    angles = product.astype(jnp.float32) * (TWO_PI / period)
    return (jnp.cos(angles), jnp.sin(angles))


def mix(equation, left, right):
    return jnp.einsum(equation, left, right, precision=HIGH)


def outer_forward(data, outer_cos, outer_sin, twist_cos, twist_sin, equation):
    source = data.astype(jnp.float32)
    real = mix(equation, outer_cos, source)
    imag = -mix(equation, outer_sin, source)
    cos_part = twist_cos[:, :, None]
    sin_part = twist_sin[:, :, None]
    return (real * cos_part + imag * sin_part, imag * cos_part - real * sin_part)


def inner_filter(spectra, inner_cos, inner_sin):
    value_re, value_im, taps_re, taps_im = spectra

    def forward(real, imag):
        out_re = mix("kr,jrc->jkc", inner_cos, real) + mix("kr,jrc->jkc", inner_sin, imag)
        out_im = mix("kr,jrc->jkc", inner_cos, imag) - mix("kr,jrc->jkc", inner_sin, real)
        return (out_re, out_im)

    value_fre, value_fim = forward(value_re, value_im)
    taps_fre, taps_fim = forward(taps_re, taps_im)
    prod_re = value_fre * taps_fre - value_fim * taps_fim
    prod_im = value_fre * taps_fim + value_fim * taps_fre
    back_re = mix("rk,jkc->jrc", inner_cos, prod_re) - mix("rk,jkc->jrc", inner_sin, prod_im)
    back_im = mix("rk,jkc->jrc", inner_cos, prod_im) + mix("rk,jkc->jrc", inner_sin, prod_re)
    return (back_re, back_im)


def untwist(real, imag, twist_cos, twist_sin):
    cos_part = twist_cos[:, :, None]
    sin_part = twist_sin[:, :, None]
    return (real * cos_part - imag * sin_part, imag * cos_part + real * sin_part)


def channels_plan(values, filter_taps):
    rows, width = values.shape
    blocks = lax.axis_size("seq")
    length = 2 * blocks * rows
    narrow = width // blocks
    whole_values, whole_taps = (
        lax.all_to_all(values, "seq", split_axis=1, concat_axis=0, tiled=True),
        lax.all_to_all(filter_taps, "seq", split_axis=1, concat_axis=0, tiled=True),
    )
    freq_ids = jnp.arange(2 * blocks, dtype=jnp.int32)
    block_ids = jnp.arange(blocks, dtype=jnp.int32)
    all_rows = jnp.arange(rows, dtype=jnp.int32)
    outer_cos, outer_sin = angle_table(freq_ids, block_ids, 2 * blocks)
    twist_cos, twist_sin = angle_table(freq_ids, all_rows, length)
    tables = (outer_cos, outer_sin, twist_cos, twist_sin, "ka,arc->krc")
    value_re, value_im = outer_forward(whole_values.reshape(blocks, rows, narrow), *tables)
    taps_re, taps_im = outer_forward(whole_taps.reshape(blocks, rows, narrow), *tables)
    inner_cos, inner_sin = angle_table(all_rows, all_rows, rows)
    back_re, back_im = inner_filter((value_re, value_im, taps_re, taps_im), inner_cos, inner_sin)
    turned_re, turned_im = untwist(back_re, back_im, twist_cos, twist_sin)
    final_cos, final_sin = angle_table(block_ids, freq_ids, 2 * blocks)
    signal = (
        mix("ak,krc->arc", final_cos, turned_re) - mix("ak,krc->arc", final_sin, turned_im)
    ) / length
    returned = lax.all_to_all(signal, "seq", split_axis=0, concat_axis=2, tiled=True)
    return returned[0]


def general_local(values, gates, filter_taps, skip_gain, out_weight):
    conv = channels_plan(values, filter_taps)
    gated = (
        gates.astype(jnp.float32) * (conv + skip_gain[None, :] * values.astype(jnp.float32))
    ).astype(jnp.bfloat16)
    projected = lax.psum_scatter(
        lax.dot_general(
            out_weight, gated, (((0,), (1,)), ((), ())), preferred_element_type=jnp.float32
        ),
        "chan",
        scatter_dimension=0,
        tiled=True,
    )
    return projected.astype(jnp.bfloat16)


def split_table(table):
    high = table.astype(ml_dtypes.bfloat16)
    low = (table - high.astype(np.float64)).astype(ml_dtypes.bfloat16)
    return high, low


@functools.lru_cache(maxsize=None)
def transform_tables(length):
    inner = length // RADIX
    k = np.arange(inner)[:, None]
    unit = TWO_PI / (4 * length)
    turns = (np.array(Q_ORDER)[:, None] * (4 * k.T + 1)) % (4 * length) * unit
    turns = np.stack([np.cos(turns), np.sin(turns)], axis=1).reshape(2 * RADIX, inner, 1)
    blocks = [np.broadcast_to(turns, (2 * RADIX, inner, LANES))]
    forward, backward = [], []
    for odd in range(2):
        m = 2 * np.arange(inner // 2)[None, :] + odd
        angles = (RADIX * m * (4 * k[: inner // 2] + 1)) % (4 * length) * unit
        table = np.concatenate([np.cos(angles), -np.sin(angles)], axis=0)
        forward.append(np.concatenate(split_table(table), axis=1))
        backward.append(np.concatenate(split_table(table.T / length), axis=0))
    for table in forward + backward:
        blocks.append(table.astype(np.float32).reshape(inner, -1, LANES).swapaxes(0, 1))
    return np.concatenate(blocks, axis=0).astype(np.float32)


def row_order(rows, turned_over=False):
    place = lax.broadcasted_iota(jnp.int32, (rows, rows), 1 if turned_over else 0)
    source = lax.broadcasted_iota(jnp.int32, (rows, rows), 0 if turned_over else 1)
    chunk = rows // RADIX
    index, within = place // chunk, place % chunk
    odd, j = within // (chunk // 2), within % (chunk // 2)
    wanted = RADIX * (2 * j + odd) + index // 4 + 4 * (index % 4)
    return jnp.where(source == wanted, 1.0, 0.0).astype(jnp.bfloat16)


def turn(point, index, sign):
    re, im = point
    index %= 16
    if index == 0:
        return point
    if index == 4:
        return (-im, re) if sign > 0 else (im, -re)
    if index == 8:
        return (-re, -im)
    half = math.sqrt(0.5)
    if index == 2:
        return ((re - im) * half, (re + im) * half) if sign > 0 else ((re + im) * half, (im - re) * half)
    if index == 6:
        return ((-re - im) * half, (re - im) * half) if sign > 0 else ((im - re) * half, (-re - im) * half)
    cos = math.cos(TWO_PI * index / 16)
    sin = sign * math.sin(TWO_PI * index / 16)
    return (re * cos - im * sin, re * sin + im * cos)


def four_points(points, sign):
    a, b, c, d = points
    ac = (a[0] + c[0], a[1] + c[1])
    am = (a[0] - c[0], a[1] - c[1])
    bd = (b[0] + d[0], b[1] + d[1])
    bm = (b[0] - d[0], b[1] - d[1])
    if sign < 0:
        side = (bm[1], -bm[0])
    else:
        side = (-bm[1], bm[0])
    return (
        (ac[0] + bd[0], ac[1] + bd[1]),
        (am[0] + side[0], am[1] + side[1]),
        (ac[0] - bd[0], ac[1] - bd[1]),
        (am[0] - side[0], am[1] - side[1]),
    )


def turned(point, cos, sin, sign):
    re, im = point
    if sign < 0:
        return (re * cos + im * sin, im * cos - re * sin)
    return (re * cos - im * sin, im * cos + re * sin)


def slot_order(blocks):
    half = blocks // 2
    across = list(range(half, blocks))
    near = list(range(1, half)) + [0]
    return [slot for pair in zip(across, near) for slot in pair]


LEAD = 5


def lead_kernel(blocks, me_ref, values_hbm, taps_hbm, *rest):
    outs, (streams, sems) = rest[:LEAD], rest[LEAD:]
    loads = []
    for i, slot in enumerate(slot_order(blocks)[:LEAD]):
        lanes = pl.ds(pl.multiple_of((me_ref[0] ^ slot) * LANES, LANES), LANES)
        for side, source in enumerate((values_hbm, taps_hbm)):
            to = pl.ds((2 * i + side) * LANES, LANES)
            loads.append(pltpu.make_async_copy(source.at[:, lanes], streams.at[:, to], sems.at[2 * i + side]))
    for load in loads:
        load.start()
    order = row_order(streams.shape[0])
    for load in loads:
        load.wait()
    moved = jnp.dot(order, streams[...], preferred_element_type=jnp.float32).astype(jnp.bfloat16)
    for i, out in enumerate(outs):
        out[...] = moved[:, 2 * i * LANES : 2 * (i + 1) * LANES]


def arrange_kernel(pieces, blocks, me_ref, values_hbm, taps_hbm, *rest):
    outs, (values_ref, taps_ref, packed, sems) = rest[: blocks - LEAD], rest[blocks - LEAD :]
    piece = values_ref.shape[1] // pieces
    loads = []
    for part in range(pieces):
        lanes = pl.ds(part * piece, piece)
        loads.append(pltpu.make_async_copy(values_hbm.at[:, lanes], values_ref.at[:, lanes], sems.at[2 * part]))
        loads.append(pltpu.make_async_copy(taps_hbm.at[:, lanes], taps_ref.at[:, lanes], sems.at[2 * part + 1]))
    for load in loads:
        load.start()
    order = row_order(values_ref.shape[0])
    for part in range(pieces):
        loads[2 * part].wait()
        loads[2 * part + 1].wait()
        lanes = pl.ds(part * piece, piece)
        both = jnp.concatenate([values_ref[:, lanes], taps_ref[:, lanes]], axis=1)
        moved = jnp.dot(order, both, preferred_element_type=jnp.float32).astype(jnp.bfloat16)
        for block in range(piece // LANES):
            for side in range(2):
                start = side * piece + block * LANES
                packed[part * piece // LANES + block, :, pl.ds(side * LANES, LANES)] = moved[:, start : start + LANES]
    for out, slot in zip(outs, slot_order(blocks)[LEAD:]):
        out[...] = packed[me_ref[0] ^ slot]


def arrange(me, values, taps, blocks):
    rows, wide = values.shape
    pieces = 4
    block = jax.ShapeDtypeStruct((rows, 2 * LANES), jnp.bfloat16)
    in_specs = [pl.BlockSpec(memory_space=pltpu.SMEM)] + [pl.BlockSpec(memory_space=pl.ANY)] * 2
    lead = pl.pallas_call(
        functools.partial(lead_kernel, blocks),
        in_specs=in_specs,
        out_specs=[pl.BlockSpec(memory_space=pltpu.VMEM)] * LEAD,
        out_shape=[block] * LEAD,
        scratch_shapes=[
            pltpu.VMEM((rows, 2 * LEAD * LANES), jnp.bfloat16),
            pltpu.SemaphoreType.DMA((2 * LEAD,)),
        ],
        compiler_params=pltpu.CompilerParams(vmem_limit_bytes=FIRST_BYTES),
        cost_estimate=pl.CostEstimate(
            flops=4 * rows * rows * LEAD * LANES, bytes_accessed=8 * rows * LEAD * LANES, transcendentals=0
        ),
        name="arrange_lead",
    )(me, values, taps)
    others = pl.pallas_call(
        functools.partial(arrange_kernel, pieces, blocks),
        in_specs=in_specs,
        out_specs=[pl.BlockSpec(memory_space=pltpu.VMEM)] * (blocks - LEAD),
        out_shape=[block] * (blocks - LEAD),
        scratch_shapes=[
            pltpu.VMEM((rows, wide), jnp.bfloat16),
            pltpu.VMEM((rows, wide), jnp.bfloat16),
            pltpu.VMEM((blocks, rows, 2 * LANES), jnp.bfloat16),
            pltpu.SemaphoreType.DMA((2 * pieces,)),
        ],
        compiler_params=pltpu.CompilerParams(vmem_limit_bytes=ARRANGE_BYTES),
        cost_estimate=pl.CostEstimate(
            flops=4 * rows * rows * wide, bytes_accessed=8 * rows * wide, transcendentals=0
        ),
        name="arrange_others",
    )(me, values, taps)
    return [*lead, *others]


def convolve_kernel(blocks, me_ref, *rest):
    slots = rest[:blocks]
    convolve_blocks(me_ref, slots, *rest[blocks:])


def convolve_blocks(
    me_ref, slots, tables_hbm, out_hbm,
    streams, turns_ref, fixed, stages, raw_even, raw_odd, columns, mixed, halves_even, halves_odd, signals, sems,
):
    blocks, rows, _ = streams.shape
    chunk = rows // RADIX
    inner = blocks * chunk
    part_rows = inner // 2
    group = rows // 4
    raws = (raw_even, raw_odd)
    halves = (halves_even, halves_odd)
    count = fixed.shape[0]
    load_fixed = []
    for part in range(2):
        taken = pl.ds(part * count // 2, count // 2)
        source = tables_hbm.at[pl.ds(2 * RADIX + part * count // 2, count // 2)]
        load_fixed.append(pltpu.make_async_copy(source, fixed.at[taken], sems.at[10 * part]))
    load_turns, stores = [], []
    for low in range(4):
        taken = pl.ds(low * group, group)
        eight = pl.ds(8 * low, 8)
        load_turns.append(pltpu.make_async_copy(tables_hbm.at[eight], turns_ref.at[eight], sems.at[1 + low]))
        stores.append(pltpu.make_async_copy(signals.at[:, taken], out_hbm.at[:, taken], sems.at[5 + low]))
    load_fixed[0].start()
    for load in load_turns:
        load.start()
    load_fixed[1].start()
    own = pltpu.make_async_copy(slots[-1], streams.at[me_ref[0]], sems.at[9])
    own.start()
    for slot, source in zip(slot_order(blocks)[:-1], slots[:-1]):
        streams[me_ref[0] ^ slot] = source[...]
    own.wait()
    width = inner // LANES

    def take_stages(part):
        load_fixed[part].wait()
        for table in range(2 * part, 2 * part + 2):
            for block in range(width):
                stages[table, :, pl.ds(block * LANES, LANES)] = fixed[table * width + block].astype(jnp.bfloat16)

    take_stages(0)

    def transform(low, pair):
        sides = [[], []]
        for part in range(2):
            taken = pl.ds(pl.multiple_of(low * group + (2 * pair + part) * chunk, chunk), chunk)
            stream = streams[:, taken].astype(jnp.float32).reshape(blocks, 2, chunk // 2, 2 * LANES)
            for odd in range(2):
                sides[odd].append(stream[:, odd].reshape(part_rows, 2 * LANES).astype(jnp.bfloat16))
        for odd in range(2):
            both = jnp.concatenate(sides[odd], axis=1)
            result = jnp.dot(
                stages[odd], jnp.concatenate([both, both], axis=0), preferred_element_type=jnp.float32
            )
            for part in range(2):
                raws[low % 2][2 * pair + part, odd] = result[:, 2 * part * LANES : 2 * (part + 1) * LANES]

    def first_pass(low, start):
        raw = raws[low % 2]
        real, imaginary = pl.ds(start, 8), pl.ds(part_rows + start, 8)
        for side in range(2):
            lanes = pl.ds(side * LANES, LANES)
            points = [[], []]
            for high in range(4):
                even = (raw[high, 0, real, lanes], raw[high, 0, imaginary, lanes])
                odd = (raw[high, 1, real, lanes], raw[high, 1, imaginary, lanes])
                points[0].append((even[0] + odd[0], even[1] + odd[1]))
                points[1].append((even[0] - odd[0], even[1] - odd[1]))
            for part in range(2):
                upper, lower = pl.ds(part * part_rows + start, 8), pl.ds(inner + part * part_rows + start, 8)
                for high in range(4):
                    if low + high:
                        turns = [turns_ref[2 * (4 * low + high) + i, upper] for i in range(2)]
                        points[part][high] = turned(points[part][high], *turns, -1)
                for k, point in enumerate(four_points(points[part], -1)):
                    point = turn(point, low * k, -1)
                    columns[4 * low + k, upper, lanes] = point[0]
                    columns[4 * low + k, lower, lanes] = point[1]

    def first_rows(low, start, count):
        for part in range(count):
            first_pass(low, pl.multiple_of(start + 8 * part, 8))

    steps = part_rows // 2

    def alone(pair, carry):
        transform(0, pair)
        return carry

    lax.fori_loop(0, 2, alone, 0)
    for low in range(1, 4):
        load_turns[low - 1].wait()

        def beside(pair, carry, low=low):
            transform(low, pair)
            first_rows(low - 1, pair * steps, steps // 8)
            return carry

        lax.fori_loop(0, 2, beside, 0)
    load_turns[3].wait()

    def middle(index, carry):
        start = pl.multiple_of(index * 8, 8)
        first_pass(3, start)
        for part in range(2):
            upper, lower = pl.ds(part * part_rows + start, 8), pl.ds(inner + part * part_rows + start, 8)
            for k in range(4):
                sides = []
                for side in range(2):
                    lanes = pl.ds(side * LANES, LANES)
                    points = [
                        (columns[4 * low + k, upper, lanes], columns[4 * low + k, lower, lanes]) for low in range(4)
                    ]
                    sides.append(four_points(points, -1))
                product = [
                    (a[0] * b[0] - a[1] * b[1], a[0] * b[1] + a[1] * b[0]) for a, b in zip(*sides)
                ]
                for high, point in enumerate(four_points(product, 1)):
                    point = turn(point, k * high, 1)
                    mixed[4 * high + k, upper] = point[0]
                    mixed[4 * high + k, lower] = point[1]
        return carry

    lax.fori_loop(0, part_rows // 8, middle, 0)

    def last_pass(low, start):
        target = halves[low % 2]
        found = []
        for part in range(2):
            upper, lower = pl.ds(part * part_rows + start, 16), pl.ds(inner + part * part_rows + start, 16)
            points = list(four_points([(mixed[4 * low + k, upper], mixed[4 * low + k, lower]) for k in range(4)], 1))
            for high in range(4):
                if low + high:
                    turns = [turns_ref[2 * (4 * low + high) + i, upper] for i in range(2)]
                    points[high] = turned(points[high], *turns, 1)
            found.append(points)
        for high in range(4):
            for i in range(2):
                taken = pl.ds(i * part_rows + start, 16)
                first, second = found[0][high][i], found[1][high][i]
                for odd, value in enumerate((first + second, first - second)):
                    rounded = value.astype(jnp.bfloat16)
                    target[high, odd, taken, pl.ds(0, LANES)] = rounded
                    target[high, odd, taken, pl.ds(LANES, LANES)] = (value - rounded.astype(jnp.float32)).astype(
                        jnp.bfloat16
                    )

    def last_rows(low, start, count):
        for part in range(count):
            last_pass(low, pl.multiple_of(start + 16 * part, 16))

    def restore(low, pair):
        sides = []
        for odd in range(2):
            both = jnp.concatenate([halves[low % 2][2 * pair + part, odd] for part in range(2)], axis=1)
            terms = jnp.dot(stages[2 + odd], both, preferred_element_type=jnp.float32)
            found = []
            for part in range(2):
                first, second = [slice((2 * part + i) * LANES, (2 * part + i + 1) * LANES) for i in range(2)]
                signal = terms[:part_rows, first] + terms[:part_rows, second] + terms[part_rows:, first]
                found.append(signal.reshape(blocks, 1, chunk // 2, LANES))
            sides.append(found)
        for part in range(2):
            signal = jnp.concatenate([sides[0][part], sides[1][part]], axis=1).reshape(blocks, chunk, LANES)
            taken = pl.ds(pl.multiple_of(low * group + (2 * pair + part) * chunk, chunk), chunk)
            signals[:, taken] = signal.astype(jnp.bfloat16)

    def prepare(index, carry):
        last_rows(0, index * steps, steps // 16)
        return carry

    take_stages(1)
    lax.fori_loop(0, 2, prepare, 0)
    for low in range(4):

        def back(pair, carry, low=low):
            restore(low, pair)
            if low < 3:
                last_rows(low + 1, pair * steps, steps // 16)
            return carry

        lax.fori_loop(0, 2, back, 0)
        stores[low].start()
    for store in stores:
        store.wait()


def convolve(me, slots):
    blocks = len(slots)
    rows, lanes = slots[0].shape
    length = blocks * rows
    inner = length // RADIX
    tables = transform_tables(length)
    return pl.pallas_call(
        functools.partial(convolve_kernel, blocks),
        in_specs=[pl.BlockSpec(memory_space=pltpu.SMEM)]
        + [pl.BlockSpec(memory_space=pltpu.VMEM)] * (blocks - 1)
        + [pl.BlockSpec(memory_space=pl.ANY)] * 2,
        out_specs=pl.BlockSpec(memory_space=pl.ANY),
        out_shape=jax.ShapeDtypeStruct((blocks, rows, LANES), jnp.bfloat16),
        scratch_shapes=[
            pltpu.VMEM((blocks, rows, lanes), jnp.bfloat16),
            pltpu.VMEM((2 * RADIX, inner, LANES), jnp.float32),
            pltpu.VMEM((tables.shape[0] - 2 * RADIX, inner, LANES), jnp.float32),
            pltpu.VMEM((4, inner, inner), jnp.bfloat16),
            pltpu.VMEM((4, 2, inner, lanes), jnp.float32),
            pltpu.VMEM((4, 2, inner, lanes), jnp.float32),
            pltpu.VMEM((RADIX, 2 * inner, lanes), jnp.float32),
            pltpu.VMEM((RADIX, 2 * inner, LANES), jnp.float32),
            pltpu.VMEM((4, 2, inner, lanes), jnp.bfloat16),
            pltpu.VMEM((4, 2, inner, lanes), jnp.bfloat16),
            pltpu.VMEM((blocks, rows, LANES), jnp.bfloat16),
            pltpu.SemaphoreType.DMA((11,)),
        ],
        compiler_params=pltpu.CompilerParams(vmem_limit_bytes=CONV_BYTES),
        cost_estimate=pl.CostEstimate(flops=5 * 10**9, bytes_accessed=9 * 10**6, transcendentals=0),
        name="long_convolution",
    )(me, *slots, jnp.asarray(tables))


PIECES = 4


def weight_loads(weight_hbm, weight_ref, side, sems):
    width, features = weight_ref.shape
    columns = pl.ds(pl.multiple_of(side * features, features), features)
    deep = width // PIECES
    loads = []
    for part in range(PIECES):
        rows = pl.ds(part * deep, deep)
        loads.append(pltpu.make_async_copy(weight_hbm.at[rows, columns], weight_ref.at[rows], sems.at[part]))
        loads[part].start()
    return loads


def gate_kernel(
    half_ref, conv_ref, gates_hbm, values_hbm, skip_ref, weight_hbm, gated_ref, out_ref,
    gates_ref, values_ref, weight_ref, sems,
):
    blocks, rows, lanes = conv_ref.shape
    streams = [
        pltpu.make_async_copy(gates_hbm, gates_ref, sems.at[PIECES]),
        pltpu.make_async_copy(values_hbm, values_ref, sems.at[PIECES + 1]),
    ]
    for stream in streams:
        stream.start()
    loads = weight_loads(weight_hbm, weight_ref, 1 - half_ref[0], sems)
    order = row_order(rows, True)
    for stream in streams:
        stream.wait()
    group = blocks // PIECES
    wide = group * lanes
    for part in range(PIECES):
        taken = pl.ds(part * wide, wide)
        conv = jnp.concatenate([conv_ref[part * group + block] for block in range(group)], axis=1)
        conv = jnp.dot(order, conv, preferred_element_type=jnp.float32)
        direct = skip_ref[:, taken] * values_ref[:, taken].astype(jnp.float32)
        gated_ref[:, taken] = (gates_ref[:, taken].astype(jnp.float32) * (conv + direct)).astype(jnp.bfloat16)
    multiply_pieces(loads, gated_ref, weight_ref, out_ref)


def multiply_pieces(loads, gated_ref, weight_ref, out_ref):
    deep = weight_ref.shape[0] // PIECES
    for part in range(PIECES):
        taken = pl.ds(part * deep, deep)
        loads[part].wait()
        term = jnp.dot(gated_ref[:, taken], weight_ref[taken], preferred_element_type=jnp.float32)
        out_ref[...] = term if part == 0 else out_ref[...] + term


def gate_and_project(half, conv, gates, values, skip_gain, weight):
    rows, width = gates.shape
    features = weight.shape[1] // 2
    anywhere, inside = pl.BlockSpec(memory_space=pl.ANY), pl.BlockSpec(memory_space=pltpu.VMEM)
    return pl.pallas_call(
        gate_kernel,
        in_specs=[pl.BlockSpec(memory_space=pltpu.SMEM), inside, anywhere, anywhere, inside, anywhere],
        out_specs=[inside] * 2,
        out_shape=[
            jax.ShapeDtypeStruct((rows, width), jnp.bfloat16),
            jax.ShapeDtypeStruct((rows, features), jnp.float32),
        ],
        scratch_shapes=[
            pltpu.VMEM((rows, width), jnp.bfloat16),
            pltpu.VMEM((rows, width), jnp.bfloat16),
            pltpu.VMEM((width, features), jnp.bfloat16),
            pltpu.SemaphoreType.DMA((PIECES + 2,)),
        ],
        compiler_params=pltpu.CompilerParams(vmem_limit_bytes=TAIL_BYTES),
        cost_estimate=pl.CostEstimate(
            flops=2 * rows * width * features, bytes_accessed=2 * width * features, transcendentals=0
        ),
        name="gate_project_sent",
    )(half, conv, gates, values, skip_gain[None, :], weight)


def kept_kernel(half_ref, gated_ref, weight_hbm, out_ref, weight_ref, sems):
    multiply_pieces(weight_loads(weight_hbm, weight_ref, half_ref[0], sems), gated_ref, weight_ref, out_ref)


def project_kept(half, gated, weight):
    rows, width = gated.shape
    features = weight.shape[1] // 2
    inside = pl.BlockSpec(memory_space=pltpu.VMEM)
    return pl.pallas_call(
        kept_kernel,
        in_specs=[pl.BlockSpec(memory_space=pltpu.SMEM), inside, pl.BlockSpec(memory_space=pl.ANY)],
        out_specs=inside,
        out_shape=jax.ShapeDtypeStruct((rows, features), jnp.float32),
        scratch_shapes=[pltpu.VMEM((width, features), jnp.bfloat16), pltpu.SemaphoreType.DMA((PIECES,))],
        compiler_params=pltpu.CompilerParams(vmem_limit_bytes=TAIL_BYTES),
        cost_estimate=pl.CostEstimate(
            flops=2 * rows * width * features, bytes_accessed=2 * width * features, transcendentals=0
        ),
        name="project_kept",
    )(half, gated, weight)


def join_kernel(kept_ref, came_ref, out_hbm, out_ref, sems):
    wide = out_ref.shape[0] // PIECES
    stores = []
    for part in range(PIECES):
        taken = pl.ds(part * wide, wide)
        out_ref[taken] = (kept_ref[:, taken] + came_ref[:, taken]).astype(jnp.bfloat16).T
        stores.append(pltpu.make_async_copy(out_ref.at[taken], out_hbm.at[taken], sems.at[part]))
        stores[part].start()
    for store in stores:
        store.wait()


def join(kept, came):
    rows, features = kept.shape
    return pl.pallas_call(
        join_kernel,
        in_specs=[pl.BlockSpec(memory_space=pltpu.VMEM)] * 2,
        out_specs=pl.BlockSpec(memory_space=pl.ANY),
        out_shape=jax.ShapeDtypeStruct((features, rows), jnp.bfloat16),
        scratch_shapes=[pltpu.VMEM((features, rows), jnp.bfloat16), pltpu.SemaphoreType.DMA((PIECES,))],
        compiler_params=pltpu.CompilerParams(vmem_limit_bytes=TAIL_BYTES),
        name="join_halves",
    )(kept, came)


def swap_blocks(array):
    return lax.all_to_all(array, "seq", split_axis=0, concat_axis=0, tiled=True)


def exchange(slots):
    blocks = len(slots)
    return [
        lax.ppermute(source, "seq", [(j, j ^ slot) for j in range(blocks)]) if slot else source
        for slot, source in zip(slot_order(blocks), slots)
    ]


def kernel_local(values, gates, filter_taps, skip_gain, out_weight):
    blocks = lax.axis_size("seq")
    me = lax.axis_index("seq").astype(jnp.int32)[None]
    half = lax.axis_index("chan").astype(jnp.int32)[None]
    conv = convolve(me, exchange(arrange(me, values, filter_taps, blocks)))
    gated, sent = gate_and_project(half, swap_blocks(conv), gates, values, skip_gain, out_weight)
    other = lax.ppermute(sent, "chan", [(0, 1), (1, 0)])
    kept = project_kept(half, gated, out_weight)
    return join(kept, other)


def takes_kernels(mesh, values, out_weight):
    blocks, halves = mesh.shape["seq"], mesh.shape["chan"]
    rows = values.shape[0] // blocks
    return (
        halves == 2
        and blocks == 16
        and rows == 256
        and values.shape[1] == halves * blocks * LANES
        and out_weight.shape[1] % (8 * LANES) == 0
    )


def solution(mesh):
    placed = (P("seq", "chan"), P("seq", "chan"), P("seq", "chan"), P("chan"), P("chan", None))

    def whole(values, gates, filter_taps, skip_gain, out_weight):
        local = kernel_local if takes_kernels(mesh, values, out_weight) else general_local
        return jax.shard_map(
            local, mesh=mesh, in_specs=placed, out_specs=P("chan", "seq"), check_vma=False
        )(values, gates, filter_taps, skip_gain, out_weight)

    return whole
```

```python
import functools
import math

import jax
import jax.numpy as jnp
import ml_dtypes
import numpy as np
from jax import lax
from jax.experimental import pallas as pl
from jax.experimental.pallas import tpu as pltpu
from jax.sharding import PartitionSpec as P

TWO_PI = 2.0 * math.pi
HIGH = lax.Precision.HIGHEST
RADIX = 16
LANES = 128
Q_ORDER = [low + 4 * high for low in range(4) for high in range(4)]
FIRST_BYTES = 60 * 1024 * 1024
ARRANGE_BYTES = 12 * 1024 * 1024
CONV_BYTES = 49 * 1024 * 1024
TAIL_BYTES = 48 * 1024 * 1024


def angle_table(first, second, period):
    product = first[:, None] * second[None, :] % period
    angles = product.astype(jnp.float32) * (TWO_PI / period)
    return (jnp.cos(angles), jnp.sin(angles))


def mix(equation, left, right):
    return jnp.einsum(equation, left, right, precision=HIGH)


def outer_forward(data, outer_cos, outer_sin, twist_cos, twist_sin, equation):
    source = data.astype(jnp.float32)
    real = mix(equation, outer_cos, source)
    imag = -mix(equation, outer_sin, source)
    cos_part = twist_cos[:, :, None]
    sin_part = twist_sin[:, :, None]
    return (real * cos_part + imag * sin_part, imag * cos_part - real * sin_part)


def inner_filter(spectra, inner_cos, inner_sin):
    value_re, value_im, taps_re, taps_im = spectra

    def forward(real, imag):
        out_re = mix("kr,jrc->jkc", inner_cos, real) + mix("kr,jrc->jkc", inner_sin, imag)
        out_im = mix("kr,jrc->jkc", inner_cos, imag) - mix("kr,jrc->jkc", inner_sin, real)
        return (out_re, out_im)

    value_fre, value_fim = forward(value_re, value_im)
    taps_fre, taps_fim = forward(taps_re, taps_im)
    prod_re = value_fre * taps_fre - value_fim * taps_fim
    prod_im = value_fre * taps_fim + value_fim * taps_fre
    back_re = mix("rk,jkc->jrc", inner_cos, prod_re) - mix("rk,jkc->jrc", inner_sin, prod_im)
    back_im = mix("rk,jkc->jrc", inner_cos, prod_im) + mix("rk,jkc->jrc", inner_sin, prod_re)
    return (back_re, back_im)


def untwist(real, imag, twist_cos, twist_sin):
    cos_part = twist_cos[:, :, None]
    sin_part = twist_sin[:, :, None]
    return (real * cos_part - imag * sin_part, imag * cos_part + real * sin_part)


def channels_plan(values, filter_taps):
    rows, width = values.shape
    blocks = lax.axis_size("seq")
    length = 2 * blocks * rows
    narrow = width // blocks
    whole_values, whole_taps = (
        lax.all_to_all(values, "seq", split_axis=1, concat_axis=0, tiled=True),
        lax.all_to_all(filter_taps, "seq", split_axis=1, concat_axis=0, tiled=True),
    )
    freq_ids = jnp.arange(2 * blocks, dtype=jnp.int32)
    block_ids = jnp.arange(blocks, dtype=jnp.int32)
    all_rows = jnp.arange(rows, dtype=jnp.int32)
    outer_cos, outer_sin = angle_table(freq_ids, block_ids, 2 * blocks)
    twist_cos, twist_sin = angle_table(freq_ids, all_rows, length)
    tables = (outer_cos, outer_sin, twist_cos, twist_sin, "ka,arc->krc")
    value_re, value_im = outer_forward(whole_values.reshape(blocks, rows, narrow), *tables)
    taps_re, taps_im = outer_forward(whole_taps.reshape(blocks, rows, narrow), *tables)
    inner_cos, inner_sin = angle_table(all_rows, all_rows, rows)
    back_re, back_im = inner_filter((value_re, value_im, taps_re, taps_im), inner_cos, inner_sin)
    turned_re, turned_im = untwist(back_re, back_im, twist_cos, twist_sin)
    final_cos, final_sin = angle_table(block_ids, freq_ids, 2 * blocks)
    signal = (
        mix("ak,krc->arc", final_cos, turned_re) - mix("ak,krc->arc", final_sin, turned_im)
    ) / length
    returned = lax.all_to_all(signal, "seq", split_axis=0, concat_axis=2, tiled=True)
    return returned[0]


def general_local(values, gates, filter_taps, skip_gain, out_weight):
    conv = channels_plan(values, filter_taps)
    gated = (
        gates.astype(jnp.float32) * (conv + skip_gain[None, :] * values.astype(jnp.float32))
    ).astype(jnp.bfloat16)
    projected = lax.psum_scatter(
        lax.dot_general(
            out_weight, gated, (((0,), (1,)), ((), ())), preferred_element_type=jnp.float32
        ),
        "chan",
        scatter_dimension=0,
        tiled=True,
    )
    return projected.astype(jnp.bfloat16)


def split_table(table):
    high = table.astype(ml_dtypes.bfloat16)
    low = (table - high.astype(np.float64)).astype(ml_dtypes.bfloat16)
    return high, low


@functools.lru_cache(maxsize=None)
def transform_tables(length):
    inner = length // RADIX
    k = np.arange(inner)[:, None]
    unit = TWO_PI / (4 * length)
    turns = (np.array(Q_ORDER)[:, None] * (4 * k.T + 1)) % (4 * length) * unit
    turns = np.stack([np.cos(turns), np.sin(turns)], axis=1).reshape(2 * RADIX, inner, 1)
    blocks = [np.broadcast_to(turns, (2 * RADIX, inner, LANES))]
    forward, backward = [], []
    for odd in range(2):
        m = 2 * np.arange(inner // 2)[None, :] + odd
        angles = (RADIX * m * (4 * k[: inner // 2] + 1)) % (4 * length) * unit
        table = np.concatenate([np.cos(angles), -np.sin(angles)], axis=0)
        forward.append(np.concatenate(split_table(table), axis=1))
        backward.append(np.concatenate(split_table(table.T / length), axis=0))
    for table in forward + backward:
        blocks.append(table.astype(np.float32).reshape(inner, -1, LANES).swapaxes(0, 1))
    return np.concatenate(blocks, axis=0).astype(np.float32)


def row_order(rows, turned_over=False):
    place = lax.broadcasted_iota(jnp.int32, (rows, rows), 1 if turned_over else 0)
    source = lax.broadcasted_iota(jnp.int32, (rows, rows), 0 if turned_over else 1)
    chunk = rows // RADIX
    index, within = place // chunk, place % chunk
    odd, j = within // (chunk // 2), within % (chunk // 2)
    wanted = RADIX * (2 * j + odd) + index // 4 + 4 * (index % 4)
    return jnp.where(source == wanted, 1.0, 0.0).astype(jnp.bfloat16)


def turn(point, index, sign):
    re, im = point
    index %= 16
    if index == 0:
        return point
    if index == 4:
        return (-im, re) if sign > 0 else (im, -re)
    if index == 8:
        return (-re, -im)
    half = math.sqrt(0.5)
    if index == 2:
        return ((re - im) * half, (re + im) * half) if sign > 0 else ((re + im) * half, (im - re) * half)
    if index == 6:
        return ((-re - im) * half, (re - im) * half) if sign > 0 else ((im - re) * half, (-re - im) * half)
    cos = math.cos(TWO_PI * index / 16)
    sin = sign * math.sin(TWO_PI * index / 16)
    return (re * cos - im * sin, re * sin + im * cos)


def four_points(points, sign):
    a, b, c, d = points
    ac = (a[0] + c[0], a[1] + c[1])
    am = (a[0] - c[0], a[1] - c[1])
    bd = (b[0] + d[0], b[1] + d[1])
    bm = (b[0] - d[0], b[1] - d[1])
    if sign < 0:
        side = (bm[1], -bm[0])
    else:
        side = (-bm[1], bm[0])
    return (
        (ac[0] + bd[0], ac[1] + bd[1]),
        (am[0] + side[0], am[1] + side[1]),
        (ac[0] - bd[0], ac[1] - bd[1]),
        (am[0] - side[0], am[1] - side[1]),
    )


def turned(point, cos, sin, sign):
    re, im = point
    if sign < 0:
        return (re * cos + im * sin, im * cos - re * sin)
    return (re * cos - im * sin, im * cos + re * sin)


def slot_order(blocks):
    half = blocks // 2
    across = [half + (i // 2 if i % 2 == 0 else half // 2 + i // 2) for i in range(half)]
    near = list(range(1, half)) + [0]
    return [slot for pair in zip(across, near) for slot in pair]


LEAD = 5


def lead_kernel(blocks, me_ref, values_hbm, taps_hbm, *rest):
    outs, (streams, sems) = rest[:LEAD], rest[LEAD:]
    loads = []
    for i, slot in enumerate(slot_order(blocks)[:LEAD]):
        lanes = pl.ds(pl.multiple_of((me_ref[0] ^ slot) * LANES, LANES), LANES)
        for side, source in enumerate((values_hbm, taps_hbm)):
            to = pl.ds((2 * i + side) * LANES, LANES)
            loads.append(pltpu.make_async_copy(source.at[:, lanes], streams.at[:, to], sems.at[2 * i + side]))
    for load in loads:
        load.start()
    order = row_order(streams.shape[0])
    for load in loads:
        load.wait()
    moved = jnp.dot(order, streams[...], preferred_element_type=jnp.float32).astype(jnp.bfloat16)
    for i, out in enumerate(outs):
        out[...] = moved[:, 2 * i * LANES : 2 * (i + 1) * LANES]


def arrange_kernel(pieces, blocks, me_ref, values_hbm, taps_hbm, *rest):
    outs, (values_ref, taps_ref, packed, sems) = rest[: blocks - LEAD], rest[blocks - LEAD :]
    piece = values_ref.shape[1] // pieces
    loads = []
    for part in range(pieces):
        lanes = pl.ds(part * piece, piece)
        loads.append(pltpu.make_async_copy(values_hbm.at[:, lanes], values_ref.at[:, lanes], sems.at[2 * part]))
        loads.append(pltpu.make_async_copy(taps_hbm.at[:, lanes], taps_ref.at[:, lanes], sems.at[2 * part + 1]))
    for load in loads:
        load.start()
    order = row_order(values_ref.shape[0])
    for part in range(pieces):
        loads[2 * part].wait()
        loads[2 * part + 1].wait()
        lanes = pl.ds(part * piece, piece)
        both = jnp.concatenate([values_ref[:, lanes], taps_ref[:, lanes]], axis=1)
        moved = jnp.dot(order, both, preferred_element_type=jnp.float32).astype(jnp.bfloat16)
        for block in range(piece // LANES):
            for side in range(2):
                start = side * piece + block * LANES
                packed[part * piece // LANES + block, :, pl.ds(side * LANES, LANES)] = moved[:, start : start + LANES]
    for out, slot in zip(outs, slot_order(blocks)[LEAD:]):
        out[...] = packed[me_ref[0] ^ slot]


def arrange(me, values, taps, blocks):
    rows, wide = values.shape
    pieces = 4
    block = jax.ShapeDtypeStruct((rows, 2 * LANES), jnp.bfloat16)
    in_specs = [pl.BlockSpec(memory_space=pltpu.SMEM)] + [pl.BlockSpec(memory_space=pl.ANY)] * 2
    lead = pl.pallas_call(
        functools.partial(lead_kernel, blocks),
        in_specs=in_specs,
        out_specs=[pl.BlockSpec(memory_space=pltpu.VMEM)] * LEAD,
        out_shape=[block] * LEAD,
        scratch_shapes=[
            pltpu.VMEM((rows, 2 * LEAD * LANES), jnp.bfloat16),
            pltpu.SemaphoreType.DMA((2 * LEAD,)),
        ],
        compiler_params=pltpu.CompilerParams(vmem_limit_bytes=FIRST_BYTES),
        cost_estimate=pl.CostEstimate(
            flops=4 * rows * rows * LEAD * LANES, bytes_accessed=8 * rows * LEAD * LANES, transcendentals=0
        ),
        name="arrange_lead",
    )(me, values, taps)
    others = pl.pallas_call(
        functools.partial(arrange_kernel, pieces, blocks),
        in_specs=in_specs,
        out_specs=[pl.BlockSpec(memory_space=pltpu.VMEM)] * (blocks - LEAD),
        out_shape=[block] * (blocks - LEAD),
        scratch_shapes=[
            pltpu.VMEM((rows, wide), jnp.bfloat16),
            pltpu.VMEM((rows, wide), jnp.bfloat16),
            pltpu.VMEM((blocks, rows, 2 * LANES), jnp.bfloat16),
            pltpu.SemaphoreType.DMA((2 * pieces,)),
        ],
        compiler_params=pltpu.CompilerParams(vmem_limit_bytes=ARRANGE_BYTES),
        cost_estimate=pl.CostEstimate(
            flops=4 * rows * rows * wide, bytes_accessed=8 * rows * wide, transcendentals=0
        ),
        name="arrange_others",
    )(me, values, taps)
    return [*lead, *others]


def convolve_kernel(blocks, me_ref, *rest):
    slots = rest[:blocks]
    convolve_blocks(me_ref, slots, *rest[blocks:])


def convolve_blocks(
    me_ref, slots, tables_hbm, out_hbm,
    streams, turns_ref, fixed, stages, raw_even, raw_odd, columns, mixed, halves_even, halves_odd, signals, sems,
):
    blocks, rows, _ = streams.shape
    chunk = rows // RADIX
    inner = blocks * chunk
    part_rows = inner // 2
    group = rows // 4
    raws = (raw_even, raw_odd)
    halves = (halves_even, halves_odd)
    count = fixed.shape[0]
    load_fixed = []
    for part in range(2):
        taken = pl.ds(part * count // 2, count // 2)
        source = tables_hbm.at[pl.ds(2 * RADIX + part * count // 2, count // 2)]
        load_fixed.append(pltpu.make_async_copy(source, fixed.at[taken], sems.at[10 * part]))
    load_turns, stores = [], []
    for low in range(4):
        taken = pl.ds(low * group, group)
        eight = pl.ds(8 * low, 8)
        load_turns.append(pltpu.make_async_copy(tables_hbm.at[eight], turns_ref.at[eight], sems.at[1 + low]))
        stores.append(pltpu.make_async_copy(signals.at[:, taken], out_hbm.at[:, taken], sems.at[5 + low]))
    load_fixed[0].start()
    for load in load_turns:
        load.start()
    load_fixed[1].start()
    own = pltpu.make_async_copy(slots[-1], streams.at[me_ref[0]], sems.at[9])
    own.start()
    for slot, source in zip(slot_order(blocks)[:-1], slots[:-1]):
        streams[me_ref[0] ^ slot] = source[...]
    own.wait()
    width = inner // LANES

    def take_stages(part):
        load_fixed[part].wait()
        for table in range(2 * part, 2 * part + 2):
            for block in range(width):
                stages[table, :, pl.ds(block * LANES, LANES)] = fixed[table * width + block].astype(jnp.bfloat16)

    take_stages(0)

    def transform(low, pair):
        sides = [[], []]
        for part in range(2):
            taken = pl.ds(pl.multiple_of(low * group + (2 * pair + part) * chunk, chunk), chunk)
            stream = streams[:, taken].astype(jnp.float32).reshape(blocks, 2, chunk // 2, 2 * LANES)
            for odd in range(2):
                sides[odd].append(stream[:, odd].reshape(part_rows, 2 * LANES).astype(jnp.bfloat16))
        for odd in range(2):
            both = jnp.concatenate(sides[odd], axis=1)
            result = jnp.dot(
                stages[odd], jnp.concatenate([both, both], axis=0), preferred_element_type=jnp.float32
            )
            for part in range(2):
                raws[low % 2][2 * pair + part, odd] = result[:, 2 * part * LANES : 2 * (part + 1) * LANES]

    def first_pass(low, start):
        raw = raws[low % 2]
        real, imaginary = pl.ds(start, 8), pl.ds(part_rows + start, 8)
        for side in range(2):
            lanes = pl.ds(side * LANES, LANES)
            points = [[], []]
            for high in range(4):
                even = (raw[high, 0, real, lanes], raw[high, 0, imaginary, lanes])
                odd = (raw[high, 1, real, lanes], raw[high, 1, imaginary, lanes])
                points[0].append((even[0] + odd[0], even[1] + odd[1]))
                points[1].append((even[0] - odd[0], even[1] - odd[1]))
            for part in range(2):
                upper, lower = pl.ds(part * part_rows + start, 8), pl.ds(inner + part * part_rows + start, 8)
                for high in range(4):
                    if low + high:
                        turns = [turns_ref[2 * (4 * low + high) + i, upper] for i in range(2)]
                        points[part][high] = turned(points[part][high], *turns, -1)
                for k, point in enumerate(four_points(points[part], -1)):
                    point = turn(point, low * k, -1)
                    columns[4 * low + k, upper, lanes] = point[0]
                    columns[4 * low + k, lower, lanes] = point[1]

    def first_rows(low, start, count):
        for part in range(count):
            first_pass(low, pl.multiple_of(start + 8 * part, 8))

    steps = part_rows // 2

    def alone(pair, carry):
        transform(0, pair)
        return carry

    lax.fori_loop(0, 2, alone, 0)
    for low in range(1, 4):
        load_turns[low - 1].wait()

        def beside(pair, carry, low=low):
            transform(low, pair)
            first_rows(low - 1, pair * steps, steps // 8)
            return carry

        lax.fori_loop(0, 2, beside, 0)
    load_turns[3].wait()

    def middle(index, carry):
        start = pl.multiple_of(index * 8, 8)
        first_pass(3, start)
        for part in range(2):
            upper, lower = pl.ds(part * part_rows + start, 8), pl.ds(inner + part * part_rows + start, 8)
            for k in range(4):
                sides = []
                for side in range(2):
                    lanes = pl.ds(side * LANES, LANES)
                    points = [
                        (columns[4 * low + k, upper, lanes], columns[4 * low + k, lower, lanes]) for low in range(4)
                    ]
                    sides.append(four_points(points, -1))
                product = [
                    (a[0] * b[0] - a[1] * b[1], a[0] * b[1] + a[1] * b[0]) for a, b in zip(*sides)
                ]
                for high, point in enumerate(four_points(product, 1)):
                    point = turn(point, k * high, 1)
                    mixed[4 * high + k, upper] = point[0]
                    mixed[4 * high + k, lower] = point[1]
        return carry

    lax.fori_loop(0, part_rows // 8, middle, 0)

    def last_pass(low, start):
        target = halves[low % 2]
        found = []
        for part in range(2):
            upper, lower = pl.ds(part * part_rows + start, 16), pl.ds(inner + part * part_rows + start, 16)
            points = list(four_points([(mixed[4 * low + k, upper], mixed[4 * low + k, lower]) for k in range(4)], 1))
            for high in range(4):
                if low + high:
                    turns = [turns_ref[2 * (4 * low + high) + i, upper] for i in range(2)]
                    points[high] = turned(points[high], *turns, 1)
            found.append(points)
        for high in range(4):
            for i in range(2):
                taken = pl.ds(i * part_rows + start, 16)
                first, second = found[0][high][i], found[1][high][i]
                for odd, value in enumerate((first + second, first - second)):
                    rounded = value.astype(jnp.bfloat16)
                    target[high, odd, taken, pl.ds(0, LANES)] = rounded
                    target[high, odd, taken, pl.ds(LANES, LANES)] = (value - rounded.astype(jnp.float32)).astype(
                        jnp.bfloat16
                    )

    def last_rows(low, start, count):
        for part in range(count):
            last_pass(low, pl.multiple_of(start + 16 * part, 16))

    def restore(low, pair):
        sides = []
        for odd in range(2):
            both = jnp.concatenate([halves[low % 2][2 * pair + part, odd] for part in range(2)], axis=1)
            terms = jnp.dot(stages[2 + odd], both, preferred_element_type=jnp.float32)
            found = []
            for part in range(2):
                first, second = [slice((2 * part + i) * LANES, (2 * part + i + 1) * LANES) for i in range(2)]
                signal = terms[:part_rows, first] + terms[:part_rows, second] + terms[part_rows:, first]
                found.append(signal.reshape(blocks, 1, chunk // 2, LANES))
            sides.append(found)
        for part in range(2):
            signal = jnp.concatenate([sides[0][part], sides[1][part]], axis=1).reshape(blocks, chunk, LANES)
            taken = pl.ds(pl.multiple_of(low * group + (2 * pair + part) * chunk, chunk), chunk)
            signals[:, taken] = signal.astype(jnp.bfloat16)

    def prepare(index, carry):
        last_rows(0, index * steps, steps // 16)
        return carry

    take_stages(1)
    lax.fori_loop(0, 2, prepare, 0)
    for low in range(4):

        def back(pair, carry, low=low):
            restore(low, pair)
            if low < 3:
                last_rows(low + 1, pair * steps, steps // 16)
            return carry

        lax.fori_loop(0, 2, back, 0)
        stores[low].start()
    for store in stores:
        store.wait()


def convolve(me, slots):
    blocks = len(slots)
    rows, lanes = slots[0].shape
    length = blocks * rows
    inner = length // RADIX
    tables = transform_tables(length)
    return pl.pallas_call(
        functools.partial(convolve_kernel, blocks),
        in_specs=[pl.BlockSpec(memory_space=pltpu.SMEM)]
        + [pl.BlockSpec(memory_space=pltpu.VMEM)] * (blocks - 1)
        + [pl.BlockSpec(memory_space=pl.ANY)] * 2,
        out_specs=pl.BlockSpec(memory_space=pl.ANY),
        out_shape=jax.ShapeDtypeStruct((blocks, rows, LANES), jnp.bfloat16),
        scratch_shapes=[
            pltpu.VMEM((blocks, rows, lanes), jnp.bfloat16),
            pltpu.VMEM((2 * RADIX, inner, LANES), jnp.float32),
            pltpu.VMEM((tables.shape[0] - 2 * RADIX, inner, LANES), jnp.float32),
            pltpu.VMEM((4, inner, inner), jnp.bfloat16),
            pltpu.VMEM((4, 2, inner, lanes), jnp.float32),
            pltpu.VMEM((4, 2, inner, lanes), jnp.float32),
            pltpu.VMEM((RADIX, 2 * inner, lanes), jnp.float32),
            pltpu.VMEM((RADIX, 2 * inner, LANES), jnp.float32),
            pltpu.VMEM((4, 2, inner, lanes), jnp.bfloat16),
            pltpu.VMEM((4, 2, inner, lanes), jnp.bfloat16),
            pltpu.VMEM((blocks, rows, LANES), jnp.bfloat16),
            pltpu.SemaphoreType.DMA((11,)),
        ],
        compiler_params=pltpu.CompilerParams(vmem_limit_bytes=CONV_BYTES),
        cost_estimate=pl.CostEstimate(flops=5 * 10**9, bytes_accessed=9 * 10**6, transcendentals=0),
        name="long_convolution",
    )(me, *slots, jnp.asarray(tables))


PIECES = 4


def weight_loads(weight_hbm, weight_ref, side, sems):
    width, features = weight_ref.shape
    columns = pl.ds(pl.multiple_of(side * features, features), features)
    deep = width // PIECES
    loads = []
    for part in range(PIECES):
        rows = pl.ds(part * deep, deep)
        loads.append(pltpu.make_async_copy(weight_hbm.at[rows, columns], weight_ref.at[rows], sems.at[part]))
        loads[part].start()
    return loads


def gate_kernel(
    half_ref, conv_ref, gates_hbm, values_hbm, skip_ref, weight_hbm, gated_ref, out_ref,
    gates_ref, values_ref, weight_ref, sems,
):
    blocks, rows, lanes = conv_ref.shape
    streams = [
        pltpu.make_async_copy(gates_hbm, gates_ref, sems.at[PIECES]),
        pltpu.make_async_copy(values_hbm, values_ref, sems.at[PIECES + 1]),
    ]
    for stream in streams:
        stream.start()
    loads = weight_loads(weight_hbm, weight_ref, 1 - half_ref[0], sems)
    order = row_order(rows, True)
    for stream in streams:
        stream.wait()
    group = blocks // PIECES
    wide = group * lanes
    for part in range(PIECES):
        taken = pl.ds(part * wide, wide)
        conv = jnp.concatenate([conv_ref[part * group + block] for block in range(group)], axis=1)
        conv = jnp.dot(order, conv, preferred_element_type=jnp.float32)
        direct = skip_ref[:, taken] * values_ref[:, taken].astype(jnp.float32)
        gated_ref[:, taken] = (gates_ref[:, taken].astype(jnp.float32) * (conv + direct)).astype(jnp.bfloat16)
    multiply_pieces(loads, gated_ref, weight_ref, out_ref)


def multiply_pieces(loads, gated_ref, weight_ref, out_ref):
    deep = weight_ref.shape[0] // PIECES
    for part in range(PIECES):
        taken = pl.ds(part * deep, deep)
        loads[part].wait()
        term = jnp.dot(gated_ref[:, taken], weight_ref[taken], preferred_element_type=jnp.float32)
        out_ref[...] = term if part == 0 else out_ref[...] + term


def gate_and_project(half, conv, gates, values, skip_gain, weight):
    rows, width = gates.shape
    features = weight.shape[1] // 2
    anywhere, inside = pl.BlockSpec(memory_space=pl.ANY), pl.BlockSpec(memory_space=pltpu.VMEM)
    return pl.pallas_call(
        gate_kernel,
        in_specs=[pl.BlockSpec(memory_space=pltpu.SMEM), inside, anywhere, anywhere, inside, anywhere],
        out_specs=[inside] * 2,
        out_shape=[
            jax.ShapeDtypeStruct((rows, width), jnp.bfloat16),
            jax.ShapeDtypeStruct((rows, features), jnp.float32),
        ],
        scratch_shapes=[
            pltpu.VMEM((rows, width), jnp.bfloat16),
            pltpu.VMEM((rows, width), jnp.bfloat16),
            pltpu.VMEM((width, features), jnp.bfloat16),
            pltpu.SemaphoreType.DMA((PIECES + 2,)),
        ],
        compiler_params=pltpu.CompilerParams(vmem_limit_bytes=TAIL_BYTES),
        cost_estimate=pl.CostEstimate(
            flops=2 * rows * width * features, bytes_accessed=2 * width * features, transcendentals=0
        ),
        name="gate_project_sent",
    )(half, conv, gates, values, skip_gain[None, :], weight)


def kept_kernel(half_ref, gated_ref, weight_hbm, out_ref, weight_ref, sems):
    multiply_pieces(weight_loads(weight_hbm, weight_ref, half_ref[0], sems), gated_ref, weight_ref, out_ref)


def project_kept(half, gated, weight):
    rows, width = gated.shape
    features = weight.shape[1] // 2
    inside = pl.BlockSpec(memory_space=pltpu.VMEM)
    return pl.pallas_call(
        kept_kernel,
        in_specs=[pl.BlockSpec(memory_space=pltpu.SMEM), inside, pl.BlockSpec(memory_space=pl.ANY)],
        out_specs=inside,
        out_shape=jax.ShapeDtypeStruct((rows, features), jnp.float32),
        scratch_shapes=[pltpu.VMEM((width, features), jnp.bfloat16), pltpu.SemaphoreType.DMA((PIECES,))],
        compiler_params=pltpu.CompilerParams(vmem_limit_bytes=TAIL_BYTES),
        cost_estimate=pl.CostEstimate(
            flops=2 * rows * width * features, bytes_accessed=2 * width * features, transcendentals=0
        ),
        name="project_kept",
    )(half, gated, weight)


def join_kernel(kept_ref, came_ref, out_hbm, out_ref, sems):
    wide = out_ref.shape[0] // PIECES
    stores = []
    for part in range(PIECES):
        taken = pl.ds(part * wide, wide)
        out_ref[taken] = (kept_ref[:, taken] + came_ref[:, taken]).astype(jnp.bfloat16).T
        stores.append(pltpu.make_async_copy(out_ref.at[taken], out_hbm.at[taken], sems.at[part]))
        stores[part].start()
    for store in stores:
        store.wait()


def join(kept, came):
    rows, features = kept.shape
    return pl.pallas_call(
        join_kernel,
        in_specs=[pl.BlockSpec(memory_space=pltpu.VMEM)] * 2,
        out_specs=pl.BlockSpec(memory_space=pl.ANY),
        out_shape=jax.ShapeDtypeStruct((features, rows), jnp.bfloat16),
        scratch_shapes=[pltpu.VMEM((features, rows), jnp.bfloat16), pltpu.SemaphoreType.DMA((PIECES,))],
        compiler_params=pltpu.CompilerParams(vmem_limit_bytes=TAIL_BYTES),
        name="join_halves",
    )(kept, came)


def swap_blocks(array):
    return lax.all_to_all(array, "seq", split_axis=0, concat_axis=0, tiled=True)


def exchange(slots):
    blocks = len(slots)
    return [
        lax.ppermute(source, "seq", [(j, j ^ slot) for j in range(blocks)]) if slot else source
        for slot, source in zip(slot_order(blocks), slots)
    ]


def kernel_local(values, gates, filter_taps, skip_gain, out_weight):
    blocks = lax.axis_size("seq")
    me = lax.axis_index("seq").astype(jnp.int32)[None]
    half = lax.axis_index("chan").astype(jnp.int32)[None]
    conv = convolve(me, exchange(arrange(me, values, filter_taps, blocks)))
    gated, sent = gate_and_project(half, swap_blocks(conv), gates, values, skip_gain, out_weight)
    other = lax.ppermute(sent, "chan", [(0, 1), (1, 0)])
    kept = project_kept(half, gated, out_weight)
    return join(kept, other)


def takes_kernels(mesh, values, out_weight):
    blocks, halves = mesh.shape["seq"], mesh.shape["chan"]
    rows = values.shape[0] // blocks
    return (
        halves == 2
        and blocks == 16
        and rows == 256
        and values.shape[1] == halves * blocks * LANES
        and out_weight.shape[1] % (8 * LANES) == 0
    )


def solution(mesh):
    placed = (P("seq", "chan"), P("seq", "chan"), P("seq", "chan"), P("chan"), P("chan", None))

    def whole(values, gates, filter_taps, skip_gain, out_weight):
        local = kernel_local if takes_kernels(mesh, values, out_weight) else general_local
        return jax.shard_map(
            local, mesh=mesh, in_specs=placed, out_specs=P("chan", "seq"), check_vma=False
        )(values, gates, filter_taps, skip_gain, out_weight)

    return whole
```

```python
import functools
import math

import jax
import jax.numpy as jnp
import ml_dtypes
import numpy as np
from jax import lax
from jax.experimental import pallas as pl
from jax.experimental.pallas import tpu as pltpu
from jax.sharding import PartitionSpec as P

TWO_PI = 2.0 * math.pi
HIGH = lax.Precision.HIGHEST
RADIX = 16
LANES = 128
Q_ORDER = [low + 4 * high for low in range(4) for high in range(4)]
FIRST_BYTES = 60 * 1024 * 1024
ARRANGE_BYTES = 12 * 1024 * 1024
CONV_BYTES = 49 * 1024 * 1024
TAIL_BYTES = 49 * 1024 * 1024


def angle_table(first, second, period):
    product = first[:, None] * second[None, :] % period
    angles = product.astype(jnp.float32) * (TWO_PI / period)
    return (jnp.cos(angles), jnp.sin(angles))


def mix(equation, left, right):
    return jnp.einsum(equation, left, right, precision=HIGH)


def outer_forward(data, outer_cos, outer_sin, twist_cos, twist_sin, equation):
    source = data.astype(jnp.float32)
    real = mix(equation, outer_cos, source)
    imag = -mix(equation, outer_sin, source)
    cos_part = twist_cos[:, :, None]
    sin_part = twist_sin[:, :, None]
    return (real * cos_part + imag * sin_part, imag * cos_part - real * sin_part)


def inner_filter(spectra, inner_cos, inner_sin):
    value_re, value_im, taps_re, taps_im = spectra

    def forward(real, imag):
        out_re = mix("kr,jrc->jkc", inner_cos, real) + mix("kr,jrc->jkc", inner_sin, imag)
        out_im = mix("kr,jrc->jkc", inner_cos, imag) - mix("kr,jrc->jkc", inner_sin, real)
        return (out_re, out_im)

    value_fre, value_fim = forward(value_re, value_im)
    taps_fre, taps_fim = forward(taps_re, taps_im)
    prod_re = value_fre * taps_fre - value_fim * taps_fim
    prod_im = value_fre * taps_fim + value_fim * taps_fre
    back_re = mix("rk,jkc->jrc", inner_cos, prod_re) - mix("rk,jkc->jrc", inner_sin, prod_im)
    back_im = mix("rk,jkc->jrc", inner_cos, prod_im) + mix("rk,jkc->jrc", inner_sin, prod_re)
    return (back_re, back_im)


def untwist(real, imag, twist_cos, twist_sin):
    cos_part = twist_cos[:, :, None]
    sin_part = twist_sin[:, :, None]
    return (real * cos_part - imag * sin_part, imag * cos_part + real * sin_part)


def channels_plan(values, filter_taps):
    rows, width = values.shape
    blocks = lax.axis_size("seq")
    length = 2 * blocks * rows
    narrow = width // blocks
    whole_values, whole_taps = (
        lax.all_to_all(values, "seq", split_axis=1, concat_axis=0, tiled=True),
        lax.all_to_all(filter_taps, "seq", split_axis=1, concat_axis=0, tiled=True),
    )
    freq_ids = jnp.arange(2 * blocks, dtype=jnp.int32)
    block_ids = jnp.arange(blocks, dtype=jnp.int32)
    all_rows = jnp.arange(rows, dtype=jnp.int32)
    outer_cos, outer_sin = angle_table(freq_ids, block_ids, 2 * blocks)
    twist_cos, twist_sin = angle_table(freq_ids, all_rows, length)
    tables = (outer_cos, outer_sin, twist_cos, twist_sin, "ka,arc->krc")
    value_re, value_im = outer_forward(whole_values.reshape(blocks, rows, narrow), *tables)
    taps_re, taps_im = outer_forward(whole_taps.reshape(blocks, rows, narrow), *tables)
    inner_cos, inner_sin = angle_table(all_rows, all_rows, rows)
    back_re, back_im = inner_filter((value_re, value_im, taps_re, taps_im), inner_cos, inner_sin)
    turned_re, turned_im = untwist(back_re, back_im, twist_cos, twist_sin)
    final_cos, final_sin = angle_table(block_ids, freq_ids, 2 * blocks)
    signal = (
        mix("ak,krc->arc", final_cos, turned_re) - mix("ak,krc->arc", final_sin, turned_im)
    ) / length
    returned = lax.all_to_all(signal, "seq", split_axis=0, concat_axis=2, tiled=True)
    return returned[0]


def general_local(values, gates, filter_taps, skip_gain, out_weight):
    conv = channels_plan(values, filter_taps)
    gated = (
        gates.astype(jnp.float32) * (conv + skip_gain[None, :] * values.astype(jnp.float32))
    ).astype(jnp.bfloat16)
    projected = lax.psum_scatter(
        lax.dot_general(
            out_weight, gated, (((0,), (1,)), ((), ())), preferred_element_type=jnp.float32
        ),
        "chan",
        scatter_dimension=0,
        tiled=True,
    )
    return projected.astype(jnp.bfloat16)


def split_table(table):
    high = table.astype(ml_dtypes.bfloat16)
    low = (table - high.astype(np.float64)).astype(ml_dtypes.bfloat16)
    return high, low


@functools.lru_cache(maxsize=None)
def transform_tables(length):
    inner = length // RADIX
    k = np.arange(inner)[:, None]
    unit = TWO_PI / (4 * length)
    turns = (np.array(Q_ORDER)[:, None] * (4 * k.T + 1)) % (4 * length) * unit
    turns = np.stack([np.cos(turns), np.sin(turns)], axis=1).reshape(2 * RADIX, inner, 1)
    blocks = [np.broadcast_to(turns, (2 * RADIX, inner, LANES))]
    forward, backward = [], []
    for odd in range(2):
        m = 2 * np.arange(inner // 2)[None, :] + odd
        angles = (RADIX * m * (4 * k[: inner // 2] + 1)) % (4 * length) * unit
        table = np.concatenate([np.cos(angles), -np.sin(angles)], axis=0)
        forward.append(np.concatenate(split_table(table), axis=1))
        backward.append(np.concatenate(split_table(table.T / length), axis=0))
    for table in forward + backward:
        blocks.append(table.astype(np.float32).reshape(inner, -1, LANES).swapaxes(0, 1))
    return np.concatenate(blocks, axis=0).astype(np.float32)


def row_order(rows, turned_over=False):
    place = lax.broadcasted_iota(jnp.int32, (rows, rows), 1 if turned_over else 0)
    source = lax.broadcasted_iota(jnp.int32, (rows, rows), 0 if turned_over else 1)
    chunk = rows // RADIX
    index, within = place // chunk, place % chunk
    odd, j = within // (chunk // 2), within % (chunk // 2)
    wanted = RADIX * (2 * j + odd) + index // 4 + 4 * (index % 4)
    return jnp.where(source == wanted, 1.0, 0.0).astype(jnp.bfloat16)


def turn(point, index, sign):
    re, im = point
    index %= 16
    if index == 0:
        return point
    if index == 4:
        return (-im, re) if sign > 0 else (im, -re)
    if index == 8:
        return (-re, -im)
    half = math.sqrt(0.5)
    if index == 2:
        return ((re - im) * half, (re + im) * half) if sign > 0 else ((re + im) * half, (im - re) * half)
    if index == 6:
        return ((-re - im) * half, (re - im) * half) if sign > 0 else ((im - re) * half, (-re - im) * half)
    cos = math.cos(TWO_PI * index / 16)
    sin = sign * math.sin(TWO_PI * index / 16)
    return (re * cos - im * sin, re * sin + im * cos)


def four_points(points, sign):
    a, b, c, d = points
    ac = (a[0] + c[0], a[1] + c[1])
    am = (a[0] - c[0], a[1] - c[1])
    bd = (b[0] + d[0], b[1] + d[1])
    bm = (b[0] - d[0], b[1] - d[1])
    if sign < 0:
        side = (bm[1], -bm[0])
    else:
        side = (-bm[1], bm[0])
    return (
        (ac[0] + bd[0], ac[1] + bd[1]),
        (am[0] + side[0], am[1] + side[1]),
        (ac[0] - bd[0], ac[1] - bd[1]),
        (am[0] - side[0], am[1] - side[1]),
    )


def turned(point, cos, sin, sign):
    re, im = point
    if sign < 0:
        return (re * cos + im * sin, im * cos - re * sin)
    return (re * cos - im * sin, im * cos + re * sin)


def slot_order(blocks):
    half = blocks // 2
    across = [half + (i // 2 if i % 2 == 0 else half // 2 + i // 2) for i in range(half)]
    near = list(range(1, half)) + [0]
    return [slot for pair in zip(across, near) for slot in pair]


LEAD = 5


def lead_kernel(blocks, me_ref, values_hbm, taps_hbm, *rest):
    outs, (streams, sems) = rest[:LEAD], rest[LEAD:]
    loads = []
    for i, slot in enumerate(slot_order(blocks)[:LEAD]):
        lanes = pl.ds(pl.multiple_of((me_ref[0] ^ slot) * LANES, LANES), LANES)
        for side, source in enumerate((values_hbm, taps_hbm)):
            to = pl.ds((2 * i + side) * LANES, LANES)
            loads.append(pltpu.make_async_copy(source.at[:, lanes], streams.at[:, to], sems.at[2 * i + side]))
    for load in loads:
        load.start()
    order = row_order(streams.shape[0])
    for load in loads:
        load.wait()
    moved = jnp.dot(order, streams[...], preferred_element_type=jnp.float32).astype(jnp.bfloat16)
    for i, out in enumerate(outs):
        out[...] = moved[:, 2 * i * LANES : 2 * (i + 1) * LANES]


def arrange_kernel(pieces, blocks, me_ref, values_hbm, taps_hbm, *rest):
    outs, (values_ref, taps_ref, packed, sems) = rest[: blocks - LEAD], rest[blocks - LEAD :]
    piece = values_ref.shape[1] // pieces
    loads = []
    for part in range(pieces):
        lanes = pl.ds(part * piece, piece)
        loads.append(pltpu.make_async_copy(values_hbm.at[:, lanes], values_ref.at[:, lanes], sems.at[2 * part]))
        loads.append(pltpu.make_async_copy(taps_hbm.at[:, lanes], taps_ref.at[:, lanes], sems.at[2 * part + 1]))
    for load in loads:
        load.start()
    order = row_order(values_ref.shape[0])
    for part in range(pieces):
        loads[2 * part].wait()
        loads[2 * part + 1].wait()
        lanes = pl.ds(part * piece, piece)
        both = jnp.concatenate([values_ref[:, lanes], taps_ref[:, lanes]], axis=1)
        moved = jnp.dot(order, both, preferred_element_type=jnp.float32).astype(jnp.bfloat16)
        for block in range(piece // LANES):
            for side in range(2):
                start = side * piece + block * LANES
                packed[part * piece // LANES + block, :, pl.ds(side * LANES, LANES)] = moved[:, start : start + LANES]
    for out, slot in zip(outs, slot_order(blocks)[LEAD:]):
        out[...] = packed[me_ref[0] ^ slot]


def arrange(me, values, taps, blocks):
    rows, wide = values.shape
    pieces = 4
    block = jax.ShapeDtypeStruct((rows, 2 * LANES), jnp.bfloat16)
    in_specs = [pl.BlockSpec(memory_space=pltpu.SMEM)] + [pl.BlockSpec(memory_space=pl.ANY)] * 2
    lead = pl.pallas_call(
        functools.partial(lead_kernel, blocks),
        in_specs=in_specs,
        out_specs=[pl.BlockSpec(memory_space=pltpu.VMEM)] * LEAD,
        out_shape=[block] * LEAD,
        scratch_shapes=[
            pltpu.VMEM((rows, 2 * LEAD * LANES), jnp.bfloat16),
            pltpu.SemaphoreType.DMA((2 * LEAD,)),
        ],
        compiler_params=pltpu.CompilerParams(vmem_limit_bytes=FIRST_BYTES),
        cost_estimate=pl.CostEstimate(
            flops=4 * rows * rows * LEAD * LANES, bytes_accessed=8 * rows * LEAD * LANES, transcendentals=0
        ),
        name="arrange_lead",
    )(me, values, taps)
    others = pl.pallas_call(
        functools.partial(arrange_kernel, pieces, blocks),
        in_specs=in_specs,
        out_specs=[pl.BlockSpec(memory_space=pltpu.VMEM)] * (blocks - LEAD),
        out_shape=[block] * (blocks - LEAD),
        scratch_shapes=[
            pltpu.VMEM((rows, wide), jnp.bfloat16),
            pltpu.VMEM((rows, wide), jnp.bfloat16),
            pltpu.VMEM((blocks, rows, 2 * LANES), jnp.bfloat16),
            pltpu.SemaphoreType.DMA((2 * pieces,)),
        ],
        compiler_params=pltpu.CompilerParams(vmem_limit_bytes=ARRANGE_BYTES),
        cost_estimate=pl.CostEstimate(
            flops=4 * rows * rows * wide, bytes_accessed=8 * rows * wide, transcendentals=0
        ),
        name="arrange_others",
    )(me, values, taps)
    return [*lead, *others]


def convolve_kernel(blocks, me_ref, *rest):
    slots = rest[:blocks]
    convolve_blocks(me_ref, slots, *rest[blocks:])


def convolve_blocks(
    me_ref, slots, tables_hbm, out_hbm,
    streams, turns_ref, fixed, stages, raw_even, raw_odd, columns, mixed, halves_even, halves_odd, signals, sems,
):
    blocks, rows, _ = streams.shape
    chunk = rows // RADIX
    inner = blocks * chunk
    part_rows = inner // 2
    group = rows // 4
    raws = (raw_even, raw_odd)
    halves = (halves_even, halves_odd)
    count = fixed.shape[0]
    load_fixed = []
    for part in range(2):
        taken = pl.ds(part * count // 2, count // 2)
        source = tables_hbm.at[pl.ds(2 * RADIX + part * count // 2, count // 2)]
        load_fixed.append(pltpu.make_async_copy(source, fixed.at[taken], sems.at[10 * part]))
    load_turns, stores = [], []
    for low in range(4):
        taken = pl.ds(low * group, group)
        eight = pl.ds(8 * low, 8)
        load_turns.append(pltpu.make_async_copy(tables_hbm.at[eight], turns_ref.at[eight], sems.at[1 + low]))
        stores.append(pltpu.make_async_copy(signals.at[:, taken], out_hbm.at[:, taken], sems.at[5 + low]))
    load_fixed[0].start()
    for load in load_turns:
        load.start()
    load_fixed[1].start()
    own = pltpu.make_async_copy(slots[-1], streams.at[me_ref[0]], sems.at[9])
    own.start()
    for slot, source in zip(slot_order(blocks)[:-1], slots[:-1]):
        streams[me_ref[0] ^ slot] = source[...]
    own.wait()
    width = inner // LANES

    def take_stages(part):
        load_fixed[part].wait()
        for table in range(2 * part, 2 * part + 2):
            for block in range(width):
                stages[table, :, pl.ds(block * LANES, LANES)] = fixed[table * width + block].astype(jnp.bfloat16)

    take_stages(0)

    def transform(low, pair):
        sides = [[], []]
        for part in range(2):
            taken = pl.ds(pl.multiple_of(low * group + (2 * pair + part) * chunk, chunk), chunk)
            stream = streams[:, taken].astype(jnp.float32).reshape(blocks, 2, chunk // 2, 2 * LANES)
            for odd in range(2):
                sides[odd].append(stream[:, odd].reshape(part_rows, 2 * LANES).astype(jnp.bfloat16))
        for odd in range(2):
            both = jnp.concatenate(sides[odd], axis=1)
            result = jnp.dot(
                stages[odd], jnp.concatenate([both, both], axis=0), preferred_element_type=jnp.float32
            )
            for part in range(2):
                raws[low % 2][2 * pair + part, odd] = result[:, 2 * part * LANES : 2 * (part + 1) * LANES]

    def first_pass(low, start):
        raw = raws[low % 2]
        real, imaginary = pl.ds(start, 8), pl.ds(part_rows + start, 8)
        for side in range(2):
            lanes = pl.ds(side * LANES, LANES)
            points = [[], []]
            for high in range(4):
                even = (raw[high, 0, real, lanes], raw[high, 0, imaginary, lanes])
                odd = (raw[high, 1, real, lanes], raw[high, 1, imaginary, lanes])
                points[0].append((even[0] + odd[0], even[1] + odd[1]))
                points[1].append((even[0] - odd[0], even[1] - odd[1]))
            for part in range(2):
                upper, lower = pl.ds(part * part_rows + start, 8), pl.ds(inner + part * part_rows + start, 8)
                for high in range(4):
                    if low + high:
                        turns = [turns_ref[2 * (4 * low + high) + i, upper] for i in range(2)]
                        points[part][high] = turned(points[part][high], *turns, -1)
                for k, point in enumerate(four_points(points[part], -1)):
                    point = turn(point, low * k, -1)
                    columns[4 * low + k, upper, lanes] = point[0]
                    columns[4 * low + k, lower, lanes] = point[1]

    def first_rows(low, start, count):
        for part in range(count):
            first_pass(low, pl.multiple_of(start + 8 * part, 8))

    steps = part_rows // 2

    def alone(pair, carry):
        transform(0, pair)
        return carry

    lax.fori_loop(0, 2, alone, 0, unroll=True)
    for low in range(1, 4):
        load_turns[low - 1].wait()

        def beside(pair, carry, low=low):
            transform(low, pair)
            first_rows(low - 1, pair * steps, steps // 8)
            return carry

        lax.fori_loop(0, 2, beside, 0)
    load_turns[3].wait()

    def middle(index, carry):
        start = pl.multiple_of(index * 8, 8)
        first_pass(3, start)
        for part in range(2):
            upper, lower = pl.ds(part * part_rows + start, 8), pl.ds(inner + part * part_rows + start, 8)
            for k in range(4):
                sides = []
                for side in range(2):
                    lanes = pl.ds(side * LANES, LANES)
                    points = [
                        (columns[4 * low + k, upper, lanes], columns[4 * low + k, lower, lanes]) for low in range(4)
                    ]
                    sides.append(four_points(points, -1))
                product = [
                    (a[0] * b[0] - a[1] * b[1], a[0] * b[1] + a[1] * b[0]) for a, b in zip(*sides)
                ]
                for high, point in enumerate(four_points(product, 1)):
                    point = turn(point, k * high, 1)
                    mixed[4 * high + k, upper] = point[0]
                    mixed[4 * high + k, lower] = point[1]
        return carry

    lax.fori_loop(0, part_rows // 8, middle, 0, unroll=2)

    def last_pass(low, start):
        target = halves[low % 2]
        found = []
        for part in range(2):
            upper, lower = pl.ds(part * part_rows + start, 16), pl.ds(inner + part * part_rows + start, 16)
            points = list(four_points([(mixed[4 * low + k, upper], mixed[4 * low + k, lower]) for k in range(4)], 1))
            for high in range(4):
                if low + high:
                    turns = [turns_ref[2 * (4 * low + high) + i, upper] for i in range(2)]
                    points[high] = turned(points[high], *turns, 1)
            found.append(points)
        for high in range(4):
            for i in range(2):
                taken = pl.ds(i * part_rows + start, 16)
                first, second = found[0][high][i], found[1][high][i]
                for odd, value in enumerate((first + second, first - second)):
                    rounded = value.astype(jnp.bfloat16)
                    target[high, odd, taken, pl.ds(0, LANES)] = rounded
                    target[high, odd, taken, pl.ds(LANES, LANES)] = (value - rounded.astype(jnp.float32)).astype(
                        jnp.bfloat16
                    )

    def last_rows(low, start, count):
        for part in range(count):
            last_pass(low, pl.multiple_of(start + 16 * part, 16))

    def restore(low, pair):
        sides = []
        for odd in range(2):
            both = jnp.concatenate([halves[low % 2][2 * pair + part, odd] for part in range(2)], axis=1)
            terms = jnp.dot(stages[2 + odd], both, preferred_element_type=jnp.float32)
            found = []
            for part in range(2):
                first, second = [slice((2 * part + i) * LANES, (2 * part + i + 1) * LANES) for i in range(2)]
                signal = terms[:part_rows, first] + terms[:part_rows, second] + terms[part_rows:, first]
                found.append(signal.reshape(blocks, 1, chunk // 2, LANES))
            sides.append(found)
        for part in range(2):
            signal = jnp.concatenate([sides[0][part], sides[1][part]], axis=1).reshape(blocks, chunk, LANES)
            taken = pl.ds(pl.multiple_of(low * group + (2 * pair + part) * chunk, chunk), chunk)
            signals[:, taken] = signal.astype(jnp.bfloat16)

    def prepare(index, carry):
        last_rows(0, index * steps, steps // 16)
        return carry

    take_stages(1)
    lax.fori_loop(0, 2, prepare, 0)
    for low in range(4):

        def back(pair, carry, low=low):
            restore(low, pair)
            if low < 3:
                last_rows(low + 1, pair * steps, steps // 16)
            return carry

        lax.fori_loop(0, 2, back, 0)
        stores[low].start()
    for store in stores:
        store.wait()


def convolve(me, slots):
    blocks = len(slots)
    rows, lanes = slots[0].shape
    length = blocks * rows
    inner = length // RADIX
    tables = transform_tables(length)
    return pl.pallas_call(
        functools.partial(convolve_kernel, blocks),
        in_specs=[pl.BlockSpec(memory_space=pltpu.SMEM)]
        + [pl.BlockSpec(memory_space=pltpu.VMEM)] * (blocks - 1)
        + [pl.BlockSpec(memory_space=pl.ANY)] * 2,
        out_specs=pl.BlockSpec(memory_space=pl.ANY),
        out_shape=jax.ShapeDtypeStruct((blocks, rows, LANES), jnp.bfloat16),
        scratch_shapes=[
            pltpu.VMEM((blocks, rows, lanes), jnp.bfloat16),
            pltpu.VMEM((2 * RADIX, inner, LANES), jnp.float32),
            pltpu.VMEM((tables.shape[0] - 2 * RADIX, inner, LANES), jnp.float32),
            pltpu.VMEM((4, inner, inner), jnp.bfloat16),
            pltpu.VMEM((4, 2, inner, lanes), jnp.float32),
            pltpu.VMEM((4, 2, inner, lanes), jnp.float32),
            pltpu.VMEM((RADIX, 2 * inner, lanes), jnp.float32),
            pltpu.VMEM((RADIX, 2 * inner, LANES), jnp.float32),
            pltpu.VMEM((4, 2, inner, lanes), jnp.bfloat16),
            pltpu.VMEM((4, 2, inner, lanes), jnp.bfloat16),
            pltpu.VMEM((blocks, rows, LANES), jnp.bfloat16),
            pltpu.SemaphoreType.DMA((11,)),
        ],
        compiler_params=pltpu.CompilerParams(vmem_limit_bytes=CONV_BYTES),
        cost_estimate=pl.CostEstimate(flops=5 * 10**9, bytes_accessed=9 * 10**6, transcendentals=0),
        name="long_convolution",
    )(me, *slots, jnp.asarray(tables))


PIECES = 4


def weight_loads(weight_hbm, weight_ref, side, sems):
    width, features = weight_ref.shape
    columns = pl.ds(pl.multiple_of(side * features, features), features)
    deep = width // PIECES
    loads = []
    for part in range(PIECES):
        rows = pl.ds(part * deep, deep)
        loads.append(pltpu.make_async_copy(weight_hbm.at[rows, columns], weight_ref.at[rows], sems.at[part]))
        loads[part].start()
    return loads


def gate_kernel(
    half_ref, conv_ref, gates_hbm, values_hbm, skip_ref, weight_hbm, gated_ref, out_ref,
    gates_ref, values_ref, weight_ref, sems,
):
    blocks, rows, lanes = conv_ref.shape
    streams = [
        pltpu.make_async_copy(gates_hbm, gates_ref, sems.at[PIECES]),
        pltpu.make_async_copy(values_hbm, values_ref, sems.at[PIECES + 1]),
    ]
    for stream in streams:
        stream.start()
    loads = weight_loads(weight_hbm, weight_ref, 1 - half_ref[0], sems)
    order = row_order(rows, True)
    for stream in streams:
        stream.wait()
    group = blocks // PIECES
    wide = group * lanes
    for part in range(PIECES):
        taken = pl.ds(part * wide, wide)
        conv = jnp.concatenate([conv_ref[part * group + block] for block in range(group)], axis=1)
        conv = jnp.dot(order, conv, preferred_element_type=jnp.float32)
        direct = skip_ref[:, taken] * values_ref[:, taken].astype(jnp.float32)
        gated_ref[:, taken] = (gates_ref[:, taken].astype(jnp.float32) * (conv + direct)).astype(jnp.bfloat16)
    multiply_pieces(loads, gated_ref, weight_ref, out_ref)


def multiply_pieces(loads, gated_ref, weight_ref, out_ref):
    deep = weight_ref.shape[0] // PIECES
    for part in range(PIECES):
        taken = pl.ds(part * deep, deep)
        loads[part].wait()
        term = jnp.dot(gated_ref[:, taken], weight_ref[taken], preferred_element_type=jnp.float32)
        out_ref[...] = term if part == 0 else out_ref[...] + term


def gate_and_project(half, conv, gates, values, skip_gain, weight):
    rows, width = gates.shape
    features = weight.shape[1] // 2
    anywhere, inside = pl.BlockSpec(memory_space=pl.ANY), pl.BlockSpec(memory_space=pltpu.VMEM)
    return pl.pallas_call(
        gate_kernel,
        in_specs=[pl.BlockSpec(memory_space=pltpu.SMEM), inside, anywhere, anywhere, inside, anywhere],
        out_specs=[inside] * 2,
        out_shape=[
            jax.ShapeDtypeStruct((rows, width), jnp.bfloat16),
            jax.ShapeDtypeStruct((rows, features), jnp.float32),
        ],
        scratch_shapes=[
            pltpu.VMEM((rows, width), jnp.bfloat16),
            pltpu.VMEM((rows, width), jnp.bfloat16),
            pltpu.VMEM((width, features), jnp.bfloat16),
            pltpu.SemaphoreType.DMA((PIECES + 2,)),
        ],
        compiler_params=pltpu.CompilerParams(vmem_limit_bytes=TAIL_BYTES),
        cost_estimate=pl.CostEstimate(
            flops=2 * rows * width * features, bytes_accessed=2 * width * features, transcendentals=0
        ),
        name="gate_project_sent",
    )(half, conv, gates, values, skip_gain[None, :], weight)


def kept_kernel(half_ref, gated_ref, weight_hbm, out_ref, weight_ref, sems):
    multiply_pieces(weight_loads(weight_hbm, weight_ref, half_ref[0], sems), gated_ref, weight_ref, out_ref)


def project_kept(half, gated, weight):
    rows, width = gated.shape
    features = weight.shape[1] // 2
    inside = pl.BlockSpec(memory_space=pltpu.VMEM)
    return pl.pallas_call(
        kept_kernel,
        in_specs=[pl.BlockSpec(memory_space=pltpu.SMEM), inside, pl.BlockSpec(memory_space=pl.ANY)],
        out_specs=inside,
        out_shape=jax.ShapeDtypeStruct((rows, features), jnp.float32),
        scratch_shapes=[pltpu.VMEM((width, features), jnp.bfloat16), pltpu.SemaphoreType.DMA((PIECES,))],
        compiler_params=pltpu.CompilerParams(vmem_limit_bytes=TAIL_BYTES),
        cost_estimate=pl.CostEstimate(
            flops=2 * rows * width * features, bytes_accessed=2 * width * features, transcendentals=0
        ),
        name="project_kept",
    )(half, gated, weight)


def join_kernel(kept_ref, came_ref, out_hbm, out_ref, sems):
    wide = out_ref.shape[0] // PIECES
    stores = []
    for part in range(PIECES):
        taken = pl.ds(part * wide, wide)
        out_ref[taken] = (kept_ref[:, taken] + came_ref[:, taken]).astype(jnp.bfloat16).T
        stores.append(pltpu.make_async_copy(out_ref.at[taken], out_hbm.at[taken], sems.at[part]))
        stores[part].start()
    for store in stores:
        store.wait()


def join(kept, came):
    rows, features = kept.shape
    return pl.pallas_call(
        join_kernel,
        in_specs=[pl.BlockSpec(memory_space=pltpu.VMEM)] * 2,
        out_specs=pl.BlockSpec(memory_space=pl.ANY),
        out_shape=jax.ShapeDtypeStruct((features, rows), jnp.bfloat16),
        scratch_shapes=[pltpu.VMEM((features, rows), jnp.bfloat16), pltpu.SemaphoreType.DMA((PIECES,))],
        compiler_params=pltpu.CompilerParams(vmem_limit_bytes=TAIL_BYTES),
        name="join_halves",
    )(kept, came)


def swap_blocks(array):
    return lax.all_to_all(array, "seq", split_axis=0, concat_axis=0, tiled=True)


def exchange(slots):
    blocks = len(slots)
    return [
        lax.ppermute(source, "seq", [(j, j ^ slot) for j in range(blocks)]) if slot else source
        for slot, source in zip(slot_order(blocks), slots)
    ]


def kernel_local(values, gates, filter_taps, skip_gain, out_weight):
    blocks = lax.axis_size("seq")
    me = lax.axis_index("seq").astype(jnp.int32)[None]
    half = lax.axis_index("chan").astype(jnp.int32)[None]
    conv = convolve(me, exchange(arrange(me, values, filter_taps, blocks)))
    gated, sent = gate_and_project(half, swap_blocks(conv), gates, values, skip_gain, out_weight)
    other = lax.ppermute(sent, "chan", [(0, 1), (1, 0)])
    kept = project_kept(half, gated, out_weight)
    return join(kept, other)


def takes_kernels(mesh, values, out_weight):
    blocks, halves = mesh.shape["seq"], mesh.shape["chan"]
    rows = values.shape[0] // blocks
    return (
        halves == 2
        and blocks == 16
        and rows == 256
        and values.shape[1] == halves * blocks * LANES
        and out_weight.shape[1] % (8 * LANES) == 0
    )


def solution(mesh):
    placed = (P("seq", "chan"), P("seq", "chan"), P("seq", "chan"), P("chan"), P("chan", None))

    def whole(values, gates, filter_taps, skip_gain, out_weight):
        local = kernel_local if takes_kernels(mesh, values, out_weight) else general_local
        return jax.shard_map(
            local, mesh=mesh, in_specs=placed, out_specs=P("chan", "seq"), check_vma=False
        )(values, gates, filter_taps, skip_gain, out_weight)

    return whole
```
